32 devices in a mesh: gx: 8 (over z, y), gy: 4 (over x, core).
Axes of the slice: x: 2, y: 2, z: 4, core: 2. Of those that a mesh axis runs over, the one named last changes fastest.
Arguments:
- intensity: float32 [512, 512, 512], P('gx', 'gy'), may hold values from -48 to 48
- template: int32 [32, 32, 32], replicated, may hold values from 0 to 1, as said below
Outputs:
- pdf: float32 [512, 512, 512], P('gx', 'gy')
The draws below stay inside these ranges and needn't reach their ends.
Inputs may be any that keep to these rules, and one draw needn't show every extreme that they name: template marks the cells of the period near its corner, within a drawn radius, and a few other cells.
All inputs are finite; a program needn't handle non-finite values.
Results may differ from the reference program's by a relative error of at most 0.0003.
Values sent between devices are 32-bit elements; how exact they have to be, the bound alone decides.
No kernel may reach another device: no remote copies, remote signals or barrier semaphores. Data moves between devices by JAX's collectives and lax.ppermute only.
A program may use at most 192 MiB of HBM per device.

```python
import math
import jax
import jax.numpy as jnp
from jax import lax

N = 512
L = 32
SWEEPS = 2


def draw_template(key, part):
    radius_key = jax.random.fold_in(key, 11)
    extra_key = jax.random.fold_in(key, 23)
    radius = jnp.minimum(jax.random.randint(radius_key, (), 2, 5, dtype=jnp.int32), L // 4)
    position = jnp.arange(L, dtype=jnp.int32)
    corner = jnp.minimum(position, L - position)
    square = corner * corner
    reach = square[:, None, None] + square[None, :, None] + square[None, None, :]
    inside = reach <= radius * radius
    extra = jax.random.randint(extra_key, (L, L, L), 0, 512, dtype=jnp.int32) == 0
    return (inside | extra).astype(jnp.int32)


def block_scale(own_key, shape, split, least, largest):
    level = 1.0
    for dim, parts in split:
        draws = jax.random.uniform(jax.random.fold_in(jax.random.fold_in(own_key, 6), dim), (parts,), jnp.float32, least / len(split), largest / len(split))
        level = level * jnp.repeat(jnp.exp(draws), shape[dim] // parts).reshape((-1,) + (1,) * (len(shape) - 1 - dim))
    return level


def scatter_about(rng, extent, width, bound, shards=(), held_as=jnp.bfloat16):
    array = width * jax.random.normal(rng, extent, jnp.float32)
    if shards:
        array = array * block_scale(rng, extent, shards, -0.22, 0.18)
    return jnp.clip(array, -bound, bound).astype(held_as)


def setup_inputs(seed: int = 0) -> dict:
    arg_keys = jax.random.split(jax.random.key(seed), 3)
    return {
        "intensity": scatter_about(arg_keys[0], (N, N, N), 8.0, 48.0, ((0, 8), (1, 4)), jnp.float32),
        "template": draw_template(jax.random.fold_in(arg_keys[2], 71), 0),
    }


AXIS_ORDERS = ((0, 1, 2), (0, 2, 1), (1, 0, 2), (1, 2, 0), (2, 0, 1), (2, 1, 0))

def mirror(values, axis):
    return jnp.roll(jnp.flip(values, axis), 1, axis)

def symmetric_marks(marks):
    for flip_axis in range(3):
        marks = jnp.maximum(marks, mirror(marks, flip_axis))
    united = marks
    for axis_order in AXIS_ORDERS[1:]:
        united = jnp.maximum(united, jnp.transpose(marks, axis_order))
    return united

def cosine_table(length):
    position = jnp.arange(length, dtype=jnp.int32)
    phases = jnp.mod(position[:, None] * position[None, :], length)
    return jnp.cos(phases.astype(jnp.float32) * (2.0 * math.pi / length)) / math.sqrt(length)

def neighbour_mean(padded):
    beside_all = padded[2:, 1:-1, 1:-1] + padded[:-2, 1:-1, 1:-1]
    beside_all = beside_all + padded[1:-1, 2:, 1:-1] + padded[1:-1, :-2, 1:-1]
    beside_all = beside_all + padded[1:-1, 1:-1, 2:] + padded[1:-1, 1:-1, :-2]
    return beside_all / 6.0

def reference(intensity, template):
    reflected = intensity
    for flip_axis in range(3):
        reflected = reflected + mirror(reflected, flip_axis)
    summed = reflected
    for axis_order in AXIS_ORDERS[1:]:
        summed = summed + jnp.transpose(reflected, axis_order)
    averaged = summed / 48.0
    united = symmetric_marks(template)
    holes = jnp.tile(united, (N // L, N // L, N // L)) == 1
    filled = jnp.where(holes, jnp.zeros_like(averaged), averaged)
    for sweep_step in range(SWEEPS):
        filled = jnp.where(holes, neighbour_mean(jnp.pad(filled, 1, mode='wrap')), filled)
    cosines = cosine_table(N)
    highest = lax.Precision.HIGHEST
    result = jnp.einsum('xyz,zc->xyc', filled, cosines, precision=highest)
    result = jnp.einsum('xyc,yb->xbc', result, cosines, precision=highest)
    result = jnp.einsum('xbc,xa->abc', result, cosines, precision=highest)
    return result
```

```python
import math

import jax
import jax.numpy as jnp
from jax import lax
from jax.experimental import pallas as pl
from jax.experimental.pallas import tpu as pltpu
from jax.sharding import PartitionSpec as P

SWEEPS = 2

AXIS_ORDERS = ((0, 1, 2), (0, 2, 1), (1, 0, 2), (1, 2, 0), (2, 0, 1), (2, 1, 0))

HIGH = lax.Precision.HIGH


def halo(array, axis, dim):
    peers, length = (lax.axis_size(axis), array.shape[dim])
    up = [(i, (i + 1) % peers) for i in range(peers)]
    down = [(j, i) for i, j in up]
    last = lax.slice_in_dim(array, length - SWEEPS, length, axis=dim)
    leading = lax.slice_in_dim(array, 0, SWEEPS, axis=dim)
    return lax.ppermute(last, axis, up), lax.ppermute(leading, axis, down)


def mirror(values, axis):
    return jnp.roll(jnp.flip(values, axis), 1, axis)


def symmetric_marks(marks):
    for flip_axis in range(3):
        marks = jnp.maximum(marks, mirror(marks, flip_axis))
    united = marks
    for axis_order in AXIS_ORDERS[1:]:
        united = jnp.maximum(united, jnp.transpose(marks, axis_order))
    return united


def cosine_table(length):
    position = jnp.arange(length, dtype=jnp.int32)
    phases = jnp.mod(position[:, None] * position[None, : length // 2 + 1], length)
    return jnp.cos(phases.astype(jnp.float32) * (2.0 * math.pi / length)) / math.sqrt(length)


MARGIN = 16
CHUNK = 16
STEP_ROWS = 16
VMEM_BYTES = 56 * 1024 * 1024


def split(values):
    high = values.astype(jnp.bfloat16)
    low = (values - high.astype(jnp.float32)).astype(jnp.bfloat16)
    return high, low


def fill_kernel(
    here, above, below, top, bottom, left, right, marks, table_high, table_low,
    spectrum, edge, punched, once, high, low,
):
    step, steps = pl.program_id(0), pl.num_programs(0)
    step_rows, cols, length = here.shape
    period = marks.shape[0]
    lane = lax.broadcasted_iota(jnp.int32, (CHUNK, edge.shape[1]), 1)
    place = lax.broadcasted_iota(jnp.int32, (CHUNK, length), 1)
    signs = jnp.where(place % 2 == 0, 1.0, -1.0).astype(jnp.float32)

    def holes(row, start, size):
        row = lax.rem(step * step_rows + row, period)
        start = start % period
        if start + size <= period:
            return marks[row, pl.ds(start, size), :]
        return jnp.concatenate(
            [marks[row, pl.ds(start, period - start), :], marks[row, pl.ds(0, start + size - period), :]],
            axis=0,
        )

    def punch(row, start, values):
        kept = jnp.where(holes(row, start, values.shape[0]) > 0.0, 0.0, values)
        punched[row, pl.ds(start, values.shape[0]), :] = kept

    def punch_row(row, source, index):
        full = step * step_rows + row
        punch(row, MARGIN - 8, left[full])
        punch(row, MARGIN + cols, right[full])
        for c in range(0, cols, CHUNK):
            punch(row, MARGIN + c, source[index, pl.ds(c, CHUNK), :])

    def neighbours(ref, row, start):
        middle = ref[row, pl.ds(start, CHUNK), :]
        total = ref[row - 1, pl.ds(start, CHUNK), :] + ref[row + 1, pl.ds(start, CHUNK), :]
        total += ref[row, pl.ds(start - 1, CHUNK), :] + ref[row, pl.ds(start + 1, CHUNK), :]
        return total + pltpu.roll(middle, 1, 1) + pltpu.roll(middle, length - 1, 1)

    for edge_rows, inside, offset, outer in (
        (above, step > 0, 0, top),
        (below, step < steps - 1, step_rows + SWEEPS, bottom),
    ):
        @pl.when(inside)
        def _():
            for r in range(SWEEPS):
                punch_row(offset + r, edge_rows, r)

        @pl.when(jnp.logical_not(inside))
        def _():
            for r in range(SWEEPS):
                punch_row(offset + r, outer, r)

    @pl.loop(0, step_rows)
    def _(r):
        punch_row(r + SWEEPS, here, r)

    @pl.loop(1, step_rows + 2 * SWEEPS - 1)
    def _(r):
        for start in range(MARGIN - 8, MARGIN + cols + 8, CHUNK):
            hole = holes(r, start, CHUNK)
            total = neighbours(punched, r, start) * (hole * (1.0 / 6.0))
            once[r, pl.ds(start, CHUNK), :] = punched[r, pl.ds(start, CHUNK), :] + total

    @pl.loop(0, step_rows)
    def _(r):
        for c in range(0, cols, CHUNK):
            start = MARGIN + c
            hole = holes(r + SWEEPS, start, CHUNK)
            total = neighbours(once, r + SWEEPS, start) * (hole * (1.0 / 6.0))
            filled = punched[r + SWEEPS, pl.ds(start, CHUNK), :] + total
            first, second = split(filled)
            spot = pl.ds(pl.multiple_of(r * cols + c, CHUNK), CHUNK)
            high[spot, :] = first
            low[spot, :] = second
            alternate = jnp.sum(filled * signs, axis=1, keepdims=True)
            old = edge[pl.ds(c, CHUNK), :]
            edge[pl.ds(c, CHUNK), :] = jnp.where(lane == step * step_rows + r, alternate, old)

    rows_each = 4
    @pl.loop(0, step_rows // rows_each)
    def _(r):
        spot = pl.ds(pl.multiple_of(r * rows_each * cols, CHUNK), rows_each * cols)
        first, second = high[spot, :], low[spot, :]
        total = jnp.dot(first, table_low[...], preferred_element_type=jnp.float32)
        total += jnp.dot(second, table_high[...], preferred_element_type=jnp.float32)
        total += jnp.dot(first, table_high[...], preferred_element_type=jnp.float32)
        spectrum[pl.ds(r * rows_each, rows_each)] = total.reshape(rows_each, cols, -1)


def filled_spectrum(intensity, template, row, col, main):
    rows, cols, length = intensity.shape
    half = main.shape[1]
    united = symmetric_marks(template)
    period = united.shape[0]
    offsets = (jnp.mod(row * rows - SWEEPS, period), jnp.mod(col * cols - MARGIN, period))
    marks = jnp.roll(united, (-offsets[0], -offsets[1]), (0, 1))
    marks = jnp.tile(marks, (1, 1, length // period)).astype(jnp.float32)
    top, bottom = halo(intensity, "gx", 0)
    tall = jnp.concatenate([top, intensity, bottom], axis=0)
    left, right = halo(tall, "gy", 1)
    left = jnp.pad(left, ((0, 0), (8 - SWEEPS, 0), (0, 0)))
    right = jnp.pad(right, ((0, 0), (0, 8 - SWEEPS), (0, 0)))
    step_rows = min(STEP_ROWS, rows)
    pairs = step_rows // SWEEPS
    last = rows // SWEEPS - 1
    whole = lambda array: pl.BlockSpec(array.shape, lambda i: (0,) * array.ndim)
    rounded = lax.reduce_precision(main, 8, 7)
    high, low = rounded.astype(jnp.bfloat16), (main - rounded).astype(jnp.bfloat16)
    spectrum, edge = pl.pallas_call(
        fill_kernel,
        grid=(rows // step_rows,),
        in_specs=[
            pl.BlockSpec((step_rows, cols, length), lambda i: (i, 0, 0)),
            pl.BlockSpec((SWEEPS, cols, length), lambda i: (jnp.maximum(i * pairs - 1, 0), 0, 0)),
            pl.BlockSpec((SWEEPS, cols, length), lambda i: (jnp.minimum((i + 1) * pairs, last), 0, 0)),
        ] + [whole(array) for array in (top, bottom, left, right, marks, high, low)],
        out_specs=[
            pl.BlockSpec((step_rows, cols, half), lambda i: (i, 0, 0)),
            pl.BlockSpec((cols, 128), lambda i: (0, 0)),
        ],
        out_shape=[
            jax.ShapeDtypeStruct((rows, cols, half), jnp.float32),
            jax.ShapeDtypeStruct((cols, 128), jnp.float32),
        ],
        scratch_shapes=[
            pltpu.VMEM((step_rows + 2 * SWEEPS, cols + 2 * MARGIN, length), jnp.float32),
            pltpu.VMEM((step_rows + 2 * SWEEPS, cols + 2 * MARGIN, length), jnp.float32),
            pltpu.VMEM((step_rows * cols, length), jnp.bfloat16),
            pltpu.VMEM((step_rows * cols, length), jnp.bfloat16),
        ],
        compiler_params=pltpu.CompilerParams(vmem_limit_bytes=VMEM_BYTES),
    )(intensity, intensity, intensity, top, bottom, left, right, marks, high, low)
    return spectrum, jnp.swapaxes(edge[:, :rows], 0, 1) / math.sqrt(length)


def on_device(intensity, template):
    rows, cols, length = intensity.shape
    gx, gy = lax.axis_size("gx"), lax.axis_size("gy")
    row, col = lax.axis_index("gx"), lax.axis_index("gy")
    devices, half = gx * gy, length // 2
    block = max(devices, rows)
    blocks, own, slabs = half // block, block // devices, gx // 2
    offsets = [block * b * (b + 1) // 2 for b in range(blocks + 1)]
    width = offsets[blocks]
    table = cosine_table(length)
    main = table[:, :half]

    spectrum, edge = filled_spectrum(intensity, template, row, col, main)

    table_rows = lax.dynamic_slice_in_dim(table, row * rows, rows, 0)
    table_cols = lax.dynamic_slice_in_dim(table, col * cols, cols, 0)
    marks = [rows * (m + 1) for m in range(slabs)]
    with_edge = jnp.concatenate([spectrum, edge[:, :, None]], axis=2)
    weights_rows = jnp.stack([table_rows[:, m] for m in marks])
    weights_cols = jnp.stack([table_cols[:, m] for m in marks])
    along0 = jnp.einsum("ma,abk->mbk", weights_rows, with_edge, precision=HIGH)
    along1 = jnp.einsum("mb,abk->mak", weights_cols, with_edge, precision=HIGH)
    along2 = jnp.stack([with_edge[:, :, m] for m in marks])
    planes = jnp.einsum("bj,mbk->mjk", table_cols, along0, precision=HIGH)
    along1 = along1 + jnp.einsum("mab,bk->mak", along2, table_cols, precision=HIGH)
    planes = planes + jnp.einsum("aj,mak->mjk", table_rows, along1, precision=HIGH)
    planes = lax.psum(planes, ("gx", "gy"))
    planes = (planes + jnp.swapaxes(planes, 1, 2)) / 6.0

    pair_rows = rows // 2
    halves = spectrum.reshape(2, pair_rows, cols, half)
    core = lax.rem(col, 2)
    kept = lax.dynamic_index_in_dim(halves, core, 0, keepdims=False)
    given = lax.dynamic_index_in_dim(halves, 1 - core, 0, keepdims=False)
    got = lax.ppermute(given, "gy", [(q, q ^ 1) for q in range(gy)])
    mates = lax.dynamic_slice_in_dim(main, (col + 1 - 2 * core) * cols, cols, 0)
    section = jnp.einsum("abk,bj->ajk", kept, table_cols[:, :half], precision=HIGH)
    section = section + jnp.einsum("abk,bj->ajk", got, mates, precision=HIGH)
    section = section + jnp.swapaxes(section, 1, 2)
    packed = jnp.concatenate(
        [section[:, b * block : (b + 1) * block, : (b + 1) * block] for b in range(blocks)], axis=2
    )
    share = block // gy
    packed = jnp.swapaxes(packed.reshape(pair_rows, gy, share, width), 0, 1)
    packed = lax.all_to_all(packed, "gy", 0, 0, tiled=True)
    packed = jnp.sum(packed.reshape(gy // 2, rows, share, width), axis=0)

    packed = jnp.swapaxes(packed, 0, 1).reshape(gx, own, rows, width)
    packed = lax.all_to_all(packed, "gx", 0, 0, tiled=True)
    values = jnp.einsum(
        "geaw,gai->eiw", packed, main.reshape(gx, rows, half), precision=HIGH
    ) / 6.0

    turned = values.reshape(own, blocks, devices, own, width)
    turned = jnp.transpose(turned, (2, 1, 3, 0, 4))
    turned = lax.all_to_all(turned, ("gy", "gx"), 0, 0, tiled=True)
    turned = jnp.transpose(turned, (1, 2, 0, 3, 4)).reshape(blocks, own, block, width)
    sums = []
    for top in range(blocks):
        size = (top + 1) * block
        part = values[:, :size, offsets[top] : offsets[top] + size]
        part = part + jnp.swapaxes(part, 1, 2)
        lower = [
            turned[top, :, :, offsets[b] : offsets[b] + (b + 1) * block] for b in range(top + 1)
        ]
        sums.append(part + square(lower, block))

    messages = []
    for slab in range(slabs):
        base = slab * rows // block
        first = slab * rows
        units = []
        for b in range(blocks):
            size = (b + 1) * block
            near = sums[b][:, first : first + rows, :size] if b >= base else None
            far = sums[base][:, b * block : size, :size] if b < base else None
            if rows == block:
                units.append(far if near is None else near)
            else:
                near = jnp.zeros((own, rows, size)) if near is None else near
                far = jnp.zeros((own, block, size)) if far is None else far
                units.append(jnp.concatenate([near, far], axis=1))
        messages.append(jnp.concatenate(units, axis=2))
    messages = jnp.stack(messages + messages[::-1])
    depth = messages.shape[2]
    got = lax.all_to_all(messages, "gx", 0, 0, tiled=True)
    got = lax.all_gather(got, "gy", axis=0, tiled=True).reshape(block, depth, width)
    slab = jnp.minimum(row, gx - 1 - row)
    base = slab * rows // block
    lower = []
    for b in range(blocks):
        lanes = slice(offsets[b], offsets[b] + (b + 1) * block)
        near = jnp.swapaxes(got[:, :rows, lanes], 0, 1)
        far = got[:, depth - block :, lanes]
        start = lax.rem(slab * rows, block)
        far = lax.dynamic_slice_in_dim(far, start, rows, 0)
        lower.append(jnp.where(b >= base, near, far))
    body = square(lower, block)

    far_row, far_col = row >= slabs, col >= gy // 2
    last = planes[slabs - 1]
    across = lax.dynamic_slice_in_dim(last, slab * rows, rows, 0)
    body = jnp.concatenate([body, across[:, None, :half]], axis=1)
    body = jnp.concatenate([body, across[:, :, None]], axis=2)
    next_plane = lax.dynamic_index_in_dim(planes, slab, 0)
    body = jnp.concatenate([body, next_plane], axis=0)
    pick_rows = jnp.arange(rows)
    pick_rows = jnp.where(far_row, rows - pick_rows, pick_rows)
    pick_cols = jnp.arange(cols)
    pick_cols = jnp.where(far_col, (gy - col) * cols - pick_cols, col * cols + pick_cols)
    body = body[pick_rows][:, pick_cols]
    return jnp.concatenate([body, jnp.flip(body[:, :, 1:half], 2)], axis=2)


def square(lower, block):
    lines = []
    for b in range(len(lower)):
        parts = [lower[b]]
        for c in range(b + 1, len(lower)):
            parts.append(jnp.swapaxes(lower[c][:, :, b * block : (b + 1) * block], 1, 2))
        lines.append(jnp.concatenate(parts, axis=2))
    return jnp.concatenate(lines, axis=1)


def solution(mesh):
    placed = (P("gx", "gy", None), P())
    return jax.shard_map(
        on_device, mesh=mesh, in_specs=placed, out_specs=P("gx", "gy", None), check_vma=False
    )
```

```python
import math

import jax
import jax.numpy as jnp
from jax import lax
from jax.experimental import pallas as pl
from jax.experimental.pallas import tpu as pltpu
from jax.sharding import PartitionSpec as P

SWEEPS = 2

AXIS_ORDERS = ((0, 1, 2), (0, 2, 1), (1, 0, 2), (1, 2, 0), (2, 0, 1), (2, 1, 0))

HIGH = lax.Precision.HIGH


def halo(array, axis, dim):
    peers, length = (lax.axis_size(axis), array.shape[dim])
    up = [(i, (i + 1) % peers) for i in range(peers)]
    down = [(j, i) for i, j in up]
    last = lax.slice_in_dim(array, length - SWEEPS, length, axis=dim)
    leading = lax.slice_in_dim(array, 0, SWEEPS, axis=dim)
    return lax.ppermute(last, axis, up), lax.ppermute(leading, axis, down)


def mirror(values, axis):
    return jnp.roll(jnp.flip(values, axis), 1, axis)


def symmetric_marks(marks):
    for flip_axis in range(3):
        marks = jnp.maximum(marks, mirror(marks, flip_axis))
    united = marks
    for axis_order in AXIS_ORDERS[1:]:
        united = jnp.maximum(united, jnp.transpose(marks, axis_order))
    return united


def cosine_table(length):
    position = jnp.arange(length, dtype=jnp.int32)
    phases = jnp.mod(position[:, None] * position[None, : length // 2 + 1], length)
    return jnp.cos(phases.astype(jnp.float32) * (2.0 * math.pi / length)) / math.sqrt(length)


MARGIN = 16
CHUNK = 16
STEP_ROWS = 16
VMEM_BYTES = 56 * 1024 * 1024


def split(values):
    high = values.astype(jnp.bfloat16)
    low = (values - high.astype(jnp.float32)).astype(jnp.bfloat16)
    return high, low


def fill_kernel(
    here, above, below, top, bottom, left, right, marks, table_high, table_low,
    spectrum, edge, punched, once, high, low,
):
    step, steps = pl.program_id(0), pl.num_programs(0)
    step_rows, cols, length = here.shape
    period = marks.shape[0]
    lane = lax.broadcasted_iota(jnp.int32, (CHUNK, edge.shape[1]), 1)
    place = lax.broadcasted_iota(jnp.int32, (CHUNK, length), 1)
    signs = jnp.where(place % 2 == 0, 1.0, -1.0).astype(jnp.float32)

    def holes(row, start, size):
        row = lax.rem(step * step_rows + row, period)
        start = start % period
        if start + size <= period:
            return marks[row, pl.ds(start, size), :]
        return jnp.concatenate(
            [marks[row, pl.ds(start, period - start), :], marks[row, pl.ds(0, start + size - period), :]],
            axis=0,
        )

    def punch(row, start, values):
        kept = jnp.where(holes(row, start, values.shape[0]) > 0.0, 0.0, values)
        punched[row, pl.ds(start, values.shape[0]), :] = kept

    def punch_row(row, source, index):
        full = step * step_rows + row
        punch(row, MARGIN - 8, left[full])
        punch(row, MARGIN + cols, right[full])
        for c in range(0, cols, CHUNK):
            punch(row, MARGIN + c, source[index, pl.ds(c, CHUNK), :])

    def neighbours(ref, row, start):
        middle = ref[row, pl.ds(start, CHUNK), :]
        total = ref[row - 1, pl.ds(start, CHUNK), :] + ref[row + 1, pl.ds(start, CHUNK), :]
        total += ref[row, pl.ds(start - 1, CHUNK), :] + ref[row, pl.ds(start + 1, CHUNK), :]
        return total + pltpu.roll(middle, 1, 1) + pltpu.roll(middle, length - 1, 1)

    for edge_rows, inside, offset, outer in (
        (above, step > 0, 0, top),
        (below, step < steps - 1, step_rows + SWEEPS, bottom),
    ):
        @pl.when(inside)
        def _():
            for r in range(SWEEPS):
                punch_row(offset + r, edge_rows, r)

        @pl.when(jnp.logical_not(inside))
        def _():
            for r in range(SWEEPS):
                punch_row(offset + r, outer, r)

    @pl.loop(0, step_rows)
    def _(r):
        punch_row(r + SWEEPS, here, r)

    @pl.loop(1, step_rows + 2 * SWEEPS - 1)
    def _(r):
        for start in range(MARGIN - 8, MARGIN + cols + 8, CHUNK):
            hole = holes(r, start, CHUNK)
            total = neighbours(punched, r, start) * (hole * (1.0 / 6.0))
            once[r, pl.ds(start, CHUNK), :] = punched[r, pl.ds(start, CHUNK), :] + total

    @pl.loop(0, step_rows)
    def _(r):
        for c in range(0, cols, CHUNK):
            start = MARGIN + c
            hole = holes(r + SWEEPS, start, CHUNK)
            total = neighbours(once, r + SWEEPS, start) * (hole * (1.0 / 6.0))
            filled = punched[r + SWEEPS, pl.ds(start, CHUNK), :] + total
            first, second = split(filled)
            spot = pl.ds(pl.multiple_of(r * cols + c, CHUNK), CHUNK)
            high[spot, :] = first
            low[spot, :] = second
            alternate = jnp.sum(filled * signs, axis=1, keepdims=True)
            old = edge[pl.ds(c, CHUNK), :]
            edge[pl.ds(c, CHUNK), :] = jnp.where(lane == step * step_rows + r, alternate, old)

    rows_each = 4
    @pl.loop(0, step_rows // rows_each)
    def _(r):
        spot = pl.ds(pl.multiple_of(r * rows_each * cols, CHUNK), rows_each * cols)
        first, second = high[spot, :], low[spot, :]
        total = jnp.dot(first, table_low[...], preferred_element_type=jnp.float32)
        total += jnp.dot(second, table_high[...], preferred_element_type=jnp.float32)
        total += jnp.dot(first, table_high[...], preferred_element_type=jnp.float32)
        spectrum[pl.ds(r * rows_each, rows_each)] = total.reshape(rows_each, cols, -1)


def filled_spectrum(intensity, template, row, col, main):
    rows, cols, length = intensity.shape
    half = main.shape[1]
    united = symmetric_marks(template)
    period = united.shape[0]
    offsets = (jnp.mod(row * rows - SWEEPS, period), jnp.mod(col * cols - MARGIN, period))
    marks = jnp.roll(united, (-offsets[0], -offsets[1]), (0, 1))
    marks = jnp.tile(marks, (1, 1, length // period)).astype(jnp.float32)
    top, bottom = halo(intensity, "gx", 0)
    tall = jnp.concatenate([top, intensity, bottom], axis=0)
    left, right = halo(tall, "gy", 1)
    left = jnp.pad(left, ((0, 0), (8 - SWEEPS, 0), (0, 0)))
    right = jnp.pad(right, ((0, 0), (0, 8 - SWEEPS), (0, 0)))
    step_rows = min(STEP_ROWS, rows)
    pairs = step_rows // SWEEPS
    last = rows // SWEEPS - 1
    whole = lambda array: pl.BlockSpec(array.shape, lambda i: (0,) * array.ndim)
    rounded = lax.reduce_precision(main, 8, 7)
    high, low = rounded.astype(jnp.bfloat16), (main - rounded).astype(jnp.bfloat16)
    spectrum, edge = pl.pallas_call(
        fill_kernel,
        grid=(rows // step_rows,),
        in_specs=[
            pl.BlockSpec((step_rows, cols, length), lambda i: (i, 0, 0)),
            pl.BlockSpec((SWEEPS, cols, length), lambda i: (jnp.maximum(i * pairs - 1, 0), 0, 0)),
            pl.BlockSpec((SWEEPS, cols, length), lambda i: (jnp.minimum((i + 1) * pairs, last), 0, 0)),
        ] + [whole(array) for array in (top, bottom, left, right, marks, high, low)],
        out_specs=[
            pl.BlockSpec((step_rows, cols, half), lambda i: (i, 0, 0)),
            pl.BlockSpec((cols, 128), lambda i: (0, 0)),
        ],
        out_shape=[
            jax.ShapeDtypeStruct((rows, cols, half), jnp.float32),
            jax.ShapeDtypeStruct((cols, 128), jnp.float32),
        ],
        scratch_shapes=[
            pltpu.VMEM((step_rows + 2 * SWEEPS, cols + 2 * MARGIN, length), jnp.float32),
            pltpu.VMEM((step_rows + 2 * SWEEPS, cols + 2 * MARGIN, length), jnp.float32),
            pltpu.VMEM((step_rows * cols, length), jnp.bfloat16),
            pltpu.VMEM((step_rows * cols, length), jnp.bfloat16),
        ],
        compiler_params=pltpu.CompilerParams(vmem_limit_bytes=VMEM_BYTES),
    )(intensity, intensity, intensity, top, bottom, left, right, marks, high, low)
    return spectrum, jnp.swapaxes(edge[:, :rows], 0, 1) / math.sqrt(length)


def on_device(intensity, template):
    rows, cols, length = intensity.shape
    gx, gy = lax.axis_size("gx"), lax.axis_size("gy")
    row, col = lax.axis_index("gx"), lax.axis_index("gy")
    devices, half = gx * gy, length // 2
    block = max(devices, rows)
    blocks, own, slabs = half // block, block // devices, gx // 2
    offsets = [block * b * (b + 1) // 2 for b in range(blocks + 1)]
    width = offsets[blocks]
    table = cosine_table(length)
    main = table[:, :half]

    spectrum, edge = filled_spectrum(intensity, template, row, col, main)

    table_rows = lax.dynamic_slice_in_dim(table, row * rows, rows, 0)
    table_cols = lax.dynamic_slice_in_dim(table, col * cols, cols, 0)
    marks = [rows * (m + 1) for m in range(slabs)]
    with_edge = jnp.concatenate([spectrum, edge[:, :, None]], axis=2)
    weights_rows = jnp.stack([table_rows[:, m] for m in marks])
    weights_cols = jnp.stack([table_cols[:, m] for m in marks])
    along0 = jnp.einsum("ma,abk->mbk", weights_rows, with_edge, precision=HIGH)
    along1 = jnp.einsum("mb,abk->mak", weights_cols, with_edge, precision=HIGH)
    along2 = jnp.stack([with_edge[:, :, m] for m in marks])
    planes = jnp.einsum("bj,mbk->mjk", table_cols, along0, precision=HIGH)
    along1 = along1 + jnp.einsum("mab,bk->mak", along2, table_cols, precision=HIGH)
    planes = planes + jnp.einsum("aj,mak->mjk", table_rows, along1, precision=HIGH)
    corner = planes[slabs - 1, half] + planes[slabs - 1, :, half]
    corner = jnp.broadcast_to(jnp.pad(corner, (0, width - half - 1)), (1, block, width))

    pair_rows = rows // 2
    halves = spectrum.reshape(2, pair_rows, cols, half)
    core = lax.rem(col, 2)
    kept = lax.dynamic_index_in_dim(halves, core, 0, keepdims=False)
    given = lax.dynamic_index_in_dim(halves, 1 - core, 0, keepdims=False)
    got = lax.ppermute(given, "gy", [(q, q ^ 1) for q in range(gy)])
    mates = lax.dynamic_slice_in_dim(main, (col + 1 - 2 * core) * cols, cols, 0)
    section = jnp.einsum("abk,bj->ajk", kept, table_cols[:, :half], precision=HIGH)
    section = section + jnp.einsum("abk,bj->ajk", got, mates, precision=HIGH)
    section = jnp.concatenate([section, planes[:, :half, :half]], axis=0)
    section = section + jnp.swapaxes(section, 1, 2)
    packed = jnp.concatenate(
        [section[:, b * block : (b + 1) * block, : (b + 1) * block] for b in range(blocks)], axis=2
    )
    packed = jnp.concatenate([packed, corner], axis=0)
    layers = packed.shape[0]
    packed = jnp.transpose(packed.reshape(layers, own, gy, gx, width), (2, 0, 1, 3, 4))
    packed = lax.all_to_all(packed, "gy", 0, 0, tiled=True)
    side = jnp.sum(packed[:, pair_rows:], axis=0)
    packed = packed[:, :pair_rows].reshape(gy // 2, rows, own, gx, width)
    packed = jnp.concatenate([jnp.sum(packed, axis=0), side], axis=0)

    packed = jnp.transpose(packed, (2, 1, 0, 3))
    packed = lax.all_to_all(packed, "gx", 0, 0, tiled=True)
    values = jnp.einsum(
        "geaw,gai->eiw", packed[:, :, :rows], main.reshape(gx, rows, half) / 6.0, precision=HIGH
    )
    side = jnp.sum(packed[:, :, rows:], axis=0) / 6.0
    side = lax.all_gather(side, ("gy", "gx"), axis=0)
    side = jnp.transpose(side, (2, 1, 0, 3)).reshape(slabs + 1, block, width)

    turned = values.reshape(own, blocks, own, devices, width)
    turned = jnp.transpose(turned, (3, 1, 2, 0, 4))
    turned = lax.all_to_all(turned, ("gy", "gx"), 0, 0, tiled=True)
    turned = jnp.transpose(turned, (1, 2, 3, 0, 4)).reshape(blocks, own, block, width)

    slab = jnp.minimum(row, gx - 1 - row)
    far_row, far_col = row >= slabs, col >= gy // 2
    pick_rows = jnp.arange(rows)
    pick_rows = slab * rows + jnp.where(far_row, rows - pick_rows, pick_rows)
    pick_cols = jnp.arange(cols)
    pick_cols = jnp.where(far_col, (gy - col) * cols - pick_cols, col * cols + pick_cols)
    last = square([side[slabs - 1][None, :, offsets[b] : offsets[b + 1]] for b in range(blocks)], block)[0]
    rim = side[slabs, 0, : half + 1]
    last = jnp.concatenate([last, rim[None, :half]], axis=0)
    last = jnp.concatenate([last, rim[:, None]], axis=1)
    across = last[pick_rows]
    next_plane = lax.dynamic_index_in_dim(side, slab, 0, keepdims=False)

    if rows == block:
        messages = slab_messages(values, turned, offsets, slabs)
        got = lax.all_to_all(messages, "gx", 0, 0, tiled=True)
        got = lax.all_gather(got, "gy", axis=0, tiled=True)
        rim_col = col == gy // 2
        rim = across[:, pick_cols]
        return result_block(
            got, next_plane, across, rim, pick_cols, slab, far_row, rim_col, offsets
        )

    sums = axis_order_sums(values, turned, offsets, block)
    messages = []
    for s in range(slabs):
        base, first = s * rows // block, s * rows
        units = []
        for b in range(blocks):
            size = (b + 1) * block
            near = jnp.zeros((own, rows, size))
            far = jnp.zeros((own, block, size))
            if b >= base:
                near = jnp.stack([sums[b][e][first : first + rows, :size] for e in range(own)])
            else:
                far = jnp.stack([sums[base][e][b * block : size, :size] for e in range(own)])
            units.append(jnp.concatenate([near, far], axis=1))
        messages.append(jnp.concatenate(units, axis=2))
    messages = jnp.stack(messages + messages[::-1])
    got = lax.all_to_all(messages, "gx", 0, 0, tiled=True)
    got = lax.all_gather(got, "gy", axis=0, tiled=True)
    got = jnp.swapaxes(got, 0, 1).reshape(block, rows + block, width)
    base = slab * rows // block
    lower = []
    for b in range(blocks):
        lanes = slice(offsets[b], offsets[b + 1])
        near = jnp.swapaxes(got[:, :rows, lanes], 0, 1)
        far = lax.dynamic_slice_in_dim(got[:, rows:, lanes], lax.rem(slab * rows, block), rows, 0)
        lower.append(jnp.where(b >= base, near, far))
    lower = jnp.concatenate(lower, axis=2)
    lower = jnp.concatenate([lower, next_plane[None]], axis=0)
    body = square([lower[:, :, offsets[b] : offsets[b + 1]] for b in range(blocks)], block)
    body = body[pick_rows - slab * rows]
    body = jnp.concatenate([body, across[:, None, :half]], axis=1)[:, pick_cols]
    body = jnp.concatenate([body, across[:, pick_cols][:, :, None]], axis=2)
    return jnp.concatenate([body, jnp.flip(body[:, :, 1:half], 2)], axis=2)


def axis_order_sums(values, turned, offsets, block):
    sums = []
    for top in range(len(offsets) - 1):
        size = (top + 1) * block
        parts = []
        for e in range(values.shape[0]):
            part = values[e, :size, offsets[top] : offsets[top] + size]
            lower = [turned[top, e, :, offsets[b] : offsets[b + 1]] for b in range(top + 1)]
            parts.append(part + part.T + square(lower, block))
        sums.append(parts)
    return sums


def message_kernel(offsets, slabs, values, turned, messages):
    blocks = len(offsets) - 1
    block = offsets[1]
    values, turned = values[...], turned[...]
    own = values.shape[0]
    sums = axis_order_sums(values, turned, offsets, block)
    for s in range(slabs):
        for e in range(own):
            units = []
            for b in range(blocks):
                size = (b + 1) * block
                if b >= s:
                    units.append(sums[b][e][s * block : (s + 1) * block, :size])
                else:
                    units.append(sums[s][e][b * block : size, :size])
            line = jnp.concatenate(units, axis=1)
            for tile in range(messages.shape[1]):
                part = line[:, tile * 128 : (tile + 1) * 128]
                messages[s, tile, e] = part
                messages[2 * slabs - 1 - s, tile, e] = part


def slab_messages(values, turned, offsets, slabs):
    own, block = values.shape[0], offsets[1]
    shape = (2 * slabs, offsets[-1] // 128, own, block, 128)
    return pl.pallas_call(
        lambda *refs: message_kernel(offsets, slabs, *refs),
        in_specs=[pl.BlockSpec(memory_space=pltpu.VMEM)] * 2,
        out_specs=pl.BlockSpec(memory_space=pltpu.VMEM),
        out_shape=jax.ShapeDtypeStruct(shape, jnp.float32),
        compiler_params=pltpu.CompilerParams(vmem_limit_bytes=VMEM_BYTES),
    )(values, turned)


def result_kernel(
    offsets, own, devices, places, got, next_plane, across, rim, pick, flip, out
):
    blocks, block = len(offsets) - 1, offsets[1]
    tiles = offsets[-1] // 128
    stride = tiles * own * block
    step_rows, cols, length = out.shape
    half = length // 2
    slab, far_row, rim_col = places[0], places[1], places[2]
    lane = lax.broadcasted_iota(jnp.int32, (block, 128), 1)
    at_rim = lax.broadcasted_iota(jnp.int32, (cols, half), 0) + (1 - rim_col) == 0
    rim_lane = lax.broadcasted_iota(jnp.int32, rim.shape, 1)
    first_lane = lax.broadcasted_iota(jnp.int32, (cols, half), 1) == 0

    @pl.loop(0, step_rows)
    def _(r):
        t = pl.program_id(0) * step_rows + r
        i = jnp.where(far_row == 1, block - t, t)
        inside = (jnp.zeros((block, 128), jnp.int32) + i) < block
        i = jnp.minimum(i, block - 1)
        source = lax.div(i, devices), lax.rem(i, devices)
        parts = []
        for tile in range(tiles):
            start = tile * own * block
            near = [
                got[pl.ds(start + e * block + i, devices, stride=stride), :] for e in range(own)
            ]
            near = jnp.concatenate(near, axis=0)
            far = pl.multiple_of(source[1] * stride + start + source[0] * block, block)
            far = got[pl.ds(far, block), :]
            kind = jnp.zeros((block, 128), jnp.int32)
            for b in range(1, blocks):
                kind += (lane + tile * 128 >= offsets[b]).astype(jnp.int32)
            line = jnp.where(kind >= slab, near, far)
            line = jnp.where(inside, line, next_plane[:, pl.ds(tile * 128, 128)])
            parts.append(line)
        line = jnp.concatenate(parts, axis=1)
        plane = square([line[:, offsets[b] : offsets[b + 1]] for b in range(blocks)], block)
        high, low = split(plane)
        left = jnp.dot(pick[...], high, preferred_element_type=jnp.float32)
        left += jnp.dot(pick[...], low, preferred_element_type=jnp.float32)
        left = jnp.where(at_rim, across[pl.ds(t, 1), :], left)
        high, low = split(left)
        right = jnp.dot(high, flip[...], preferred_element_type=jnp.float32)
        right += jnp.dot(low, flip[...], preferred_element_type=jnp.float32)
        edge = jnp.sum(jnp.where(rim_lane == t, rim[...], 0.0), axis=1, keepdims=True)
        out[r, :, pl.ds(0, half)] = left
        out[r, :, pl.ds(half, half)] = jnp.where(first_lane, edge, right)


def result_block(got, next_plane, across, rim, pick_cols, slab, far_row, rim_col, offsets):
    devices, tiles, own, block, _ = got.shape
    rows, half = across.shape[0], across.shape[1] - 1
    cols = pick_cols.shape[0]
    step_rows = 8
    places = jnp.stack([slab, far_row.astype(jnp.int32), rim_col.astype(jnp.int32)])
    cell = jnp.arange(half)
    pick = (pick_cols[:, None] == cell[None, :]).astype(jnp.bfloat16)
    flip = (cell[:, None] + cell[None, :] == half).astype(jnp.bfloat16)
    rim = jnp.pad(rim.T, ((0, 0), (0, 128 - rows)))
    whole = lambda array: pl.BlockSpec(array.shape, lambda i: (0,) * array.ndim)
    arrays = (got.reshape(-1, 128), next_plane, across[:, :half], rim, pick, flip)
    return pl.pallas_call(
        lambda *refs: result_kernel(offsets, own, devices, *refs),
        grid=(rows // step_rows,),
        in_specs=[pl.BlockSpec(memory_space=pltpu.SMEM)] + [whole(array) for array in arrays],
        out_specs=pl.BlockSpec((step_rows, cols, 2 * half), lambda i: (i, 0, 0)),
        out_shape=jax.ShapeDtypeStruct((rows, cols, 2 * half), jnp.float32),
        compiler_params=pltpu.CompilerParams(vmem_limit_bytes=VMEM_BYTES),
    )(places, *arrays)


def square(lower, block):
    lines = []
    for b in range(len(lower)):
        parts = [lower[b]]
        for c in range(b + 1, len(lower)):
            part = lower[c][..., b * block : (b + 1) * block]
            parts.append(jnp.swapaxes(part, -1, -2))
        lines.append(jnp.concatenate(parts, axis=-1))
    return jnp.concatenate(lines, axis=-2)


def solution(mesh):
    placed = (P("gx", "gy", None), P())
    return jax.shard_map(
        on_device, mesh=mesh, in_specs=placed, out_specs=P("gx", "gy", None), check_vma=False
    )
```

```python
import math

import jax
import jax.numpy as jnp
from jax import lax
from jax.experimental import pallas as pl
from jax.experimental.pallas import tpu as pltpu
from jax.sharding import PartitionSpec as P

SWEEPS = 2

AXIS_ORDERS = ((0, 1, 2), (0, 2, 1), (1, 0, 2), (1, 2, 0), (2, 0, 1), (2, 1, 0))

HIGH = lax.Precision.HIGH


def ring(axis):
    peers = lax.axis_size(axis)
    up = [(i, (i + 1) % peers) for i in range(peers)]
    return up, [(j, i) for i, j in up]


def halos(block):
    rows, cols, _ = block.shape
    up, down = ring("gx")
    right, left = ring("gy")
    top = lax.ppermute(block[rows - SWEEPS :], "gx", up)
    bottom = lax.ppermute(block[:SWEEPS], "gx", down)
    before = lax.ppermute(block[:, cols - SWEEPS :], "gy", right)
    after = lax.ppermute(block[:, :SWEEPS], "gy", left)
    sides = jnp.concatenate([before, after], axis=1)
    above = lax.ppermute(sides[rows - SWEEPS :], "gx", up)
    below = lax.ppermute(sides[:SWEEPS], "gx", down)
    sides = jnp.concatenate([above, sides, below], axis=0)
    free = ((0, 0), (8 - SWEEPS, 8 - SWEEPS), (0, 0))
    return top, bottom, jnp.pad(sides, free)


def mirror(values, axis):
    return jnp.roll(jnp.flip(values, axis), 1, axis)


def symmetric_marks(marks):
    for flip_axis in range(3):
        marks = jnp.maximum(marks, mirror(marks, flip_axis))
    united = marks
    for axis_order in AXIS_ORDERS[1:]:
        united = jnp.maximum(united, jnp.transpose(marks, axis_order))
    return united


def cosine_table(length):
    position = jnp.arange(length, dtype=jnp.int32)
    phases = jnp.mod(position[:, None] * position[None, : length // 2 + 1], length)
    return jnp.cos(phases.astype(jnp.float32) * (2.0 * math.pi / length)) / math.sqrt(length)


MARGIN = 16
CHUNK = 16
STEP_ROWS = 16
PART_ROWS = 16
VMEM_BYTES = 56 * 1024 * 1024


def split(values):
    high = values.astype(jnp.bfloat16)
    low = (values - high.astype(jnp.float32)).astype(jnp.bfloat16)
    return high, low


def fill_kernel(
    base, here, above, below, top, bottom, sides, marks, table_high, table_low,
    spectrum, alternate, edge, punched, once, high, low,
):
    step_rows, cols, length = here.shape
    step = pl.program_id(0) + base[0]
    first_row = step * step_rows
    local_row = pl.program_id(0) * step_rows
    period = marks.shape[0]
    lane = lax.broadcasted_iota(jnp.int32, (CHUNK, edge.shape[1]), 1)
    place = lax.broadcasted_iota(jnp.int32, (CHUNK, length), 1)
    signs = jnp.where(place % 2 == 0, 1.0, -1.0).astype(jnp.float32)
    inner = pl.ds(8 - SWEEPS, 2 * SWEEPS)

    def holes(row, start, size):
        row = lax.rem(first_row + row, period)
        start = start % period
        if start + size <= period:
            part = marks[row, pl.ds(start, size), :]
        else:
            part = jnp.concatenate(
                [marks[row, pl.ds(start, period - start), :], marks[row, pl.ds(0, start + size - period), :]],
                axis=0,
            )
        return jnp.concatenate([part] * (length // 128), axis=1)

    def punch(row, start, values):
        kept = jnp.where(holes(row, start, values.shape[0]) > 0.0, 0.0, values)
        punched[row, pl.ds(start, values.shape[0]), :] = kept

    def punch_row(row, source, index):
        full = first_row + row
        punch(row, MARGIN - 8, sides[full, pl.ds(0, 8), :])
        punch(row, MARGIN + cols, sides[full, pl.ds(8, 8), :])
        for c in range(0, cols, CHUNK):
            punch(row, MARGIN + c, source[index, pl.ds(c, CHUNK), :])

    def neighbours(ref, row, start):
        middle = ref[row, pl.ds(start, CHUNK), :]
        total = ref[row - 1, pl.ds(start, CHUNK), :] + ref[row + 1, pl.ds(start, CHUNK), :]
        total += ref[row, pl.ds(start - 1, CHUNK), :] + ref[row, pl.ds(start + 1, CHUNK), :]
        return total + pltpu.roll(middle, 1, 1) + pltpu.roll(middle, length - 1, 1)

    last = (sides.shape[0] - 2 * SWEEPS) // step_rows - 1
    for edge_rows, inside, offset, outer in (
        (above, step > 0, 0, top),
        (below, step < last, step_rows + SWEEPS, bottom),
    ):
        @pl.when(inside)
        def _():
            for r in range(SWEEPS):
                punch_row(offset + r, edge_rows, r)

        @pl.when(jnp.logical_not(inside))
        def _():
            for r in range(SWEEPS):
                punch_row(offset + r, outer, r)

    @pl.loop(0, step_rows)
    def _(r):
        punch_row(r + SWEEPS, here, r)

    @pl.loop(1, step_rows + 2 * SWEEPS - 1)
    def _(r):
        for start in range(MARGIN - 8, MARGIN + cols + 8, CHUNK):
            total = neighbours(punched, r, start) * holes(r, start, CHUNK)
            once[r, pl.ds(start, CHUNK), :] = punched[r, pl.ds(start, CHUNK), :] + total

    @pl.loop(0, step_rows)
    def _(r):
        for c in range(0, cols, CHUNK):
            start = MARGIN + c
            total = neighbours(once, r + SWEEPS, start) * holes(r + SWEEPS, start, CHUNK)
            filled = punched[r + SWEEPS, pl.ds(start, CHUNK), :] + total
            first, second = split(filled)
            spot = pl.ds(pl.multiple_of(r * cols + c, CHUNK), CHUNK)
            high[spot, :] = first
            low[spot, :] = second
            signed = jnp.sum(filled * signs, axis=1, keepdims=True)
            old = edge[pl.ds(c, CHUNK), :]
            edge[pl.ds(c, CHUNK), :] = jnp.where(lane == local_row + r, signed, old)

    rows_each = 8
    half = spectrum.shape[2]
    order = lax.broadcasted_iota(jnp.int32, (rows_each, cols, half), 1)

    @pl.loop(0, step_rows // rows_each)
    def _(r):
        spot = pl.ds(pl.multiple_of(r * rows_each * cols, CHUNK), rows_each * cols)
        first, second = high[spot, :], low[spot, :]
        total = jnp.dot(first, table_low[...], preferred_element_type=jnp.float32)
        total += jnp.dot(second, table_high[...], preferred_element_type=jnp.float32)
        total += jnp.dot(first, table_high[...], preferred_element_type=jnp.float32)
        total = total.reshape(rows_each, cols, half)
        spectrum[pl.ds(r * rows_each, rows_each)] = total
        signed = jnp.sum(jnp.where(order % 2 == 0, total, -total), axis=1)
        alternate[pl.ds(pl.multiple_of(r * rows_each, rows_each), rows_each), :] = signed


def rounded_parts(table):
    rounded = lax.reduce_precision(table, 8, 7)
    return rounded.astype(jnp.bfloat16), (table - rounded).astype(jnp.bfloat16)


def fill_arrays(intensity, template, row, col, main):
    rows, cols, length = intensity.shape
    united = symmetric_marks(template)
    period = united.shape[0]
    offsets = (jnp.mod(row * rows - SWEEPS, period), jnp.mod(col * cols - MARGIN, period))
    marks = jnp.roll(united, (-offsets[0], -offsets[1]), (0, 1)).astype(jnp.float32) / 6.0
    marks = jnp.tile(marks, (1, 1, 128 // period))
    return halos(intensity) + (marks,) + rounded_parts(main)


def filled_spectrum(intensity, arrays, first, count):
    rows, cols, length = intensity.shape
    half = length // 2
    step_rows = min(STEP_ROWS, count)
    pairs = step_rows // SWEEPS
    last = rows // SWEEPS - 1
    whole = lambda array: pl.BlockSpec(array.shape, lambda i, b: (0,) * array.ndim)
    before = lambda i, b: (jnp.maximum((i + b[0]) * pairs - 1, 0), 0, 0)
    after = lambda i, b: (jnp.minimum((i + b[0] + 1) * pairs, last), 0, 0)
    padded = (step_rows + 2 * SWEEPS, cols + 2 * MARGIN, length)
    return pl.pallas_call(
        fill_kernel,
        grid_spec=pltpu.PrefetchScalarGridSpec(
            num_scalar_prefetch=1,
            grid=(count // step_rows,),
            in_specs=[
                pl.BlockSpec((step_rows, cols, length), lambda i, b: (i + b[0], 0, 0)),
                pl.BlockSpec((SWEEPS, cols, length), before),
                pl.BlockSpec((SWEEPS, cols, length), after),
            ] + [whole(array) for array in arrays],
            out_specs=[
                pl.BlockSpec((step_rows, cols, half), lambda i, b: (i, 0, 0)),
                pl.BlockSpec((step_rows, half), lambda i, b: (i, 0)),
                pl.BlockSpec((cols, 128), lambda i, b: (0, 0)),
            ],
            scratch_shapes=[
                pltpu.VMEM(padded, jnp.float32),
                pltpu.VMEM(padded, jnp.float32),
                pltpu.VMEM((step_rows * cols, length), jnp.bfloat16),
                pltpu.VMEM((step_rows * cols, length), jnp.bfloat16),
            ],
        ),
        out_shape=[
            jax.ShapeDtypeStruct((count, cols, half), jnp.float32),
            jax.ShapeDtypeStruct((count, half), jnp.float32),
            jax.ShapeDtypeStruct((cols, 128), jnp.float32),
        ],
        compiler_params=pltpu.CompilerParams(vmem_limit_bytes=VMEM_BYTES),
        cost_estimate=pl.CostEstimate(
            flops=count * cols * length * half * 6,
            bytes_accessed=count * cols * length * 40,
            transcendentals=0,
        ),
    )((first // step_rows).reshape(1), intensity, intensity, intensity, *arrays)


def pack(section, offsets):
    block = offsets[1]
    units = [section[b * block : (b + 1) * block, : (b + 1) * block] for b in range(len(offsets) - 1)]
    return jnp.concatenate(units, axis=1)


def three_dots(left, right):
    total = jnp.dot(left[1], right[0], preferred_element_type=jnp.float32)
    total += jnp.dot(left[0], right[1], preferred_element_type=jnp.float32)
    return total + jnp.dot(left[0], right[0], preferred_element_type=jnp.float32)


def section_kernel(
    offsets, closing, weights, kept, got, cols_high, cols_low, rows_high, rows_low,
    rim, corner, before, out, total, lines,
):
    step, steps = pl.program_id(0), pl.num_programs(0)
    step_rows = kept.shape[0]
    half, count = rows_high.shape
    planes, block, width = before.shape
    gy, _, own, gx, _ = out.shape

    def place(layer, values):
        for e in range(own):
            for q in range(gy):
                start = (e * gy + q) * gx
                out[q, layer, e] = values[start : start + gx]

    @pl.when(step == 0)
    def _():
        total[...] = before[...]

    @pl.loop(0, step_rows)
    def _(r):
        layer = step * step_rows + r
        values = jnp.concatenate([kept[r], got[r]], axis=0)
        section = three_dots((cols_high[...], cols_low[...]), split(values))
        section = section + section.T
        line = pack(section, offsets)
        place(layer, line)
        for m in range(planes):
            total[m] += weights[m, layer] * line
        for m in range(planes - 1):
            row = (m + 1) * (half // planes)
            lines[m, pl.ds(layer, 1), :] = section[row : row + 1]

    @pl.when(step == steps - 1)
    def _():
        for m in range(planes - 1):
            plane = three_dots((rows_high[...], rows_low[...]), split(lines[m]))
            total[m] += pack(plane + plane.T, offsets)
        if closing:
            total[planes - 1] += pack(rim[...] + rim[...].T, offsets)
            for m in range(planes):
                place(count + m, total[m])
            place(count + planes, jnp.zeros((block, width), jnp.float32) + corner[...])


def packed_section(kept, got, table_pair, table_rows, marks, rim, corner, before, offsets, shape, closing):
    count, cols, half = kept.shape
    planes, block, width = before.shape
    gx, gy = shape
    step_rows = 4
    layers = count + (planes + 1 if closing else 0)
    whole = lambda array: pl.BlockSpec(array.shape, lambda i: (0,) * array.ndim)
    weights = jnp.stack([table_rows[:, m] for m in marks])
    arrays = rounded_parts(table_pair.T) + rounded_parts(table_rows[:, :half].T)
    arrays += (rim, corner[None], before)
    outs = [
        jax.ShapeDtypeStruct((gy, layers, block // (gx * gy), gx, width), jnp.float32),
        jax.ShapeDtypeStruct(before.shape, jnp.float32),
    ]
    rows_spec = pl.BlockSpec((step_rows, cols, half), lambda i: (i, 0, 0))
    return pl.pallas_call(
        lambda *refs: section_kernel(offsets, closing, *refs),
        grid=(count // step_rows,),
        in_specs=[pl.BlockSpec(memory_space=pltpu.SMEM), rows_spec, rows_spec]
        + [whole(array) for array in arrays],
        out_specs=[whole(out) for out in outs],
        out_shape=outs,
        scratch_shapes=[pltpu.VMEM((planes, count, half), jnp.float32)],
        compiler_params=pltpu.CompilerParams(vmem_limit_bytes=VMEM_BYTES),
        cost_estimate=pl.CostEstimate(
            flops=count * 12 * cols * half * half,
            bytes_accessed=count * cols * half * 60,
            transcendentals=0,
        ),
    )(weights, kept, got, *arrays)


def on_device(intensity, template):
    rows, cols, length = intensity.shape
    gx, gy = lax.axis_size("gx"), lax.axis_size("gy")
    row, col = lax.axis_index("gx"), lax.axis_index("gy")
    devices, half = gx * gy, length // 2
    block = max(devices, rows)
    blocks, own, slabs = half // block, block // devices, gx // 2
    offsets = [block * b * (b + 1) // 2 for b in range(blocks + 1)]
    width = offsets[blocks]
    table = cosine_table(length)
    main = table[:, :half]

    pair_rows = rows // 2
    parts = max(pair_rows // PART_ROWS, 1)
    count = pair_rows // parts
    core = lax.rem(col, 2)
    arrays = fill_arrays(intensity, template, row, col, main)
    given_first, kept_first = (1 - core) * pair_rows, core * pair_rows
    given, kept, got = [], [], []
    for c in range(parts):
        given.append(filled_spectrum(intensity, arrays, given_first + c * count, count))
        got.append(lax.ppermute(given[c][0], "gy", [(q, q ^ 1) for q in range(gy)]))
        kept.append(filled_spectrum(intensity, arrays, kept_first + c * count, count))

    table_cols = lax.dynamic_slice_in_dim(table, col * cols, cols, 0)
    given_rows = lax.dynamic_slice_in_dim(table, row * rows + given_first, pair_rows, 0)
    kept_rows = lax.dynamic_slice_in_dim(table, row * rows + kept_first, pair_rows, 0)
    ordered_rows = jnp.concatenate([given_rows, kept_rows], axis=0)
    alternate = jnp.concatenate([piece[1] for piece in given + kept], axis=0) / math.sqrt(length)
    edge = jnp.concatenate([piece[2][:, :count] for piece in given + kept], axis=1)
    edge = jnp.einsum("ba,bk->ak", edge / math.sqrt(length), table_cols, precision=HIGH)
    edge = edge + jnp.concatenate([alternate, edge[:, half:]], axis=1)
    rim = jnp.einsum("aj,ak->jk", ordered_rows[:, :half], edge[:, :half], precision=HIGH)
    corner = 2.0 * jnp.einsum("a,ak->k", ordered_rows[:, half], edge, precision=HIGH)
    corner = corner + jnp.einsum("aj,a->j", ordered_rows, edge[:, half], precision=HIGH)
    corner = jnp.pad(corner, (0, width - half - 1))

    marks = [rows * (m + 1) for m in range(slabs)]
    mates = lax.dynamic_slice_in_dim(main, (col + 1 - 2 * core) * cols, cols, 0)
    table_pair = jnp.concatenate([table_cols[:, :half], mates], axis=0)
    table_parts = main.reshape(gx, 2, parts, count, half) / 6.0
    side = jnp.zeros((slabs, block, width), jnp.float32)
    values = 0.0
    for c in range(parts):
        closing = c == parts - 1
        packed, side = packed_section(
            kept[c][0], got[c], table_pair, kept_rows[c * count : (c + 1) * count], marks,
            rim, corner, side, offsets, (gx, gy), closing,
        )
        packed = lax.all_to_all(packed, "gy", 0, 0, tiled=True)
        lines = packed[:, :count].reshape(gy // 2, 2 * count, own, gx, width)
        lines = jnp.sum(lines, axis=0)
        if closing:
            lines = jnp.concatenate([lines, jnp.sum(packed[:, count:], axis=0)], axis=0)
        lines = jnp.transpose(lines, (2, 1, 0, 3))
        lines = lax.all_to_all(lines, "gx", 0, 0, tiled=True)
        table_part = table_parts[:, :, c].reshape(gx, 2 * count, half)
        values = values + jnp.einsum(
            "geaw,gai->eiw", lines[:, :, : 2 * count], table_part, precision=HIGH
        )
    side = jnp.sum(lines[:, :, 2 * count :], axis=0) / 6.0
    side = lax.all_gather(side, ("gy", "gx"), axis=0)
    side = jnp.transpose(side, (2, 1, 0, 3)).reshape(slabs + 1, block, width)

    turned = values.reshape(own, blocks, own, devices, width)
    turned = jnp.transpose(turned, (3, 1, 2, 0, 4))
    turned = lax.all_to_all(turned, ("gy", "gx"), 0, 0, tiled=True)
    turned = jnp.transpose(turned, (1, 2, 3, 0, 4)).reshape(blocks, own, block, width)

    slab = jnp.minimum(row, gx - 1 - row)
    far_row, far_col = row >= slabs, col >= gy // 2
    pick_rows = jnp.arange(rows)
    pick_rows = slab * rows + jnp.where(far_row, rows - pick_rows, pick_rows)
    pick_cols = jnp.arange(cols)
    pick_cols = jnp.where(far_col, (gy - col) * cols - pick_cols, col * cols + pick_cols)
    last = square([side[slabs - 1][None, :, offsets[b] : offsets[b + 1]] for b in range(blocks)], block)[0]
    rim = side[slabs, 0, : half + 1]
    last = jnp.concatenate([last, rim[None, :half]], axis=0)
    last = jnp.concatenate([last, rim[:, None]], axis=1)
    across = last[pick_rows]
    next_plane = lax.dynamic_index_in_dim(side, slab, 0, keepdims=False)

    if rows == block:
        messages = slab_messages(values, turned, offsets, slabs)
        got = lax.all_to_all(messages, "gx", 0, 0, tiled=True)
        got = lax.all_gather(got, "gy", axis=0, tiled=True)
        rim_col = col == gy // 2
        rim = across[:, pick_cols]
        return result_block(
            got, next_plane, across, rim, pick_cols, slab, far_row, rim_col, offsets
        )

    sums = axis_order_sums(values, turned, offsets, block)
    messages = []
    for s in range(slabs):
        base, first = s * rows // block, s * rows
        units = []
        for b in range(blocks):
            size = (b + 1) * block
            near = jnp.zeros((own, rows, size))
            far = jnp.zeros((own, block, size))
            if b >= base:
                near = jnp.stack([sums[b][e][first : first + rows, :size] for e in range(own)])
            else:
                far = jnp.stack([sums[base][e][b * block : size, :size] for e in range(own)])
            units.append(jnp.concatenate([near, far], axis=1))
        messages.append(jnp.concatenate(units, axis=2))
    messages = jnp.stack(messages + messages[::-1])
    got = lax.all_to_all(messages, "gx", 0, 0, tiled=True)
    got = lax.all_gather(got, "gy", axis=0, tiled=True)
    got = jnp.swapaxes(got, 0, 1).reshape(block, rows + block, width)
    base = slab * rows // block
    lower = []
    for b in range(blocks):
        lanes = slice(offsets[b], offsets[b + 1])
        near = jnp.swapaxes(got[:, :rows, lanes], 0, 1)
        far = lax.dynamic_slice_in_dim(got[:, rows:, lanes], lax.rem(slab * rows, block), rows, 0)
        lower.append(jnp.where(b >= base, near, far))
    lower = jnp.concatenate(lower, axis=2)
    lower = jnp.concatenate([lower, next_plane[None]], axis=0)
    body = square([lower[:, :, offsets[b] : offsets[b + 1]] for b in range(blocks)], block)
    body = body[pick_rows - slab * rows]
    body = jnp.concatenate([body, across[:, None, :half]], axis=1)[:, pick_cols]
    body = jnp.concatenate([body, across[:, pick_cols][:, :, None]], axis=2)
    return jnp.concatenate([body, jnp.flip(body[:, :, 1:half], 2)], axis=2)


def axis_order_sums(values, turned, offsets, block):
    sums = []
    for top in range(len(offsets) - 1):
        size = (top + 1) * block
        parts = []
        for e in range(values.shape[0]):
            part = values[e, :size, offsets[top] : offsets[top] + size]
            lower = [turned[top, e, :, offsets[b] : offsets[b + 1]] for b in range(top + 1)]
            parts.append(part + part.T + square(lower, block))
        sums.append(parts)
    return sums


def message_kernel(offsets, slabs, values, turned, messages):
    blocks = len(offsets) - 1
    block = offsets[1]
    values, turned = values[...], turned[...]
    own = values.shape[0]
    sums = axis_order_sums(values, turned, offsets, block)
    for s in range(slabs):
        for e in range(own):
            units = []
            for b in range(blocks):
                size = (b + 1) * block
                if b >= s:
                    units.append(sums[b][e][s * block : (s + 1) * block, :size])
                else:
                    units.append(sums[s][e][b * block : size, :size])
            line = jnp.concatenate(units, axis=1)
            for tile in range(messages.shape[1]):
                part = line[:, tile * 128 : (tile + 1) * 128]
                messages[s, tile, e] = part
                messages[2 * slabs - 1 - s, tile, e] = part


def slab_messages(values, turned, offsets, slabs):
    own, block = values.shape[0], offsets[1]
    shape = (2 * slabs, offsets[-1] // 128, own, block, 128)
    return pl.pallas_call(
        lambda *refs: message_kernel(offsets, slabs, *refs),
        in_specs=[pl.BlockSpec(memory_space=pltpu.VMEM)] * 2,
        out_specs=pl.BlockSpec(memory_space=pltpu.VMEM),
        out_shape=jax.ShapeDtypeStruct(shape, jnp.float32),
        compiler_params=pltpu.CompilerParams(vmem_limit_bytes=VMEM_BYTES),
    )(values, turned)


def result_kernel(
    offsets, own, devices, places, got, next_plane, across, rim, pick, flip, out
):
    blocks, block = len(offsets) - 1, offsets[1]
    tiles = offsets[-1] // 128
    stride = tiles * own * block
    step_rows, cols, length = out.shape
    half = length // 2
    slab, far_row, rim_col = places[0], places[1], places[2]
    lane = lax.broadcasted_iota(jnp.int32, (block, 128), 1)
    at_rim = lax.broadcasted_iota(jnp.int32, (cols, half), 0) + (1 - rim_col) == 0
    rim_lane = lax.broadcasted_iota(jnp.int32, rim.shape, 1)
    first_lane = lax.broadcasted_iota(jnp.int32, (cols, half), 1) == 0

    @pl.loop(0, step_rows)
    def _(r):
        t = pl.program_id(0) * step_rows + r
        i = jnp.where(far_row == 1, block - t, t)
        inside = (jnp.zeros((block, 128), jnp.int32) + i) < block
        i = jnp.minimum(i, block - 1)
        source = lax.div(i, devices), lax.rem(i, devices)
        parts = []
        for tile in range(tiles):
            start = tile * own * block
            near = [
                got[pl.ds(start + e * block + i, devices, stride=stride), :] for e in range(own)
            ]
            near = jnp.concatenate(near, axis=0)
            far = pl.multiple_of(source[1] * stride + start + source[0] * block, block)
            far = got[pl.ds(far, block), :]
            kind = jnp.zeros((block, 128), jnp.int32)
            for b in range(1, blocks):
                kind += (lane + tile * 128 >= offsets[b]).astype(jnp.int32)
            line = jnp.where(kind >= slab, near, far)
            line = jnp.where(inside, line, next_plane[:, pl.ds(tile * 128, 128)])
            parts.append(line)
        line = jnp.concatenate(parts, axis=1)
        plane = square([line[:, offsets[b] : offsets[b + 1]] for b in range(blocks)], block)
        high, low = split(plane)
        left = jnp.dot(pick[...], high, preferred_element_type=jnp.float32)
        left += jnp.dot(pick[...], low, preferred_element_type=jnp.float32)
        left = jnp.where(at_rim, across[pl.ds(t, 1), :], left)
        high, low = split(left)
        right = jnp.dot(high, flip[...], preferred_element_type=jnp.float32)
        right += jnp.dot(low, flip[...], preferred_element_type=jnp.float32)
        edge = jnp.sum(jnp.where(rim_lane == t, rim[...], 0.0), axis=1, keepdims=True)
        out[r, :, pl.ds(0, half)] = left
        out[r, :, pl.ds(half, half)] = jnp.where(first_lane, edge, right)


def result_block(got, next_plane, across, rim, pick_cols, slab, far_row, rim_col, offsets):
    devices, tiles, own, block, _ = got.shape
    rows, half = across.shape[0], across.shape[1] - 1
    cols = pick_cols.shape[0]
    step_rows = 8
    places = jnp.stack([slab, far_row.astype(jnp.int32), rim_col.astype(jnp.int32)])
    cell = jnp.arange(half)
    pick = (pick_cols[:, None] == cell[None, :]).astype(jnp.bfloat16)
    flip = (cell[:, None] + cell[None, :] == half).astype(jnp.bfloat16)
    rim = jnp.pad(rim.T, ((0, 0), (0, 128 - rows)))
    whole = lambda array: pl.BlockSpec(array.shape, lambda i: (0,) * array.ndim)
    arrays = (got.reshape(-1, 128), next_plane, across[:, :half], rim, pick, flip)
    return pl.pallas_call(
        lambda *refs: result_kernel(offsets, own, devices, *refs),
        grid=(rows // step_rows,),
        in_specs=[pl.BlockSpec(memory_space=pltpu.SMEM)] + [whole(array) for array in arrays],
        out_specs=pl.BlockSpec((step_rows, cols, 2 * half), lambda i: (i, 0, 0)),
        out_shape=jax.ShapeDtypeStruct((rows, cols, 2 * half), jnp.float32),
        compiler_params=pltpu.CompilerParams(vmem_limit_bytes=VMEM_BYTES),
    )(places, *arrays)


def square(lower, block):
    lines = []
    for b in range(len(lower)):
        parts = [lower[b]]
        for c in range(b + 1, len(lower)):
            part = lower[c][..., b * block : (b + 1) * block]
            parts.append(jnp.swapaxes(part, -1, -2))
        lines.append(jnp.concatenate(parts, axis=-1))
    return jnp.concatenate(lines, axis=-2)


def solution(mesh):
    placed = (P("gx", "gy", None), P())
    return jax.shard_map(
        on_device, mesh=mesh, in_specs=placed, out_specs=P("gx", "gy", None), check_vma=False
    )
```

```python
import math

import jax
import jax.numpy as jnp
from jax import lax
from jax.experimental import pallas as pl
from jax.experimental.pallas import tpu as pltpu
from jax.sharding import PartitionSpec as P

SWEEPS = 2

AXIS_ORDERS = ((0, 1, 2), (0, 2, 1), (1, 0, 2), (1, 2, 0), (2, 0, 1), (2, 1, 0))

HIGH = lax.Precision.HIGH


def ring(axis):
    peers = lax.axis_size(axis)
    up = [(i, (i + 1) % peers) for i in range(peers)]
    return up, [(j, i) for i, j in up]


def halos(block):
    rows, cols, _ = block.shape
    up, down = ring("gx")
    right, left = ring("gy")
    top = lax.ppermute(block[rows - SWEEPS :], "gx", up)
    bottom = lax.ppermute(block[:SWEEPS], "gx", down)
    before = lax.ppermute(block[:, cols - SWEEPS :], "gy", right)
    after = lax.ppermute(block[:, :SWEEPS], "gy", left)
    sides = jnp.concatenate([before, after], axis=1)
    above = lax.ppermute(sides[rows - SWEEPS :], "gx", up)
    below = lax.ppermute(sides[:SWEEPS], "gx", down)
    sides = jnp.concatenate([above, sides, below], axis=0)
    free = ((0, 0), (8 - SWEEPS, 8 - SWEEPS), (0, 0))
    return top, bottom, jnp.pad(sides, free)


def mirror(values, axis):
    return jnp.roll(jnp.flip(values, axis), 1, axis)


def symmetric_marks(marks):
    for flip_axis in range(3):
        marks = jnp.maximum(marks, mirror(marks, flip_axis))
    united = marks
    for axis_order in AXIS_ORDERS[1:]:
        united = jnp.maximum(united, jnp.transpose(marks, axis_order))
    return united


def cosine_table(length):
    position = jnp.arange(length, dtype=jnp.int32)
    phases = jnp.mod(position[:, None] * position[None, : length // 2 + 1], length)
    return jnp.cos(phases.astype(jnp.float32) * (2.0 * math.pi / length)) / math.sqrt(length)


MARGIN = 16
CHUNK = 16
STEP_ROWS = 16
PART_ROWS = 16
VMEM_BYTES = 56 * 1024 * 1024


def split(values):
    high = values.astype(jnp.bfloat16)
    low = (values - high.astype(jnp.float32)).astype(jnp.bfloat16)
    return high, low


def fill_kernel(
    base, here, above, below, top, bottom, sides, marks, table_high, table_low,
    spectrum, alternate, edge, punched, once, high, low, folded,
):
    step_rows, cols, length = here.shape
    step = pl.program_id(0) + base[0]
    first_row = step * step_rows
    local_row = pl.program_id(0) * step_rows
    period = marks.shape[0]
    lane = lax.broadcasted_iota(jnp.int32, (128, 128), 1)
    signs = jnp.where(lax.broadcasted_iota(jnp.int32, (128, 128), 0) % 2 == 0, 1.0, -1.0)

    @pl.when(pl.program_id(0) == 0)
    def _():
        edge[...] = jnp.zeros_like(edge)

    def holes(row, start, size):
        row = lax.rem(first_row + row, period)
        start = start % period
        if start + size <= period:
            part = marks[row, pl.ds(start, size), :]
        else:
            part = jnp.concatenate(
                [marks[row, pl.ds(start, period - start), :], marks[row, pl.ds(0, start + size - period), :]],
                axis=0,
            )
        return jnp.concatenate([part] * (length // 128), axis=1)

    def punch(row, start, values):
        kept = jnp.where(holes(row, start, values.shape[0]) > 0.0, 0.0, values)
        punched[row, pl.ds(start, values.shape[0]), :] = kept

    def punch_row(row, source, index):
        full = first_row + row
        punch(row, MARGIN - 8, sides[full, pl.ds(0, 8), :])
        punch(row, MARGIN + cols, sides[full, pl.ds(8, 8), :])
        for c in range(0, cols, CHUNK):
            punch(row, MARGIN + c, source[index, pl.ds(c, CHUNK), :])

    def neighbours(ref, row, start):
        middle = ref[row, pl.ds(start, CHUNK), :]
        total = ref[row - 1, pl.ds(start, CHUNK), :] + ref[row + 1, pl.ds(start, CHUNK), :]
        total += ref[row, pl.ds(start - 1, CHUNK), :] + ref[row, pl.ds(start + 1, CHUNK), :]
        return total + pltpu.roll(middle, 1, 1) + pltpu.roll(middle, length - 1, 1)

    last = (sides.shape[0] - 2 * SWEEPS) // step_rows - 1
    for edge_rows, inside, offset, outer in (
        (above, step > 0, 0, top),
        (below, step < last, step_rows + SWEEPS, bottom),
    ):
        @pl.when(inside)
        def _():
            for r in range(SWEEPS):
                punch_row(offset + r, edge_rows, r)

        @pl.when(jnp.logical_not(inside))
        def _():
            for r in range(SWEEPS):
                punch_row(offset + r, outer, r)

    @pl.loop(0, step_rows)
    def _(r):
        punch_row(r + SWEEPS, here, r)

    @pl.loop(1, step_rows + 2 * SWEEPS - 1, unroll=2)
    def _(r):
        for start in range(MARGIN - 8, MARGIN + cols + 8, CHUNK):
            total = neighbours(punched, r, start) * holes(r, start, CHUNK)
            once[r, pl.ds(start, CHUNK), :] = punched[r, pl.ds(start, CHUNK), :] + total

    @pl.loop(0, step_rows)
    def _(r):
        for c in range(0, cols, CHUNK):
            start = MARGIN + c
            total = neighbours(once, r + SWEEPS, start) * holes(r + SWEEPS, start, CHUNK)
            filled = punched[r + SWEEPS, pl.ds(start, CHUNK), :] + total
            first, second = split(filled)
            spot = pl.ds(pl.multiple_of(r * cols + c, CHUNK), CHUNK)
            high[spot, :] = first
            low[spot, :] = second
            wrapped = filled[:, :128]
            for tile in range(1, length // 128):
                wrapped += filled[:, tile * 128 : (tile + 1) * 128]
            folded[pl.ds(c, CHUNK), :] = wrapped
        column = jnp.where(lane == local_row + r, signs, 0.0).astype(jnp.bfloat16)
        first, second = split(folded[...])
        total = jnp.dot(first, column, preferred_element_type=jnp.float32)
        total += jnp.dot(second, column, preferred_element_type=jnp.float32)
        edge[...] += total

    rows_each = 8
    half = spectrum.shape[2]
    order = lax.broadcasted_iota(jnp.int32, (rows_each, cols, half), 1)

    @pl.loop(0, step_rows // rows_each)
    def _(r):
        spot = pl.ds(pl.multiple_of(r * rows_each * cols, CHUNK), rows_each * cols)
        first, second = high[spot, :], low[spot, :]
        total = jnp.dot(first, table_low[...], preferred_element_type=jnp.float32)
        total += jnp.dot(second, table_high[...], preferred_element_type=jnp.float32)
        total += jnp.dot(first, table_high[...], preferred_element_type=jnp.float32)
        total = total.reshape(rows_each, cols, half)
        spectrum[pl.ds(r * rows_each, rows_each)] = total
        signed = jnp.sum(jnp.where(order % 2 == 0, total, -total), axis=1)
        alternate[pl.ds(pl.multiple_of(r * rows_each, rows_each), rows_each), :] = signed


def rounded_parts(table):
    rounded = lax.reduce_precision(table, 8, 7)
    return rounded.astype(jnp.bfloat16), (table - rounded).astype(jnp.bfloat16)


def fill_arrays(intensity, template, row, col, main):
    rows, cols, length = intensity.shape
    united = symmetric_marks(template)
    period = united.shape[0]
    offsets = (jnp.mod(row * rows - SWEEPS, period), jnp.mod(col * cols - MARGIN, period))
    marks = jnp.roll(united, (-offsets[0], -offsets[1]), (0, 1)).astype(jnp.float32) / 6.0
    marks = jnp.tile(marks, (1, 1, 128 // period))
    return halos(intensity) + (marks,) + rounded_parts(main)


def filled_spectrum(intensity, arrays, first, count):
    rows, cols, length = intensity.shape
    half = length // 2
    step_rows = min(STEP_ROWS, count)
    pairs = step_rows // SWEEPS
    last = rows // SWEEPS - 1
    whole = lambda array: pl.BlockSpec(array.shape, lambda i, b: (0,) * array.ndim)
    before = lambda i, b: (jnp.maximum((i + b[0]) * pairs - 1, 0), 0, 0)
    after = lambda i, b: (jnp.minimum((i + b[0] + 1) * pairs, last), 0, 0)
    padded = (step_rows + 2 * SWEEPS, cols + 2 * MARGIN, length)
    return pl.pallas_call(
        fill_kernel,
        grid_spec=pltpu.PrefetchScalarGridSpec(
            num_scalar_prefetch=1,
            grid=(count // step_rows,),
            in_specs=[
                pl.BlockSpec((step_rows, cols, length), lambda i, b: (i + b[0], 0, 0)),
                pl.BlockSpec((SWEEPS, cols, length), before),
                pl.BlockSpec((SWEEPS, cols, length), after),
            ] + [whole(array) for array in arrays],
            out_specs=[
                pl.BlockSpec((step_rows, cols, half), lambda i, b: (i, 0, 0)),
                pl.BlockSpec((step_rows, half), lambda i, b: (i, 0)),
                pl.BlockSpec((cols, 128), lambda i, b: (0, 0)),
            ],
            scratch_shapes=[
                pltpu.VMEM(padded, jnp.float32),
                pltpu.VMEM(padded, jnp.float32),
                pltpu.VMEM((step_rows * cols, length), jnp.bfloat16),
                pltpu.VMEM((step_rows * cols, length), jnp.bfloat16),
                pltpu.VMEM((cols, 128), jnp.float32),
            ],
        ),
        out_shape=[
            jax.ShapeDtypeStruct((count, cols, half), jnp.float32),
            jax.ShapeDtypeStruct((count, half), jnp.float32),
            jax.ShapeDtypeStruct((cols, 128), jnp.float32),
        ],
        compiler_params=pltpu.CompilerParams(vmem_limit_bytes=VMEM_BYTES),
        cost_estimate=pl.CostEstimate(
            flops=count * cols * length * half * 6,
            bytes_accessed=count * cols * length * 40,
            transcendentals=0,
        ),
    )((first // step_rows).reshape(1), intensity, intensity, intensity, *arrays)


def pack(section, offsets):
    block = offsets[1]
    units = [section[b * block : (b + 1) * block, : (b + 1) * block] for b in range(len(offsets) - 1)]
    return jnp.concatenate(units, axis=1)


def three_dots(left, right):
    total = jnp.dot(left[1], right[0], preferred_element_type=jnp.float32)
    total += jnp.dot(left[0], right[1], preferred_element_type=jnp.float32)
    return total + jnp.dot(left[0], right[0], preferred_element_type=jnp.float32)


def section_kernel(
    offsets, closing, me, weights, kept, got, cols_high, cols_low, rows_high, rows_low,
    rim, corner, before, out, total, lines,
):
    step, steps = pl.program_id(0), pl.num_programs(0)
    step_rows = kept.shape[0]
    half, count = rows_high.shape
    planes, block, width = before.shape
    gy, _, own, gx, _ = out.shape

    def place(layer, values):
        for e in range(own):
            for q in range(gy):
                start = (e * gy + q) * gx
                out[q ^ me[0], layer, e] = values[start : start + gx]

    @pl.when(step == 0)
    def _():
        total[...] = before[...]

    @pl.loop(0, step_rows, unroll=True)
    def _(r):
        layer = step * step_rows + r
        values = jnp.concatenate([kept[r], got[r]], axis=0)
        section = three_dots((cols_high[...], cols_low[...]), split(values))
        section = section + section.T
        line = pack(section, offsets)
        place(layer, line)
        for m in range(planes):
            total[m] += weights[m, layer] * line
        for m in range(planes - 1):
            row = (m + 1) * (half // planes)
            lines[m, pl.ds(layer, 1), :] = section[row : row + 1]

    @pl.when(step == steps - 1)
    def _():
        for m in range(planes - 1):
            plane = three_dots((rows_high[...], rows_low[...]), split(lines[m]))
            total[m] += pack(plane + plane.T, offsets)
        if closing:
            total[planes - 1] += pack(rim[...] + rim[...].T, offsets)
            for m in range(planes):
                place(count + m, total[m])
            place(count + planes, jnp.zeros((block, width), jnp.float32) + corner[...])


def packed_section(col, kept, got, table_pair, table_rows, marks, rim, corner, before, offsets, shape, closing):
    count, cols, half = kept.shape
    planes, block, width = before.shape
    gx, gy = shape
    step_rows = 4
    layers = count + (planes + 1 if closing else 0)
    whole = lambda array: pl.BlockSpec(array.shape, lambda i: (0,) * array.ndim)
    weights = jnp.stack([table_rows[:, m] for m in marks])
    arrays = rounded_parts(table_pair.T) + rounded_parts(table_rows[:, :half].T)
    arrays += (rim, corner[None], before)
    outs = [
        jax.ShapeDtypeStruct((gy, layers, block // (gx * gy), gx, width), jnp.float32),
        jax.ShapeDtypeStruct(before.shape, jnp.float32),
    ]
    rows_spec = pl.BlockSpec((step_rows, cols, half), lambda i: (i, 0, 0))
    return pl.pallas_call(
        lambda *refs: section_kernel(offsets, closing, *refs),
        grid=(count // step_rows,),
        in_specs=[pl.BlockSpec(memory_space=pltpu.SMEM)] * 2 + [rows_spec, rows_spec]
        + [whole(array) for array in arrays],
        out_specs=[whole(out) for out in outs],
        out_shape=outs,
        scratch_shapes=[pltpu.VMEM((planes, count, half), jnp.float32)],
        compiler_params=pltpu.CompilerParams(vmem_limit_bytes=VMEM_BYTES),
        cost_estimate=pl.CostEstimate(
            flops=count * 12 * cols * half * half,
            bytes_accessed=count * cols * half * 60,
            transcendentals=0,
        ),
    )(col.reshape(1), weights, kept, got, *arrays)


def on_device(intensity, template):
    rows, cols, length = intensity.shape
    gx, gy = lax.axis_size("gx"), lax.axis_size("gy")
    row, col = lax.axis_index("gx"), lax.axis_index("gy")
    devices, half = gx * gy, length // 2
    block = max(devices, rows)
    blocks, own, slabs = half // block, block // devices, gx // 2
    offsets = [block * b * (b + 1) // 2 for b in range(blocks + 1)]
    width = offsets[blocks]
    table = cosine_table(length)
    main = table[:, :half]

    pair_rows = rows // 2
    parts = max(pair_rows // PART_ROWS, 1)
    count = pair_rows // parts
    core = lax.rem(col, 2)
    arrays = fill_arrays(intensity, template, row, col, main)
    given_first, kept_first = (1 - core) * pair_rows, core * pair_rows
    given, kept, got = [], [], []

    def fill_part(c, after):
        starts = given_first + c * count, kept_first + c * count
        if after is not None:
            starts, after = lax.optimization_barrier((starts, after))
        given.append(filled_spectrum(intensity, arrays, starts[0], count))
        got.append(lax.ppermute(given[c][0], "gy", swap(gy, 1)))
        kept.append(filled_spectrum(intensity, arrays, starts[1], count))
        return after

    table_cols = lax.dynamic_slice_in_dim(table, col * cols, cols, 0)
    kept_rows = lax.dynamic_slice_in_dim(table, row * rows + kept_first, pair_rows, 0)
    marks = [rows * (m + 1) for m in range(slabs)]
    mates = lax.dynamic_slice_in_dim(main, (col + 1 - 2 * core) * cols, cols, 0)
    table_pair = jnp.concatenate([table_cols[:, :half], mates], axis=0)
    table_parts = main.reshape(gx, 2, parts, count, half) / 6.0
    table_parts = jnp.where(core == 0, table_parts, table_parts[:, ::-1])
    side = jnp.zeros((slabs, block, width), jnp.float32)
    rim, corner = jnp.zeros((half, half), jnp.float32), jnp.zeros((width,), jnp.float32)
    values, packed = 0.0, None
    for c in range(parts):
        closing = c == parts - 1
        packed = fill_part(c, packed)
        if c > 0:
            values = values + first_axis(packed, count, table_parts[:, :, c - 1])[0]
        if closing:
            given_rows = lax.dynamic_slice_in_dim(table, row * rows + given_first, pair_rows, 0)
            ordered_rows = jnp.concatenate([given_rows, kept_rows], axis=0)
            alternate = jnp.concatenate([piece[1] for piece in given + kept], axis=0) / math.sqrt(length)
            edge = jnp.concatenate([piece[2][:, :count] for piece in given + kept], axis=1)
            edge = jnp.einsum("ba,bk->ak", edge / math.sqrt(length), table_cols, precision=HIGH)
            edge = edge + jnp.concatenate([alternate, edge[:, half:]], axis=1)
            rim = jnp.einsum("aj,ak->jk", ordered_rows[:, :half], edge[:, :half], precision=HIGH)
            corner = 2.0 * jnp.einsum("a,ak->k", ordered_rows[:, half], edge, precision=HIGH)
            corner = corner + jnp.einsum("aj,a->j", ordered_rows, edge[:, half], precision=HIGH)
            corner = jnp.pad(corner, (0, width - half - 1))

        packed, side = packed_section(
            col, kept[c][0], got[c], table_pair, kept_rows[c * count : (c + 1) * count], marks,
            rim, corner, side, offsets, (gx, gy), closing,
        )
    last_values, side = first_axis(packed, count, table_parts[:, :, parts - 1])
    values = values + last_values
    side = lax.all_gather(side, ("gy", "gx"), axis=0)
    side = jnp.transpose(side, (2, 1, 0, 3)).reshape(slabs + 1, block, width)

    turned = values.reshape(own, blocks, own, devices, width)
    turned = jnp.transpose(turned, (3, 1, 2, 0, 4))
    turned = [turned[:, b, :, :, : offsets[b + 1]] for b in range(blocks)]
    turned = lax.all_to_all(jnp.concatenate(turned, axis=3), ("gy", "gx"), 0, 0, tiled=True)
    turned = jnp.transpose(turned, (1, 2, 0, 3)).reshape(own, block, -1)

    slab = jnp.minimum(row, gx - 1 - row)
    far_row, far_col = row >= slabs, col >= gy // 2
    pick_rows = jnp.arange(rows)
    pick_rows = slab * rows + jnp.where(far_row, rows - pick_rows, pick_rows)
    pick_cols = jnp.arange(cols)
    pick_cols = jnp.where(far_col, (gy - col) * cols - pick_cols, col * cols + pick_cols)
    last = square([side[slabs - 1][None, :, offsets[b] : offsets[b + 1]] for b in range(blocks)], block)[0]
    rim = side[slabs, 0, : half + 1]
    last = jnp.concatenate([last, rim[None, :half]], axis=0)
    last = jnp.concatenate([last, rim[:, None]], axis=1)
    across = last[pick_rows]
    next_plane = lax.dynamic_index_in_dim(side, slab, 0, keepdims=False)

    if rows == block:
        messages = slab_messages(values, turned, offsets, slabs)
        got = []
        for group in tile_groups(messages.shape[1]):
            piece = lax.all_to_all(messages[:, group], "gx", 0, 0, tiled=True)
            got.append(gathered(piece, gy))
        rim_col = col == gy // 2
        rim = across[:, pick_cols]
        return result_block(
            got, next_plane, across, rim, pick_cols, slab, far_row, rim_col, col, offsets
        )

    sums = axis_order_sums(values, turned, offsets, block)
    messages = []
    for s in range(slabs):
        base, first = s * rows // block, s * rows
        units = []
        for b in range(blocks):
            size = (b + 1) * block
            near = jnp.zeros((own, rows, size))
            far = jnp.zeros((own, block, size))
            if b >= base:
                near = jnp.stack([sums[b][e][first : first + rows, :size] for e in range(own)])
            else:
                far = jnp.stack([sums[base][e][b * block : size, :size] for e in range(own)])
            units.append(jnp.concatenate([near, far], axis=1))
        messages.append(jnp.concatenate(units, axis=2))
    messages = jnp.stack(messages + messages[::-1])
    got = lax.all_to_all(messages, "gx", 0, 0, tiled=True)
    got = lax.all_gather(got, "gy", axis=0, tiled=True)
    got = jnp.swapaxes(got, 0, 1).reshape(block, rows + block, width)
    base = slab * rows // block
    lower = []
    for b in range(blocks):
        lanes = slice(offsets[b], offsets[b + 1])
        near = jnp.swapaxes(got[:, :rows, lanes], 0, 1)
        far = lax.dynamic_slice_in_dim(got[:, rows:, lanes], lax.rem(slab * rows, block), rows, 0)
        lower.append(jnp.where(b >= base, near, far))
    lower = jnp.concatenate(lower, axis=2)
    lower = jnp.concatenate([lower, next_plane[None]], axis=0)
    body = square([lower[:, :, offsets[b] : offsets[b + 1]] for b in range(blocks)], block)
    body = body[pick_rows - slab * rows]
    body = jnp.concatenate([body, across[:, None, :half]], axis=1)[:, pick_cols]
    body = jnp.concatenate([body, across[:, pick_cols][:, :, None]], axis=2)
    return jnp.concatenate([body, jnp.flip(body[:, :, 1:half], 2)], axis=2)


def axis_order_sums(values, turned, offsets, block):
    start = 0
    sums = []
    for top in range(len(offsets) - 1):
        size = (top + 1) * block
        parts = []
        for e in range(values.shape[0]):
            part = values[e, :size, offsets[top] : offsets[top] + size]
            lower = [turned[e, :, start + offsets[b] : start + offsets[b + 1]] for b in range(top + 1)]
            parts.append(part + part.T + square(lower, block))
        sums.append(parts)
        start += offsets[top + 1]
    return sums


def message_kernel(offsets, slabs, values, turned, messages):
    blocks = len(offsets) - 1
    block = offsets[1]
    values, turned = values[...], turned[...]
    own = values.shape[0]
    sums = axis_order_sums(values, turned, offsets, block)
    for s in range(slabs):
        for e in range(own):
            units = []
            for b in range(blocks):
                size = (b + 1) * block
                if b >= s:
                    units.append(sums[b][e][s * block : (s + 1) * block, :size])
                else:
                    units.append(sums[s][e][b * block : size, :size])
            line = jnp.concatenate(units, axis=1)
            for tile in range(messages.shape[1]):
                part = line[:, tile * 128 : (tile + 1) * 128]
                messages[s, tile, e] = part
                messages[2 * slabs - 1 - s, tile, e] = part


def slab_messages(values, turned, offsets, slabs):
    own, block = values.shape[0], offsets[1]
    shape = (2 * slabs, offsets[-1] // 128, own, block, 128)
    return pl.pallas_call(
        lambda *refs: message_kernel(offsets, slabs, *refs),
        in_specs=[pl.BlockSpec(memory_space=pltpu.VMEM)] * 2,
        out_specs=pl.BlockSpec(memory_space=pltpu.VMEM),
        out_shape=jax.ShapeDtypeStruct(shape, jnp.float32),
        compiler_params=pltpu.CompilerParams(vmem_limit_bytes=VMEM_BYTES),
    )(values, turned)


def result_kernel(
    offsets, own, devices, groups, places, next_plane, across, rim, pick, flip, *refs
):
    blocks, block = len(offsets) - 1, offsets[1]
    tiles = offsets[-1] // 128
    peers = (len(refs) - 2) // len(groups) - 1
    pieces, out = refs[: peers * len(groups)], refs[peers * len(groups)]
    held, sems = refs[peers * len(groups) + 1 : -1], refs[-1]
    step_rows, cols, length = out.shape
    half = length // 2
    slab, far_row, rim_col, me = places[0], places[1], places[2], places[3]
    lane = lax.broadcasted_iota(jnp.int32, (block, 128), 1)
    at_rim = lax.broadcasted_iota(jnp.int32, (cols, half), 0) + (1 - rim_col) == 0
    rim_lane = lax.broadcasted_iota(jnp.int32, rim.shape, 1)
    first_lane = lax.broadcasted_iota(jnp.int32, (cols, half), 1) == 0

    @pl.when(pl.program_id(0) == 0)
    def _():
        copies = []
        for g in range(len(groups)):
            for peer in range(peers):
                piece = pieces[g * peers + peer]
                size = piece.shape[0]
                spot = pl.ds(pl.multiple_of((me ^ peer) * size, size), size)
                copies.append(pltpu.make_async_copy(piece, held[g].at[spot], sems.at[g, peer]))
        for copy in copies:
            copy.start()
        for copy in copies:
            copy.wait()

    @pl.loop(0, step_rows, unroll=4)
    def _(r):
        t = pl.program_id(0) * step_rows + r
        i = jnp.where(far_row == 1, block - t, t)
        inside = (jnp.zeros((block, 128), jnp.int32) + i) < block
        i = jnp.minimum(i, block - 1)
        source = lax.div(i, devices), lax.rem(i, devices)
        parts = []
        for g, group in enumerate(groups):
            stride = (group.stop - group.start) * own * block
            for tile in range(group.start, group.stop):
                start = (tile - group.start) * own * block
                near = [
                    held[g][pl.ds(start + e * block + i, devices, stride=stride), :]
                    for e in range(own)
                ]
                near = jnp.concatenate(near, axis=0)
                far = pl.multiple_of(source[1] * stride + start + source[0] * block, block)
                far = held[g][pl.ds(far, block), :]
                kind = jnp.zeros((block, 128), jnp.int32)
                for b in range(1, blocks):
                    kind += (lane + tile * 128 >= offsets[b]).astype(jnp.int32)
                line = jnp.where(kind >= slab, near, far)
                line = jnp.where(inside, line, next_plane[:, pl.ds(tile * 128, 128)])
                parts.append(line)
        line = jnp.concatenate(parts, axis=1)
        plane = square([line[:, offsets[b] : offsets[b + 1]] for b in range(blocks)], block)
        high, low = split(plane)
        left = jnp.dot(pick[...], high, preferred_element_type=jnp.float32)
        left += jnp.dot(pick[...], low, preferred_element_type=jnp.float32)
        left = jnp.where(at_rim, across[pl.ds(t, 1), :], left)
        high, low = split(left)
        right = jnp.dot(high, flip[...], preferred_element_type=jnp.float32)
        right += jnp.dot(low, flip[...], preferred_element_type=jnp.float32)
        edge = jnp.sum(jnp.where(rim_lane == t, rim[...], 0.0), axis=1, keepdims=True)
        out[r, :, pl.ds(0, half)] = left
        out[r, :, pl.ds(half, half)] = jnp.where(first_lane, edge, right)


def result_block(got, next_plane, across, rim, pick_cols, slab, far_row, rim_col, col, offsets):
    gx, _, own, block, _ = got[0][0].shape
    groups = tile_groups(offsets[-1] // 128)
    devices = gx * len(got[0])
    rows, half = across.shape[0], across.shape[1] - 1
    cols = pick_cols.shape[0]
    step_rows = 8
    places = jnp.stack([slab, far_row.astype(jnp.int32), rim_col.astype(jnp.int32), col])
    cell = jnp.arange(half)
    pick = (pick_cols[:, None] == cell[None, :]).astype(jnp.bfloat16)
    flip = (cell[:, None] + cell[None, :] == half).astype(jnp.bfloat16)
    rim = jnp.pad(rim.T, ((0, 0), (0, 128 - rows)))
    whole = lambda array: pl.BlockSpec(array.shape, lambda i: (0,) * array.ndim)
    arrays = (next_plane, across[:, :half], rim, pick, flip)
    pieces = [piece.reshape(-1, 128) for group in got for piece in group]
    return pl.pallas_call(
        lambda *refs: result_kernel(offsets, own, devices, groups, *refs),
        grid=(rows // step_rows,),
        in_specs=[pl.BlockSpec(memory_space=pltpu.SMEM)] + [whole(array) for array in arrays]
        + [pl.BlockSpec(memory_space=pl.ANY)] * len(pieces),
        out_specs=pl.BlockSpec((step_rows, cols, 2 * half), lambda i: (i, 0, 0)),
        out_shape=jax.ShapeDtypeStruct((rows, cols, 2 * half), jnp.float32),
        scratch_shapes=[
            pltpu.VMEM((devices * (group.stop - group.start) * own * block, 128), jnp.float32)
            for group in groups
        ] + [pltpu.SemaphoreType.DMA((len(groups), len(got[0])))],
        compiler_params=pltpu.CompilerParams(vmem_limit_bytes=VMEM_BYTES),
    )(places, *arrays, *pieces)


def tile_groups(tiles):
    middle = (tiles + 1) // 2
    return [slice(0, middle), slice(middle, tiles)]


def swap(peers, bit):
    return [(q, q ^ bit) for q in range(peers)]


def gathered(piece, peers):
    pieces, bit = {0: piece}, peers // 2
    while bit:
        for place in list(pieces):
            pieces[place ^ bit] = lax.ppermute(pieces[place], "gy", swap(peers, bit))
        bit //= 2
    return [pieces[place] for place in range(peers)]


def first_axis(packed, count, table):
    gy, _, own, gx, width = packed.shape
    half = table.shape[-1]
    got = [packed[0]] + [lax.ppermute(packed[p], "gy", swap(gy, p)) for p in range(1, gy)]
    lines = [sum(got[p][:count] for p in range(first, gy, 2)) for first in range(2)]
    lines = jnp.concatenate(lines + [sum(piece[count:] for piece in got)], axis=0)
    lines = jnp.transpose(lines, (2, 1, 0, 3))
    lines = lax.all_to_all(lines, "gx", 0, 0, tiled=True)
    table = table.reshape(gx, 2 * count, half)
    values = jnp.einsum("geaw,gai->eiw", lines[:, :, : 2 * count], table, precision=HIGH)
    return values, jnp.sum(lines[:, :, 2 * count :], axis=0) / 6.0


def square(lower, block):
    lines = []
    for b in range(len(lower)):
        parts = [lower[b]]
        for c in range(b + 1, len(lower)):
            part = lower[c][..., b * block : (b + 1) * block]
            parts.append(jnp.swapaxes(part, -1, -2))
        lines.append(jnp.concatenate(parts, axis=-1))
    return jnp.concatenate(lines, axis=-2)


def solution(mesh):
    placed = (P("gx", "gy", None), P())
    return jax.shard_map(
        on_device, mesh=mesh, in_specs=placed, out_specs=P("gx", "gy", None), check_vma=False
    )
```

```python
import math

import jax
import jax.numpy as jnp
from jax import lax
from jax.experimental import pallas as pl
from jax.experimental.pallas import tpu as pltpu
from jax.sharding import PartitionSpec as P

SWEEPS = 2

AXIS_ORDERS = ((0, 1, 2), (0, 2, 1), (1, 0, 2), (1, 2, 0), (2, 0, 1), (2, 1, 0))

HIGH = lax.Precision.HIGH


def ring(axis):
    peers = lax.axis_size(axis)
    up = [(i, (i + 1) % peers) for i in range(peers)]
    return up, [(j, i) for i, j in up]


def halos(block):
    rows, cols, _ = block.shape
    up, down = ring("gx")
    right, left = ring("gy")
    top = lax.ppermute(block[rows - SWEEPS :], "gx", up)
    bottom = lax.ppermute(block[:SWEEPS], "gx", down)
    before = lax.ppermute(block[:, cols - SWEEPS :], "gy", right)
    after = lax.ppermute(block[:, :SWEEPS], "gy", left)
    sides = jnp.concatenate([before, after], axis=1)
    above = lax.ppermute(sides[rows - SWEEPS :], "gx", up)
    below = lax.ppermute(sides[:SWEEPS], "gx", down)
    sides = jnp.concatenate([above, sides, below], axis=0)
    free = ((0, 0), (8 - SWEEPS, 8 - SWEEPS), (0, 0))
    return top, bottom, jnp.pad(sides, free)


def mirror(values, axis):
    return jnp.roll(jnp.flip(values, axis), 1, axis)


def symmetric_marks(marks):
    for flip_axis in range(3):
        marks = jnp.maximum(marks, mirror(marks, flip_axis))
    united = marks
    for axis_order in AXIS_ORDERS[1:]:
        united = jnp.maximum(united, jnp.transpose(marks, axis_order))
    return united


def cosine_table(length):
    position = jnp.arange(length, dtype=jnp.int32)
    phases = jnp.mod(position[:, None] * position[None, : length // 2 + 1], length)
    return jnp.cos(phases.astype(jnp.float32) * (2.0 * math.pi / length)) / math.sqrt(length)


MARGIN = 16
CHUNK = 16
STEP_ROWS = 16
PART_ROWS = 16
VMEM_BYTES = 56 * 1024 * 1024


def split(values):
    high = values.astype(jnp.bfloat16)
    low = (values - high.astype(jnp.float32)).astype(jnp.bfloat16)
    return high, low


def fill_kernel(
    base, here, above, below, top, bottom, sides, marks, table_high, table_low,
    spectrum, alternate, edge, punched, once, high, low, folded,
):
    step_rows, cols, length = here.shape
    step = pl.program_id(0) + base[0]
    first_row = step * step_rows
    local_row = pl.program_id(0) * step_rows
    period = marks.shape[0]
    lane = lax.broadcasted_iota(jnp.int32, (128, 128), 1)
    signs = jnp.where(lax.broadcasted_iota(jnp.int32, (128, 128), 0) % 2 == 0, 1.0, -1.0)

    @pl.when(pl.program_id(0) == 0)
    def _():
        edge[...] = jnp.zeros_like(edge)

    def holes(row, start, size):
        row = lax.rem(first_row + row, period)
        start = start % period
        if start + size <= period:
            part = marks[row, pl.ds(start, size), :]
        else:
            part = jnp.concatenate(
                [marks[row, pl.ds(start, period - start), :], marks[row, pl.ds(0, start + size - period), :]],
                axis=0,
            )
        return jnp.concatenate([part] * (length // 128), axis=1)

    def punch(row, start, values):
        kept = jnp.where(holes(row, start, values.shape[0]) > 0.0, 0.0, values)
        punched[row, pl.ds(start, values.shape[0]), :] = kept

    def punch_row(row, source, index):
        full = first_row + row
        punch(row, MARGIN - 8, sides[full, pl.ds(0, 8), :])
        punch(row, MARGIN + cols, sides[full, pl.ds(8, 8), :])
        for c in range(0, cols, CHUNK):
            punch(row, MARGIN + c, source[index, pl.ds(c, CHUNK), :])

    def neighbours(ref, row, start):
        middle = ref[row, pl.ds(start, CHUNK), :]
        total = ref[row - 1, pl.ds(start, CHUNK), :] + ref[row + 1, pl.ds(start, CHUNK), :]
        total += ref[row, pl.ds(start - 1, CHUNK), :] + ref[row, pl.ds(start + 1, CHUNK), :]
        return total + pltpu.roll(middle, 1, 1) + pltpu.roll(middle, length - 1, 1)

    last = (sides.shape[0] - 2 * SWEEPS) // step_rows - 1
    for edge_rows, inside, offset, outer in (
        (above, step > 0, 0, top),
        (below, step < last, step_rows + SWEEPS, bottom),
    ):
        @pl.when(inside)
        def _():
            for r in range(SWEEPS):
                punch_row(offset + r, edge_rows, r)

        @pl.when(jnp.logical_not(inside))
        def _():
            for r in range(SWEEPS):
                punch_row(offset + r, outer, r)

    @pl.loop(0, step_rows)
    def _(r):
        punch_row(r + SWEEPS, here, r)

    @pl.loop(1, step_rows + 2 * SWEEPS - 1, unroll=2)
    def _(r):
        for start in range(MARGIN - 8, MARGIN + cols + 8, CHUNK):
            total = neighbours(punched, r, start) * holes(r, start, CHUNK)
            once[r, pl.ds(start, CHUNK), :] = punched[r, pl.ds(start, CHUNK), :] + total

    @pl.loop(0, step_rows)
    def _(r):
        for c in range(0, cols, CHUNK):
            start = MARGIN + c
            total = neighbours(once, r + SWEEPS, start) * holes(r + SWEEPS, start, CHUNK)
            filled = punched[r + SWEEPS, pl.ds(start, CHUNK), :] + total
            first, second = split(filled)
            spot = pl.ds(pl.multiple_of(r * cols + c, CHUNK), CHUNK)
            high[spot, :] = first
            low[spot, :] = second
            wrapped = filled[:, :128]
            for tile in range(1, length // 128):
                wrapped += filled[:, tile * 128 : (tile + 1) * 128]
            folded[pl.ds(c, CHUNK), :] = wrapped
        column = jnp.where(lane == local_row + r, signs, 0.0).astype(jnp.bfloat16)
        first, second = split(folded[...])
        total = jnp.dot(first, column, preferred_element_type=jnp.float32)
        total += jnp.dot(second, column, preferred_element_type=jnp.float32)
        edge[...] += total

    rows_each = 8
    half = spectrum.shape[2]
    order = lax.broadcasted_iota(jnp.int32, (rows_each, cols, half), 1)

    @pl.loop(0, step_rows // rows_each)
    def _(r):
        spot = pl.ds(pl.multiple_of(r * rows_each * cols, CHUNK), rows_each * cols)
        first, second = high[spot, :], low[spot, :]
        total = jnp.dot(first, table_low[...], preferred_element_type=jnp.float32)
        total += jnp.dot(second, table_high[...], preferred_element_type=jnp.float32)
        total += jnp.dot(first, table_high[...], preferred_element_type=jnp.float32)
        total = total.reshape(rows_each, cols, half)
        spectrum[pl.ds(r * rows_each, rows_each)] = total
        signed = jnp.sum(jnp.where(order % 2 == 0, total, -total), axis=1)
        alternate[pl.ds(pl.multiple_of(r * rows_each, rows_each), rows_each), :] = signed


def rounded_parts(table):
    rounded = lax.reduce_precision(table, 8, 7)
    return rounded.astype(jnp.bfloat16), (table - rounded).astype(jnp.bfloat16)


def fill_arrays(intensity, template, row, col, main):
    rows, cols, length = intensity.shape
    united = symmetric_marks(template)
    period = united.shape[0]
    offsets = (jnp.mod(row * rows - SWEEPS, period), jnp.mod(col * cols - MARGIN, period))
    marks = jnp.roll(united, (-offsets[0], -offsets[1]), (0, 1)).astype(jnp.float32) / 6.0
    marks = jnp.tile(marks, (1, 1, 128 // period))
    return halos(intensity) + (marks,) + rounded_parts(main)


def filled_spectrum(intensity, arrays, first, count):
    rows, cols, length = intensity.shape
    half = length // 2
    step_rows = min(STEP_ROWS, count)
    pairs = step_rows // SWEEPS
    last = rows // SWEEPS - 1
    whole = lambda array: pl.BlockSpec(array.shape, lambda i, b: (0,) * array.ndim)
    before = lambda i, b: (jnp.maximum((i + b[0]) * pairs - 1, 0), 0, 0)
    after = lambda i, b: (jnp.minimum((i + b[0] + 1) * pairs, last), 0, 0)
    padded = (step_rows + 2 * SWEEPS, cols + 2 * MARGIN, length)
    return pl.pallas_call(
        fill_kernel,
        grid_spec=pltpu.PrefetchScalarGridSpec(
            num_scalar_prefetch=1,
            grid=(count // step_rows,),
            in_specs=[
                pl.BlockSpec((step_rows, cols, length), lambda i, b: (i + b[0], 0, 0)),
                pl.BlockSpec((SWEEPS, cols, length), before),
                pl.BlockSpec((SWEEPS, cols, length), after),
            ] + [whole(array) for array in arrays],
            out_specs=[
                pl.BlockSpec((step_rows, cols, half), lambda i, b: (i, 0, 0)),
                pl.BlockSpec((step_rows, half), lambda i, b: (i, 0)),
                pl.BlockSpec((cols, 128), lambda i, b: (0, 0)),
            ],
            scratch_shapes=[
                pltpu.VMEM(padded, jnp.float32),
                pltpu.VMEM(padded, jnp.float32),
                pltpu.VMEM((step_rows * cols, length), jnp.bfloat16),
                pltpu.VMEM((step_rows * cols, length), jnp.bfloat16),
                pltpu.VMEM((cols, 128), jnp.float32),
            ],
        ),
        out_shape=[
            jax.ShapeDtypeStruct((count, cols, half), jnp.float32),
            jax.ShapeDtypeStruct((count, half), jnp.float32),
            jax.ShapeDtypeStruct((cols, 128), jnp.float32),
        ],
        compiler_params=pltpu.CompilerParams(vmem_limit_bytes=VMEM_BYTES),
        cost_estimate=pl.CostEstimate(
            flops=count * cols * length * half * 6,
            bytes_accessed=count * cols * length * 40,
            transcendentals=0,
        ),
    )((first // step_rows).reshape(1), intensity, intensity, intensity, *arrays)


def pack(section, offsets):
    block = offsets[1]
    units = [section[b * block : (b + 1) * block, : (b + 1) * block] for b in range(len(offsets) - 1)]
    return jnp.concatenate(units, axis=1)


def three_dots(left, right):
    total = jnp.dot(left[1], right[0], preferred_element_type=jnp.float32)
    total += jnp.dot(left[0], right[1], preferred_element_type=jnp.float32)
    return total + jnp.dot(left[0], right[0], preferred_element_type=jnp.float32)


def section_kernel(
    offsets, closing, me, weights, kept, got, cols_high, cols_low, rows_high, rows_low,
    rim, corner, before, out, total, lines,
):
    step, steps = pl.program_id(0), pl.num_programs(0)
    step_rows = kept.shape[0]
    half, count = rows_high.shape
    planes, block, width = before.shape
    gy, _, own, gx, _ = out.shape

    def place(layer, values):
        for e in range(own):
            for q in range(gy):
                start = (e * gy + q) * gx
                out[q ^ me[0], layer, e] = values[start : start + gx]

    @pl.when(step == 0)
    def _():
        total[...] = before[...]

    @pl.loop(0, step_rows, unroll=True)
    def _(r):
        layer = step * step_rows + r
        values = jnp.concatenate([kept[r], got[r]], axis=0)
        section = three_dots((cols_high[...], cols_low[...]), split(values))
        section = section + section.T
        line = pack(section, offsets)
        place(layer, line)
        for m in range(planes):
            total[m] += weights[m, layer] * line
        for m in range(planes - 1):
            row = (m + 1) * (half // planes)
            lines[m, pl.ds(layer, 1), :] = section[row : row + 1]

    @pl.when(step == steps - 1)
    def _():
        for m in range(planes - 1):
            plane = three_dots((rows_high[...], rows_low[...]), split(lines[m]))
            total[m] += pack(plane + plane.T, offsets)
        if closing:
            total[planes - 1] += pack(rim[...] + rim[...].T, offsets)
            for m in range(planes):
                place(count + m, total[m])
            place(count + planes, jnp.zeros((block, width), jnp.float32) + corner[...])


def packed_section(col, kept, got, table_pair, table_rows, marks, rim, corner, before, offsets, shape, closing):
    count, cols, half = kept.shape
    planes, block, width = before.shape
    gx, gy = shape
    step_rows = 4
    layers = count + (planes + 1 if closing else 0)
    whole = lambda array: pl.BlockSpec(array.shape, lambda i: (0,) * array.ndim)
    weights = jnp.stack([table_rows[:, m] for m in marks])
    arrays = rounded_parts(table_pair.T) + rounded_parts(table_rows[:, :half].T)
    arrays += (rim, corner[None], before)
    outs = [
        jax.ShapeDtypeStruct((gy, layers, block // (gx * gy), gx, width), jnp.float32),
        jax.ShapeDtypeStruct(before.shape, jnp.float32),
    ]
    rows_spec = pl.BlockSpec((step_rows, cols, half), lambda i: (i, 0, 0))
    return pl.pallas_call(
        lambda *refs: section_kernel(offsets, closing, *refs),
        grid=(count // step_rows,),
        in_specs=[pl.BlockSpec(memory_space=pltpu.SMEM)] * 2 + [rows_spec, rows_spec]
        + [whole(array) for array in arrays],
        out_specs=[whole(out) for out in outs],
        out_shape=outs,
        scratch_shapes=[pltpu.VMEM((planes, count, half), jnp.float32)],
        compiler_params=pltpu.CompilerParams(vmem_limit_bytes=VMEM_BYTES),
        cost_estimate=pl.CostEstimate(
            flops=count * 12 * cols * half * half,
            bytes_accessed=count * cols * half * 60,
            transcendentals=0,
        ),
    )(col.reshape(1), weights, kept, got, *arrays)


def on_device(intensity, template):
    rows, cols, length = intensity.shape
    gx, gy = lax.axis_size("gx"), lax.axis_size("gy")
    row, col = lax.axis_index("gx"), lax.axis_index("gy")
    devices, half = gx * gy, length // 2
    block = max(devices, rows)
    blocks, own, slabs = half // block, block // devices, gx // 2
    offsets = [block * b * (b + 1) // 2 for b in range(blocks + 1)]
    width = offsets[blocks]
    table = cosine_table(length)
    main = table[:, :half]

    pair_rows = rows // 2
    parts = max(pair_rows // PART_ROWS, 1)
    count = pair_rows // parts
    core = lax.rem(col, 2)
    arrays = fill_arrays(intensity, template, row, col, main)
    given_first, kept_first = (1 - core) * pair_rows, core * pair_rows
    given, kept, got = [], [], []

    def fill_part(c, after):
        starts = given_first + c * count, kept_first + c * count
        if after is not None:
            starts, after = lax.optimization_barrier((starts, after))
        given.append(filled_spectrum(intensity, arrays, starts[0], count))
        got.append(lax.ppermute(given[c][0], "gy", swap(gy, 1)))
        kept.append(filled_spectrum(intensity, arrays, starts[1], count))
        return after

    table_cols = lax.dynamic_slice_in_dim(table, col * cols, cols, 0)
    kept_rows = lax.dynamic_slice_in_dim(table, row * rows + kept_first, pair_rows, 0)
    marks = [rows * (m + 1) for m in range(slabs)]
    mates = lax.dynamic_slice_in_dim(main, (col + 1 - 2 * core) * cols, cols, 0)
    table_pair = jnp.concatenate([table_cols[:, :half], mates], axis=0)
    table_parts = main.reshape(gx, 2, parts, count, half) / 6.0
    table_parts = jnp.where(core == 0, table_parts, table_parts[:, ::-1])
    side = jnp.zeros((slabs, block, width), jnp.float32)
    rim, corner = jnp.zeros((half, half), jnp.float32), jnp.zeros((width,), jnp.float32)
    values, packed = 0.0, None
    for c in range(parts):
        closing = c == parts - 1
        packed = fill_part(c, packed)
        held = kept[c][0]
        if c > 0:
            held, lines = lax.optimization_barrier((held, exchanged(packed)))
            values = values + first_axis(lines, count, table_parts[:, :, c - 1])[0]
        if closing:
            given_rows = lax.dynamic_slice_in_dim(table, row * rows + given_first, pair_rows, 0)
            ordered_rows = jnp.concatenate([given_rows, kept_rows], axis=0)
            alternate = jnp.concatenate([piece[1] for piece in given + kept], axis=0) / math.sqrt(length)
            edge = jnp.concatenate([piece[2][:, :count] for piece in given + kept], axis=1)
            edge = jnp.einsum("ba,bk->ak", edge / math.sqrt(length), table_cols, precision=HIGH)
            edge = edge + jnp.concatenate([alternate, edge[:, half:]], axis=1)
            rim = jnp.einsum("aj,ak->jk", ordered_rows[:, :half], edge[:, :half], precision=HIGH)
            corner = 2.0 * jnp.einsum("a,ak->k", ordered_rows[:, half], edge, precision=HIGH)
            corner = corner + jnp.einsum("aj,a->j", ordered_rows, edge[:, half], precision=HIGH)
            corner = jnp.pad(corner, (0, width - half - 1))

        packed, side = packed_section(
            col, held, got[c], table_pair, kept_rows[c * count : (c + 1) * count], marks,
            rim, corner, side, offsets, (gx, gy), closing,
        )
    last_values, side = first_axis(exchanged(packed), count, table_parts[:, :, parts - 1])
    values = values + last_values
    turned = values.reshape(own, blocks, own, devices, width)
    turned = jnp.transpose(turned, (3, 1, 2, 0, 4))
    turned = [turned[:, b, :, :, : offsets[b + 1]] for b in range(blocks)]
    turned = lax.all_to_all(jnp.concatenate(turned, axis=3), ("gy", "gx"), 0, 0, tiled=True)
    turned = jnp.transpose(turned, (1, 2, 0, 3)).reshape(own, block, -1)

    slab = jnp.minimum(row, gx - 1 - row)
    far_row, far_col = row >= slabs, col >= gy // 2
    pick_rows = jnp.arange(rows)
    pick_rows = slab * rows + jnp.where(far_row, rows - pick_rows, pick_rows)
    pick_cols = jnp.arange(cols)
    pick_cols = jnp.where(far_col, (gy - col) * cols - pick_cols, col * cols + pick_cols)

    if rows == block:
        got = []
        for messages in slab_messages(values, turned, side, offsets, slabs):
            got.append(gathered(lax.all_to_all(messages, "gx", 0, 0, tiled=True), gy))
        tiles = width // 128
        start = tile_groups(tiles)[0].stop * own * block
        side = jnp.stack([piece[:, start : start + 3 * own * tiles] for piece in got[0]])
        bit = gy // 2
        while bit:
            paired = side.reshape((-1, 2, bit) + side.shape[1:])
            side = jnp.where((col & bit) == 0, paired, paired[:, ::-1]).reshape(side.shape)
            bit //= 2
        side = side.reshape(devices, own, 3, width)
        side = jnp.transpose(side, (2, 1, 0, 3)).reshape(3, block, width)
        next_plane, across = side[0], rim_rows(side[1:], offsets, pick_rows)
        rim_col = col == gy // 2
        rim = across[:, pick_cols]
        return result_block(
            got, next_plane, across, rim, pick_cols, slab, far_row, rim_col, col, offsets
        )

    side = lax.all_gather(side, ("gy", "gx"), axis=0)
    side = jnp.transpose(side, (2, 1, 0, 3)).reshape(slabs + 1, block, width)
    across = rim_rows(side[slabs - 1 :], offsets, pick_rows)
    next_plane = lax.dynamic_index_in_dim(side, slab, 0, keepdims=False)
    sums = axis_order_sums(values, turned, offsets, block)
    messages = []
    for s in range(slabs):
        base, first = s * rows // block, s * rows
        units = []
        for b in range(blocks):
            size = (b + 1) * block
            near = jnp.zeros((own, rows, size))
            far = jnp.zeros((own, block, size))
            if b >= base:
                near = jnp.stack([sums[b][e][first : first + rows, :size] for e in range(own)])
            else:
                far = jnp.stack([sums[base][e][b * block : size, :size] for e in range(own)])
            units.append(jnp.concatenate([near, far], axis=1))
        messages.append(jnp.concatenate(units, axis=2))
    messages = jnp.stack(messages + messages[::-1])
    got = lax.all_to_all(messages, "gx", 0, 0, tiled=True)
    got = lax.all_gather(got, "gy", axis=0, tiled=True)
    got = jnp.swapaxes(got, 0, 1).reshape(block, rows + block, width)
    base = slab * rows // block
    lower = []
    for b in range(blocks):
        lanes = slice(offsets[b], offsets[b + 1])
        near = jnp.swapaxes(got[:, :rows, lanes], 0, 1)
        far = lax.dynamic_slice_in_dim(got[:, rows:, lanes], lax.rem(slab * rows, block), rows, 0)
        lower.append(jnp.where(b >= base, near, far))
    lower = jnp.concatenate(lower, axis=2)
    lower = jnp.concatenate([lower, next_plane[None]], axis=0)
    body = square([lower[:, :, offsets[b] : offsets[b + 1]] for b in range(blocks)], block)
    body = body[pick_rows - slab * rows]
    body = jnp.concatenate([body, across[:, None, :half]], axis=1)[:, pick_cols]
    body = jnp.concatenate([body, across[:, pick_cols][:, :, None]], axis=2)
    return jnp.concatenate([body, jnp.flip(body[:, :, 1:half], 2)], axis=2)


def rim_rows(side, offsets, pick_rows):
    blocks, block = len(offsets) - 1, offsets[1]
    half = blocks * block
    last = square([side[0][:, offsets[b] : offsets[b + 1]] for b in range(blocks)], block)
    rim = side[1, 0, : half + 1]
    last = jnp.concatenate([last, rim[None, :half]], axis=0)
    return jnp.concatenate([last, rim[:, None]], axis=1)[pick_rows]


def axis_order_sums(values, turned, offsets, block):
    start = 0
    sums = []
    for top in range(len(offsets) - 1):
        size = (top + 1) * block
        parts = []
        for e in range(values.shape[0]):
            part = values[e, :size, offsets[top] : offsets[top] + size]
            lower = [turned[e, :, start + offsets[b] : start + offsets[b + 1]] for b in range(top + 1)]
            parts.append(part + part.T + square(lower, block))
        sums.append(parts)
        start += offsets[top + 1]
    return sums


def message_kernel(offsets, slabs, values, turned, side, *messages):
    blocks, block = len(offsets) - 1, offsets[1]
    values, turned = values[...], turned[...]
    own = values.shape[0]
    sums = axis_order_sums(values, turned, offsets, block)
    groups = tile_groups(offsets[-1] // 128)
    side_start = groups[0].stop * own * block
    messages[0][:, side_start:] = jnp.zeros_like(messages[0][:, side_start:])
    for s in range(slabs):
        places = s, 2 * slabs - 1 - s
        for e in range(own):
            units = []
            for b in range(blocks):
                size = (b + 1) * block
                if b >= s:
                    units.append(sums[b][e][s * block : (s + 1) * block, :size])
                else:
                    units.append(sums[s][e][b * block : size, :size])
            line = jnp.concatenate(units, axis=1)
            for group, out in zip(groups, messages):
                for tile in range(group.start, group.stop):
                    start = ((tile - group.start) * own + e) * block
                    for place in places:
                        out[place, start : start + block] = line[:, tile * 128 : (tile + 1) * 128]
            row = side_start + 3 * e * groups[-1].stop
            for plane in (s, slabs - 1, slabs):
                for tile in range(groups[-1].stop):
                    part = side[e, plane : plane + 1, tile * 128 : (tile + 1) * 128]
                    for place in places:
                        messages[0][place, row : row + 1] = part
                    row += 1


def slab_messages(values, turned, side, offsets, slabs):
    own, block, tiles = values.shape[0], offsets[1], offsets[-1] // 128
    sizes = [(group.stop - group.start) * own * block for group in tile_groups(tiles)]
    sizes[0] += -(-3 * own * tiles // 8) * 8
    return pl.pallas_call(
        lambda *refs: message_kernel(offsets, slabs, *refs),
        in_specs=[pl.BlockSpec(memory_space=pltpu.VMEM)] * 3,
        out_specs=[pl.BlockSpec(memory_space=pltpu.VMEM)] * 2,
        out_shape=[jax.ShapeDtypeStruct((2 * slabs, size, 128), jnp.float32) for size in sizes],
        compiler_params=pltpu.CompilerParams(vmem_limit_bytes=VMEM_BYTES),
    )(values, turned, side)


def result_kernel(
    offsets, own, devices, groups, places, next_plane, across, rim, pick, flip, *refs
):
    blocks, block = len(offsets) - 1, offsets[1]
    tiles = offsets[-1] // 128
    peers = (len(refs) - 2) // len(groups) - 1
    pieces, out = refs[: peers * len(groups)], refs[peers * len(groups)]
    held, sems = refs[peers * len(groups) + 1 : -1], refs[-1]
    step_rows, cols, length = out.shape
    half = length // 2
    slab, far_row, rim_col, me = places[0], places[1], places[2], places[3]
    lane = lax.broadcasted_iota(jnp.int32, (block, 128), 1)
    at_rim = lax.broadcasted_iota(jnp.int32, (cols, half), 0) + (1 - rim_col) == 0
    rim_lane = lax.broadcasted_iota(jnp.int32, rim.shape, 1)
    first_lane = lax.broadcasted_iota(jnp.int32, (cols, half), 1) == 0

    @pl.when(pl.program_id(0) == 0)
    def _():
        copies = []
        for g in range(len(groups)):
            for peer in range(peers):
                piece = pieces[g * peers + peer]
                size = piece.shape[0]
                spot = pl.ds(pl.multiple_of((me ^ peer) * size, size), size)
                copies.append(pltpu.make_async_copy(piece, held[g].at[spot], sems.at[g, peer]))
        for copy in copies:
            copy.start()
        for copy in copies:
            copy.wait()

    @pl.loop(0, step_rows, unroll=4)
    def _(r):
        t = pl.program_id(0) * step_rows + r
        i = jnp.where(far_row == 1, block - t, t)
        inside = (jnp.zeros((block, 128), jnp.int32) + i) < block
        i = jnp.minimum(i, block - 1)
        source = lax.div(i, devices), lax.rem(i, devices)
        parts = []
        for g, group in enumerate(groups):
            stride = held[g].shape[0] // devices
            for tile in range(group.start, group.stop):
                start = (tile - group.start) * own * block
                near = [
                    held[g][pl.ds(start + e * block + i, devices, stride=stride), :]
                    for e in range(own)
                ]
                near = jnp.concatenate(near, axis=0)
                far = pl.multiple_of(source[1] * stride + start + source[0] * block, 8)
                far = held[g][pl.ds(far, block), :]
                kind = jnp.zeros((block, 128), jnp.int32)
                for b in range(1, blocks):
                    kind += (lane + tile * 128 >= offsets[b]).astype(jnp.int32)
                line = jnp.where(kind >= slab, near, far)
                line = jnp.where(inside, line, next_plane[:, pl.ds(tile * 128, 128)])
                parts.append(line)
        line = jnp.concatenate(parts, axis=1)
        plane = square([line[:, offsets[b] : offsets[b + 1]] for b in range(blocks)], block)
        high, low = split(plane)
        left = jnp.dot(pick[...], high, preferred_element_type=jnp.float32)
        left += jnp.dot(pick[...], low, preferred_element_type=jnp.float32)
        left = jnp.where(at_rim, across[pl.ds(t, 1), :], left)
        high, low = split(left)
        right = jnp.dot(high, flip[...], preferred_element_type=jnp.float32)
        right += jnp.dot(low, flip[...], preferred_element_type=jnp.float32)
        edge = jnp.sum(jnp.where(rim_lane == t, rim[...], 0.0), axis=1, keepdims=True)
        out[r, :, pl.ds(0, half)] = left
        out[r, :, pl.ds(half, half)] = jnp.where(first_lane, edge, right)


def result_block(got, next_plane, across, rim, pick_cols, slab, far_row, rim_col, col, offsets):
    block = offsets[1]
    gx = got[0][0].shape[0]
    groups = tile_groups(offsets[-1] // 128)
    devices = gx * len(got[0])
    own = block // devices
    rows, half = across.shape[0], across.shape[1] - 1
    cols = pick_cols.shape[0]
    step_rows = 8
    places = jnp.stack([slab, far_row.astype(jnp.int32), rim_col.astype(jnp.int32), col])
    cell = jnp.arange(half)
    pick = (pick_cols[:, None] == cell[None, :]).astype(jnp.bfloat16)
    flip = (cell[:, None] + cell[None, :] == half).astype(jnp.bfloat16)
    rim = jnp.pad(rim.T, ((0, 0), (0, 128 - rows)))
    whole = lambda array: pl.BlockSpec(array.shape, lambda i: (0,) * array.ndim)
    arrays = (next_plane, across[:, :half], rim, pick, flip)
    pieces = [piece.reshape(-1, 128) for group in got for piece in group]
    return pl.pallas_call(
        lambda *refs: result_kernel(offsets, own, devices, groups, *refs),
        grid=(rows // step_rows,),
        in_specs=[pl.BlockSpec(memory_space=pltpu.SMEM)] + [whole(array) for array in arrays]
        + [pl.BlockSpec(memory_space=pl.ANY)] * len(pieces),
        out_specs=pl.BlockSpec((step_rows, cols, 2 * half), lambda i: (i, 0, 0)),
        out_shape=jax.ShapeDtypeStruct((rows, cols, 2 * half), jnp.float32),
        scratch_shapes=[
            pltpu.VMEM((devices * group[0].shape[1], 128), jnp.float32) for group in got
        ] + [pltpu.SemaphoreType.DMA((len(groups), len(got[0])))],
        compiler_params=pltpu.CompilerParams(vmem_limit_bytes=VMEM_BYTES),
    )(places, *arrays, *pieces)


def tile_groups(tiles):
    middle = (tiles + 1) // 2
    return [slice(0, middle), slice(middle, tiles)]


def swap(peers, bit):
    return [(q, q ^ bit) for q in range(peers)]


def gathered(piece, peers):
    pieces, bit = {0: piece}, peers // 2
    while bit:
        for place in list(pieces):
            pieces[place ^ bit] = lax.ppermute(pieces[place], "gy", swap(peers, bit))
        bit //= 2
    return [pieces[place] for place in range(peers)]


def exchanged(packed):
    gy = packed.shape[0]
    return [packed[0]] + [lax.ppermute(packed[p], "gy", swap(gy, p)) for p in range(1, gy)]


def first_axis(got, count, table):
    gy, (_, own, gx, width) = len(got), got[0].shape
    half = table.shape[-1]
    lines = [sum(got[p][:count] for p in range(first, gy, 2)) for first in range(2)]
    lines = jnp.concatenate(lines + [sum(piece[count:] for piece in got)], axis=0)
    lines = jnp.transpose(lines, (2, 1, 0, 3))
    lines = lax.all_to_all(lines, "gx", 0, 0, tiled=True)
    table = table.reshape(gx, 2 * count, half)
    values = jnp.einsum("geaw,gai->eiw", lines[:, :, : 2 * count], table, precision=HIGH)
    return values, jnp.sum(lines[:, :, 2 * count :], axis=0) / 6.0


def square(lower, block):
    lines = []
    for b in range(len(lower)):
        parts = [lower[b]]
        for c in range(b + 1, len(lower)):
            part = lower[c][..., b * block : (b + 1) * block]
            parts.append(jnp.swapaxes(part, -1, -2))
        lines.append(jnp.concatenate(parts, axis=-1))
    return jnp.concatenate(lines, axis=-2)


def solution(mesh):
    placed = (P("gx", "gy", None), P())
    return jax.shard_map(
        on_device, mesh=mesh, in_specs=placed, out_specs=P("gx", "gy", None), check_vma=False
    )
```

```python
import math

import jax
import jax.numpy as jnp
from jax import lax
from jax.experimental import pallas as pl
from jax.experimental.pallas import tpu as pltpu
from jax.sharding import PartitionSpec as P

SWEEPS = 2

AXIS_ORDERS = ((0, 1, 2), (0, 2, 1), (1, 0, 2), (1, 2, 0), (2, 0, 1), (2, 1, 0))

HIGH = lax.Precision.HIGH


def ring(axis):
    peers = lax.axis_size(axis)
    up = [(i, (i + 1) % peers) for i in range(peers)]
    return up, [(j, i) for i, j in up]


def halos(block):
    rows, cols, _ = block.shape
    up, down = ring("gx")
    right, left = ring("gy")
    top = lax.ppermute(block[rows - SWEEPS :], "gx", up)
    bottom = lax.ppermute(block[:SWEEPS], "gx", down)
    before = lax.ppermute(block[:, cols - SWEEPS :], "gy", right)
    after = lax.ppermute(block[:, :SWEEPS], "gy", left)
    sides = jnp.concatenate([before, after], axis=1)
    above = lax.ppermute(sides[rows - SWEEPS :], "gx", up)
    below = lax.ppermute(sides[:SWEEPS], "gx", down)
    sides = jnp.concatenate([above, sides, below], axis=0)
    free = ((0, 0), (8 - SWEEPS, 8 - SWEEPS), (0, 0))
    return top, bottom, jnp.pad(sides, free)


def mirror(values, axis):
    return jnp.roll(jnp.flip(values, axis), 1, axis)


def symmetric_marks(marks):
    for flip_axis in range(3):
        marks = jnp.maximum(marks, mirror(marks, flip_axis))
    united = marks
    for axis_order in AXIS_ORDERS[1:]:
        united = jnp.maximum(united, jnp.transpose(marks, axis_order))
    return united


def cosine_table(length):
    position = jnp.arange(length, dtype=jnp.int32)
    phases = jnp.mod(position[:, None] * position[None, : length // 2 + 1], length)
    return jnp.cos(phases.astype(jnp.float32) * (2.0 * math.pi / length)) / math.sqrt(length)


MARGIN = 16
CHUNK = 16
STEP_ROWS = 16
PART_STEP = 8
VMEM_BYTES = 56 * 1024 * 1024


def split(values):
    high = values.astype(jnp.bfloat16)
    low = (values - high.astype(jnp.float32)).astype(jnp.bfloat16)
    return high, low


def fill_kernel(
    base, here, above, below, top, bottom, sides, marks, table_high, table_low,
    spectrum, alternate, edge, punched, once, high, low, folded,
):
    step_rows, cols, length = here.shape
    step = pl.program_id(0) + base[0]
    first_row = step * step_rows
    local_row = pl.program_id(0) * step_rows
    period = marks.shape[0]
    lane = lax.broadcasted_iota(jnp.int32, (128, 128), 1)
    signs = jnp.where(lax.broadcasted_iota(jnp.int32, (128, 128), 0) % 2 == 0, 1.0, -1.0)

    @pl.when(pl.program_id(0) == 0)
    def _():
        edge[...] = jnp.zeros_like(edge)

    def holes(row, start, size):
        row = lax.rem(first_row + row, period)
        start = start % period
        if start + size <= period:
            part = marks[row, pl.ds(start, size), :]
        else:
            part = jnp.concatenate(
                [marks[row, pl.ds(start, period - start), :], marks[row, pl.ds(0, start + size - period), :]],
                axis=0,
            )
        return jnp.concatenate([part] * (length // 128), axis=1)

    def punch(row, start, values):
        kept = jnp.where(holes(row, start, values.shape[0]) > 0.0, 0.0, values)
        punched[row, pl.ds(start, values.shape[0]), :] = kept

    def punch_row(row, source, index):
        full = first_row + row
        punch(row, MARGIN - 8, sides[full, pl.ds(0, 8), :])
        punch(row, MARGIN + cols, sides[full, pl.ds(8, 8), :])
        for c in range(0, cols, CHUNK):
            punch(row, MARGIN + c, source[index, pl.ds(c, CHUNK), :])

    def neighbours(ref, row, start):
        middle = ref[row, pl.ds(start, CHUNK), :]
        total = ref[row - 1, pl.ds(start, CHUNK), :] + ref[row + 1, pl.ds(start, CHUNK), :]
        total += ref[row, pl.ds(start - 1, CHUNK), :] + ref[row, pl.ds(start + 1, CHUNK), :]
        return total + pltpu.roll(middle, 1, 1) + pltpu.roll(middle, length - 1, 1)

    last = (sides.shape[0] - 2 * SWEEPS) // step_rows - 1
    for edge_rows, inside, offset, outer in (
        (above, step > 0, 0, top),
        (below, step < last, step_rows + SWEEPS, bottom),
    ):
        @pl.when(inside)
        def _():
            for r in range(SWEEPS):
                punch_row(offset + r, edge_rows, r)

        @pl.when(jnp.logical_not(inside))
        def _():
            for r in range(SWEEPS):
                punch_row(offset + r, outer, r)

    @pl.loop(0, step_rows)
    def _(r):
        punch_row(r + SWEEPS, here, r)

    @pl.loop(1, step_rows + 2 * SWEEPS - 1, unroll=2)
    def _(r):
        for start in range(MARGIN - 8, MARGIN + cols + 8, CHUNK):
            total = neighbours(punched, r, start) * holes(r, start, CHUNK)
            once[r, pl.ds(start, CHUNK), :] = punched[r, pl.ds(start, CHUNK), :] + total

    @pl.loop(0, step_rows)
    def _(r):
        for c in range(0, cols, CHUNK):
            start = MARGIN + c
            total = neighbours(once, r + SWEEPS, start) * holes(r + SWEEPS, start, CHUNK)
            filled = punched[r + SWEEPS, pl.ds(start, CHUNK), :] + total
            first, second = split(filled)
            spot = pl.ds(pl.multiple_of(r * cols + c, CHUNK), CHUNK)
            high[spot, :] = first
            low[spot, :] = second
            wrapped = filled[:, :128]
            for tile in range(1, length // 128):
                wrapped += filled[:, tile * 128 : (tile + 1) * 128]
            folded[pl.ds(c, CHUNK), :] = wrapped
        column = jnp.where(lane == local_row + r, signs, 0.0).astype(jnp.bfloat16)
        first, second = split(folded[...])
        total = jnp.dot(first, column, preferred_element_type=jnp.float32)
        total += jnp.dot(second, column, preferred_element_type=jnp.float32)
        edge[...] += total

    rows_each = 8
    half = spectrum.shape[2]
    order = lax.broadcasted_iota(jnp.int32, (rows_each, cols, half), 1)

    @pl.loop(0, step_rows // rows_each)
    def _(r):
        spot = pl.ds(pl.multiple_of(r * rows_each * cols, CHUNK), rows_each * cols)
        first, second = high[spot, :], low[spot, :]
        total = jnp.dot(first, table_low[...], preferred_element_type=jnp.float32)
        total += jnp.dot(second, table_high[...], preferred_element_type=jnp.float32)
        total += jnp.dot(first, table_high[...], preferred_element_type=jnp.float32)
        total = total.reshape(rows_each, cols, half)
        spectrum[pl.ds(r * rows_each, rows_each)] = total
        signed = jnp.sum(jnp.where(order % 2 == 0, total, -total), axis=1)
        alternate[pl.ds(pl.multiple_of(r * rows_each, rows_each), rows_each), :] = signed


def rounded_parts(table):
    rounded = lax.reduce_precision(table, 8, 7)
    return rounded.astype(jnp.bfloat16), (table - rounded).astype(jnp.bfloat16)


def fill_arrays(intensity, template, row, col, main):
    rows, cols, length = intensity.shape
    united = symmetric_marks(template)
    period = united.shape[0]
    offsets = (jnp.mod(row * rows - SWEEPS, period), jnp.mod(col * cols - MARGIN, period))
    marks = jnp.roll(united, (-offsets[0], -offsets[1]), (0, 1)).astype(jnp.float32) / 6.0
    marks = jnp.tile(marks, (1, 1, 128 // period))
    return halos(intensity) + (marks,) + rounded_parts(main)


def filled_spectrum(intensity, arrays, first, count):
    rows, cols, length = intensity.shape
    half = length // 2
    step_rows = min(STEP_ROWS, count)
    pairs = step_rows // SWEEPS
    last = rows // SWEEPS - 1
    whole = lambda array: pl.BlockSpec(array.shape, lambda i, b: (0,) * array.ndim)
    before = lambda i, b: (jnp.maximum((i + b[0]) * pairs - 1, 0), 0, 0)
    after = lambda i, b: (jnp.minimum((i + b[0] + 1) * pairs, last), 0, 0)
    padded = (step_rows + 2 * SWEEPS, cols + 2 * MARGIN, length)
    return pl.pallas_call(
        fill_kernel,
        grid_spec=pltpu.PrefetchScalarGridSpec(
            num_scalar_prefetch=1,
            grid=(count // step_rows,),
            in_specs=[
                pl.BlockSpec((step_rows, cols, length), lambda i, b: (i + b[0], 0, 0)),
                pl.BlockSpec((SWEEPS, cols, length), before),
                pl.BlockSpec((SWEEPS, cols, length), after),
            ] + [whole(array) for array in arrays],
            out_specs=[
                pl.BlockSpec((step_rows, cols, half), lambda i, b: (i, 0, 0)),
                pl.BlockSpec((step_rows, half), lambda i, b: (i, 0)),
                pl.BlockSpec((cols, 128), lambda i, b: (0, 0)),
            ],
            scratch_shapes=[
                pltpu.VMEM(padded, jnp.float32),
                pltpu.VMEM(padded, jnp.float32),
                pltpu.VMEM((step_rows * cols, length), jnp.bfloat16),
                pltpu.VMEM((step_rows * cols, length), jnp.bfloat16),
                pltpu.VMEM((cols, 128), jnp.float32),
            ],
        ),
        out_shape=[
            jax.ShapeDtypeStruct((count, cols, half), jnp.float32),
            jax.ShapeDtypeStruct((count, half), jnp.float32),
            jax.ShapeDtypeStruct((cols, 128), jnp.float32),
        ],
        compiler_params=pltpu.CompilerParams(vmem_limit_bytes=VMEM_BYTES),
        cost_estimate=pl.CostEstimate(
            flops=count * cols * length * half * 6,
            bytes_accessed=count * cols * (length + half) * 4,
            transcendentals=0,
        ),
    )((first // step_rows).reshape(1), intensity, intensity, intensity, *arrays)


def pack(section, offsets):
    block = offsets[1]
    units = [section[b * block : (b + 1) * block, : (b + 1) * block] for b in range(len(offsets) - 1)]
    return jnp.concatenate(units, axis=1)


def three_dots(left, right):
    total = jnp.dot(left[1], right[0], preferred_element_type=jnp.float32)
    total += jnp.dot(left[0], right[1], preferred_element_type=jnp.float32)
    return total + jnp.dot(left[0], right[0], preferred_element_type=jnp.float32)


def section_kernel(
    offsets, closing, me, weights, kept, got, cols_high, cols_low, rows_high, rows_low,
    rim, corner, before, out, total, lines,
):
    step, steps = pl.program_id(0), pl.num_programs(0)
    step_rows = kept.shape[0]
    half, count = rows_high.shape
    planes, block, width = before.shape
    gy, _, own, gx, _ = out.shape

    def place(layer, values):
        for e in range(own):
            for q in range(gy):
                start = (e * gy + q) * gx
                out[q ^ me[0], layer, e] = values[start : start + gx]

    @pl.when(step == 0)
    def _():
        total[...] = before[...]

    @pl.loop(0, step_rows, unroll=True)
    def _(r):
        layer = step * step_rows + r
        values = jnp.concatenate([kept[r], got[r]], axis=0)
        section = three_dots((cols_high[...], cols_low[...]), split(values))
        section = section + section.T
        line = pack(section, offsets)
        place(layer, line)
        for m in range(planes):
            total[m] += weights[m, layer] * line
        for m in range(planes - 1):
            row = (m + 1) * (half // planes)
            lines[m, pl.ds(layer, 1), :] = section[row : row + 1]

    @pl.when(step == steps - 1)
    def _():
        for m in range(planes - 1):
            plane = three_dots((rows_high[...], rows_low[...]), split(lines[m]))
            total[m] += pack(plane + plane.T, offsets)
        if closing:
            total[planes - 1] += pack(rim[...] + rim[...].T, offsets)
            for m in range(planes):
                place(count + m, total[m])
            place(count + planes, jnp.zeros((block, width), jnp.float32) + corner[...])


def packed_section(col, kept, got, table_pair, table_rows, marks, rim, corner, before, offsets, shape, closing):
    count, cols, half = kept.shape
    planes, block, width = before.shape
    gx, gy = shape
    step_rows = 4
    layers = count + (planes + 1 if closing else 0)
    whole = lambda array: pl.BlockSpec(array.shape, lambda i: (0,) * array.ndim)
    weights = jnp.stack([table_rows[:, m] for m in marks])
    arrays = rounded_parts(table_pair.T) + rounded_parts(table_rows[:, :half].T)
    arrays += (rim, corner[None], before)
    outs = [
        jax.ShapeDtypeStruct((gy, layers, block // (gx * gy), gx, width), jnp.float32),
        jax.ShapeDtypeStruct(before.shape, jnp.float32),
    ]
    rows_spec = pl.BlockSpec((step_rows, cols, half), lambda i: (i, 0, 0))
    return pl.pallas_call(
        lambda *refs: section_kernel(offsets, closing, *refs),
        grid=(count // step_rows,),
        in_specs=[pl.BlockSpec(memory_space=pltpu.SMEM)] * 2 + [rows_spec, rows_spec]
        + [whole(array) for array in arrays],
        out_specs=[whole(out) for out in outs],
        out_shape=outs,
        scratch_shapes=[pltpu.VMEM((planes, count, half), jnp.float32)],
        compiler_params=pltpu.CompilerParams(vmem_limit_bytes=VMEM_BYTES),
        cost_estimate=pl.CostEstimate(
            flops=count * 12 * cols * half * half,
            bytes_accessed=count * cols * half * 16,
            transcendentals=0,
        ),
    )(col.reshape(1), weights, kept, got, *arrays)


def on_device(intensity, template):
    rows, cols, length = intensity.shape
    gx, gy = lax.axis_size("gx"), lax.axis_size("gy")
    row, col = lax.axis_index("gx"), lax.axis_index("gy")
    devices, half = gx * gy, length // 2
    block = max(devices, rows)
    blocks, own, slabs = half // block, block // devices, gx // 2
    offsets = [block * b * (b + 1) // 2 for b in range(blocks + 1)]
    width = offsets[blocks]
    table = cosine_table(length)
    main = table[:, :half]

    pair_rows = rows // 2
    counts = part_counts(pair_rows)
    ends = [sum(counts[: c + 1]) for c in range(len(counts))]
    core = lax.rem(col, 2)
    arrays = fill_arrays(intensity, template, row, col, main)
    given_first, kept_first = (1 - core) * pair_rows, core * pair_rows
    given, kept, got = [], [], []

    def fill_part(c, after):
        count, start = counts[c], ends[c] - counts[c]
        starts = given_first + start, kept_first + start
        if after is not None:
            starts, after = lax.optimization_barrier((starts, after))
        given.append(filled_spectrum(intensity, arrays, starts[0], count))
        got.append(lax.ppermute(given[c][0], "gy", swap(gy, 1)))
        kept.append(filled_spectrum(intensity, arrays, starts[1], count))
        return after

    table_cols = lax.dynamic_slice_in_dim(table, col * cols, cols, 0)
    kept_rows = lax.dynamic_slice_in_dim(table, row * rows + kept_first, pair_rows, 0)
    marks = [rows * (m + 1) for m in range(slabs)]
    mates = lax.dynamic_slice_in_dim(main, (col + 1 - 2 * core) * cols, cols, 0)
    table_pair = jnp.concatenate([table_cols[:, :half], mates], axis=0)
    table_parts = main.reshape(gx, 2, pair_rows, half) / 6.0
    table_parts = jnp.where(core == 0, table_parts, table_parts[:, ::-1])
    table_parts = [table_parts[:, :, end - count : end] for count, end in zip(counts, ends)]
    side = jnp.zeros((slabs, block, width), jnp.float32)
    rim, corner = jnp.zeros((half, half), jnp.float32), jnp.zeros((width,), jnp.float32)
    values, packed, lines = 0.0, None, None
    for c, count in enumerate(counts):
        closing = c == len(counts) - 1
        packed = fill_part(c, packed)
        held = kept[c][0]
        if c > 0:
            held, got_lines = lax.optimization_barrier((held, exchanged(packed)))
            lines = sent_lines(got_lines, counts[c - 1], lines)
            values = values + first_axis(lines, table_parts[c - 1])
        if closing:
            given_rows = lax.dynamic_slice_in_dim(table, row * rows + given_first, pair_rows, 0)
            ordered_rows = jnp.concatenate([given_rows, kept_rows], axis=0)
            alternate = jnp.concatenate([piece[1] for piece in given + kept], axis=0) / math.sqrt(length)
            edge = [piece[2][:, : piece[1].shape[0]] for piece in given + kept]
            edge = jnp.concatenate(edge, axis=1)
            edge = jnp.einsum("ba,bk->ak", edge / math.sqrt(length), table_cols, precision=HIGH)
            edge = edge + jnp.concatenate([alternate, edge[:, half:]], axis=1)
            rim = jnp.einsum("aj,ak->jk", ordered_rows[:, :half], edge[:, :half], precision=HIGH)
            corner = 2.0 * jnp.einsum("a,ak->k", ordered_rows[:, half], edge, precision=HIGH)
            corner = corner + jnp.einsum("aj,a->j", ordered_rows, edge[:, half], precision=HIGH)
            corner = jnp.pad(corner, (0, width - half - 1))

        packed, side = packed_section(
            col, held, got[c], table_pair, kept_rows[ends[c] - count : ends[c]], marks,
            rim, corner, side, offsets, (gx, gy), closing,
        )
    lines = sent_lines(exchanged(packed), counts[-1], lines)
    values = values + first_axis(lines, table_parts[-1])
    side = jnp.sum(lines[:, :, 2 * counts[-1] :], axis=0) / 6.0
    turned = values.reshape(own, blocks, own, devices, width)
    turned = jnp.transpose(turned, (3, 1, 2, 0, 4))
    turned = [turned[:, b, :, :, : offsets[b + 1]] for b in range(blocks)]
    turned = lax.all_to_all(jnp.concatenate(turned, axis=3), ("gy", "gx"), 0, 0, tiled=True)
    turned = jnp.transpose(turned, (1, 2, 0, 3)).reshape(own, block, -1)

    slab = jnp.minimum(row, gx - 1 - row)
    far_row, far_col = row >= slabs, col >= gy // 2
    pick_rows = jnp.arange(rows)
    pick_rows = slab * rows + jnp.where(far_row, rows - pick_rows, pick_rows)
    pick_cols = jnp.arange(cols)
    pick_cols = jnp.where(far_col, (gy - col) * cols - pick_cols, col * cols + pick_cols)

    if rows == block:
        got = []
        for messages in slab_messages(values, turned, side, offsets, slabs):
            got.append(gathered(lax.all_to_all(messages, "gx", 0, 0, tiled=True), gy))
        tiles = width // 128
        start = tile_groups(tiles)[0].stop * own * block
        side = jnp.stack([piece[:, start : start + 3 * own * tiles] for piece in got[0]])
        bit = gy // 2
        while bit:
            paired = side.reshape((-1, 2, bit) + side.shape[1:])
            side = jnp.where((col & bit) == 0, paired, paired[:, ::-1]).reshape(side.shape)
            bit //= 2
        side = side.reshape(devices, own, 3, width)
        side = jnp.transpose(side, (2, 1, 0, 3)).reshape(3, block, width)
        next_plane, across = side[0], rim_rows(side[1:], offsets, pick_rows)
        rim_col = col == gy // 2
        rim = across[:, pick_cols]
        return result_block(
            got, next_plane, across, rim, pick_cols, slab, far_row, rim_col, col, offsets
        )

    side = lax.all_gather(side, ("gy", "gx"), axis=0)
    side = jnp.transpose(side, (2, 1, 0, 3)).reshape(slabs + 1, block, width)
    across = rim_rows(side[slabs - 1 :], offsets, pick_rows)
    next_plane = lax.dynamic_index_in_dim(side, slab, 0, keepdims=False)
    sums = axis_order_sums(values, turned, offsets, block)
    messages = []
    for s in range(slabs):
        base, first = s * rows // block, s * rows
        units = []
        for b in range(blocks):
            size = (b + 1) * block
            near = jnp.zeros((own, rows, size))
            far = jnp.zeros((own, block, size))
            if b >= base:
                near = jnp.stack([sums[b][e][first : first + rows, :size] for e in range(own)])
            else:
                far = jnp.stack([sums[base][e][b * block : size, :size] for e in range(own)])
            units.append(jnp.concatenate([near, far], axis=1))
        messages.append(jnp.concatenate(units, axis=2))
    messages = jnp.stack(messages + messages[::-1])
    got = lax.all_to_all(messages, "gx", 0, 0, tiled=True)
    got = lax.all_gather(got, "gy", axis=0, tiled=True)
    got = jnp.swapaxes(got, 0, 1).reshape(block, rows + block, width)
    base = slab * rows // block
    lower = []
    for b in range(blocks):
        lanes = slice(offsets[b], offsets[b + 1])
        near = jnp.swapaxes(got[:, :rows, lanes], 0, 1)
        far = lax.dynamic_slice_in_dim(got[:, rows:, lanes], lax.rem(slab * rows, block), rows, 0)
        lower.append(jnp.where(b >= base, near, far))
    lower = jnp.concatenate(lower, axis=2)
    lower = jnp.concatenate([lower, next_plane[None]], axis=0)
    body = square([lower[:, :, offsets[b] : offsets[b + 1]] for b in range(blocks)], block)
    body = body[pick_rows - slab * rows]
    body = jnp.concatenate([body, across[:, None, :half]], axis=1)[:, pick_cols]
    body = jnp.concatenate([body, across[:, pick_cols][:, :, None]], axis=2)
    return jnp.concatenate([body, jnp.flip(body[:, :, 1:half], 2)], axis=2)


def rim_rows(side, offsets, pick_rows):
    blocks, block = len(offsets) - 1, offsets[1]
    half = blocks * block
    last = square([side[0][:, offsets[b] : offsets[b + 1]] for b in range(blocks)], block)
    rim = side[1, 0, : half + 1]
    last = jnp.concatenate([last, rim[None, :half]], axis=0)
    return jnp.concatenate([last, rim[:, None]], axis=1)[pick_rows]


def axis_order_sums(values, turned, offsets, block):
    start = 0
    sums = []
    for top in range(len(offsets) - 1):
        size = (top + 1) * block
        parts = []
        for e in range(values.shape[0]):
            part = values[e, :size, offsets[top] : offsets[top] + size]
            lower = [turned[e, :, start + offsets[b] : start + offsets[b + 1]] for b in range(top + 1)]
            parts.append(part + part.T + square(lower, block))
        sums.append(parts)
        start += offsets[top + 1]
    return sums


def message_kernel(offsets, slabs, values, turned, side, *messages):
    blocks, block = len(offsets) - 1, offsets[1]
    values, turned = values[...], turned[...]
    own = values.shape[0]
    sums = axis_order_sums(values, turned, offsets, block)
    groups = tile_groups(offsets[-1] // 128)
    side_start = groups[0].stop * own * block
    messages[0][:, side_start:] = jnp.zeros_like(messages[0][:, side_start:])
    for s in range(slabs):
        places = s, 2 * slabs - 1 - s
        for e in range(own):
            units = []
            for b in range(blocks):
                size = (b + 1) * block
                if b >= s:
                    units.append(sums[b][e][s * block : (s + 1) * block, :size])
                else:
                    units.append(sums[s][e][b * block : size, :size])
            line = jnp.concatenate(units, axis=1)
            for group, out in zip(groups, messages):
                for tile in range(group.start, group.stop):
                    start = ((tile - group.start) * own + e) * block
                    for place in places:
                        out[place, start : start + block] = line[:, tile * 128 : (tile + 1) * 128]
            row = side_start + 3 * e * groups[-1].stop
            for plane in (s, slabs - 1, slabs):
                for tile in range(groups[-1].stop):
                    part = side[e, plane : plane + 1, tile * 128 : (tile + 1) * 128]
                    for place in places:
                        messages[0][place, row : row + 1] = part
                    row += 1


def slab_messages(values, turned, side, offsets, slabs):
    own, block, tiles = values.shape[0], offsets[1], offsets[-1] // 128
    sizes = [(group.stop - group.start) * own * block for group in tile_groups(tiles)]
    sizes[0] += -(-3 * own * tiles // 8) * 8
    return pl.pallas_call(
        lambda *refs: message_kernel(offsets, slabs, *refs),
        in_specs=[pl.BlockSpec(memory_space=pltpu.VMEM)] * 3,
        out_specs=[pl.BlockSpec(memory_space=pltpu.VMEM)] * len(sizes),
        out_shape=[jax.ShapeDtypeStruct((2 * slabs, size, 128), jnp.float32) for size in sizes],
        compiler_params=pltpu.CompilerParams(vmem_limit_bytes=VMEM_BYTES),
    )(values, turned, side)


def result_kernel(
    offsets, own, devices, groups, places, next_plane, across, rim, pick, flip, *refs
):
    blocks, block = len(offsets) - 1, offsets[1]
    tiles = offsets[-1] // 128
    peers = (len(refs) - 2) // len(groups) - 1
    pieces, out = refs[: peers * len(groups)], refs[peers * len(groups)]
    held, sems = refs[peers * len(groups) + 1 : -1], refs[-1]
    step_rows, cols, length = out.shape
    half = length // 2
    slab, far_row, rim_col, me = places[0], places[1], places[2], places[3]
    lane = lax.broadcasted_iota(jnp.int32, (block, 128), 1)
    at_rim = lax.broadcasted_iota(jnp.int32, (cols, half), 0) + (1 - rim_col) == 0
    rim_lane = lax.broadcasted_iota(jnp.int32, rim.shape, 1)
    first_lane = lax.broadcasted_iota(jnp.int32, (cols, half), 1) == 0

    @pl.when(pl.program_id(0) == 0)
    def _():
        copies = []
        for g in range(len(groups)):
            for peer in range(peers):
                piece = pieces[g * peers + peer]
                size = piece.shape[0]
                spot = pl.ds(pl.multiple_of((me ^ peer) * size, size), size)
                copies.append(pltpu.make_async_copy(piece, held[g].at[spot], sems.at[g, peer]))
        for copy in copies:
            copy.start()
        for copy in copies:
            copy.wait()

    @pl.loop(0, step_rows, unroll=4)
    def _(r):
        t = pl.program_id(0) * step_rows + r
        i = jnp.where(far_row == 1, block - t, t)
        inside = (jnp.zeros((block, 128), jnp.int32) + i) < block
        i = jnp.minimum(i, block - 1)
        source = lax.div(i, devices), lax.rem(i, devices)
        parts = []
        for g, group in enumerate(groups):
            stride = held[g].shape[0] // devices
            for tile in range(group.start, group.stop):
                start = (tile - group.start) * own * block
                near = [
                    held[g][pl.ds(start + e * block + i, devices, stride=stride), :]
                    for e in range(own)
                ]
                near = jnp.concatenate(near, axis=0)
                far = pl.multiple_of(source[1] * stride + start + source[0] * block, 8)
                far = held[g][pl.ds(far, block), :]
                kind = jnp.zeros((block, 128), jnp.int32)
                for b in range(1, blocks):
                    kind += (lane + tile * 128 >= offsets[b]).astype(jnp.int32)
                line = jnp.where(kind >= slab, near, far)
                line = jnp.where(inside, line, next_plane[:, pl.ds(tile * 128, 128)])
                parts.append(line)
        line = jnp.concatenate(parts, axis=1)
        plane = square([line[:, offsets[b] : offsets[b + 1]] for b in range(blocks)], block)
        high, low = split(plane)
        left = jnp.dot(pick[...], high, preferred_element_type=jnp.float32)
        left += jnp.dot(pick[...], low, preferred_element_type=jnp.float32)
        left = jnp.where(at_rim, across[pl.ds(t, 1), :], left)
        high, low = split(left)
        right = jnp.dot(high, flip[...], preferred_element_type=jnp.float32)
        right += jnp.dot(low, flip[...], preferred_element_type=jnp.float32)
        edge = jnp.sum(jnp.where(rim_lane == t, rim[...], 0.0), axis=1, keepdims=True)
        out[r, :, pl.ds(0, half)] = left
        out[r, :, pl.ds(half, half)] = jnp.where(first_lane, edge, right)


def result_block(got, next_plane, across, rim, pick_cols, slab, far_row, rim_col, col, offsets):
    block = offsets[1]
    gx = got[0][0].shape[0]
    groups = tile_groups(offsets[-1] // 128)
    devices = gx * len(got[0])
    own = block // devices
    rows, half = across.shape[0], across.shape[1] - 1
    cols = pick_cols.shape[0]
    step_rows = 8
    places = jnp.stack([slab, far_row.astype(jnp.int32), rim_col.astype(jnp.int32), col])
    cell = jnp.arange(half)
    pick = (pick_cols[:, None] == cell[None, :]).astype(jnp.bfloat16)
    flip = (cell[:, None] + cell[None, :] == half).astype(jnp.bfloat16)
    rim = jnp.pad(rim.T, ((0, 0), (0, 128 - rows)))
    whole = lambda array: pl.BlockSpec(array.shape, lambda i: (0,) * array.ndim)
    arrays = (next_plane, across[:, :half], rim, pick, flip)
    pieces = [piece.reshape(-1, 128) for group in got for piece in group]
    return pl.pallas_call(
        lambda *refs: result_kernel(offsets, own, devices, groups, *refs),
        grid=(rows // step_rows,),
        in_specs=[pl.BlockSpec(memory_space=pltpu.SMEM)] + [whole(array) for array in arrays]
        + [pl.BlockSpec(memory_space=pl.ANY)] * len(pieces),
        out_specs=pl.BlockSpec((step_rows, cols, 2 * half), lambda i: (i, 0, 0)),
        out_shape=jax.ShapeDtypeStruct((rows, cols, 2 * half), jnp.float32),
        scratch_shapes=[
            pltpu.VMEM((devices * group[0].shape[1], 128), jnp.float32) for group in got
        ] + [pltpu.SemaphoreType.DMA((len(groups), len(got[0])))],
        compiler_params=pltpu.CompilerParams(vmem_limit_bytes=VMEM_BYTES),
    )(places, *arrays, *pieces)


def tile_groups(tiles):
    return [slice(tile, min(tile + 2, tiles)) for tile in range(0, tiles, 2)]


def swap(peers, bit):
    return [(q, q ^ bit) for q in range(peers)]


def gathered(piece, peers):
    pieces, bit = {0: piece}, peers // 2
    while bit:
        for place in list(pieces):
            pieces[place ^ bit] = lax.ppermute(pieces[place], "gy", swap(peers, bit))
        bit //= 2
    return [pieces[place] for place in range(peers)]


def exchanged(packed):
    gy = packed.shape[0]
    return [packed[0]] + [lax.ppermute(packed[p], "gy", swap(gy, p)) for p in range(1, gy)]


def sent_lines(got, count, after):
    gy = len(got)
    lines = [sum(got[p][:count] for p in range(first, gy, 2)) for first in range(2)]
    lines = jnp.concatenate(lines + [sum(piece[count:] for piece in got)], axis=0)
    lines = jnp.transpose(lines, (2, 1, 0, 3))
    if after is not None:
        lines, _ = lax.optimization_barrier((lines, after))
    return lax.all_to_all(lines, "gx", 0, 0, tiled=True)


def first_axis(lines, table):
    gx, _, count, half = table.shape
    table = table.reshape(gx, 2 * count, half)
    return jnp.einsum("geaw,gai->eiw", lines[:, :, : 2 * count], table, precision=HIGH)


def part_counts(rows):
    if rows < 4 * PART_STEP:
        return [rows]
    return [rows - 2 * PART_STEP] + [PART_STEP] * 2


def square(lower, block):
    lines = []
    for b in range(len(lower)):
        parts = [lower[b]]
        for c in range(b + 1, len(lower)):
            part = lower[c][..., b * block : (b + 1) * block]
            parts.append(jnp.swapaxes(part, -1, -2))
        lines.append(jnp.concatenate(parts, axis=-1))
    return jnp.concatenate(lines, axis=-2)


def solution(mesh):
    placed = (P("gx", "gy", None), P())
    return jax.shard_map(
        on_device, mesh=mesh, in_specs=placed, out_specs=P("gx", "gy", None), check_vma=False
    )
```

```python
import math

import jax
import jax.numpy as jnp
from jax import lax
from jax.experimental import pallas as pl
from jax.experimental.pallas import tpu as pltpu
from jax.sharding import PartitionSpec as P

SWEEPS = 2

AXIS_ORDERS = ((0, 1, 2), (0, 2, 1), (1, 0, 2), (1, 2, 0), (2, 0, 1), (2, 1, 0))

HIGH = lax.Precision.HIGH


def ring(axis):
    peers = lax.axis_size(axis)
    up = [(i, (i + 1) % peers) for i in range(peers)]
    return up, [(j, i) for i, j in up]


def halos(block):
    rows, cols, _ = block.shape
    up, down = ring("gx")
    right, left = ring("gy")
    top = lax.ppermute(block[rows - SWEEPS :], "gx", up)
    bottom = lax.ppermute(block[:SWEEPS], "gx", down)
    before = lax.ppermute(block[:, cols - SWEEPS :], "gy", right)
    after = lax.ppermute(block[:, :SWEEPS], "gy", left)
    sides = jnp.concatenate([before, after], axis=1)
    above = lax.ppermute(sides[rows - SWEEPS :], "gx", up)
    below = lax.ppermute(sides[:SWEEPS], "gx", down)
    sides = jnp.concatenate([above, sides, below], axis=0)
    free = ((0, 0), (8 - SWEEPS, 8 - SWEEPS), (0, 0))
    return top, bottom, jnp.pad(sides, free)


def mirror(values, axis):
    return jnp.roll(jnp.flip(values, axis), 1, axis)


def symmetric_marks(marks):
    for flip_axis in range(3):
        marks = jnp.maximum(marks, mirror(marks, flip_axis))
    united = marks
    for axis_order in AXIS_ORDERS[1:]:
        united = jnp.maximum(united, jnp.transpose(marks, axis_order))
    return united


def cosine_table(length):
    position = jnp.arange(length, dtype=jnp.int32)
    phases = jnp.mod(position[:, None] * position[None, : length // 2 + 1], length)
    return jnp.cos(phases.astype(jnp.float32) * (2.0 * math.pi / length)) / math.sqrt(length)


MARGIN = 16
CHUNK = 16
STEP_ROWS = 16
PART_STEP = 8
VMEM_BYTES = 56 * 1024 * 1024


def split(values):
    high = values.astype(jnp.bfloat16)
    low = (values - high.astype(jnp.float32)).astype(jnp.bfloat16)
    return high, low


def fill_kernel(
    base, here, above, below, top, bottom, sides, marks, table_high, table_low,
    spectrum, alternate, edge, punched, once, high, low, folded,
):
    step_rows, cols, length = here.shape
    step = pl.program_id(0) + base[0]
    first_row = step * step_rows
    local_row = pl.program_id(0) * step_rows
    period = marks.shape[0]
    lane = lax.broadcasted_iota(jnp.int32, (128, 128), 1)
    signs = jnp.where(lax.broadcasted_iota(jnp.int32, (128, 128), 0) % 2 == 0, 1.0, -1.0)

    @pl.when(pl.program_id(0) == 0)
    def _():
        edge[...] = jnp.zeros_like(edge)

    def holes(row, start, size):
        row = lax.rem(first_row + row, period)
        start = start % period
        if start + size <= period:
            part = marks[row, pl.ds(start, size), :]
        else:
            part = jnp.concatenate(
                [marks[row, pl.ds(start, period - start), :], marks[row, pl.ds(0, start + size - period), :]],
                axis=0,
            )
        return jnp.concatenate([part] * (length // 128), axis=1)

    def punch(row, start, values):
        kept = jnp.where(holes(row, start, values.shape[0]) > 0.0, 0.0, values)
        punched[row, pl.ds(start, values.shape[0]), :] = kept

    def punch_row(row, source, index):
        full = first_row + row
        punch(row, MARGIN - 8, sides[full, pl.ds(0, 8), :])
        punch(row, MARGIN + cols, sides[full, pl.ds(8, 8), :])
        for c in range(0, cols, CHUNK):
            punch(row, MARGIN + c, source[index, pl.ds(c, CHUNK), :])

    def neighbours(ref, row, start):
        middle = ref[row, pl.ds(start, CHUNK), :]
        total = ref[row - 1, pl.ds(start, CHUNK), :] + ref[row + 1, pl.ds(start, CHUNK), :]
        total += ref[row, pl.ds(start - 1, CHUNK), :] + ref[row, pl.ds(start + 1, CHUNK), :]
        return total + pltpu.roll(middle, 1, 1) + pltpu.roll(middle, length - 1, 1)

    last = (sides.shape[0] - 2 * SWEEPS) // step_rows - 1
    for edge_rows, inside, offset, outer in (
        (above, step > 0, 0, top),
        (below, step < last, step_rows + SWEEPS, bottom),
    ):
        @pl.when(inside)
        def _():
            for r in range(SWEEPS):
                punch_row(offset + r, edge_rows, r)

        @pl.when(jnp.logical_not(inside))
        def _():
            for r in range(SWEEPS):
                punch_row(offset + r, outer, r)

    @pl.loop(0, step_rows)
    def _(r):
        punch_row(r + SWEEPS, here, r)

    @pl.loop(1, step_rows + 2 * SWEEPS - 1, unroll=2)
    def _(r):
        for start in range(MARGIN - 8, MARGIN + cols + 8, CHUNK):
            total = neighbours(punched, r, start) * holes(r, start, CHUNK)
            once[r, pl.ds(start, CHUNK), :] = punched[r, pl.ds(start, CHUNK), :] + total

    @pl.loop(0, step_rows)
    def _(r):
        for c in range(0, cols, CHUNK):
            start = MARGIN + c
            total = neighbours(once, r + SWEEPS, start) * holes(r + SWEEPS, start, CHUNK)
            filled = punched[r + SWEEPS, pl.ds(start, CHUNK), :] + total
            first, second = split(filled)
            spot = pl.ds(pl.multiple_of(r * cols + c, CHUNK), CHUNK)
            high[spot, :] = first
            low[spot, :] = second
            wrapped = filled[:, :128]
            for tile in range(1, length // 128):
                wrapped += filled[:, tile * 128 : (tile + 1) * 128]
            folded[pl.ds(c, CHUNK), :] = wrapped
        column = jnp.where(lane == local_row + r, signs, 0.0).astype(jnp.bfloat16)
        first, second = split(folded[...])
        total = jnp.dot(first, column, preferred_element_type=jnp.float32)
        total += jnp.dot(second, column, preferred_element_type=jnp.float32)
        edge[...] += total

    rows_each = 8
    half = spectrum.shape[2]
    order = lax.broadcasted_iota(jnp.int32, (rows_each, cols, half), 1)

    @pl.loop(0, step_rows // rows_each)
    def _(r):
        spot = pl.ds(pl.multiple_of(r * rows_each * cols, CHUNK), rows_each * cols)
        first, second = high[spot, :], low[spot, :]
        total = jnp.dot(first, table_low[...], preferred_element_type=jnp.float32)
        total += jnp.dot(second, table_high[...], preferred_element_type=jnp.float32)
        total += jnp.dot(first, table_high[...], preferred_element_type=jnp.float32)
        total = total.reshape(rows_each, cols, half)
        spectrum[pl.ds(r * rows_each, rows_each)] = total
        signed = jnp.sum(jnp.where(order % 2 == 0, total, -total), axis=1)
        alternate[pl.ds(pl.multiple_of(r * rows_each, rows_each), rows_each), :] = signed


def rounded_parts(table):
    rounded = lax.reduce_precision(table, 8, 7)
    return rounded.astype(jnp.bfloat16), (table - rounded).astype(jnp.bfloat16)


def fill_arrays(intensity, template, row, col, main):
    rows, cols, length = intensity.shape
    united = symmetric_marks(template)
    period = united.shape[0]
    offsets = (jnp.mod(row * rows - SWEEPS, period), jnp.mod(col * cols - MARGIN, period))
    marks = jnp.roll(united, (-offsets[0], -offsets[1]), (0, 1)).astype(jnp.float32) / 6.0
    marks = jnp.tile(marks, (1, 1, 128 // period))
    return halos(intensity) + (marks,) + rounded_parts(main)


def filled_spectrum(intensity, arrays, first, count):
    rows, cols, length = intensity.shape
    half = length // 2
    step_rows = min(STEP_ROWS, count)
    pairs = step_rows // SWEEPS
    last = rows // SWEEPS - 1
    whole = lambda array: pl.BlockSpec(array.shape, lambda i, b: (0,) * array.ndim)
    before = lambda i, b: (jnp.maximum((i + b[0]) * pairs - 1, 0), 0, 0)
    after = lambda i, b: (jnp.minimum((i + b[0] + 1) * pairs, last), 0, 0)
    padded = (step_rows + 2 * SWEEPS, cols + 2 * MARGIN, length)
    return pl.pallas_call(
        fill_kernel,
        grid_spec=pltpu.PrefetchScalarGridSpec(
            num_scalar_prefetch=1,
            grid=(count // step_rows,),
            in_specs=[
                pl.BlockSpec((step_rows, cols, length), lambda i, b: (i + b[0], 0, 0)),
                pl.BlockSpec((SWEEPS, cols, length), before),
                pl.BlockSpec((SWEEPS, cols, length), after),
            ] + [whole(array) for array in arrays],
            out_specs=[
                pl.BlockSpec((step_rows, cols, half), lambda i, b: (i, 0, 0)),
                pl.BlockSpec((step_rows, half), lambda i, b: (i, 0)),
                pl.BlockSpec((cols, 128), lambda i, b: (0, 0)),
            ],
            scratch_shapes=[
                pltpu.VMEM(padded, jnp.float32),
                pltpu.VMEM(padded, jnp.float32),
                pltpu.VMEM((step_rows * cols, length), jnp.bfloat16),
                pltpu.VMEM((step_rows * cols, length), jnp.bfloat16),
                pltpu.VMEM((cols, 128), jnp.float32),
            ],
        ),
        out_shape=[
            jax.ShapeDtypeStruct((count, cols, half), jnp.float32),
            jax.ShapeDtypeStruct((count, half), jnp.float32),
            jax.ShapeDtypeStruct((cols, 128), jnp.float32),
        ],
        compiler_params=pltpu.CompilerParams(vmem_limit_bytes=VMEM_BYTES),
        cost_estimate=pl.CostEstimate(flops=1, bytes_accessed=1, transcendentals=0),
    )((first // step_rows).reshape(1), intensity, intensity, intensity, *arrays)


def pack(section, offsets):
    block = offsets[1]
    units = [section[b * block : (b + 1) * block, : (b + 1) * block] for b in range(len(offsets) - 1)]
    return jnp.concatenate(units, axis=1)


def three_dots(left, right):
    total = jnp.dot(left[1], right[0], preferred_element_type=jnp.float32)
    total += jnp.dot(left[0], right[1], preferred_element_type=jnp.float32)
    return total + jnp.dot(left[0], right[0], preferred_element_type=jnp.float32)


def section_kernel(
    offsets, closing, me, weights, kept, got, cols_high, cols_low, rows_high, rows_low,
    rim, corner, before, out, total, lines,
):
    step, steps = pl.program_id(0), pl.num_programs(0)
    step_rows = kept.shape[0]
    half, count = rows_high.shape
    planes, block, width = before.shape
    gy, _, own, gx, _ = out.shape

    def place(layer, values):
        for e in range(own):
            for q in range(gy):
                start = (e * gy + q) * gx
                out[q ^ me[0], layer, e] = values[start : start + gx]

    @pl.when(step == 0)
    def _():
        total[...] = before[...]

    @pl.loop(0, step_rows, unroll=True)
    def _(r):
        layer = step * step_rows + r
        values = jnp.concatenate([kept[r], got[r]], axis=0)
        section = three_dots((cols_high[...], cols_low[...]), split(values))
        section = section + section.T
        line = pack(section, offsets)
        place(layer, line)
        for m in range(planes):
            total[m] += weights[m, layer] * line
        for m in range(planes - 1):
            row = (m + 1) * (half // planes)
            lines[m, pl.ds(layer, 1), :] = section[row : row + 1]

    @pl.when(step == steps - 1)
    def _():
        for m in range(planes - 1):
            plane = three_dots((rows_high[...], rows_low[...]), split(lines[m]))
            total[m] += pack(plane + plane.T, offsets)
        if closing:
            total[planes - 1] += pack(rim[...] + rim[...].T, offsets)
            for m in range(planes):
                place(count + m, total[m])
            place(count + planes, jnp.zeros((block, width), jnp.float32) + corner[...])


def packed_section(col, kept, got, table_pair, table_rows, marks, rim, corner, before, offsets, shape, closing):
    count, cols, half = kept.shape
    planes, block, width = before.shape
    gx, gy = shape
    step_rows = 4
    layers = count + (planes + 1 if closing else 0)
    whole = lambda array: pl.BlockSpec(array.shape, lambda i: (0,) * array.ndim)
    weights = jnp.stack([table_rows[:, m] for m in marks])
    arrays = rounded_parts(table_pair.T) + rounded_parts(table_rows[:, :half].T)
    arrays += (rim, corner[None], before)
    outs = [
        jax.ShapeDtypeStruct((gy, layers, block // (gx * gy), gx, width), jnp.float32),
        jax.ShapeDtypeStruct(before.shape, jnp.float32),
    ]
    rows_spec = pl.BlockSpec((step_rows, cols, half), lambda i: (i, 0, 0))
    return pl.pallas_call(
        lambda *refs: section_kernel(offsets, closing, *refs),
        grid=(count // step_rows,),
        in_specs=[pl.BlockSpec(memory_space=pltpu.SMEM)] * 2 + [rows_spec, rows_spec]
        + [whole(array) for array in arrays],
        out_specs=[whole(out) for out in outs],
        out_shape=outs,
        scratch_shapes=[pltpu.VMEM((planes, count, half), jnp.float32)],
        compiler_params=pltpu.CompilerParams(vmem_limit_bytes=VMEM_BYTES),
        cost_estimate=pl.CostEstimate(
            flops=count * 12 * cols * half * half,
            bytes_accessed=count * cols * half * 16,
            transcendentals=0,
        ),
    )(col.reshape(1), weights, kept, got, *arrays)


def on_device(intensity, template):
    rows, cols, length = intensity.shape
    gx, gy = lax.axis_size("gx"), lax.axis_size("gy")
    row, col = lax.axis_index("gx"), lax.axis_index("gy")
    devices, half = gx * gy, length // 2
    block = max(devices, rows)
    blocks, own, slabs = half // block, block // devices, gx // 2
    offsets = [block * b * (b + 1) // 2 for b in range(blocks + 1)]
    width = offsets[blocks]
    table = cosine_table(length)
    main = table[:, :half]

    pair_rows = rows // 2
    parts = row_parts(pair_rows)
    counts = [part.stop - part.start for part in parts]
    core = lax.rem(col, 2)
    arrays = fill_arrays(intensity, template, row, col, main)
    given_first, kept_first = (1 - core) * pair_rows, core * pair_rows
    given, kept, got = [], [], []

    def fill_part(c, after):
        count, start = counts[c], parts[c].start
        starts = given_first + start, kept_first + start
        if after is not None:
            starts, after = lax.optimization_barrier((starts, after))
        given.append(filled_spectrum(intensity, arrays, starts[0], count))
        got.append(lax.ppermute(given[c][0], "gy", swap(gy, 1)))
        kept.append(filled_spectrum(intensity, arrays, starts[1], count))
        return after

    table_cols = lax.dynamic_slice_in_dim(table, col * cols, cols, 0)
    kept_rows = lax.dynamic_slice_in_dim(table, row * rows + kept_first, pair_rows, 0)
    marks = [rows * (m + 1) for m in range(slabs)]
    mates = lax.dynamic_slice_in_dim(main, (col + 1 - 2 * core) * cols, cols, 0)
    table_pair = jnp.concatenate([table_cols[:, :half], mates], axis=0)
    table_parts = main.reshape(gx, 2, pair_rows, half) / 6.0
    table_parts = jnp.where(core == 0, table_parts, table_parts[:, ::-1])
    table_parts = [table_parts[:, :, part] for part in parts]
    side = jnp.zeros((slabs, block, width), jnp.float32)
    rim, corner = jnp.zeros((half, half), jnp.float32), jnp.zeros((width,), jnp.float32)
    values, packed, lines = 0.0, None, None
    for c, count in enumerate(counts):
        closing = c == len(counts) - 1
        packed = fill_part(c, packed)
        held = kept[c][0]
        if c > 0:
            held, got_lines = lax.optimization_barrier((held, exchanged(packed)))
            lines = sent_lines(got_lines, counts[c - 1], lines)
            values = values + first_axis(lines, table_parts[c - 1])
        if closing:
            given_rows = lax.dynamic_slice_in_dim(table, row * rows + given_first, pair_rows, 0)
            ordered_rows = [held_rows[part] for held_rows in (given_rows, kept_rows) for part in parts]
            ordered_rows = jnp.concatenate(ordered_rows, axis=0)
            alternate = jnp.concatenate([piece[1] for piece in given + kept], axis=0) / math.sqrt(length)
            edge = [piece[2][:, : piece[1].shape[0]] for piece in given + kept]
            edge = jnp.concatenate(edge, axis=1)
            edge = jnp.einsum("ba,bk->ak", edge / math.sqrt(length), table_cols, precision=HIGH)
            edge = edge + jnp.concatenate([alternate, edge[:, half:]], axis=1)
            rim = jnp.einsum("aj,ak->jk", ordered_rows[:, :half], edge[:, :half], precision=HIGH)
            corner = 2.0 * jnp.einsum("a,ak->k", ordered_rows[:, half], edge, precision=HIGH)
            corner = corner + jnp.einsum("aj,a->j", ordered_rows, edge[:, half], precision=HIGH)
            corner = jnp.pad(corner, (0, width - half - 1))

        packed, side = packed_section(
            col, held, got[c], table_pair, kept_rows[parts[c]], marks,
            rim, corner, side, offsets, (gx, gy), closing,
        )
    lines = sent_lines(exchanged(packed), counts[-1], lines)
    values = values + first_axis(lines, table_parts[-1])
    side = jnp.sum(lines[:, :, 2 * counts[-1] :], axis=0) / 6.0
    turned = values.reshape(own, blocks, own, devices, width)
    turned = jnp.transpose(turned, (3, 1, 2, 0, 4))
    turned = [turned[:, b, :, :, : offsets[b + 1]] for b in range(blocks)]
    turned = lax.all_to_all(jnp.concatenate(turned, axis=3), ("gy", "gx"), 0, 0, tiled=True)
    turned = jnp.transpose(turned, (1, 2, 0, 3)).reshape(own, block, -1)

    slab = jnp.minimum(row, gx - 1 - row)
    far_row, far_col = row >= slabs, col >= gy // 2
    pick_rows = jnp.arange(rows)
    pick_rows = slab * rows + jnp.where(far_row, rows - pick_rows, pick_rows)
    pick_cols = jnp.arange(cols)
    pick_cols = jnp.where(far_col, (gy - col) * cols - pick_cols, col * cols + pick_cols)

    if rows == block:
        got = []
        for messages in slab_messages(values, turned, side, offsets, slabs):
            got.append(gathered(lax.all_to_all(messages, "gx", 0, 0, tiled=True), gy))
        tiles = width // 128
        start = tile_groups(tiles)[0].stop * own * block
        side = jnp.stack([piece[:, start : start + 3 * own * tiles] for piece in got[0]])
        bit = gy // 2
        while bit:
            paired = side.reshape((-1, 2, bit) + side.shape[1:])
            side = jnp.where((col & bit) == 0, paired, paired[:, ::-1]).reshape(side.shape)
            bit //= 2
        side = side.reshape(devices, own, 3, width)
        side = jnp.transpose(side, (2, 1, 0, 3)).reshape(3, block, width)
        next_plane, across = side[0], rim_rows(side[1:], offsets, pick_rows)
        rim_col = col == gy // 2
        rim = across[:, pick_cols]
        return result_block(
            got, next_plane, across, rim, pick_cols, slab, far_row, rim_col, col, offsets
        )

    side = lax.all_gather(side, ("gy", "gx"), axis=0)
    side = jnp.transpose(side, (2, 1, 0, 3)).reshape(slabs + 1, block, width)
    across = rim_rows(side[slabs - 1 :], offsets, pick_rows)
    next_plane = lax.dynamic_index_in_dim(side, slab, 0, keepdims=False)
    sums = axis_order_sums(values, turned, offsets, block)
    messages = []
    for s in range(slabs):
        base, first = s * rows // block, s * rows
        units = []
        for b in range(blocks):
            size = (b + 1) * block
            near = jnp.zeros((own, rows, size))
            far = jnp.zeros((own, block, size))
            if b >= base:
                near = jnp.stack([sums[b][e][first : first + rows, :size] for e in range(own)])
            else:
                far = jnp.stack([sums[base][e][b * block : size, :size] for e in range(own)])
            units.append(jnp.concatenate([near, far], axis=1))
        messages.append(jnp.concatenate(units, axis=2))
    messages = jnp.stack(messages + messages[::-1])
    got = lax.all_to_all(messages, "gx", 0, 0, tiled=True)
    got = lax.all_gather(got, "gy", axis=0, tiled=True)
    got = jnp.swapaxes(got, 0, 1).reshape(block, rows + block, width)
    base = slab * rows // block
    lower = []
    for b in range(blocks):
        lanes = slice(offsets[b], offsets[b + 1])
        near = jnp.swapaxes(got[:, :rows, lanes], 0, 1)
        far = lax.dynamic_slice_in_dim(got[:, rows:, lanes], lax.rem(slab * rows, block), rows, 0)
        lower.append(jnp.where(b >= base, near, far))
    lower = jnp.concatenate(lower, axis=2)
    lower = jnp.concatenate([lower, next_plane[None]], axis=0)
    body = square([lower[:, :, offsets[b] : offsets[b + 1]] for b in range(blocks)], block)
    body = body[pick_rows - slab * rows]
    body = jnp.concatenate([body, across[:, None, :half]], axis=1)[:, pick_cols]
    body = jnp.concatenate([body, across[:, pick_cols][:, :, None]], axis=2)
    return jnp.concatenate([body, jnp.flip(body[:, :, 1:half], 2)], axis=2)


def rim_rows(side, offsets, pick_rows):
    blocks, block = len(offsets) - 1, offsets[1]
    half = blocks * block
    last = square([side[0][:, offsets[b] : offsets[b + 1]] for b in range(blocks)], block)
    rim = side[1, 0, : half + 1]
    last = jnp.concatenate([last, rim[None, :half]], axis=0)
    return jnp.concatenate([last, rim[:, None]], axis=1)[pick_rows]


def axis_order_sums(values, turned, offsets, block):
    start = 0
    sums = []
    for top in range(len(offsets) - 1):
        size = (top + 1) * block
        parts = []
        for e in range(values.shape[0]):
            part = values[e, :size, offsets[top] : offsets[top] + size]
            lower = [turned[e, :, start + offsets[b] : start + offsets[b + 1]] for b in range(top + 1)]
            parts.append(part + part.T + square(lower, block))
        sums.append(parts)
        start += offsets[top + 1]
    return sums


def message_kernel(offsets, slabs, values, turned, side, *messages):
    blocks, block = len(offsets) - 1, offsets[1]
    values, turned = values[...], turned[...]
    own = values.shape[0]
    sums = axis_order_sums(values, turned, offsets, block)
    groups = tile_groups(offsets[-1] // 128)
    side_start = groups[0].stop * own * block
    messages[0][:, side_start:] = jnp.zeros_like(messages[0][:, side_start:])
    for s in range(slabs):
        places = s, 2 * slabs - 1 - s
        for e in range(own):
            units = []
            for b in range(blocks):
                size = (b + 1) * block
                if b >= s:
                    units.append(sums[b][e][s * block : (s + 1) * block, :size])
                else:
                    units.append(sums[s][e][b * block : size, :size])
            line = jnp.concatenate(units, axis=1)
            for group, out in zip(groups, messages):
                for tile in range(group.start, group.stop):
                    start = ((tile - group.start) * own + e) * block
                    for place in places:
                        out[place, start : start + block] = line[:, tile * 128 : (tile + 1) * 128]
            row = side_start + 3 * e * groups[-1].stop
            for plane in (s, slabs - 1, slabs):
                for tile in range(groups[-1].stop):
                    part = side[e, plane : plane + 1, tile * 128 : (tile + 1) * 128]
                    for place in places:
                        messages[0][place, row : row + 1] = part
                    row += 1


def slab_messages(values, turned, side, offsets, slabs):
    own, block, tiles = values.shape[0], offsets[1], offsets[-1] // 128
    sizes = [(group.stop - group.start) * own * block for group in tile_groups(tiles)]
    sizes[0] += -(-3 * own * tiles // 8) * 8
    return pl.pallas_call(
        lambda *refs: message_kernel(offsets, slabs, *refs),
        in_specs=[pl.BlockSpec(memory_space=pltpu.VMEM)] * 3,
        out_specs=[pl.BlockSpec(memory_space=pltpu.VMEM)] * len(sizes),
        out_shape=[jax.ShapeDtypeStruct((2 * slabs, size, 128), jnp.float32) for size in sizes],
        compiler_params=pltpu.CompilerParams(vmem_limit_bytes=VMEM_BYTES),
    )(values, turned, side)


def result_kernel(
    offsets, own, devices, groups, places, next_plane, across, rim, pick, flip, *refs
):
    blocks, block = len(offsets) - 1, offsets[1]
    tiles = offsets[-1] // 128
    peers = (len(refs) - 2) // len(groups) - 1
    pieces, out = refs[: peers * len(groups)], refs[peers * len(groups)]
    held, sems = refs[peers * len(groups) + 1 : -1], refs[-1]
    step_rows, cols, length = out.shape
    half = length // 2
    slab, far_row, rim_col, me = places[0], places[1], places[2], places[3]
    lane = lax.broadcasted_iota(jnp.int32, (block, 128), 1)
    at_rim = lax.broadcasted_iota(jnp.int32, (cols, half), 0) + (1 - rim_col) == 0
    rim_lane = lax.broadcasted_iota(jnp.int32, rim.shape, 1)
    first_lane = lax.broadcasted_iota(jnp.int32, (cols, half), 1) == 0

    @pl.when(pl.program_id(0) == 0)
    def _():
        copies = []
        for g in range(len(groups)):
            for peer in range(peers):
                piece = pieces[g * peers + peer]
                size = piece.shape[0]
                spot = pl.ds(pl.multiple_of((me ^ peer) * size, size), size)
                copies.append(pltpu.make_async_copy(piece, held[g].at[spot], sems.at[g, peer]))
        for copy in copies:
            copy.start()
        for copy in copies:
            copy.wait()

    def left_half(r):
        t = pl.program_id(0) * step_rows + r
        i = jnp.where(far_row == 1, block - t, t)
        inside = (jnp.zeros((block, 128), jnp.int32) + i) < block
        i = jnp.minimum(i, block - 1)
        source = lax.div(i, devices), lax.rem(i, devices)
        parts = []
        for g, group in enumerate(groups):
            stride = held[g].shape[0] // devices
            for tile in range(group.start, group.stop):
                start = (tile - group.start) * own * block
                near = [
                    held[g][pl.ds(start + e * block + i, devices, stride=stride), :]
                    for e in range(own)
                ]
                near = jnp.concatenate(near, axis=0)
                far = pl.multiple_of(source[1] * stride + start + source[0] * block, 8)
                far = held[g][pl.ds(far, block), :]
                kind = jnp.zeros((block, 128), jnp.int32)
                for b in range(1, blocks):
                    kind += (lane + tile * 128 >= offsets[b]).astype(jnp.int32)
                line = jnp.where(kind >= slab, near, far)
                line = jnp.where(inside, line, next_plane[:, pl.ds(tile * 128, 128)])
                parts.append(line)
        line = jnp.concatenate(parts, axis=1)
        plane = square([line[:, offsets[b] : offsets[b + 1]] for b in range(blocks)], block)
        high, low = split(plane)
        left = jnp.dot(pick[...], high, preferred_element_type=jnp.float32)
        left += jnp.dot(pick[...], low, preferred_element_type=jnp.float32)
        left = jnp.where(at_rim, across[pl.ds(t, 1), :], left)
        out[r, :, pl.ds(0, half)] = left
        return left

    together = 4

    @pl.loop(0, step_rows // together)
    def _(c):
        left = [left_half(c * together + n) for n in range(together)]
        high, low = split(jnp.concatenate(left, axis=0))
        right = jnp.dot(high, flip[...], preferred_element_type=jnp.float32)
        right += jnp.dot(low, flip[...], preferred_element_type=jnp.float32)
        for n in range(together):
            r = c * together + n
            t = pl.program_id(0) * step_rows + r
            edge = jnp.sum(jnp.where(rim_lane == t, rim[...], 0.0), axis=1, keepdims=True)
            part = right[n * cols : (n + 1) * cols]
            out[r, :, pl.ds(half, half)] = jnp.where(first_lane, edge, part)


def result_block(got, next_plane, across, rim, pick_cols, slab, far_row, rim_col, col, offsets):
    block = offsets[1]
    gx = got[0][0].shape[0]
    groups = tile_groups(offsets[-1] // 128)
    devices = gx * len(got[0])
    own = block // devices
    rows, half = across.shape[0], across.shape[1] - 1
    cols = pick_cols.shape[0]
    step_rows = 8
    places = jnp.stack([slab, far_row.astype(jnp.int32), rim_col.astype(jnp.int32), col])
    cell = jnp.arange(half)
    pick = (pick_cols[:, None] == cell[None, :]).astype(jnp.bfloat16)
    flip = (cell[:, None] + cell[None, :] == half).astype(jnp.bfloat16)
    rim = jnp.pad(rim.T, ((0, 0), (0, 128 - rows)))
    whole = lambda array: pl.BlockSpec(array.shape, lambda i: (0,) * array.ndim)
    arrays = (next_plane, across[:, :half], rim, pick, flip)
    pieces = [piece.reshape(-1, 128) for group in got for piece in group]
    return pl.pallas_call(
        lambda *refs: result_kernel(offsets, own, devices, groups, *refs),
        grid=(rows // step_rows,),
        in_specs=[pl.BlockSpec(memory_space=pltpu.SMEM)] + [whole(array) for array in arrays]
        + [pl.BlockSpec(memory_space=pl.ANY)] * len(pieces),
        out_specs=pl.BlockSpec((step_rows, cols, 2 * half), lambda i: (i, 0, 0)),
        out_shape=jax.ShapeDtypeStruct((rows, cols, 2 * half), jnp.float32),
        scratch_shapes=[
            pltpu.VMEM((devices * group[0].shape[1], 128), jnp.float32) for group in got
        ] + [pltpu.SemaphoreType.DMA((len(groups), len(got[0])))],
        compiler_params=pltpu.CompilerParams(vmem_limit_bytes=VMEM_BYTES),
    )(places, *arrays, *pieces)


def tile_groups(tiles):
    stops = [1] + ([3] if tiles > 4 else []) + list(range(4 if tiles > 4 else 2, tiles + 1))
    return [slice(start, stop) for start, stop in zip([0] + stops, stops)]


def swap(peers, bit):
    return [(q, q ^ bit) for q in range(peers)]


def gathered(piece, peers):
    pieces, bit = {0: piece}, peers // 2
    while bit:
        for place in list(pieces):
            pieces[place ^ bit] = lax.ppermute(pieces[place], "gy", swap(peers, bit))
        bit //= 2
    return [pieces[place] for place in range(peers)]


def exchanged(packed):
    gy = packed.shape[0]
    return [packed[0]] + [lax.ppermute(packed[p], "gy", swap(gy, p)) for p in range(1, gy)]


def sent_lines(got, count, after):
    gy = len(got)
    lines = [sum(got[p][:count] for p in range(first, gy, 2)) for first in range(2)]
    lines = jnp.concatenate(lines + [sum(piece[count:] for piece in got)], axis=0)
    lines = jnp.transpose(lines, (2, 1, 0, 3))
    if after is not None:
        lines, _ = lax.optimization_barrier((lines, after))
    return lax.all_to_all(lines, "gx", 0, 0, tiled=True)


def first_axis(lines, table):
    gx, _, count, half = table.shape
    table = table.reshape(gx, 2 * count, half)
    return jnp.einsum("geaw,gai->eiw", lines[:, :, : 2 * count], table, precision=HIGH)


def row_parts(rows):
    if rows < 4 * PART_STEP:
        return [slice(0, rows)]
    middle = rows - 2 * PART_STEP
    return [slice(middle, middle + PART_STEP), slice(0, middle), slice(middle + PART_STEP, rows)]


def square(lower, block):
    lines = []
    for b in range(len(lower)):
        parts = [lower[b]]
        for c in range(b + 1, len(lower)):
            part = lower[c][..., b * block : (b + 1) * block]
            parts.append(jnp.swapaxes(part, -1, -2))
        lines.append(jnp.concatenate(parts, axis=-1))
    return jnp.concatenate(lines, axis=-2)


def solution(mesh):
    placed = (P("gx", "gy", None), P())
    return jax.shard_map(
        on_device, mesh=mesh, in_specs=placed, out_specs=P("gx", "gy", None), check_vma=False
    )
```

```python
import math

import jax
import jax.numpy as jnp
from jax import lax
from jax.experimental import pallas as pl
from jax.experimental.pallas import tpu as pltpu
from jax.sharding import PartitionSpec as P

SWEEPS = 2

AXIS_ORDERS = ((0, 1, 2), (0, 2, 1), (1, 0, 2), (1, 2, 0), (2, 0, 1), (2, 1, 0))

HIGH = lax.Precision.HIGH


def ring(axis):
    peers = lax.axis_size(axis)
    up = [(i, (i + 1) % peers) for i in range(peers)]
    return up, [(j, i) for i, j in up]


def halos(block):
    rows, cols, _ = block.shape
    up, down = ring("gx")
    right, left = ring("gy")
    top = lax.ppermute(block[rows - SWEEPS :], "gx", up)
    bottom = lax.ppermute(block[:SWEEPS], "gx", down)
    before = lax.ppermute(block[:, cols - SWEEPS :], "gy", right)
    after = lax.ppermute(block[:, :SWEEPS], "gy", left)
    sides = jnp.concatenate([before, after], axis=1)
    above = lax.ppermute(sides[rows - SWEEPS :], "gx", up)
    below = lax.ppermute(sides[:SWEEPS], "gx", down)
    free = (8 - SWEEPS, 8 - SWEEPS), (0, 0)
    inner = jnp.pad(sides, ((SWEEPS, SWEEPS),) + free)
    sides = jnp.pad(jnp.concatenate([above, sides, below], axis=0), ((0, 0),) + free)
    return (block[:SWEEPS], block[:SWEEPS], inner), (top, bottom, sides)


def mirror(values, axis):
    return jnp.roll(jnp.flip(values, axis), 1, axis)


def symmetric_marks(marks):
    for flip_axis in range(3):
        marks = jnp.maximum(marks, mirror(marks, flip_axis))
    united = marks
    for axis_order in AXIS_ORDERS[1:]:
        united = jnp.maximum(united, jnp.transpose(marks, axis_order))
    return united


def cosine_table(length):
    position = jnp.arange(length, dtype=jnp.int32)
    phases = jnp.mod(position[:, None] * position[None, : length // 2 + 1], length)
    return jnp.cos(phases.astype(jnp.float32) * (2.0 * math.pi / length)) / math.sqrt(length)


MARGIN = 16
CHUNK = 16
STEP_ROWS = 16
PART_STEP = 8
VMEM_BYTES = 56 * 1024 * 1024


def split(values):
    high = values.astype(jnp.bfloat16)
    low = (values - high.astype(jnp.float32)).astype(jnp.bfloat16)
    return high, low


def fill_block(step, base, steps):
    return jnp.where(step < steps, base[0] + step, base[1] + step - steps)


def fill_kernel(
    base, here, above, below, top, bottom, sides, marks, table_high, table_low,
    given, kept, alternate, edge, punched, once, high, low, folded,
):
    step_rows, cols, length = here.shape
    step = fill_block(pl.program_id(0), base, pl.num_programs(0) // 2)
    is_given = pl.program_id(0) < pl.num_programs(0) // 2
    first_row = step * step_rows
    local_row = pl.program_id(0) * step_rows
    period = marks.shape[0]
    lane = lax.broadcasted_iota(jnp.int32, (128, 128), 1)
    signs = jnp.where(lax.broadcasted_iota(jnp.int32, (128, 128), 0) % 2 == 0, 1.0, -1.0)

    @pl.when(pl.program_id(0) == 0)
    def _():
        edge[...] = jnp.zeros_like(edge)

    def holes(row, start, size):
        row = lax.rem(first_row + row, period)
        start = start % period
        if start + size <= period:
            part = marks[row, pl.ds(start, size), :]
        else:
            part = jnp.concatenate(
                [marks[row, pl.ds(start, period - start), :], marks[row, pl.ds(0, start + size - period), :]],
                axis=0,
            )
        return jnp.concatenate([part] * (length // 128), axis=1)

    def punch(row, start, values):
        kept = jnp.where(holes(row, start, values.shape[0]) > 0.0, 0.0, values)
        punched[row, pl.ds(start, values.shape[0]), :] = kept

    def punch_row(row, source, index):
        full = first_row + row
        punch(row, MARGIN - 8, sides[full, pl.ds(0, 8), :])
        punch(row, MARGIN + cols, sides[full, pl.ds(8, 8), :])
        for c in range(0, cols, CHUNK):
            punch(row, MARGIN + c, source[index, pl.ds(c, CHUNK), :])

    def neighbours(ref, row, start):
        middle = ref[row, pl.ds(start, CHUNK), :]
        total = ref[row - 1, pl.ds(start, CHUNK), :] + ref[row + 1, pl.ds(start, CHUNK), :]
        total += ref[row, pl.ds(start - 1, CHUNK), :] + ref[row, pl.ds(start + 1, CHUNK), :]
        return total + pltpu.roll(middle, 1, 1) + pltpu.roll(middle, length - 1, 1)

    last = (sides.shape[0] - 2 * SWEEPS) // step_rows - 1
    for edge_rows, inside, offset, outer in (
        (above, step > 0, 0, top),
        (below, step < last, step_rows + SWEEPS, bottom),
    ):
        @pl.when(inside)
        def _():
            for r in range(SWEEPS):
                punch_row(offset + r, edge_rows, r)

        @pl.when(jnp.logical_not(inside))
        def _():
            for r in range(SWEEPS):
                punch_row(offset + r, outer, r)

    @pl.loop(0, step_rows)
    def _(r):
        punch_row(r + SWEEPS, here, r)

    @pl.loop(1, step_rows + 2 * SWEEPS - 1, unroll=2)
    def _(r):
        for start in range(MARGIN - 8, MARGIN + cols + 8, CHUNK):
            total = neighbours(punched, r, start) * holes(r, start, CHUNK)
            once[r, pl.ds(start, CHUNK), :] = punched[r, pl.ds(start, CHUNK), :] + total

    @pl.loop(0, step_rows)
    def _(r):
        for c in range(0, cols, CHUNK):
            start = MARGIN + c
            total = neighbours(once, r + SWEEPS, start) * holes(r + SWEEPS, start, CHUNK)
            filled = punched[r + SWEEPS, pl.ds(start, CHUNK), :] + total
            first, second = split(filled)
            spot = pl.ds(pl.multiple_of(r * cols + c, CHUNK), CHUNK)
            high[spot, :] = first
            low[spot, :] = second
            wrapped = filled[:, :128]
            for tile in range(1, length // 128):
                wrapped += filled[:, tile * 128 : (tile + 1) * 128]
            folded[pl.ds(c, CHUNK), :] = wrapped
        column = jnp.where(lane == local_row + r, signs, 0.0).astype(jnp.bfloat16)
        first, second = split(folded[...])
        total = jnp.dot(first, column, preferred_element_type=jnp.float32)
        total += jnp.dot(second, column, preferred_element_type=jnp.float32)
        edge[...] += total

    rows_each = 8
    half = given.shape[2]
    order = lax.broadcasted_iota(jnp.int32, (rows_each, cols, half), 1)

    @pl.loop(0, step_rows // rows_each)
    def _(r):
        spot = pl.ds(pl.multiple_of(r * rows_each * cols, CHUNK), rows_each * cols)
        first, second = high[spot, :], low[spot, :]
        total = jnp.dot(first, table_low[...], preferred_element_type=jnp.float32)
        total += jnp.dot(second, table_high[...], preferred_element_type=jnp.float32)
        total += jnp.dot(first, table_high[...], preferred_element_type=jnp.float32)
        total = total.reshape(rows_each, cols, half)

        @pl.when(is_given)
        def _():
            given[pl.ds(r * rows_each, rows_each)] = total

        @pl.when(jnp.logical_not(is_given))
        def _():
            kept[pl.ds(r * rows_each, rows_each)] = total

        signed = jnp.sum(jnp.where(order % 2 == 0, total, -total), axis=1)
        alternate[pl.ds(pl.multiple_of(r * rows_each, rows_each), rows_each), :] = signed


def rounded_parts(table):
    rounded = lax.reduce_precision(table, 8, 7)
    return rounded.astype(jnp.bfloat16), (table - rounded).astype(jnp.bfloat16)


def fill_arrays(intensity, template, row, col, main):
    rows, cols, length = intensity.shape
    united = symmetric_marks(template)
    period = united.shape[0]
    offsets = (jnp.mod(row * rows - SWEEPS, period), jnp.mod(col * cols - MARGIN, period))
    marks = jnp.roll(united, (-offsets[0], -offsets[1]), (0, 1)).astype(jnp.float32) / 6.0
    marks = jnp.tile(marks, (1, 1, 128 // period))
    constants = (marks,) + rounded_parts(main)
    inner, outer = halos(intensity)
    return inner + constants, outer + constants


def filled_spectrum(intensity, arrays, starts, count):
    rows, cols, length = intensity.shape
    half = length // 2
    step_rows = min(STEP_ROWS, count)
    steps = count // step_rows
    pairs = step_rows // SWEEPS
    last = rows // SWEEPS - 1
    whole = lambda array: pl.BlockSpec(array.shape, lambda i, b: (0,) * array.ndim)
    here = lambda i, b: (fill_block(i, b, steps), 0, 0)
    before = lambda i, b: (jnp.maximum(fill_block(i, b, steps) * pairs - 1, 0), 0, 0)
    after = lambda i, b: (jnp.minimum((fill_block(i, b, steps) + 1) * pairs, last), 0, 0)
    padded = (step_rows + 2 * SWEEPS, cols + 2 * MARGIN, length)
    out_block = (step_rows, cols, half)
    out = jax.ShapeDtypeStruct((count, cols, half), jnp.float32)
    return pl.pallas_call(
        fill_kernel,
        grid_spec=pltpu.PrefetchScalarGridSpec(
            num_scalar_prefetch=1,
            grid=(2 * steps,),
            in_specs=[
                pl.BlockSpec((step_rows, cols, length), here),
                pl.BlockSpec((SWEEPS, cols, length), before),
                pl.BlockSpec((SWEEPS, cols, length), after),
            ] + [whole(array) for array in arrays],
            out_specs=[
                pl.BlockSpec(out_block, lambda i, b: (jnp.minimum(i, steps - 1), 0, 0)),
                pl.BlockSpec(out_block, lambda i, b: (jnp.maximum(i - steps, 0), 0, 0)),
                pl.BlockSpec((step_rows, half), lambda i, b: (i, 0)),
                pl.BlockSpec((cols, 128), lambda i, b: (0, 0)),
            ],
            scratch_shapes=[
                pltpu.VMEM(padded, jnp.float32),
                pltpu.VMEM(padded, jnp.float32),
                pltpu.VMEM((step_rows * cols, length), jnp.bfloat16),
                pltpu.VMEM((step_rows * cols, length), jnp.bfloat16),
                pltpu.VMEM((cols, 128), jnp.float32),
            ],
        ),
        out_shape=[
            out,
            out,
            jax.ShapeDtypeStruct((2 * count, half), jnp.float32),
            jax.ShapeDtypeStruct((cols, 128), jnp.float32),
        ],
        compiler_params=pltpu.CompilerParams(vmem_limit_bytes=VMEM_BYTES),
        cost_estimate=pl.CostEstimate(
            flops=count * cols * length * half * 12,
            bytes_accessed=count * cols * (length + half) * 8,
            transcendentals=0,
        ),
    )(jnp.stack(starts) // step_rows, intensity, intensity, intensity, *arrays)


def pack(section, offsets):
    block = offsets[1]
    units = [section[b * block : (b + 1) * block, : (b + 1) * block] for b in range(len(offsets) - 1)]
    return jnp.concatenate(units, axis=1)


def three_dots(left, right):
    total = jnp.dot(left[1], right[0], preferred_element_type=jnp.float32)
    total += jnp.dot(left[0], right[1], preferred_element_type=jnp.float32)
    return total + jnp.dot(left[0], right[0], preferred_element_type=jnp.float32)


def section_kernel(
    offsets, closing, me, weights, kept, got, cols_high, cols_low, rows_high, rows_low,
    rim, corner, before, *refs
):
    step, steps = pl.program_id(0), pl.num_programs(0)
    step_rows = kept.shape[0]
    half, count = rows_high.shape
    planes, block, width = before.shape
    *outs, total, lines, packed = refs
    gy, (_, own, gx, _) = len(outs), outs[0].shape

    def place(layer, values, slot=0):
        packed[slot] = values
        for e in range(own):
            for p in range(gy):
                start = pl.multiple_of((e * gy + (p ^ me[0])) * gx, gx)
                outs[p][layer, e] = packed[slot, pl.ds(start, gx), :]

    @pl.when(step == 0)
    def _():
        total[...] = before[...]

    for r in range(step_rows):
        layer = step * step_rows + r
        values = jnp.concatenate([kept[r], got[r]], axis=0)
        section = three_dots((cols_high[...], cols_low[...]), split(values))
        section = section + section.T
        line = pack(section, offsets)
        place(layer, line, r)
        for m in range(planes):
            total[m] += weights[m, layer] * line
        for m in range(planes - 1):
            row = (m + 1) * (half // planes)
            lines[m, pl.ds(layer, 1), :] = section[row : row + 1]

    @pl.when(step == steps - 1)
    def _():
        for m in range(planes - 1):
            plane = three_dots((rows_high[...], rows_low[...]), split(lines[m]))
            total[m] += pack(plane + plane.T, offsets)
        if closing:
            total[planes - 1] += pack(rim[...] + rim[...].T, offsets)
            for m in range(planes):
                place(count + m, total[m])
            place(count + planes, jnp.zeros((block, width), jnp.float32) + corner[...])


def packed_section(col, kept, got, table_pair, table_rows, marks, rim, corner, before, offsets, shape, closing):
    count, cols, half = kept.shape
    planes, block, width = before.shape
    gx, gy = shape
    step_rows = 4
    layers = count + (planes + 1 if closing else 0)
    whole = lambda array: pl.BlockSpec(array.shape, lambda i: (0,) * array.ndim)
    weights = jnp.stack([table_rows[:, m] for m in marks])
    arrays = rounded_parts(table_pair.T) + rounded_parts(table_rows[:, :half].T)
    arrays += (rim, corner[None], before)
    out = jax.ShapeDtypeStruct((layers, block // (gx * gy), gx, width), jnp.float32)
    outs = [out] * gy + [jax.ShapeDtypeStruct(before.shape, jnp.float32)]
    rows_spec = pl.BlockSpec((step_rows, cols, half), lambda i: (i, 0, 0))
    return pl.pallas_call(
        lambda *refs: section_kernel(offsets, closing, *refs),
        grid=(count // step_rows,),
        in_specs=[pl.BlockSpec(memory_space=pltpu.SMEM)] * 2 + [rows_spec, rows_spec]
        + [whole(array) for array in arrays],
        out_specs=[whole(out) for out in outs],
        out_shape=outs,
        scratch_shapes=[
            pltpu.VMEM((planes, count, half), jnp.float32),
            pltpu.VMEM((step_rows, block, width), jnp.float32),
        ],
        compiler_params=pltpu.CompilerParams(vmem_limit_bytes=VMEM_BYTES),
        cost_estimate=pl.CostEstimate(
            flops=count * 12 * cols * half * half,
            bytes_accessed=count * cols * half * 16,
            transcendentals=0,
        ),
    )(col.reshape(1), weights, kept, got, *arrays)


def on_device(intensity, template):
    rows, cols, length = intensity.shape
    gx, gy = lax.axis_size("gx"), lax.axis_size("gy")
    row, col = lax.axis_index("gx"), lax.axis_index("gy")
    devices, half = gx * gy, length // 2
    block = max(devices, rows)
    blocks, own, slabs = half // block, block // devices, gx // 2
    offsets = [block * b * (b + 1) // 2 for b in range(blocks + 1)]
    width = offsets[blocks]
    table = cosine_table(length)
    main = table[:, :half]

    pair_rows = rows // 2
    parts = row_parts(pair_rows)
    counts = [part.stop - part.start for part in parts]
    core = lax.rem(col, 2)
    inner_arrays, arrays = fill_arrays(intensity, template, row, col, main)
    given_first, kept_first = (1 - core) * pair_rows, core * pair_rows
    pieces = []

    def fill_part(c, after):
        starts = given_first + parts[c].start, kept_first + parts[c].start
        if after is not None:
            starts, after = lax.optimization_barrier((starts, after))
        inner = parts[c].start >= SWEEPS and parts[c].stop <= pair_rows - SWEEPS
        pieces.append(
            filled_spectrum(intensity, inner_arrays if inner else arrays, starts, counts[c])
        )
        return lax.ppermute(pieces[c][0], "gy", swap(gy, 1)), after

    table_cols = lax.dynamic_slice_in_dim(table, col * cols, cols, 0)
    kept_rows = lax.dynamic_slice_in_dim(table, row * rows + kept_first, pair_rows, 0)
    marks = [rows * (m + 1) for m in range(slabs)]
    mates = lax.dynamic_slice_in_dim(main, (col + 1 - 2 * core) * cols, cols, 0)
    table_pair = jnp.concatenate([table_cols[:, :half], mates], axis=0)
    table_parts = main.reshape(gx, 2, pair_rows, half) / 6.0
    table_parts = jnp.where(core == 0, table_parts, table_parts[:, ::-1])
    table_parts = [table_parts[:, :, part] for part in parts]
    side = jnp.zeros((slabs, block, width), jnp.float32)
    rim, corner = jnp.zeros((half, half), jnp.float32), jnp.zeros((width,), jnp.float32)
    values, packed, lines = 0.0, None, None
    for c, count in enumerate(counts):
        closing = c == len(counts) - 1
        got, packed = fill_part(c, packed)
        held = pieces[c][1]
        if c > 0:
            held, got_lines = lax.optimization_barrier((held, exchanged(packed)))
            lines = sent_lines(got_lines, counts[c - 1], lines)
            values = values + first_axis(lines, table_parts[c - 1])
        if closing:
            given_rows = lax.dynamic_slice_in_dim(table, row * rows + given_first, pair_rows, 0)
            ordered_rows = [held_rows[part] for part in parts for held_rows in (given_rows, kept_rows)]
            ordered_rows = jnp.concatenate(ordered_rows, axis=0)
            alternate = jnp.concatenate([piece[2] for piece in pieces], axis=0) / math.sqrt(length)
            edge = [piece[3][:, : piece[2].shape[0]] for piece in pieces]
            edge = jnp.concatenate(edge, axis=1)
            edge = jnp.einsum("ba,bk->ak", edge / math.sqrt(length), table_cols, precision=HIGH)
            edge = edge + jnp.concatenate([alternate, edge[:, half:]], axis=1)
            rim = jnp.einsum("aj,ak->jk", ordered_rows[:, :half], edge[:, :half], precision=HIGH)
            corner = 2.0 * jnp.einsum("a,ak->k", ordered_rows[:, half], edge, precision=HIGH)
            corner = corner + jnp.einsum("aj,a->j", ordered_rows, edge[:, half], precision=HIGH)
            corner = jnp.pad(corner, (0, width - half - 1))

        *packed, side = packed_section(
            col, held, got, table_pair, kept_rows[parts[c]], marks,
            rim, corner, side, offsets, (gx, gy), closing,
        )
    lines = sent_lines(exchanged(packed), counts[-1], lines)
    values = values + first_axis(lines, table_parts[-1])
    side = jnp.sum(lines[:, :, 2 * counts[-1] :], axis=0) / 6.0
    turned = values.reshape(own, blocks, own, devices, width)
    turned = jnp.transpose(turned, (3, 1, 2, 0, 4))
    turned = [turned[:, b, :, :, : offsets[b + 1]] for b in range(blocks)]
    turned = lax.all_to_all(jnp.concatenate(turned, axis=3), ("gy", "gx"), 0, 0, tiled=True)
    turned = jnp.transpose(turned, (1, 2, 0, 3)).reshape(own, block, -1)

    slab = jnp.minimum(row, gx - 1 - row)
    far_row, far_col = row >= slabs, col >= gy // 2
    pick_rows = jnp.arange(rows)
    pick_rows = slab * rows + jnp.where(far_row, rows - pick_rows, pick_rows)
    pick_cols = jnp.arange(cols)
    pick_cols = jnp.where(far_col, (gy - col) * cols - pick_cols, col * cols + pick_cols)

    if rows == block:
        got, piece = [], None
        for messages in slab_messages(values, turned, side, offsets, slabs):
            if piece is not None:
                messages, piece = lax.optimization_barrier((messages, piece))
                got.append(gathered(piece, gy, got[-1] if got else None))
            piece = lax.all_to_all(messages, "gx", 0, 0, tiled=True)
        got.append(gathered(piece, gy, got[-1] if got else None))
        tiles = width // 128
        start = tile_groups(tiles)[0].stop * own * block
        side = jnp.stack([piece[:, start : start + 3 * own * tiles] for piece in got[0]])
        bit = gy // 2
        while bit:
            paired = side.reshape((-1, 2, bit) + side.shape[1:])
            side = jnp.where((col & bit) == 0, paired, paired[:, ::-1]).reshape(side.shape)
            bit //= 2
        side = side.reshape(devices, own, 3, width)
        side = jnp.transpose(side, (2, 1, 0, 3)).reshape(3, block, width)
        next_plane, across = side[0], rim_rows(side[1:], offsets, pick_rows)
        rim_col = col == gy // 2
        rim = across[:, pick_cols]
        return result_block(
            got, next_plane, across, rim, pick_cols, slab, far_row, rim_col, col, offsets
        )

    side = lax.all_gather(side, ("gy", "gx"), axis=0)
    side = jnp.transpose(side, (2, 1, 0, 3)).reshape(slabs + 1, block, width)
    across = rim_rows(side[slabs - 1 :], offsets, pick_rows)
    next_plane = lax.dynamic_index_in_dim(side, slab, 0, keepdims=False)
    sums = axis_order_sums(values, turned, offsets, block)
    messages = []
    for s in range(slabs):
        base, first = s * rows // block, s * rows
        units = []
        for b in range(blocks):
            size = (b + 1) * block
            near = jnp.zeros((own, rows, size))
            far = jnp.zeros((own, block, size))
            if b >= base:
                near = jnp.stack([sums[b][e][first : first + rows, :size] for e in range(own)])
            else:
                far = jnp.stack([sums[base][e][b * block : size, :size] for e in range(own)])
            units.append(jnp.concatenate([near, far], axis=1))
        messages.append(jnp.concatenate(units, axis=2))
    messages = jnp.stack(messages + messages[::-1])
    got = lax.all_to_all(messages, "gx", 0, 0, tiled=True)
    got = lax.all_gather(got, "gy", axis=0, tiled=True)
    got = jnp.swapaxes(got, 0, 1).reshape(block, rows + block, width)
    base = slab * rows // block
    lower = []
    for b in range(blocks):
        lanes = slice(offsets[b], offsets[b + 1])
        near = jnp.swapaxes(got[:, :rows, lanes], 0, 1)
        far = lax.dynamic_slice_in_dim(got[:, rows:, lanes], lax.rem(slab * rows, block), rows, 0)
        lower.append(jnp.where(b >= base, near, far))
    lower = jnp.concatenate(lower, axis=2)
    lower = jnp.concatenate([lower, next_plane[None]], axis=0)
    body = square([lower[:, :, offsets[b] : offsets[b + 1]] for b in range(blocks)], block)
    body = body[pick_rows - slab * rows]
    body = jnp.concatenate([body, across[:, None, :half]], axis=1)[:, pick_cols]
    body = jnp.concatenate([body, across[:, pick_cols][:, :, None]], axis=2)
    return jnp.concatenate([body, jnp.flip(body[:, :, 1:half], 2)], axis=2)


def rim_rows(side, offsets, pick_rows):
    blocks, block = len(offsets) - 1, offsets[1]
    half = blocks * block
    last = square([side[0][:, offsets[b] : offsets[b + 1]] for b in range(blocks)], block)
    rim = side[1, 0, : half + 1]
    last = jnp.concatenate([last, rim[None, :half]], axis=0)
    return jnp.concatenate([last, rim[:, None]], axis=1)[pick_rows]


def axis_order_sums(values, turned, offsets, block):
    start = 0
    sums = []
    for top in range(len(offsets) - 1):
        size = (top + 1) * block
        parts = []
        for e in range(values.shape[0]):
            part = values[e, :size, offsets[top] : offsets[top] + size]
            lower = [turned[e, :, start + offsets[b] : start + offsets[b + 1]] for b in range(top + 1)]
            parts.append(part + part.T + square(lower, block))
        sums.append(parts)
        start += offsets[top + 1]
    return sums


def message_kernel(offsets, slabs, values, turned, side, *messages):
    blocks, block = len(offsets) - 1, offsets[1]
    values, turned = values[...], turned[...]
    own = values.shape[0]
    sums = axis_order_sums(values, turned, offsets, block)
    groups = tile_groups(offsets[-1] // 128)
    side_start = groups[0].stop * own * block
    messages[0][:, side_start:] = jnp.zeros_like(messages[0][:, side_start:])
    for s in range(slabs):
        places = s, 2 * slabs - 1 - s
        for e in range(own):
            units = []
            for b in range(blocks):
                size = (b + 1) * block
                if b >= s:
                    units.append(sums[b][e][s * block : (s + 1) * block, :size])
                else:
                    units.append(sums[s][e][b * block : size, :size])
            line = jnp.concatenate(units, axis=1)
            for group, out in zip(groups, messages):
                for tile in range(group.start, group.stop):
                    start = ((tile - group.start) * own + e) * block
                    for place in places:
                        out[place, start : start + block] = line[:, tile * 128 : (tile + 1) * 128]
            row = side_start + 3 * e * groups[-1].stop
            for plane in (s, slabs - 1, slabs):
                for tile in range(groups[-1].stop):
                    part = side[e, plane : plane + 1, tile * 128 : (tile + 1) * 128]
                    for place in places:
                        messages[0][place, row : row + 1] = part
                    row += 1


def slab_messages(values, turned, side, offsets, slabs):
    own, block, tiles = values.shape[0], offsets[1], offsets[-1] // 128
    sizes = [(group.stop - group.start) * own * block for group in tile_groups(tiles)]
    sizes[0] += -(-3 * own * tiles // 8) * 8
    return pl.pallas_call(
        lambda *refs: message_kernel(offsets, slabs, *refs),
        in_specs=[pl.BlockSpec(memory_space=pltpu.VMEM)] * 3,
        out_specs=[pl.BlockSpec(memory_space=pltpu.VMEM)] * len(sizes),
        out_shape=[jax.ShapeDtypeStruct((2 * slabs, size, 128), jnp.float32) for size in sizes],
        compiler_params=pltpu.CompilerParams(vmem_limit_bytes=VMEM_BYTES),
    )(values, turned, side)


def result_kernel(
    offsets, own, devices, groups, places, next_plane, across, rim, pick, flip, *refs
):
    blocks, block = len(offsets) - 1, offsets[1]
    tiles = offsets[-1] // 128
    peers = (len(refs) - 2) // len(groups) - 1
    pieces, out = refs[: peers * len(groups)], refs[peers * len(groups)]
    held, sems = refs[peers * len(groups) + 1 : -1], refs[-1]
    step_rows, cols, length = out.shape
    half = length // 2
    slab, far_row, rim_col, me = places[0], places[1], places[2], places[3]
    lane = lax.broadcasted_iota(jnp.int32, (block, 128), 1)
    at_rim = lax.broadcasted_iota(jnp.int32, (cols, half), 0) + (1 - rim_col) == 0
    rim_lane = lax.broadcasted_iota(jnp.int32, rim.shape, 1)
    first_lane = lax.broadcasted_iota(jnp.int32, (cols, half), 1) == 0

    @pl.when(pl.program_id(0) == 0)
    def _():
        copies = []
        for g in range(len(groups)):
            for peer in range(peers):
                piece = pieces[g * peers + peer]
                size = piece.shape[0]
                spot = pl.ds(pl.multiple_of((me ^ peer) * size, size), size)
                copies.append(pltpu.make_async_copy(piece, held[g].at[spot], sems.at[g, peer]))
        for copy in copies:
            copy.start()
        for copy in copies:
            copy.wait()

    def left_half(r):
        t = pl.program_id(0) * step_rows + r
        i = jnp.where(far_row == 1, block - t, t)
        inside = (jnp.zeros((block, 128), jnp.int32) + i) < block
        i = jnp.minimum(i, block - 1)
        source = lax.div(i, devices), lax.rem(i, devices)
        parts = []
        for g, group in enumerate(groups):
            stride = held[g].shape[0] // devices
            for tile in range(group.start, group.stop):
                start = (tile - group.start) * own * block
                near = [
                    held[g][pl.ds(start + e * block + i, devices, stride=stride), :]
                    for e in range(own)
                ]
                near = jnp.concatenate(near, axis=0)
                far = pl.multiple_of(source[1] * stride + start + source[0] * block, 8)
                far = held[g][pl.ds(far, block), :]
                kind = jnp.zeros((block, 128), jnp.int32)
                for b in range(1, blocks):
                    kind += (lane + tile * 128 >= offsets[b]).astype(jnp.int32)
                line = jnp.where(kind >= slab, near, far)
                line = jnp.where(inside, line, next_plane[:, pl.ds(tile * 128, 128)])
                parts.append(line)
        line = jnp.concatenate(parts, axis=1)
        plane = square([line[:, offsets[b] : offsets[b + 1]] for b in range(blocks)], block)
        high, low = split(plane)
        left = jnp.dot(pick[...], high, preferred_element_type=jnp.float32)
        left += jnp.dot(pick[...], low, preferred_element_type=jnp.float32)
        left = jnp.where(at_rim, across[pl.ds(t, 1), :], left)
        out[r, :, pl.ds(0, half)] = left
        return left

    together = 4

    @pl.loop(0, step_rows // together)
    def _(c):
        left = [left_half(c * together + n) for n in range(together)]
        high, low = split(jnp.concatenate(left, axis=0))
        right = jnp.dot(high, flip[...], preferred_element_type=jnp.float32)
        right += jnp.dot(low, flip[...], preferred_element_type=jnp.float32)
        for n in range(together):
            r = c * together + n
            t = pl.program_id(0) * step_rows + r
            edge = jnp.sum(jnp.where(rim_lane == t, rim[...], 0.0), axis=1, keepdims=True)
            part = right[n * cols : (n + 1) * cols]
            out[r, :, pl.ds(half, half)] = jnp.where(first_lane, edge, part)


def result_block(got, next_plane, across, rim, pick_cols, slab, far_row, rim_col, col, offsets):
    block = offsets[1]
    gx = got[0][0].shape[0]
    groups = tile_groups(offsets[-1] // 128)
    devices = gx * len(got[0])
    own = block // devices
    rows, half = across.shape[0], across.shape[1] - 1
    cols = pick_cols.shape[0]
    step_rows = 8
    places = jnp.stack([slab, far_row.astype(jnp.int32), rim_col.astype(jnp.int32), col])
    cell = jnp.arange(half)
    pick = (pick_cols[:, None] == cell[None, :]).astype(jnp.bfloat16)
    flip = (cell[:, None] + cell[None, :] == half).astype(jnp.bfloat16)
    rim = jnp.pad(rim.T, ((0, 0), (0, 128 - rows)))
    whole = lambda array: pl.BlockSpec(array.shape, lambda i: (0,) * array.ndim)
    arrays = (next_plane, across[:, :half], rim, pick, flip)
    pieces = [piece.reshape(-1, 128) for group in got for piece in group]
    return pl.pallas_call(
        lambda *refs: result_kernel(offsets, own, devices, groups, *refs),
        grid=(rows // step_rows,),
        in_specs=[pl.BlockSpec(memory_space=pltpu.SMEM)] + [whole(array) for array in arrays]
        + [pl.BlockSpec(memory_space=pl.ANY)] * len(pieces),
        out_specs=pl.BlockSpec((step_rows, cols, 2 * half), lambda i: (i, 0, 0)),
        out_shape=jax.ShapeDtypeStruct((rows, cols, 2 * half), jnp.float32),
        scratch_shapes=[
            pltpu.VMEM((devices * group[0].shape[1], 128), jnp.float32) for group in got
        ] + [pltpu.SemaphoreType.DMA((len(groups), len(got[0])))],
        compiler_params=pltpu.CompilerParams(vmem_limit_bytes=VMEM_BYTES),
    )(places, *arrays, *pieces)


def tile_groups(tiles):
    return [slice(tile, min(tile + 2, tiles)) for tile in range(0, tiles, 2)]


def swap(peers, bit):
    return [(q, q ^ bit) for q in range(peers)]


def gathered(piece, peers, after):
    if after is not None:
        piece, first_hops = lax.optimization_barrier((piece, after[1:3]))
        after[1:3] = first_hops
    pieces, bit = {0: piece}, peers // 2
    while bit:
        for place in list(pieces):
            pieces[place ^ bit] = lax.ppermute(pieces[place], "gy", swap(peers, bit))
        bit //= 2
    return [pieces[place] for place in range(peers)]


def exchanged(packed):
    gy = len(packed)
    return [packed[0]] + [lax.ppermute(packed[p], "gy", swap(gy, p)) for p in range(1, gy)]


def sent_lines(got, count, after):
    gy = len(got)
    lines = [sum(got[p][:count] for p in range(first, gy, 2)) for first in range(2)]
    lines = jnp.concatenate(lines + [sum(piece[count:] for piece in got)], axis=0)
    lines = jnp.transpose(lines, (2, 1, 0, 3))
    if after is not None:
        lines, _ = lax.optimization_barrier((lines, after))
    return lax.all_to_all(lines, "gx", 0, 0, tiled=True)


def first_axis(lines, table):
    gx, _, count, half = table.shape
    table = table.reshape(gx, 2 * count, half)
    return jnp.einsum("geaw,gai->eiw", lines[:, :, : 2 * count], table, precision=HIGH)


def row_parts(rows):
    if rows < 4 * PART_STEP:
        return [slice(0, rows)]
    middle = rows - 2 * PART_STEP
    return [slice(middle, middle + PART_STEP), slice(0, middle), slice(middle + PART_STEP, rows)]


def square(lower, block):
    lines = []
    for b in range(len(lower)):
        parts = [lower[b]]
        for c in range(b + 1, len(lower)):
            part = lower[c][..., b * block : (b + 1) * block]
            parts.append(jnp.swapaxes(part, -1, -2))
        lines.append(jnp.concatenate(parts, axis=-1))
    return jnp.concatenate(lines, axis=-2)


def solution(mesh):
    placed = (P("gx", "gy", None), P())
    return jax.shard_map(
        on_device, mesh=mesh, in_specs=placed, out_specs=P("gx", "gy", None), check_vma=False
    )
```

```python
import math

import jax
import jax.numpy as jnp
from jax import lax
from jax.experimental import pallas as pl
from jax.experimental.pallas import tpu as pltpu
from jax.sharding import PartitionSpec as P

SWEEPS = 2

AXIS_ORDERS = ((0, 1, 2), (0, 2, 1), (1, 0, 2), (1, 2, 0), (2, 0, 1), (2, 1, 0))

HIGH = lax.Precision.HIGH


def ring(axis):
    peers = lax.axis_size(axis)
    up = [(i, (i + 1) % peers) for i in range(peers)]
    return up, [(j, i) for i, j in up]


def halos(block):
    rows, cols, _ = block.shape
    up, down = ring("gx")
    right, left = ring("gy")
    top = lax.ppermute(block[rows - SWEEPS :], "gx", up)
    bottom = lax.ppermute(block[:SWEEPS], "gx", down)
    before = lax.ppermute(block[:, cols - SWEEPS :], "gy", right)
    after = lax.ppermute(block[:, :SWEEPS], "gy", left)
    sides = jnp.concatenate([before, after], axis=1)
    above = lax.ppermute(sides[rows - SWEEPS :], "gx", up)
    below = lax.ppermute(sides[:SWEEPS], "gx", down)
    free = (8 - SWEEPS, 8 - SWEEPS), (0, 0)
    sides, top, bottom = lax.optimization_barrier((sides, top, bottom))
    inner = jnp.pad(sides, ((SWEEPS, SWEEPS),) + free)
    sides = jnp.pad(jnp.concatenate([above, sides, below], axis=0), ((0, 0),) + free)
    return (block[:SWEEPS], block[:SWEEPS], inner), (top, bottom, sides)


def mirror(values, axis):
    return jnp.roll(jnp.flip(values, axis), 1, axis)


def symmetric_marks(marks):
    for flip_axis in range(3):
        marks = jnp.maximum(marks, mirror(marks, flip_axis))
    united = marks
    for axis_order in AXIS_ORDERS[1:]:
        united = jnp.maximum(united, jnp.transpose(marks, axis_order))
    return united


def cosine_table(length):
    position = jnp.arange(length, dtype=jnp.int32)
    phases = jnp.mod(position[:, None] * position[None, : length // 2 + 1], length)
    return jnp.cos(phases.astype(jnp.float32) * (2.0 * math.pi / length)) / math.sqrt(length)


MARGIN = 16
CHUNK = 16
STEP_ROWS = 16
PART_STEP = 8
VMEM_BYTES = 56 * 1024 * 1024


def split(values):
    high = values.astype(jnp.bfloat16)
    low = (values - high.astype(jnp.float32)).astype(jnp.bfloat16)
    return high, low


def fill_kernel(
    base, here, above, below, top, bottom, sides, marks, table_high, table_low,
    spectrum, alternate, edge, punched, once, high, low, folded,
):
    step_rows, cols, length = here.shape
    step = pl.program_id(0) + base[0]
    first_row = step * step_rows
    local_row = pl.program_id(0) * step_rows
    period = marks.shape[0]
    lane = lax.broadcasted_iota(jnp.int32, (128, 128), 1)
    signs = jnp.where(lax.broadcasted_iota(jnp.int32, (128, 128), 0) % 2 == 0, 1.0, -1.0)

    @pl.when(pl.program_id(0) == 0)
    def _():
        edge[...] = jnp.zeros_like(edge)

    def holes(row, start, size):
        row = lax.rem(first_row + row, period)
        start = start % period
        if start + size <= period:
            part = marks[row, pl.ds(start, size), :]
        else:
            part = jnp.concatenate(
                [marks[row, pl.ds(start, period - start), :], marks[row, pl.ds(0, start + size - period), :]],
                axis=0,
            )
        return jnp.concatenate([part] * (length // 128), axis=1)

    def punch(row, start, values):
        kept = jnp.where(holes(row, start, values.shape[0]) > 0.0, 0.0, values)
        punched[row, pl.ds(start, values.shape[0]), :] = kept

    def punch_row(row, source, index):
        full = first_row + row
        punch(row, MARGIN - 8, sides[full, pl.ds(0, 8), :])
        punch(row, MARGIN + cols, sides[full, pl.ds(8, 8), :])
        for c in range(0, cols, CHUNK):
            punch(row, MARGIN + c, source[index, pl.ds(c, CHUNK), :])

    def neighbours(ref, row, start):
        middle = ref[row, pl.ds(start, CHUNK), :]
        total = ref[row - 1, pl.ds(start, CHUNK), :] + ref[row + 1, pl.ds(start, CHUNK), :]
        total += ref[row, pl.ds(start - 1, CHUNK), :] + ref[row, pl.ds(start + 1, CHUNK), :]
        return total + pltpu.roll(middle, 1, 1) + pltpu.roll(middle, length - 1, 1)

    last = (sides.shape[0] - 2 * SWEEPS) // step_rows - 1
    for edge_rows, inside, offset, outer in (
        (above, step > 0, 0, top),
        (below, step < last, step_rows + SWEEPS, bottom),
    ):
        @pl.when(inside)
        def _():
            for r in range(SWEEPS):
                punch_row(offset + r, edge_rows, r)

        @pl.when(jnp.logical_not(inside))
        def _():
            for r in range(SWEEPS):
                punch_row(offset + r, outer, r)

    @pl.loop(0, step_rows)
    def _(r):
        punch_row(r + SWEEPS, here, r)

    @pl.loop(1, step_rows + 2 * SWEEPS - 1, unroll=2)
    def _(r):
        for start in range(MARGIN - 8, MARGIN + cols + 8, CHUNK):
            total = neighbours(punched, r, start) * holes(r, start, CHUNK)
            once[r, pl.ds(start, CHUNK), :] = punched[r, pl.ds(start, CHUNK), :] + total

    @pl.loop(0, step_rows)
    def _(r):
        for c in range(0, cols, CHUNK):
            start = MARGIN + c
            total = neighbours(once, r + SWEEPS, start) * holes(r + SWEEPS, start, CHUNK)
            filled = punched[r + SWEEPS, pl.ds(start, CHUNK), :] + total
            first, second = split(filled)
            spot = pl.ds(pl.multiple_of(r * cols + c, CHUNK), CHUNK)
            high[spot, :] = first
            low[spot, :] = second
            wrapped = filled[:, :128]
            for tile in range(1, length // 128):
                wrapped += filled[:, tile * 128 : (tile + 1) * 128]
            folded[pl.ds(c, CHUNK), :] = wrapped
        column = jnp.where(lane == local_row + r, signs, 0.0).astype(jnp.bfloat16)
        first, second = split(folded[...])
        total = jnp.dot(first, column, preferred_element_type=jnp.float32)
        total += jnp.dot(second, column, preferred_element_type=jnp.float32)
        edge[...] += total

    rows_each = 8
    half = spectrum.shape[2]
    order = lax.broadcasted_iota(jnp.int32, (rows_each, cols, half), 1)

    @pl.loop(0, step_rows // rows_each)
    def _(r):
        spot = pl.ds(pl.multiple_of(r * rows_each * cols, CHUNK), rows_each * cols)
        first, second = high[spot, :], low[spot, :]
        total = jnp.dot(first, table_low[...], preferred_element_type=jnp.float32)
        total += jnp.dot(second, table_high[...], preferred_element_type=jnp.float32)
        total += jnp.dot(first, table_high[...], preferred_element_type=jnp.float32)
        total = total.reshape(rows_each, cols, half)
        spectrum[pl.ds(r * rows_each, rows_each)] = total
        signed = jnp.sum(jnp.where(order % 2 == 0, total, -total), axis=1)
        alternate[pl.ds(pl.multiple_of(r * rows_each, rows_each), rows_each), :] = signed


def rounded_parts(table):
    rounded = lax.reduce_precision(table, 8, 7)
    return rounded.astype(jnp.bfloat16), (table - rounded).astype(jnp.bfloat16)


def fill_arrays(intensity, template, row, col, main):
    rows, cols, length = intensity.shape
    united = symmetric_marks(template)
    period = united.shape[0]
    offsets = (jnp.mod(row * rows - SWEEPS, period), jnp.mod(col * cols - MARGIN, period))
    marks = jnp.roll(united, (-offsets[0], -offsets[1]), (0, 1)).astype(jnp.float32) / 6.0
    marks = jnp.tile(marks, (1, 1, 128 // period))
    constants = (marks,) + rounded_parts(main)
    inner, outer = halos(intensity)
    return inner + constants, outer + constants


def filled_spectrum(intensity, arrays, first, part):
    rows, cols, length = intensity.shape
    half, count = length // 2, part.stop - part.start
    step_rows = STEP_ROWS if part.start % STEP_ROWS == 0 and count % STEP_ROWS == 0 else PART_STEP
    pairs = step_rows // SWEEPS
    last = rows // SWEEPS - 1
    whole = lambda array: pl.BlockSpec(array.shape, lambda i, b: (0,) * array.ndim)
    before = lambda i, b: (jnp.maximum((i + b[0]) * pairs - 1, 0), 0, 0)
    after = lambda i, b: (jnp.minimum((i + b[0] + 1) * pairs, last), 0, 0)
    padded = (step_rows + 2 * SWEEPS, cols + 2 * MARGIN, length)
    return pl.pallas_call(
        fill_kernel,
        grid_spec=pltpu.PrefetchScalarGridSpec(
            num_scalar_prefetch=1,
            grid=(count // step_rows,),
            in_specs=[
                pl.BlockSpec((step_rows, cols, length), lambda i, b: (i + b[0], 0, 0)),
                pl.BlockSpec((SWEEPS, cols, length), before),
                pl.BlockSpec((SWEEPS, cols, length), after),
            ] + [whole(array) for array in arrays],
            out_specs=[
                pl.BlockSpec((step_rows, cols, half), lambda i, b: (i, 0, 0)),
                pl.BlockSpec((step_rows, half), lambda i, b: (i, 0)),
                pl.BlockSpec((cols, 128), lambda i, b: (0, 0)),
            ],
            scratch_shapes=[
                pltpu.VMEM(padded, jnp.float32),
                pltpu.VMEM(padded, jnp.float32),
                pltpu.VMEM((step_rows * cols, length), jnp.bfloat16),
                pltpu.VMEM((step_rows * cols, length), jnp.bfloat16),
                pltpu.VMEM((cols, 128), jnp.float32),
            ],
        ),
        out_shape=[
            jax.ShapeDtypeStruct((count, cols, half), jnp.float32),
            jax.ShapeDtypeStruct((count, half), jnp.float32),
            jax.ShapeDtypeStruct((cols, 128), jnp.float32),
        ],
        compiler_params=pltpu.CompilerParams(vmem_limit_bytes=VMEM_BYTES),
        cost_estimate=pl.CostEstimate(
            flops=count * cols * length * half * 6,
            bytes_accessed=count * cols * (length + half) * 4,
            transcendentals=0,
        ),
    )((first // step_rows).reshape(1), intensity, intensity, intensity, *arrays)


def pack(section, offsets):
    block = offsets[1]
    units = [section[b * block : (b + 1) * block, : (b + 1) * block] for b in range(len(offsets) - 1)]
    return jnp.concatenate(units, axis=1)


def three_dots(left, right):
    total = jnp.dot(left[1], right[0], preferred_element_type=jnp.float32)
    total += jnp.dot(left[0], right[1], preferred_element_type=jnp.float32)
    return total + jnp.dot(left[0], right[0], preferred_element_type=jnp.float32)


def section_kernel(
    offsets, closing, me, weights, kept, got, cols_high, cols_low, rows_high, rows_low,
    rim, corner, before, *refs
):
    step, steps = pl.program_id(0), pl.num_programs(0)
    step_rows = kept.shape[0]
    half, count = rows_high.shape
    planes, block, width = before.shape
    *outs, total, lines, packed = refs
    gy, (_, own, gx, _) = len(outs), outs[0].shape

    def place(layer, values, slot=0):
        packed[slot] = values
        for e in range(own):
            for p in range(gy):
                start = pl.multiple_of((e * gy + (p ^ me[0])) * gx, gx)
                outs[p][layer, e] = packed[slot, pl.ds(start, gx), :]

    @pl.when(step == 0)
    def _():
        total[...] = before[...]

    for r in range(step_rows):
        layer = step * step_rows + r
        values = jnp.concatenate([kept[r], got[r]], axis=0)
        section = three_dots((cols_high[...], cols_low[...]), split(values))
        section = section + section.T
        line = pack(section, offsets)
        place(layer, line, r)
        for m in range(planes):
            total[m] += weights[m, layer] * line
        for m in range(planes - 1):
            row = (m + 1) * (half // planes)
            lines[m, pl.ds(layer, 1), :] = section[row : row + 1]

    @pl.when(step == steps - 1)
    def _():
        for m in range(planes - 1):
            plane = three_dots((rows_high[...], rows_low[...]), split(lines[m]))
            total[m] += pack(plane + plane.T, offsets)
        if closing:
            total[planes - 1] += pack(rim[...] + rim[...].T, offsets)
            for m in range(planes):
                place(count + m, total[m])
            place(count + planes, jnp.zeros((block, width), jnp.float32) + corner[...])


def packed_section(col, kept, got, table_pair, table_rows, marks, rim, corner, before, offsets, shape, closing):
    count, cols, half = kept.shape
    planes, block, width = before.shape
    gx, gy = shape
    step_rows = 4
    layers = count + (planes + 1 if closing else 0)
    whole = lambda array: pl.BlockSpec(array.shape, lambda i: (0,) * array.ndim)
    weights = jnp.stack([table_rows[:, m] for m in marks])
    arrays = rounded_parts(table_pair.T) + rounded_parts(table_rows[:, :half].T)
    arrays += (rim, corner[None], before)
    out = jax.ShapeDtypeStruct((layers, block // (gx * gy), gx, width), jnp.float32)
    outs = [out] * gy + [jax.ShapeDtypeStruct(before.shape, jnp.float32)]
    rows_spec = pl.BlockSpec((step_rows, cols, half), lambda i: (i, 0, 0))
    return pl.pallas_call(
        lambda *refs: section_kernel(offsets, closing, *refs),
        grid=(count // step_rows,),
        in_specs=[pl.BlockSpec(memory_space=pltpu.SMEM)] * 2 + [rows_spec, rows_spec]
        + [whole(array) for array in arrays],
        out_specs=[whole(out) for out in outs],
        out_shape=outs,
        scratch_shapes=[
            pltpu.VMEM((planes, count, half), jnp.float32),
            pltpu.VMEM((step_rows, block, width), jnp.float32),
        ],
        compiler_params=pltpu.CompilerParams(vmem_limit_bytes=VMEM_BYTES),
        cost_estimate=pl.CostEstimate(
            flops=count * 12 * cols * half * half,
            bytes_accessed=count * cols * half * 16,
            transcendentals=0,
        ),
    )(col.reshape(1), weights, kept, got, *arrays)


def on_device(intensity, template):
    rows, cols, length = intensity.shape
    gx, gy = lax.axis_size("gx"), lax.axis_size("gy")
    row, col = lax.axis_index("gx"), lax.axis_index("gy")
    devices, half = gx * gy, length // 2
    block = max(devices, rows)
    blocks, own, slabs = half // block, block // devices, gx // 2
    offsets = [block * b * (b + 1) // 2 for b in range(blocks + 1)]
    width = offsets[blocks]
    table = cosine_table(length)
    main = table[:, :half]

    pair_rows = rows // 2
    parts = row_parts(pair_rows)
    counts = [part.stop - part.start for part in parts]
    core = lax.rem(col, 2)
    inner_arrays, arrays = fill_arrays(intensity, template, row, col, main)
    given_first, kept_first = (1 - core) * pair_rows, core * pair_rows
    given, kept = [], []

    def fill_part(c, after):
        part = parts[c]
        starts = given_first + part.start, kept_first + part.start
        if after is not None:
            starts, after = lax.optimization_barrier((starts, after))
        inner = part.start >= SWEEPS and part.stop <= pair_rows - SWEEPS
        use = inner_arrays if inner else arrays
        given.append(filled_spectrum(intensity, use, starts[0], part))
        got = lax.ppermute(given[c][0], "gy", swap(gy, 1))
        kept.append(filled_spectrum(intensity, use, starts[1], part))
        return got, after

    table_cols = lax.dynamic_slice_in_dim(table, col * cols, cols, 0)
    kept_rows = lax.dynamic_slice_in_dim(table, row * rows + kept_first, pair_rows, 0)
    marks = [rows * (m + 1) for m in range(slabs)]
    mates = lax.dynamic_slice_in_dim(main, (col + 1 - 2 * core) * cols, cols, 0)
    table_pair = jnp.concatenate([table_cols[:, :half], mates], axis=0)
    table_parts = main.reshape(gx, 2, pair_rows, half) / 6.0
    table_parts = jnp.where(core == 0, table_parts, table_parts[:, ::-1])
    table_parts = [table_parts[:, :, part] for part in parts]
    side = jnp.zeros((slabs, block, width), jnp.float32)
    rim, corner = jnp.zeros((half, half), jnp.float32), jnp.zeros((width,), jnp.float32)
    values, packed, lines = 0.0, None, None
    for c, count in enumerate(counts):
        closing = c == len(counts) - 1
        got, packed = fill_part(c, packed)
        held = kept[c][0]
        if c > 0:
            held, got_lines = lax.optimization_barrier((held, exchanged(packed)))
            lines = sent_lines(got_lines, counts[c - 1], lines)
            values = values + first_axis(lines, table_parts[c - 1])
        if closing:
            given_rows = lax.dynamic_slice_in_dim(table, row * rows + given_first, pair_rows, 0)
            ordered_rows = [held_rows[part] for held_rows in (given_rows, kept_rows) for part in parts]
            ordered_rows = jnp.concatenate(ordered_rows, axis=0)
            alternate = jnp.concatenate([piece[1] for piece in given + kept], axis=0) / math.sqrt(length)
            edge = [piece[2][:, : piece[1].shape[0]] for piece in given + kept]
            edge = jnp.concatenate(edge, axis=1)
            edge = jnp.einsum("ba,bk->ak", edge / math.sqrt(length), table_cols, precision=HIGH)
            edge = edge + jnp.concatenate([alternate, edge[:, half:]], axis=1)
            rim = jnp.einsum("aj,ak->jk", ordered_rows[:, :half], edge[:, :half], precision=HIGH)
            corner = 2.0 * jnp.einsum("a,ak->k", ordered_rows[:, half], edge, precision=HIGH)
            corner = corner + jnp.einsum("aj,a->j", ordered_rows, edge[:, half], precision=HIGH)
            corner = jnp.pad(corner, (0, width - half - 1))

        *packed, side = packed_section(
            col, held, got, table_pair, kept_rows[parts[c]], marks,
            rim, corner, side, offsets, (gx, gy), closing,
        )
    lines = sent_lines(exchanged(packed), counts[-1], lines)
    values = values + first_axis(lines, table_parts[-1])
    side = jnp.sum(lines[:, :, 2 * counts[-1] :], axis=0) / 6.0
    turned = values.reshape(own, blocks, own, devices, width)
    turned = jnp.transpose(turned, (3, 1, 2, 0, 4))
    turned = [turned[:, b, :, :, : offsets[b + 1]] for b in range(blocks)]
    turned = lax.all_to_all(jnp.concatenate(turned, axis=3), ("gy", "gx"), 0, 0, tiled=True)
    turned = jnp.transpose(turned, (1, 2, 0, 3)).reshape(own, block, -1)

    slab = jnp.minimum(row, gx - 1 - row)
    far_row, far_col = row >= slabs, col >= gy // 2
    pick_rows = jnp.arange(rows)
    pick_rows = slab * rows + jnp.where(far_row, rows - pick_rows, pick_rows)
    pick_cols = jnp.arange(cols)
    pick_cols = jnp.where(far_col, (gy - col) * cols - pick_cols, col * cols + pick_cols)

    if rows == block:
        got, piece = [], None
        for messages in slab_messages(values, turned, side, offsets, slabs):
            if piece is not None:
                messages, piece = lax.optimization_barrier((messages, piece))
                got.append(gathered(piece, gy, got[-1] if got else None))
            piece = lax.all_to_all(messages, "gx", 0, 0, tiled=True)
        got.append(gathered(piece, gy, got[-1] if got else None))
        tiles = width // 128
        start = tile_groups(tiles)[0].stop * own * block
        side = jnp.stack([piece[:, start : start + 3 * own * tiles] for piece in got[0]])
        bit = gy // 2
        while bit:
            paired = side.reshape((-1, 2, bit) + side.shape[1:])
            side = jnp.where((col & bit) == 0, paired, paired[:, ::-1]).reshape(side.shape)
            bit //= 2
        side = side.reshape(devices, own, 3, width)
        side = jnp.transpose(side, (2, 1, 0, 3)).reshape(3, block, width)
        next_plane, across = side[0], rim_rows(side[1:], offsets, pick_rows)
        rim_col = col == gy // 2
        rim = across[:, pick_cols]
        return result_block(
            got, next_plane, across, rim, pick_cols, slab, far_row, rim_col, col, offsets
        )

    side = lax.all_gather(side, ("gy", "gx"), axis=0)
    side = jnp.transpose(side, (2, 1, 0, 3)).reshape(slabs + 1, block, width)
    across = rim_rows(side[slabs - 1 :], offsets, pick_rows)
    next_plane = lax.dynamic_index_in_dim(side, slab, 0, keepdims=False)
    sums = axis_order_sums(values, turned, offsets, block)
    messages = []
    for s in range(slabs):
        base, first = s * rows // block, s * rows
        units = []
        for b in range(blocks):
            size = (b + 1) * block
            near = jnp.zeros((own, rows, size))
            far = jnp.zeros((own, block, size))
            if b >= base:
                near = jnp.stack([sums[b][e][first : first + rows, :size] for e in range(own)])
            else:
                far = jnp.stack([sums[base][e][b * block : size, :size] for e in range(own)])
            units.append(jnp.concatenate([near, far], axis=1))
        messages.append(jnp.concatenate(units, axis=2))
    messages = jnp.stack(messages + messages[::-1])
    got = lax.all_to_all(messages, "gx", 0, 0, tiled=True)
    got = lax.all_gather(got, "gy", axis=0, tiled=True)
    got = jnp.swapaxes(got, 0, 1).reshape(block, rows + block, width)
    base = slab * rows // block
    lower = []
    for b in range(blocks):
        lanes = slice(offsets[b], offsets[b + 1])
        near = jnp.swapaxes(got[:, :rows, lanes], 0, 1)
        far = lax.dynamic_slice_in_dim(got[:, rows:, lanes], lax.rem(slab * rows, block), rows, 0)
        lower.append(jnp.where(b >= base, near, far))
    lower = jnp.concatenate(lower, axis=2)
    lower = jnp.concatenate([lower, next_plane[None]], axis=0)
    body = square([lower[:, :, offsets[b] : offsets[b + 1]] for b in range(blocks)], block)
    body = body[pick_rows - slab * rows]
    body = jnp.concatenate([body, across[:, None, :half]], axis=1)[:, pick_cols]
    body = jnp.concatenate([body, across[:, pick_cols][:, :, None]], axis=2)
    return jnp.concatenate([body, jnp.flip(body[:, :, 1:half], 2)], axis=2)


def rim_rows(side, offsets, pick_rows):
    blocks, block = len(offsets) - 1, offsets[1]
    half = blocks * block
    last = square([side[0][:, offsets[b] : offsets[b + 1]] for b in range(blocks)], block)
    rim = side[1, 0, : half + 1]
    last = jnp.concatenate([last, rim[None, :half]], axis=0)
    return jnp.concatenate([last, rim[:, None]], axis=1)[pick_rows]


def axis_order_sums(values, turned, offsets, block):
    start = 0
    sums = []
    for top in range(len(offsets) - 1):
        size = (top + 1) * block
        parts = []
        for e in range(values.shape[0]):
            part = values[e, :size, offsets[top] : offsets[top] + size]
            lower = [turned[e, :, start + offsets[b] : start + offsets[b + 1]] for b in range(top + 1)]
            parts.append(part + part.T + square(lower, block))
        sums.append(parts)
        start += offsets[top + 1]
    return sums


def message_kernel(offsets, slabs, values, turned, side, *messages):
    blocks, block = len(offsets) - 1, offsets[1]
    values, turned = values[...], turned[...]
    own = values.shape[0]
    sums = axis_order_sums(values, turned, offsets, block)
    groups = tile_groups(offsets[-1] // 128)
    side_start = groups[0].stop * own * block
    messages[0][:, side_start:] = jnp.zeros_like(messages[0][:, side_start:])
    for s in range(slabs):
        places = s, 2 * slabs - 1 - s
        for e in range(own):
            units = []
            for b in range(blocks):
                size = (b + 1) * block
                if b >= s:
                    units.append(sums[b][e][s * block : (s + 1) * block, :size])
                else:
                    units.append(sums[s][e][b * block : size, :size])
            line = jnp.concatenate(units, axis=1)
            for group, out in zip(groups, messages):
                for tile in range(group.start, group.stop):
                    start = ((tile - group.start) * own + e) * block
                    for place in places:
                        out[place, start : start + block] = line[:, tile * 128 : (tile + 1) * 128]
            row = side_start + 3 * e * groups[-1].stop
            for plane in (s, slabs - 1, slabs):
                for tile in range(groups[-1].stop):
                    part = side[e, plane : plane + 1, tile * 128 : (tile + 1) * 128]
                    for place in places:
                        messages[0][place, row : row + 1] = part
                    row += 1


def slab_messages(values, turned, side, offsets, slabs):
    own, block, tiles = values.shape[0], offsets[1], offsets[-1] // 128
    sizes = [(group.stop - group.start) * own * block for group in tile_groups(tiles)]
    sizes[0] += -(-3 * own * tiles // 8) * 8
    return pl.pallas_call(
        lambda *refs: message_kernel(offsets, slabs, *refs),
        in_specs=[pl.BlockSpec(memory_space=pltpu.VMEM)] * 3,
        out_specs=[pl.BlockSpec(memory_space=pltpu.VMEM)] * len(sizes),
        out_shape=[jax.ShapeDtypeStruct((2 * slabs, size, 128), jnp.float32) for size in sizes],
        compiler_params=pltpu.CompilerParams(vmem_limit_bytes=VMEM_BYTES),
    )(values, turned, side)


def result_kernel(
    offsets, own, devices, groups, places, next_plane, across, rim, pick, flip, *refs
):
    blocks, block = len(offsets) - 1, offsets[1]
    tiles = offsets[-1] // 128
    peers = (len(refs) - 2) // len(groups) - 1
    pieces, out = refs[: peers * len(groups)], refs[peers * len(groups)]
    held, sems = refs[peers * len(groups) + 1 : -1], refs[-1]
    step_rows, cols, length = out.shape
    half = length // 2
    slab, far_row, rim_col, me = places[0], places[1], places[2], places[3]
    lane = lax.broadcasted_iota(jnp.int32, (block, 128), 1)
    at_rim = lax.broadcasted_iota(jnp.int32, (cols, half), 0) + (1 - rim_col) == 0
    rim_lane = lax.broadcasted_iota(jnp.int32, rim.shape, 1)
    first_lane = lax.broadcasted_iota(jnp.int32, (cols, half), 1) == 0

    @pl.when(pl.program_id(0) == 0)
    def _():
        copies = []
        for g in range(len(groups)):
            for peer in range(peers):
                piece = pieces[g * peers + peer]
                size = piece.shape[0]
                spot = pl.ds(pl.multiple_of((me ^ peer) * size, size), size)
                copies.append(pltpu.make_async_copy(piece, held[g].at[spot], sems.at[g, peer]))
        for copy in copies:
            copy.start()
        for copy in copies:
            copy.wait()

    def left_half(r):
        t = pl.program_id(0) * step_rows + r
        i = jnp.where(far_row == 1, block - t, t)
        inside = (jnp.zeros((block, 128), jnp.int32) + i) < block
        i = jnp.minimum(i, block - 1)
        source = lax.div(i, devices), lax.rem(i, devices)
        parts = []
        for g, group in enumerate(groups):
            stride = held[g].shape[0] // devices
            for tile in range(group.start, group.stop):
                start = (tile - group.start) * own * block
                near = [
                    held[g][pl.ds(start + e * block + i, devices, stride=stride), :]
                    for e in range(own)
                ]
                near = jnp.concatenate(near, axis=0)
                far = pl.multiple_of(source[1] * stride + start + source[0] * block, 8)
                far = held[g][pl.ds(far, block), :]
                kind = jnp.zeros((block, 128), jnp.int32)
                for b in range(1, blocks):
                    kind += (lane + tile * 128 >= offsets[b]).astype(jnp.int32)
                line = jnp.where(kind >= slab, near, far)
                line = jnp.where(inside, line, next_plane[:, pl.ds(tile * 128, 128)])
                parts.append(line)
        line = jnp.concatenate(parts, axis=1)
        plane = square([line[:, offsets[b] : offsets[b + 1]] for b in range(blocks)], block)
        high, low = split(plane)
        left = jnp.dot(pick[...], high, preferred_element_type=jnp.float32)
        left += jnp.dot(pick[...], low, preferred_element_type=jnp.float32)
        left = jnp.where(at_rim, across[pl.ds(t, 1), :], left)
        out[r, :, pl.ds(0, half)] = left
        return left

    together = 4

    @pl.loop(0, step_rows // together)
    def _(c):
        left = [left_half(c * together + n) for n in range(together)]
        high, low = split(jnp.concatenate(left, axis=0))
        right = jnp.dot(high, flip[...], preferred_element_type=jnp.float32)
        right += jnp.dot(low, flip[...], preferred_element_type=jnp.float32)
        for n in range(together):
            r = c * together + n
            t = pl.program_id(0) * step_rows + r
            edge = jnp.sum(jnp.where(rim_lane == t, rim[...], 0.0), axis=1, keepdims=True)
            part = right[n * cols : (n + 1) * cols]
            out[r, :, pl.ds(half, half)] = jnp.where(first_lane, edge, part)


def result_block(got, next_plane, across, rim, pick_cols, slab, far_row, rim_col, col, offsets):
    block = offsets[1]
    gx = got[0][0].shape[0]
    groups = tile_groups(offsets[-1] // 128)
    devices = gx * len(got[0])
    own = block // devices
    rows, half = across.shape[0], across.shape[1] - 1
    cols = pick_cols.shape[0]
    step_rows = 8
    places = jnp.stack([slab, far_row.astype(jnp.int32), rim_col.astype(jnp.int32), col])
    cell = jnp.arange(half)
    pick = (pick_cols[:, None] == cell[None, :]).astype(jnp.bfloat16)
    flip = (cell[:, None] + cell[None, :] == half).astype(jnp.bfloat16)
    rim = jnp.pad(rim.T, ((0, 0), (0, 128 - rows)))
    whole = lambda array: pl.BlockSpec(array.shape, lambda i: (0,) * array.ndim)
    arrays = (next_plane, across[:, :half], rim, pick, flip)
    pieces = [piece.reshape(-1, 128) for group in got for piece in group]
    return pl.pallas_call(
        lambda *refs: result_kernel(offsets, own, devices, groups, *refs),
        grid=(rows // step_rows,),
        in_specs=[pl.BlockSpec(memory_space=pltpu.SMEM)] + [whole(array) for array in arrays]
        + [pl.BlockSpec(memory_space=pl.ANY)] * len(pieces),
        out_specs=pl.BlockSpec((step_rows, cols, 2 * half), lambda i: (i, 0, 0)),
        out_shape=jax.ShapeDtypeStruct((rows, cols, 2 * half), jnp.float32),
        scratch_shapes=[
            pltpu.VMEM((devices * group[0].shape[1], 128), jnp.float32) for group in got
        ] + [pltpu.SemaphoreType.DMA((len(groups), len(got[0])))],
        compiler_params=pltpu.CompilerParams(vmem_limit_bytes=VMEM_BYTES),
    )(places, *arrays, *pieces)


def tile_groups(tiles):
    return [slice(tile, min(tile + 2, tiles)) for tile in range(0, tiles, 2)]


def swap(peers, bit):
    return [(q, q ^ bit) for q in range(peers)]


def gathered(piece, peers, after):
    if after is not None:
        piece, first_hops = lax.optimization_barrier((piece, after[1:3]))
        after[1:3] = first_hops
    pieces, bit = {0: piece}, peers // 2
    while bit:
        for place in list(pieces):
            pieces[place ^ bit] = lax.ppermute(pieces[place], "gy", swap(peers, bit))
        bit //= 2
    return [pieces[place] for place in range(peers)]


def exchanged(packed):
    gy = len(packed)
    return [packed[0]] + [lax.ppermute(packed[p], "gy", swap(gy, p)) for p in range(1, gy)]


def sent_lines(got, count, after):
    gy = len(got)
    lines = [sum(got[p][:count] for p in range(first, gy, 2)) for first in range(2)]
    lines = jnp.concatenate(lines + [sum(piece[count:] for piece in got)], axis=0)
    lines = jnp.transpose(lines, (2, 1, 0, 3))
    if after is not None:
        lines, _ = lax.optimization_barrier((lines, after))
    return lax.all_to_all(lines, "gx", 0, 0, tiled=True)


def first_axis(lines, table):
    gx, _, count, half = table.shape
    table = table.reshape(gx, 2 * count, half)
    return jnp.einsum("geaw,gai->eiw", lines[:, :, : 2 * count], table, precision=HIGH)


def row_parts(rows):
    if rows < 4 * PART_STEP:
        return [slice(0, rows)]
    return [slice(PART_STEP, rows - PART_STEP), slice(0, PART_STEP), slice(rows - PART_STEP, rows)]


def square(lower, block):
    lines = []
    for b in range(len(lower)):
        parts = [lower[b]]
        for c in range(b + 1, len(lower)):
            part = lower[c][..., b * block : (b + 1) * block]
            parts.append(jnp.swapaxes(part, -1, -2))
        lines.append(jnp.concatenate(parts, axis=-1))
    return jnp.concatenate(lines, axis=-2)


def solution(mesh):
    placed = (P("gx", "gy", None), P())
    return jax.shard_map(
        on_device, mesh=mesh, in_specs=placed, out_specs=P("gx", "gy", None), check_vma=False
    )
```

```python
import math

import jax
import jax.numpy as jnp
import numpy as np
from jax import lax
from jax.experimental import pallas as pl
from jax.experimental.pallas import tpu as pltpu
from jax.sharding import PartitionSpec as P

SWEEPS = 2

AXIS_ORDERS = ((0, 1, 2), (0, 2, 1), (1, 0, 2), (1, 2, 0), (2, 0, 1), (2, 1, 0))

HIGH = lax.Precision.HIGH


def ring(axis):
    peers = lax.axis_size(axis)
    up = [(i, (i + 1) % peers) for i in range(peers)]
    return up, [(j, i) for i, j in up]


FREE = ((8 - SWEEPS, 8 - SWEEPS), (0, 0))


def faces(block):
    rows, cols, _ = block.shape
    up, down = ring("gx")
    right, left = ring("gy")
    top = lax.ppermute(block[rows - SWEEPS :], "gx", up)
    bottom = lax.ppermute(block[:SWEEPS], "gx", down)
    before = lax.ppermute(block[:, cols - SWEEPS :], "gy", right)
    after = lax.ppermute(block[:, :SWEEPS], "gy", left)
    return lax.optimization_barrier((top, bottom, jnp.concatenate([before, after], axis=1)))


def corners(sides):
    up, down = ring("gx")
    above = lax.ppermute(sides[sides.shape[0] - SWEEPS :], "gx", up)
    return above, lax.ppermute(sides[:SWEEPS], "gx", down)


def with_corners(sides, ends):
    return jnp.pad(jnp.concatenate([ends[0], sides, ends[1]], axis=0), ((0, 0),) + FREE)


def mirror(values, axis):
    return jnp.roll(jnp.flip(values, axis), 1, axis)


def symmetric_marks(marks):
    for flip_axis in range(3):
        marks = jnp.maximum(marks, mirror(marks, flip_axis))
    united = marks
    for axis_order in AXIS_ORDERS[1:]:
        united = jnp.maximum(united, jnp.transpose(marks, axis_order))
    return united


def cosine_table(length):
    position = np.arange(length)
    phases = np.mod(position[:, None] * position[None, : length // 2 + 1], length)
    return (np.cos(phases * (2.0 * math.pi / length)) / math.sqrt(length)).astype(np.float32)


MARGIN = 16
CHUNK = 16
STEP_ROWS = 16
PART_STEP = 8
VMEM_BYTES = 56 * 1024 * 1024


def split(values):
    high = values.astype(jnp.bfloat16)
    low = (values - high.astype(jnp.float32)).astype(jnp.bfloat16)
    return high, low


def fill_kernel(
    base, here, above, below, top, bottom, sides, marks, table_high, table_low,
    spectrum, alternate, edge, punched, once, high, low, folded,
):
    step_rows, cols, length = here.shape
    step = pl.program_id(0) + base[0]
    first_row = step * step_rows
    local_row = pl.program_id(0) * step_rows
    period = marks.shape[0]
    lane = lax.broadcasted_iota(jnp.int32, (128, 128), 1)
    signs = jnp.where(lax.broadcasted_iota(jnp.int32, (128, 128), 0) % 2 == 0, 1.0, -1.0)

    @pl.when(pl.program_id(0) == 0)
    def _():
        edge[...] = jnp.zeros_like(edge)

    def holes(row, start, size):
        row = lax.rem(first_row + row, period)
        start = start % period
        if start + size <= period:
            part = marks[row, pl.ds(start, size), :]
        else:
            part = jnp.concatenate(
                [marks[row, pl.ds(start, period - start), :], marks[row, pl.ds(0, start + size - period), :]],
                axis=0,
            )
        return jnp.concatenate([part] * (length // 128), axis=1)

    def punch(row, start, values):
        kept = jnp.where(holes(row, start, values.shape[0]) > 0.0, 0.0, values)
        punched[row, pl.ds(start, values.shape[0]), :] = kept

    def punch_row(row, source, index):
        full = first_row + row
        punch(row, MARGIN - 8, sides[full, pl.ds(0, 8), :])
        punch(row, MARGIN + cols, sides[full, pl.ds(8, 8), :])
        for c in range(0, cols, CHUNK):
            punch(row, MARGIN + c, source[index, pl.ds(c, CHUNK), :])

    def neighbours(ref, row, start):
        middle = ref[row, pl.ds(start, CHUNK), :]
        total = ref[row - 1, pl.ds(start, CHUNK), :] + ref[row + 1, pl.ds(start, CHUNK), :]
        total += ref[row, pl.ds(start - 1, CHUNK), :] + ref[row, pl.ds(start + 1, CHUNK), :]
        return total + pltpu.roll(middle, 1, 1) + pltpu.roll(middle, length - 1, 1)

    last = (sides.shape[0] - 2 * SWEEPS) // step_rows - 1
    for edge_rows, inside, offset, outer in (
        (above, step > 0, 0, top),
        (below, step < last, step_rows + SWEEPS, bottom),
    ):
        @pl.when(inside)
        def _():
            for r in range(SWEEPS):
                punch_row(offset + r, edge_rows, r)

        @pl.when(jnp.logical_not(inside))
        def _():
            for r in range(SWEEPS):
                punch_row(offset + r, outer, r)

    @pl.loop(0, step_rows)
    def _(r):
        punch_row(r + SWEEPS, here, r)

    @pl.loop(1, step_rows + 2 * SWEEPS - 1, unroll=2)
    def _(r):
        for start in range(MARGIN - 8, MARGIN + cols + 8, CHUNK):
            total = neighbours(punched, r, start) * holes(r, start, CHUNK)
            once[r, pl.ds(start, CHUNK), :] = punched[r, pl.ds(start, CHUNK), :] + total

    @pl.loop(0, step_rows)
    def _(r):
        for c in range(0, cols, CHUNK):
            start = MARGIN + c
            total = neighbours(once, r + SWEEPS, start) * holes(r + SWEEPS, start, CHUNK)
            filled = punched[r + SWEEPS, pl.ds(start, CHUNK), :] + total
            first, second = split(filled)
            spot = pl.ds(pl.multiple_of(r * cols + c, CHUNK), CHUNK)
            high[spot, :] = first
            low[spot, :] = second
            wrapped = filled[:, :128]
            for tile in range(1, length // 128):
                wrapped += filled[:, tile * 128 : (tile + 1) * 128]
            folded[pl.ds(c, CHUNK), :] = wrapped
        column = jnp.where(lane == local_row + r, signs, 0.0).astype(jnp.bfloat16)
        first, second = split(folded[...])
        total = jnp.dot(first, column, preferred_element_type=jnp.float32)
        total += jnp.dot(second, column, preferred_element_type=jnp.float32)
        edge[...] += total

    rows_each = 8
    half = spectrum.shape[2]
    order = lax.broadcasted_iota(jnp.int32, (rows_each, cols, half), 1)

    @pl.loop(0, step_rows // rows_each)
    def _(r):
        spot = pl.ds(pl.multiple_of(r * rows_each * cols, CHUNK), rows_each * cols)
        first, second = high[spot, :], low[spot, :]
        total = jnp.dot(first, table_low[...], preferred_element_type=jnp.float32)
        total += jnp.dot(second, table_high[...], preferred_element_type=jnp.float32)
        total += jnp.dot(first, table_high[...], preferred_element_type=jnp.float32)
        total = total.reshape(rows_each, cols, half)
        spectrum[pl.ds(r * rows_each, rows_each)] = total
        signed = jnp.sum(jnp.where(order % 2 == 0, total, -total), axis=1)
        alternate[pl.ds(pl.multiple_of(r * rows_each, rows_each), rows_each), :] = signed


def rounded_parts(table):
    rounded = lax.reduce_precision(table, 8, 7)
    return rounded.astype(jnp.bfloat16), (table - rounded).astype(jnp.bfloat16)


def marks_kernel(shifts, template, out, held):
    period = template.shape[0]
    repeats = held.shape[1] // period
    line = lax.broadcasted_iota(jnp.int32, (period, period), 0)
    across = lax.broadcasted_iota(jnp.int32, (period, period), 1)
    flip = jnp.where((line + across) % period == 0, 1.0, 0.0)
    for i in range(period):
        plane = jnp.maximum(template[i], template[-i % period]).astype(jnp.float32)
        plane = jnp.maximum(plane, jnp.dot(flip, plane, preferred_element_type=jnp.float32))
        plane = jnp.maximum(plane, jnp.dot(plane, flip, preferred_element_type=jnp.float32))
        plane = jnp.maximum(plane, plane.T)
        held[i * period : (i + 1) * period, :] = jnp.concatenate([plane] * repeats, axis=1)
    for i in range(period):
        plane = held[i * period : (i + 1) * period, :]
        turned = held[pl.ds(i, period, stride=period), :]
        back = turned[:, :period].T
        plane = jnp.maximum(jnp.maximum(plane, turned), jnp.concatenate([back] * repeats, axis=1))
        plane = jnp.where(plane == 1.0, 1.0 / 6.0, 0.0)
        shift = shifts[1]
        out[(i - shifts[0]) % period] = jnp.concatenate([plane[shift:], plane[:shift]], axis=0)


def hole_marks(template, row, col, rows, cols):
    period = template.shape[0]
    shape = (period, period, 128)
    if rows % period == 0 and cols % period == 0:
        shifts = (-SWEEPS % period, -MARGIN % period)
        return pl.pallas_call(
            lambda *refs: marks_kernel(shifts, *refs),
            in_specs=[pl.BlockSpec(memory_space=pltpu.VMEM)],
            out_specs=pl.BlockSpec(memory_space=pltpu.VMEM),
            out_shape=jax.ShapeDtypeStruct(shape, jnp.float32),
            scratch_shapes=[pltpu.VMEM((period * period, 128), jnp.float32)],
        )(template)
    shifts = (jnp.mod(row * rows - SWEEPS, period), jnp.mod(col * cols - MARGIN, period))
    marks = jnp.roll(symmetric_marks(template), (-shifts[0], -shifts[1]), (0, 1))
    return jnp.tile(marks.astype(jnp.float32) / 6.0, (1, 1, 128 // period))


def fill_constants(intensity, template, row, col, main):
    rows, cols, _ = intensity.shape
    high = main.astype(jnp.bfloat16)
    low = (main - high.astype(np.float32)).astype(jnp.bfloat16)
    return hole_marks(template, row, col, rows, cols), jnp.asarray(high), jnp.asarray(low)


def filled_spectrum(intensity, arrays, first, part):
    rows, cols, length = intensity.shape
    half, count = length // 2, part.stop - part.start
    step_rows = STEP_ROWS if part.start % STEP_ROWS == 0 and count % STEP_ROWS == 0 else PART_STEP
    pairs = step_rows // SWEEPS
    last = rows // SWEEPS - 1
    whole = lambda array: pl.BlockSpec(array.shape, lambda i, b: (0,) * array.ndim)
    before = lambda i, b: (jnp.maximum((i + b[0]) * pairs - 1, 0), 0, 0)
    after = lambda i, b: (jnp.minimum((i + b[0] + 1) * pairs, last), 0, 0)
    padded = (step_rows + 2 * SWEEPS, cols + 2 * MARGIN, length)
    return pl.pallas_call(
        fill_kernel,
        grid_spec=pltpu.PrefetchScalarGridSpec(
            num_scalar_prefetch=1,
            grid=(count // step_rows,),
            in_specs=[
                pl.BlockSpec((step_rows, cols, length), lambda i, b: (i + b[0], 0, 0)),
                pl.BlockSpec((SWEEPS, cols, length), before),
                pl.BlockSpec((SWEEPS, cols, length), after),
            ] + [whole(array) for array in arrays],
            out_specs=[
                pl.BlockSpec((step_rows, cols, half), lambda i, b: (i, 0, 0)),
                pl.BlockSpec((step_rows, half), lambda i, b: (i, 0)),
                pl.BlockSpec((cols, 128), lambda i, b: (0, 0)),
            ],
            scratch_shapes=[
                pltpu.VMEM(padded, jnp.float32),
                pltpu.VMEM(padded, jnp.float32),
                pltpu.VMEM((step_rows * cols, length), jnp.bfloat16),
                pltpu.VMEM((step_rows * cols, length), jnp.bfloat16),
                pltpu.VMEM((cols, 128), jnp.float32),
            ],
        ),
        out_shape=[
            jax.ShapeDtypeStruct((count, cols, half), jnp.float32),
            jax.ShapeDtypeStruct((count, half), jnp.float32),
            jax.ShapeDtypeStruct((cols, 128), jnp.float32),
        ],
        compiler_params=pltpu.CompilerParams(vmem_limit_bytes=VMEM_BYTES),
        cost_estimate=pl.CostEstimate(
            flops=count * cols * length * half * 6,
            bytes_accessed=count * cols * (length + half) * 4,
            transcendentals=0,
        ),
    )((first // step_rows).reshape(1), intensity, intensity, intensity, *arrays)


def pack(section, offsets):
    block = offsets[1]
    units = [section[b * block : (b + 1) * block, : (b + 1) * block] for b in range(len(offsets) - 1)]
    return jnp.concatenate(units, axis=1)


def three_dots(left, right):
    total = jnp.dot(left[1], right[0], preferred_element_type=jnp.float32)
    total += jnp.dot(left[0], right[1], preferred_element_type=jnp.float32)
    return total + jnp.dot(left[0], right[0], preferred_element_type=jnp.float32)


def section_kernel(
    offsets, closing, me, weights, kept, got, cols_high, cols_low, rows_high, rows_low,
    rim, corner, before, *refs
):
    step, steps = pl.program_id(0), pl.num_programs(0)
    step_rows = kept.shape[0]
    half, count = rows_high.shape
    planes, block, width = before.shape
    *outs, total, lines, packed = refs
    gy, (_, own, gx, _) = len(outs), outs[0].shape

    def place(layer, values, slot=0):
        packed[slot] = values
        for e in range(own):
            for p in range(gy):
                start = pl.multiple_of((e * gy + (p ^ me[0])) * gx, gx)
                outs[p][layer, e] = packed[slot, pl.ds(start, gx), :]

    @pl.when(step == 0)
    def _():
        total[...] = before[...]

    for r in range(step_rows):
        layer = step * step_rows + r
        values = jnp.concatenate([kept[r], got[r]], axis=0)
        section = three_dots((cols_high[...], cols_low[...]), split(values))
        section = section + section.T
        line = pack(section, offsets)
        place(layer, line, r)
        for m in range(planes):
            total[m] += weights[m, layer] * line
        for m in range(planes - 1):
            row = (m + 1) * (half // planes)
            lines[m, pl.ds(layer, 1), :] = section[row : row + 1]

    @pl.when(step == steps - 1)
    def _():
        for m in range(planes - 1):
            plane = three_dots((rows_high[...], rows_low[...]), split(lines[m]))
            total[m] += pack(plane + plane.T, offsets)
        if closing:
            total[planes - 1] += pack(rim[...] + rim[...].T, offsets)
            for m in range(planes):
                place(count + m, total[m])
            place(count + planes, jnp.zeros((block, width), jnp.float32) + corner[...])


def packed_section(col, kept, got, table_pair, table_rows, marks, rim, corner, before, offsets, shape, closing):
    count, cols, half = kept.shape
    planes, block, width = before.shape
    gx, gy = shape
    step_rows = 4
    layers = count + (planes + 1 if closing else 0)
    whole = lambda array: pl.BlockSpec(array.shape, lambda i: (0,) * array.ndim)
    weights = jnp.stack([table_rows[:, m] for m in marks])
    arrays = rounded_parts(table_pair.T) + rounded_parts(table_rows[:, :half].T)
    arrays += (rim, corner[None], before)
    out = jax.ShapeDtypeStruct((layers, block // (gx * gy), gx, width), jnp.float32)
    outs = [out] * gy + [jax.ShapeDtypeStruct(before.shape, jnp.float32)]
    rows_spec = pl.BlockSpec((step_rows, cols, half), lambda i: (i, 0, 0))
    return pl.pallas_call(
        lambda *refs: section_kernel(offsets, closing, *refs),
        grid=(count // step_rows,),
        in_specs=[pl.BlockSpec(memory_space=pltpu.SMEM)] * 2 + [rows_spec, rows_spec]
        + [whole(array) for array in arrays],
        out_specs=[whole(out) for out in outs],
        out_shape=outs,
        scratch_shapes=[
            pltpu.VMEM((planes, count, half), jnp.float32),
            pltpu.VMEM((step_rows, block, width), jnp.float32),
        ],
        compiler_params=pltpu.CompilerParams(vmem_limit_bytes=VMEM_BYTES),
        cost_estimate=pl.CostEstimate(
            flops=count * 12 * cols * half * half,
            bytes_accessed=count * cols * half * 16,
            transcendentals=0,
        ),
    )(col.reshape(1), weights, kept, got, *arrays)


def on_device(intensity, template):
    rows, cols, length = intensity.shape
    gx, gy = lax.axis_size("gx"), lax.axis_size("gy")
    row, col = lax.axis_index("gx"), lax.axis_index("gy")
    devices, half = gx * gy, length // 2
    block = max(devices, rows)
    blocks, own, slabs = half // block, block // devices, gx // 2
    offsets = [block * b * (b + 1) // 2 for b in range(blocks + 1)]
    width = offsets[blocks]
    table = jnp.asarray(cosine_table(length))
    main = table[:, :half]

    pair_rows = rows // 2
    parts = row_parts(pair_rows)
    counts = [part.stop - part.start for part in parts]
    core = lax.rem(col, 2)
    constants = fill_constants(intensity, template, row, col, cosine_table(length)[:, :half])
    top, bottom, sides = faces(intensity)
    given_first, kept_first = (1 - core) * pair_rows, core * pair_rows
    given, kept = [], []
    blank = intensity[:SWEEPS]
    inner_faces = blank, blank, jnp.pad(sides, ((SWEEPS, SWEEPS),) + FREE)
    outer_faces = []

    def fill_part(c, packed):
        part = parts[c]
        starts = given_first + part.start, kept_first + part.start
        if packed is not None:
            starts, packed = lax.optimization_barrier((starts, packed))
        lines = None if packed is None else exchanged(packed)
        inner = part.start >= SWEEPS and part.stop <= pair_rows - SWEEPS
        if not inner and not outer_faces:
            outer_faces.extend((top, bottom, with_corners(sides, corners(sides))))
        use = (inner_faces if inner else tuple(outer_faces)) + constants
        piece = filled_spectrum(intensity, use, starts[0], part)
        if inner and not outer_faces:
            piece, after = lax.optimization_barrier((piece, sides))
            ends = corners(after)
        given.append(piece)
        got = lax.ppermute(given[c][0], "gy", swap(gy, 1))
        if c == 1:
            starts, lines = lax.optimization_barrier((starts, lines))
        kept.append(filled_spectrum(intensity, use, starts[1], part))
        if inner and not outer_faces:
            kept[c], ends = lax.optimization_barrier((kept[c], ends))
            outer_faces.extend((top, bottom, with_corners(sides, ends)))
        return got, lines

    table_cols = lax.dynamic_slice_in_dim(table, col * cols, cols, 0)
    kept_rows = lax.dynamic_slice_in_dim(table, row * rows + kept_first, pair_rows, 0)
    marks = [rows * (m + 1) for m in range(slabs)]
    mates = lax.dynamic_slice_in_dim(main, (col + 1 - 2 * core) * cols, cols, 0)
    table_pair = jnp.concatenate([table_cols[:, :half], mates], axis=0)
    table_parts = main.reshape(gx, 2, pair_rows, half) / 6.0
    table_parts = jnp.where(core == 0, table_parts, table_parts[:, ::-1])
    table_parts = [table_parts[:, :, part] for part in parts]
    side = jnp.zeros((slabs, block, width), jnp.float32)
    rim, corner = jnp.zeros((half, half), jnp.float32), jnp.zeros((width,), jnp.float32)
    values, packed, lines = 0.0, None, None
    for c, count in enumerate(counts):
        closing = c == len(counts) - 1
        got, got_lines = fill_part(c, packed)
        held = kept[c][0]
        if c > 0:
            held, got_lines = lax.optimization_barrier((held, got_lines))
            lines = sent_lines(got_lines, counts[c - 1], lines)
            values = values + first_axis(lines, table_parts[c - 1])
        if closing:
            given_rows = lax.dynamic_slice_in_dim(table, row * rows + given_first, pair_rows, 0)
            ordered_rows = [held_rows[part] for held_rows in (given_rows, kept_rows) for part in parts]
            ordered_rows = jnp.concatenate(ordered_rows, axis=0)
            alternate = jnp.concatenate([piece[1] for piece in given + kept], axis=0) / math.sqrt(length)
            edge = [piece[2][:, : piece[1].shape[0]] for piece in given + kept]
            edge = jnp.concatenate(edge, axis=1)
            edge = jnp.einsum("ba,bk->ak", edge / math.sqrt(length), table_cols, precision=HIGH)
            edge = edge + jnp.concatenate([alternate, edge[:, half:]], axis=1)
            rim = jnp.einsum("aj,ak->jk", ordered_rows[:, :half], edge[:, :half], precision=HIGH)
            corner = 2.0 * jnp.einsum("a,ak->k", ordered_rows[:, half], edge, precision=HIGH)
            corner = corner + jnp.einsum("aj,a->j", ordered_rows, edge[:, half], precision=HIGH)
            corner = jnp.pad(corner, (0, width - half - 1))

        *packed, side = packed_section(
            col, held, got, table_pair, kept_rows[parts[c]], marks,
            rim, corner, side, offsets, (gx, gy), closing,
        )
    lines = sent_lines(exchanged(packed), counts[-1], lines)
    values = values + first_axis(lines, table_parts[-1])
    side = jnp.sum(lines[:, :, 2 * counts[-1] :], axis=0) / 6.0
    turned = values.reshape(own, blocks, own, devices, width)
    turned = jnp.transpose(turned, (3, 1, 2, 0, 4))
    turned = [turned[:, b, :, :, : offsets[b + 1]] for b in range(blocks)]
    turned = lax.all_to_all(jnp.concatenate(turned, axis=3), ("gy", "gx"), 0, 0, tiled=True)
    turned = jnp.transpose(turned, (1, 2, 0, 3)).reshape(own, block, -1)

    slab = jnp.minimum(row, gx - 1 - row)
    far_row, far_col = row >= slabs, col >= gy // 2
    pick_rows = jnp.arange(rows)
    pick_rows = slab * rows + jnp.where(far_row, rows - pick_rows, pick_rows)
    pick_cols = jnp.arange(cols)
    pick_cols = jnp.where(far_col, (gy - col) * cols - pick_cols, col * cols + pick_cols)

    if rows == block:
        got, piece = [], None
        for messages in slab_messages(values, turned, side, offsets, slabs):
            if piece is not None:
                messages, piece = lax.optimization_barrier((messages, piece))
                got.append(gathered(piece, gy, got[-1] if got else None))
            piece = lax.all_to_all(messages, "gx", 0, 0, tiled=True)
        got.append(gathered(piece, gy, got[-1] if got else None))
        tiles = width // 128
        start = tile_groups(tiles)[0].stop * own * block
        side = jnp.stack([piece[:, start : start + 3 * own * tiles] for piece in got[0]])
        bit = gy // 2
        while bit:
            paired = side.reshape((-1, 2, bit) + side.shape[1:])
            side = jnp.where((col & bit) == 0, paired, paired[:, ::-1]).reshape(side.shape)
            bit //= 2
        side = side.reshape(devices, own, 3, width)
        side = jnp.transpose(side, (2, 1, 0, 3)).reshape(3, block, width)
        next_plane, across = side[0], rim_rows(side[1:], offsets, pick_rows)
        rim_col = col == gy // 2
        rim = across[:, pick_cols]
        return result_block(
            got, next_plane, across, rim, pick_cols, slab, far_row, rim_col, col, offsets
        )

    side = lax.all_gather(side, ("gy", "gx"), axis=0)
    side = jnp.transpose(side, (2, 1, 0, 3)).reshape(slabs + 1, block, width)
    across = rim_rows(side[slabs - 1 :], offsets, pick_rows)
    next_plane = lax.dynamic_index_in_dim(side, slab, 0, keepdims=False)
    sums = axis_order_sums(values, turned, offsets, block)
    messages = []
    for s in range(slabs):
        base, first = s * rows // block, s * rows
        units = []
        for b in range(blocks):
            size = (b + 1) * block
            near = jnp.zeros((own, rows, size))
            far = jnp.zeros((own, block, size))
            if b >= base:
                near = jnp.stack([sums[b][e][first : first + rows, :size] for e in range(own)])
            else:
                far = jnp.stack([sums[base][e][b * block : size, :size] for e in range(own)])
            units.append(jnp.concatenate([near, far], axis=1))
        messages.append(jnp.concatenate(units, axis=2))
    messages = jnp.stack(messages + messages[::-1])
    got = lax.all_to_all(messages, "gx", 0, 0, tiled=True)
    got = lax.all_gather(got, "gy", axis=0, tiled=True)
    got = jnp.swapaxes(got, 0, 1).reshape(block, rows + block, width)
    base = slab * rows // block
    lower = []
    for b in range(blocks):
        lanes = slice(offsets[b], offsets[b + 1])
        near = jnp.swapaxes(got[:, :rows, lanes], 0, 1)
        far = lax.dynamic_slice_in_dim(got[:, rows:, lanes], lax.rem(slab * rows, block), rows, 0)
        lower.append(jnp.where(b >= base, near, far))
    lower = jnp.concatenate(lower, axis=2)
    lower = jnp.concatenate([lower, next_plane[None]], axis=0)
    body = square([lower[:, :, offsets[b] : offsets[b + 1]] for b in range(blocks)], block)
    body = body[pick_rows - slab * rows]
    body = jnp.concatenate([body, across[:, None, :half]], axis=1)[:, pick_cols]
    body = jnp.concatenate([body, across[:, pick_cols][:, :, None]], axis=2)
    return jnp.concatenate([body, jnp.flip(body[:, :, 1:half], 2)], axis=2)


def rim_rows(side, offsets, pick_rows):
    blocks, block = len(offsets) - 1, offsets[1]
    half = blocks * block
    last = square([side[0][:, offsets[b] : offsets[b + 1]] for b in range(blocks)], block)
    rim = side[1, 0, : half + 1]
    last = jnp.concatenate([last, rim[None, :half]], axis=0)
    return jnp.concatenate([last, rim[:, None]], axis=1)[pick_rows]


def axis_order_sums(values, turned, offsets, block):
    start = 0
    sums = []
    for top in range(len(offsets) - 1):
        size = (top + 1) * block
        parts = []
        for e in range(values.shape[0]):
            part = values[e, :size, offsets[top] : offsets[top] + size]
            lower = [turned[e, :, start + offsets[b] : start + offsets[b + 1]] for b in range(top + 1)]
            parts.append(part + part.T + square(lower, block))
        sums.append(parts)
        start += offsets[top + 1]
    return sums


def message_kernel(offsets, slabs, values, turned, side, *messages):
    blocks, block = len(offsets) - 1, offsets[1]
    values, turned = values[...], turned[...]
    own = values.shape[0]
    sums = axis_order_sums(values, turned, offsets, block)
    groups = tile_groups(offsets[-1] // 128)
    side_start = groups[0].stop * own * block
    messages[0][:, side_start:] = jnp.zeros_like(messages[0][:, side_start:])
    for s in range(slabs):
        places = s, 2 * slabs - 1 - s
        for e in range(own):
            units = []
            for b in range(blocks):
                size = (b + 1) * block
                if b >= s:
                    units.append(sums[b][e][s * block : (s + 1) * block, :size])
                else:
                    units.append(sums[s][e][b * block : size, :size])
            line = jnp.concatenate(units, axis=1)
            for group, out in zip(groups, messages):
                for tile in range(group.start, group.stop):
                    start = ((tile - group.start) * own + e) * block
                    for place in places:
                        out[place, start : start + block] = line[:, tile * 128 : (tile + 1) * 128]
            row = side_start + 3 * e * groups[-1].stop
            for plane in (s, slabs - 1, slabs):
                for tile in range(groups[-1].stop):
                    part = side[e, plane : plane + 1, tile * 128 : (tile + 1) * 128]
                    for place in places:
                        messages[0][place, row : row + 1] = part
                    row += 1


def slab_messages(values, turned, side, offsets, slabs):
    own, block, tiles = values.shape[0], offsets[1], offsets[-1] // 128
    sizes = [(group.stop - group.start) * own * block for group in tile_groups(tiles)]
    sizes[0] += -(-3 * own * tiles // 8) * 8
    return pl.pallas_call(
        lambda *refs: message_kernel(offsets, slabs, *refs),
        in_specs=[pl.BlockSpec(memory_space=pltpu.VMEM)] * 3,
        out_specs=[pl.BlockSpec(memory_space=pltpu.VMEM)] * len(sizes),
        out_shape=[jax.ShapeDtypeStruct((2 * slabs, size, 128), jnp.float32) for size in sizes],
        compiler_params=pltpu.CompilerParams(vmem_limit_bytes=VMEM_BYTES),
    )(values, turned, side)


def result_kernel(
    offsets, own, devices, groups, places, next_plane, across, rim, pick, flip, *refs
):
    blocks, block = len(offsets) - 1, offsets[1]
    tiles = offsets[-1] // 128
    peers = (len(refs) - 2) // len(groups) - 1
    pieces, out = refs[: peers * len(groups)], refs[peers * len(groups)]
    held, sems = refs[peers * len(groups) + 1 : -1], refs[-1]
    step_rows, cols, length = out.shape
    half = length // 2
    slab, far_row, rim_col, me = places[0], places[1], places[2], places[3]
    lane = lax.broadcasted_iota(jnp.int32, (block, 128), 1)
    at_rim = lax.broadcasted_iota(jnp.int32, (cols, half), 0) + (1 - rim_col) == 0
    rim_lane = lax.broadcasted_iota(jnp.int32, rim.shape, 1)
    first_lane = lax.broadcasted_iota(jnp.int32, (cols, half), 1) == 0

    @pl.when(pl.program_id(0) == 0)
    def _():
        copies = []
        for g in range(len(groups)):
            for peer in range(peers):
                piece = pieces[g * peers + peer]
                size = piece.shape[0]
                spot = pl.ds(pl.multiple_of((me ^ peer) * size, size), size)
                copies.append(pltpu.make_async_copy(piece, held[g].at[spot], sems.at[g, peer]))
        for copy in copies:
            copy.start()
        for copy in copies:
            copy.wait()

    def left_half(r):
        t = pl.program_id(0) * step_rows + r
        i = jnp.where(far_row == 1, block - t, t)
        inside = (jnp.zeros((block, 128), jnp.int32) + i) < block
        i = jnp.minimum(i, block - 1)
        source = lax.div(i, devices), lax.rem(i, devices)
        parts = []
        for g, group in enumerate(groups):
            stride = held[g].shape[0] // devices
            for tile in range(group.start, group.stop):
                start = (tile - group.start) * own * block
                near = [
                    held[g][pl.ds(start + e * block + i, devices, stride=stride), :]
                    for e in range(own)
                ]
                near = jnp.concatenate(near, axis=0)
                far = pl.multiple_of(source[1] * stride + start + source[0] * block, 8)
                far = held[g][pl.ds(far, block), :]
                kind = jnp.zeros((block, 128), jnp.int32)
                for b in range(1, blocks):
                    kind += (lane + tile * 128 >= offsets[b]).astype(jnp.int32)
                line = jnp.where(kind >= slab, near, far)
                line = jnp.where(inside, line, next_plane[:, pl.ds(tile * 128, 128)])
                parts.append(line)
        line = jnp.concatenate(parts, axis=1)
        plane = square([line[:, offsets[b] : offsets[b + 1]] for b in range(blocks)], block)
        high, low = split(plane)
        left = jnp.dot(pick[...], high, preferred_element_type=jnp.float32)
        left += jnp.dot(pick[...], low, preferred_element_type=jnp.float32)
        left = jnp.where(at_rim, across[pl.ds(t, 1), :], left)
        out[r, :, pl.ds(0, half)] = left
        return left

    together = 4

    @pl.loop(0, step_rows // together)
    def _(c):
        left = [left_half(c * together + n) for n in range(together)]
        high, low = split(jnp.concatenate(left, axis=0))
        right = jnp.dot(high, flip[...], preferred_element_type=jnp.float32)
        right += jnp.dot(low, flip[...], preferred_element_type=jnp.float32)
        for n in range(together):
            r = c * together + n
            t = pl.program_id(0) * step_rows + r
            edge = jnp.sum(jnp.where(rim_lane == t, rim[...], 0.0), axis=1, keepdims=True)
            part = right[n * cols : (n + 1) * cols]
            out[r, :, pl.ds(half, half)] = jnp.where(first_lane, edge, part)


def result_block(got, next_plane, across, rim, pick_cols, slab, far_row, rim_col, col, offsets):
    block = offsets[1]
    gx = got[0][0].shape[0]
    groups = tile_groups(offsets[-1] // 128)
    devices = gx * len(got[0])
    own = block // devices
    rows, half = across.shape[0], across.shape[1] - 1
    cols = pick_cols.shape[0]
    step_rows = 8
    places = jnp.stack([slab, far_row.astype(jnp.int32), rim_col.astype(jnp.int32), col])
    cell = jnp.arange(half)
    pick = (pick_cols[:, None] == cell[None, :]).astype(jnp.bfloat16)
    flip = (cell[:, None] + cell[None, :] == half).astype(jnp.bfloat16)
    rim = jnp.pad(rim.T, ((0, 0), (0, 128 - rows)))
    whole = lambda array: pl.BlockSpec(array.shape, lambda i: (0,) * array.ndim)
    arrays = (next_plane, across[:, :half], rim, pick, flip)
    pieces = [piece.reshape(-1, 128) for group in got for piece in group]
    return pl.pallas_call(
        lambda *refs: result_kernel(offsets, own, devices, groups, *refs),
        grid=(rows // step_rows,),
        in_specs=[pl.BlockSpec(memory_space=pltpu.SMEM)] + [whole(array) for array in arrays]
        + [pl.BlockSpec(memory_space=pl.ANY)] * len(pieces),
        out_specs=pl.BlockSpec((step_rows, cols, 2 * half), lambda i: (i, 0, 0)),
        out_shape=jax.ShapeDtypeStruct((rows, cols, 2 * half), jnp.float32),
        scratch_shapes=[
            pltpu.VMEM((devices * group[0].shape[1], 128), jnp.float32) for group in got
        ] + [pltpu.SemaphoreType.DMA((len(groups), len(got[0])))],
        compiler_params=pltpu.CompilerParams(vmem_limit_bytes=VMEM_BYTES),
    )(places, *arrays, *pieces)


def tile_groups(tiles):
    return [slice(tile, min(tile + 2, tiles)) for tile in range(0, tiles, 2)]


def swap(peers, bit):
    return [(q, q ^ bit) for q in range(peers)]


def gathered(piece, peers, after):
    if after is not None:
        piece, first_hops = lax.optimization_barrier((piece, after[1:3]))
        after[1:3] = first_hops
    pieces, bit = {0: piece}, peers // 2
    while bit:
        for place in list(pieces):
            pieces[place ^ bit] = lax.ppermute(pieces[place], "gy", swap(peers, bit))
        bit //= 2
    return [pieces[place] for place in range(peers)]


def exchanged(packed):
    gy = len(packed)
    return [packed[0]] + [lax.ppermute(packed[p], "gy", swap(gy, p)) for p in range(1, gy)]


def sent_lines(got, count, after):
    gy = len(got)
    lines = [sum(got[p][:count] for p in range(first, gy, 2)) for first in range(2)]
    lines = jnp.concatenate(lines + [sum(piece[count:] for piece in got)], axis=0)
    lines = jnp.transpose(lines, (2, 1, 0, 3))
    if after is not None:
        lines, _ = lax.optimization_barrier((lines, after))
    return lax.all_to_all(lines, "gx", 0, 0, tiled=True)


def first_axis(lines, table):
    gx, _, count, half = table.shape
    table = table.reshape(gx, 2 * count, half)
    return jnp.einsum("geaw,gai->eiw", lines[:, :, : 2 * count], table, precision=HIGH)


def row_parts(rows):
    if rows < 4 * PART_STEP:
        return [slice(0, rows)]
    return [slice(PART_STEP, rows - PART_STEP), slice(0, PART_STEP), slice(rows - PART_STEP, rows)]


def square(lower, block):
    lines = []
    for b in range(len(lower)):
        parts = [lower[b]]
        for c in range(b + 1, len(lower)):
            part = lower[c][..., b * block : (b + 1) * block]
            parts.append(jnp.swapaxes(part, -1, -2))
        lines.append(jnp.concatenate(parts, axis=-1))
    return jnp.concatenate(lines, axis=-2)


def solution(mesh):
    placed = (P("gx", "gy", None), P())
    return jax.shard_map(
        on_device, mesh=mesh, in_specs=placed, out_specs=P("gx", "gy", None), check_vma=False
    )
```

```python
import math

import jax
import jax.numpy as jnp
import numpy as np
from jax import lax
from jax.experimental import pallas as pl
from jax.experimental.pallas import tpu as pltpu
from jax.sharding import PartitionSpec as P

SWEEPS = 2

AXIS_ORDERS = ((0, 1, 2), (0, 2, 1), (1, 0, 2), (1, 2, 0), (2, 0, 1), (2, 1, 0))

HIGH = lax.Precision.HIGH


def ring(axis):
    peers = lax.axis_size(axis)
    up = [(i, (i + 1) % peers) for i in range(peers)]
    return up, [(j, i) for i, j in up]


FREE = ((8 - SWEEPS, 8 - SWEEPS), (0, 0))


def faces(block):
    rows, cols, _ = block.shape
    up, down = ring("gx")
    right, left = ring("gy")
    top = lax.ppermute(block[rows - SWEEPS :], "gx", up)
    bottom = lax.ppermute(block[:SWEEPS], "gx", down)
    before = lax.ppermute(block[:, cols - SWEEPS :], "gy", right)
    after = lax.ppermute(block[:, :SWEEPS], "gy", left)
    return top, bottom, jnp.concatenate([before, after], axis=1)


def corners(sides):
    up, down = ring("gx")
    above = lax.ppermute(sides[sides.shape[0] - SWEEPS :], "gx", up)
    return above, lax.ppermute(sides[:SWEEPS], "gx", down)


def with_corners(sides, ends):
    return jnp.pad(jnp.concatenate([ends[0], sides, ends[1]], axis=0), ((0, 0),) + FREE)


def mirror(values, axis):
    return jnp.roll(jnp.flip(values, axis), 1, axis)


def symmetric_marks(marks):
    for flip_axis in range(3):
        marks = jnp.maximum(marks, mirror(marks, flip_axis))
    united = marks
    for axis_order in AXIS_ORDERS[1:]:
        united = jnp.maximum(united, jnp.transpose(marks, axis_order))
    return united


def cosine_table(length):
    position = np.arange(length)
    phases = np.mod(position[:, None] * position[None, : length // 2 + 1], length)
    return (np.cos(phases * (2.0 * math.pi / length)) / math.sqrt(length)).astype(np.float32)


MARGIN = 16
CHUNK = 16
STEP_ROWS = 16
PART_STEP = 8
VMEM_BYTES = 56 * 1024 * 1024


def split(values):
    high = values.astype(jnp.bfloat16)
    low = (values - high.astype(jnp.float32)).astype(jnp.bfloat16)
    return high, low


def fill_kernel(
    base, here, above, below, top, bottom, sides, marks, table_high, table_low,
    spectrum, alternate, edge, punched, once, high, low, folded,
):
    step_rows, cols, length = here.shape
    step = pl.program_id(0) + base[0]
    first_row = step * step_rows
    local_row = pl.program_id(0) * step_rows
    period = marks.shape[0]
    lane = lax.broadcasted_iota(jnp.int32, (128, 128), 1)
    signs = jnp.where(lax.broadcasted_iota(jnp.int32, (128, 128), 0) % 2 == 0, 1.0, -1.0)

    @pl.when(pl.program_id(0) == 0)
    def _():
        edge[...] = jnp.zeros_like(edge)

    def holes(row, start, size):
        row = lax.rem(first_row + row, period)
        start = start % period
        if start + size <= period:
            part = marks[row, pl.ds(start, size), :]
        else:
            part = jnp.concatenate(
                [marks[row, pl.ds(start, period - start), :], marks[row, pl.ds(0, start + size - period), :]],
                axis=0,
            )
        return jnp.concatenate([part] * (length // 128), axis=1)

    def punch(row, start, values):
        kept = jnp.where(holes(row, start, values.shape[0]) > 0.0, 0.0, values)
        punched[row, pl.ds(start, values.shape[0]), :] = kept

    def punch_row(row, source, index):
        full = first_row + row
        punch(row, MARGIN - 8, sides[full, pl.ds(0, 8), :])
        punch(row, MARGIN + cols, sides[full, pl.ds(8, 8), :])
        for c in range(0, cols, CHUNK):
            punch(row, MARGIN + c, source[index, pl.ds(c, CHUNK), :])

    def neighbours(ref, row, start):
        middle = ref[row, pl.ds(start, CHUNK), :]
        total = ref[row - 1, pl.ds(start, CHUNK), :] + ref[row + 1, pl.ds(start, CHUNK), :]
        total += ref[row, pl.ds(start - 1, CHUNK), :] + ref[row, pl.ds(start + 1, CHUNK), :]
        return total + pltpu.roll(middle, 1, 1) + pltpu.roll(middle, length - 1, 1)

    last = (sides.shape[0] - 2 * SWEEPS) // step_rows - 1
    for edge_rows, inside, offset, outer in (
        (above, step > 0, 0, top),
        (below, step < last, step_rows + SWEEPS, bottom),
    ):
        @pl.when(inside)
        def _():
            for r in range(SWEEPS):
                punch_row(offset + r, edge_rows, r)

        @pl.when(jnp.logical_not(inside))
        def _():
            for r in range(SWEEPS):
                punch_row(offset + r, outer, r)

    @pl.loop(0, step_rows)
    def _(r):
        punch_row(r + SWEEPS, here, r)

    @pl.loop(1, step_rows + 2 * SWEEPS - 1, unroll=2)
    def _(r):
        for start in range(MARGIN - 8, MARGIN + cols + 8, CHUNK):
            total = neighbours(punched, r, start) * holes(r, start, CHUNK)
            once[r, pl.ds(start, CHUNK), :] = punched[r, pl.ds(start, CHUNK), :] + total

    @pl.loop(0, step_rows)
    def _(r):
        for c in range(0, cols, CHUNK):
            start = MARGIN + c
            total = neighbours(once, r + SWEEPS, start) * holes(r + SWEEPS, start, CHUNK)
            filled = punched[r + SWEEPS, pl.ds(start, CHUNK), :] + total
            first, second = split(filled)
            spot = pl.ds(pl.multiple_of(r * cols + c, CHUNK), CHUNK)
            high[spot, :] = first
            low[spot, :] = second
            wrapped = filled[:, :128]
            for tile in range(1, length // 128):
                wrapped += filled[:, tile * 128 : (tile + 1) * 128]
            folded[pl.ds(c, CHUNK), :] = wrapped
        column = jnp.where(lane == local_row + r, signs, 0.0).astype(jnp.bfloat16)
        first, second = split(folded[...])
        total = jnp.dot(first, column, preferred_element_type=jnp.float32)
        total += jnp.dot(second, column, preferred_element_type=jnp.float32)
        edge[...] += total

    rows_each = 8
    half = spectrum.shape[2]
    order = lax.broadcasted_iota(jnp.int32, (rows_each, cols, half), 1)

    @pl.loop(0, step_rows // rows_each)
    def _(r):
        spot = pl.ds(pl.multiple_of(r * rows_each * cols, CHUNK), rows_each * cols)
        first, second = high[spot, :], low[spot, :]
        total = jnp.dot(first, table_low[...], preferred_element_type=jnp.float32)
        total += jnp.dot(second, table_high[...], preferred_element_type=jnp.float32)
        total += jnp.dot(first, table_high[...], preferred_element_type=jnp.float32)
        total = total.reshape(rows_each, cols, half)
        spectrum[pl.ds(r * rows_each, rows_each)] = total
        signed = jnp.sum(jnp.where(order % 2 == 0, total, -total), axis=1)
        alternate[pl.ds(pl.multiple_of(r * rows_each, rows_each), rows_each), :] = signed


def rounded_parts(table):
    rounded = lax.reduce_precision(table, 8, 7)
    return rounded.astype(jnp.bfloat16), (table - rounded).astype(jnp.bfloat16)


def marks_kernel(shifts, template, out, held):
    period = template.shape[0]
    repeats = held.shape[1] // period
    line = lax.broadcasted_iota(jnp.int32, (period, period), 0)
    across = lax.broadcasted_iota(jnp.int32, (period, period), 1)
    flip = jnp.where((line + across) % period == 0, 1.0, 0.0)
    for i in range(period):
        plane = jnp.maximum(template[i], template[-i % period]).astype(jnp.float32)
        plane = jnp.maximum(plane, jnp.dot(flip, plane, preferred_element_type=jnp.float32))
        plane = jnp.maximum(plane, jnp.dot(plane, flip, preferred_element_type=jnp.float32))
        plane = jnp.maximum(plane, plane.T)
        held[i * period : (i + 1) * period, :] = jnp.concatenate([plane] * repeats, axis=1)
    for i in range(period):
        plane = held[i * period : (i + 1) * period, :]
        turned = held[pl.ds(i, period, stride=period), :]
        back = turned[:, :period].T
        plane = jnp.maximum(jnp.maximum(plane, turned), jnp.concatenate([back] * repeats, axis=1))
        plane = jnp.where(plane == 1.0, 1.0 / 6.0, 0.0)
        shift = shifts[1]
        out[(i - shifts[0]) % period] = jnp.concatenate([plane[shift:], plane[:shift]], axis=0)


def hole_marks(template, row, col, rows, cols):
    period = template.shape[0]
    shape = (period, period, 128)
    if rows % period == 0 and cols % period == 0:
        shifts = (-SWEEPS % period, -MARGIN % period)
        return pl.pallas_call(
            lambda *refs: marks_kernel(shifts, *refs),
            in_specs=[pl.BlockSpec(memory_space=pltpu.VMEM)],
            out_specs=pl.BlockSpec(memory_space=pltpu.VMEM),
            out_shape=jax.ShapeDtypeStruct(shape, jnp.float32),
            scratch_shapes=[pltpu.VMEM((period * period, 128), jnp.float32)],
        )(template)
    shifts = (jnp.mod(row * rows - SWEEPS, period), jnp.mod(col * cols - MARGIN, period))
    marks = jnp.roll(symmetric_marks(template), (-shifts[0], -shifts[1]), (0, 1))
    return jnp.tile(marks.astype(jnp.float32) / 6.0, (1, 1, 128 // period))


def fill_constants(intensity, template, row, col, main):
    rows, cols, _ = intensity.shape
    high = main.astype(jnp.bfloat16)
    low = (main - high.astype(np.float32)).astype(jnp.bfloat16)
    return hole_marks(template, row, col, rows, cols), jnp.asarray(high), jnp.asarray(low)


def filled_spectrum(intensity, arrays, first, part):
    rows, cols, length = intensity.shape
    half, count = length // 2, part.stop - part.start
    step_rows = STEP_ROWS if part.start % STEP_ROWS == 0 and count % STEP_ROWS == 0 else PART_STEP
    pairs = step_rows // SWEEPS
    last = rows // SWEEPS - 1
    whole = lambda array: pl.BlockSpec(array.shape, lambda i, b: (0,) * array.ndim)
    before = lambda i, b: (jnp.maximum((i + b[0]) * pairs - 1, 0), 0, 0)
    after = lambda i, b: (jnp.minimum((i + b[0] + 1) * pairs, last), 0, 0)
    padded = (step_rows + 2 * SWEEPS, cols + 2 * MARGIN, length)
    return pl.pallas_call(
        fill_kernel,
        grid_spec=pltpu.PrefetchScalarGridSpec(
            num_scalar_prefetch=1,
            grid=(count // step_rows,),
            in_specs=[
                pl.BlockSpec((step_rows, cols, length), lambda i, b: (i + b[0], 0, 0)),
                pl.BlockSpec((SWEEPS, cols, length), before),
                pl.BlockSpec((SWEEPS, cols, length), after),
            ] + [whole(array) for array in arrays],
            out_specs=[
                pl.BlockSpec((step_rows, cols, half), lambda i, b: (i, 0, 0)),
                pl.BlockSpec((step_rows, half), lambda i, b: (i, 0)),
                pl.BlockSpec((cols, 128), lambda i, b: (0, 0)),
            ],
            scratch_shapes=[
                pltpu.VMEM(padded, jnp.float32),
                pltpu.VMEM(padded, jnp.float32),
                pltpu.VMEM((step_rows * cols, length), jnp.bfloat16),
                pltpu.VMEM((step_rows * cols, length), jnp.bfloat16),
                pltpu.VMEM((cols, 128), jnp.float32),
            ],
        ),
        out_shape=[
            jax.ShapeDtypeStruct((count, cols, half), jnp.float32),
            jax.ShapeDtypeStruct((count, half), jnp.float32),
            jax.ShapeDtypeStruct((cols, 128), jnp.float32),
        ],
        compiler_params=pltpu.CompilerParams(vmem_limit_bytes=VMEM_BYTES),
        cost_estimate=pl.CostEstimate(
            flops=count * cols * length * half * 6,
            bytes_accessed=count * cols * (length + half) * 4,
            transcendentals=0,
        ),
    )((first // step_rows).reshape(1), intensity, intensity, intensity, *arrays)


def pack(section, offsets):
    block = offsets[1]
    units = [section[b * block : (b + 1) * block, : (b + 1) * block] for b in range(len(offsets) - 1)]
    return jnp.concatenate(units, axis=1)


def three_dots(left, right):
    total = jnp.dot(left[1], right[0], preferred_element_type=jnp.float32)
    total += jnp.dot(left[0], right[1], preferred_element_type=jnp.float32)
    return total + jnp.dot(left[0], right[0], preferred_element_type=jnp.float32)


def section_kernel(
    offsets, closing, me, weights, kept, got, cols_high, cols_low, rows_high, rows_low,
    rim, corner, before, *refs
):
    step, steps = pl.program_id(0), pl.num_programs(0)
    step_rows = kept.shape[0]
    half, count = rows_high.shape
    planes, block, width = before.shape
    *outs, total, lines, packed = refs
    gy, (_, own, gx, _) = len(outs), outs[0].shape

    def place(layer, values, slot=0):
        packed[slot] = values
        for e in range(own):
            for p in range(gy):
                start = pl.multiple_of((e * gy + (p ^ me[0])) * gx, gx)
                outs[p][layer, e] = packed[slot, pl.ds(start, gx), :]

    @pl.when(step == 0)
    def _():
        total[...] = before[...]

    for r in range(step_rows):
        layer = step * step_rows + r
        values = jnp.concatenate([kept[r], got[r]], axis=0)
        section = three_dots((cols_high[...], cols_low[...]), split(values))
        section = section + section.T
        line = pack(section, offsets)
        place(layer, line, r)
        for m in range(planes):
            total[m] += weights[m, layer] * line
        for m in range(planes - 1):
            row = (m + 1) * (half // planes)
            lines[m, pl.ds(layer, 1), :] = section[row : row + 1]

    @pl.when(step == steps - 1)
    def _():
        for m in range(planes - 1):
            plane = three_dots((rows_high[...], rows_low[...]), split(lines[m]))
            total[m] += pack(plane + plane.T, offsets)
        if closing:
            total[planes - 1] += pack(rim[...] + rim[...].T, offsets)
            for m in range(planes):
                place(count + m, total[m])
            place(count + planes, jnp.zeros((block, width), jnp.float32) + corner[...])


def packed_section(col, kept, got, table_pair, table_rows, marks, rim, corner, before, offsets, shape, closing):
    count, cols, half = kept.shape
    planes, block, width = before.shape
    gx, gy = shape
    step_rows = 4
    layers = count + (planes + 1 if closing else 0)
    whole = lambda array: pl.BlockSpec(array.shape, lambda i: (0,) * array.ndim)
    weights = jnp.stack([table_rows[:, m] for m in marks])
    arrays = rounded_parts(table_pair.T) + rounded_parts(table_rows[:, :half].T)
    arrays += (rim, corner[None], before)
    out = jax.ShapeDtypeStruct((layers, block // (gx * gy), gx, width), jnp.float32)
    outs = [out] * gy + [jax.ShapeDtypeStruct(before.shape, jnp.float32)]
    rows_spec = pl.BlockSpec((step_rows, cols, half), lambda i: (i, 0, 0))
    return pl.pallas_call(
        lambda *refs: section_kernel(offsets, closing, *refs),
        grid=(count // step_rows,),
        in_specs=[pl.BlockSpec(memory_space=pltpu.SMEM)] * 2 + [rows_spec, rows_spec]
        + [whole(array) for array in arrays],
        out_specs=[whole(out) for out in outs],
        out_shape=outs,
        scratch_shapes=[
            pltpu.VMEM((planes, count, half), jnp.float32),
            pltpu.VMEM((step_rows, block, width), jnp.float32),
        ],
        compiler_params=pltpu.CompilerParams(vmem_limit_bytes=VMEM_BYTES),
        cost_estimate=pl.CostEstimate(
            flops=count * 12 * cols * half * half,
            bytes_accessed=count * cols * half * 16,
            transcendentals=0,
        ),
    )(col.reshape(1), weights, kept, got, *arrays)


def on_device(intensity, template):
    rows, cols, length = intensity.shape
    gx, gy = lax.axis_size("gx"), lax.axis_size("gy")
    row, col = lax.axis_index("gx"), lax.axis_index("gy")
    devices, half = gx * gy, length // 2
    block = max(devices, rows)
    blocks, own, slabs = half // block, block // devices, gx // 2
    offsets = [block * b * (b + 1) // 2 for b in range(blocks + 1)]
    width = offsets[blocks]
    table = jnp.asarray(cosine_table(length))
    main = table[:, :half]

    pair_rows = rows // 2
    parts = row_parts(pair_rows)
    counts = [part.stop - part.start for part in parts]
    core = lax.rem(col, 2)
    constants = fill_constants(intensity, template, row, col, cosine_table(length)[:, :half])
    top, bottom, sides = faces(intensity)
    given_first, kept_first = (1 - core) * pair_rows, core * pair_rows
    given, kept = [], []
    blank = intensity[:SWEEPS]
    inner_faces = blank, blank, jnp.pad(sides, ((SWEEPS, SWEEPS),) + FREE)
    outer_faces = []

    def fill(c, start):
        part = parts[c]
        inner = part.start >= SWEEPS and part.stop <= pair_rows - SWEEPS
        use = (inner_faces if inner else tuple(outer_faces)) + constants
        return list(filled_spectrum(intensity, use, start + part.start, part))

    if not (parts[0].start >= SWEEPS and parts[0].stop <= pair_rows - SWEEPS):
        outer_faces.extend((top, bottom, with_corners(sides, corners(sides))))
    given.append(fill(0, given_first))
    if not outer_faces:
        given[0], late_sides = lax.optimization_barrier((given[0], sides))
        outer_faces.extend((top, bottom, with_corners(sides, corners(late_sides))))
    kept.append(fill(0, kept_first))

    table_cols = lax.dynamic_slice_in_dim(table, col * cols, cols, 0)
    kept_rows = lax.dynamic_slice_in_dim(table, row * rows + kept_first, pair_rows, 0)
    marks = [rows * (m + 1) for m in range(slabs)]
    mates = lax.dynamic_slice_in_dim(main, (col + 1 - 2 * core) * cols, cols, 0)
    table_pair = jnp.concatenate([table_cols[:, :half], mates], axis=0)
    table_parts = main.reshape(gx, 2, pair_rows, half) / 6.0
    table_parts = jnp.where(core == 0, table_parts, table_parts[:, ::-1])
    table_parts = [table_parts[:, :, part] for part in parts]
    side = jnp.zeros((slabs, block, width), jnp.float32)
    rim, corner = jnp.zeros((half, half), jnp.float32), jnp.zeros((width,), jnp.float32)
    values, packed, lines = 0.0, None, None
    for c, count in enumerate(counts):
        closing = c == len(counts) - 1
        got_lines = None
        if c > 0:
            (starts, packed) = lax.optimization_barrier(((given_first, kept_first), packed))
            given.append(fill(c, starts[0]))
            if c == 1:
                kept.extend(fill(later, starts[1]) for later in range(1, len(counts)))
            got_lines = exchanged(packed)
        got = lax.ppermute(given[c][0], "gy", swap(gy, 1))
        held = kept[c][0]
        if c > 0:
            behind = [held, got_lines] + [piece[0] for piece in kept[c + 1 :]]
            held, got_lines, *later = lax.optimization_barrier(behind)
            for n, spectrum in enumerate(later):
                kept[c + 1 + n][0] = spectrum
            lines = sent_lines(got_lines, counts[c - 1], lines)
            values = values + first_axis(lines, table_parts[c - 1])
        if closing:
            given_rows = lax.dynamic_slice_in_dim(table, row * rows + given_first, pair_rows, 0)
            ordered_rows = [held_rows[part] for held_rows in (given_rows, kept_rows) for part in parts]
            ordered_rows = jnp.concatenate(ordered_rows, axis=0)
            alternate = jnp.concatenate([piece[1] for piece in given + kept], axis=0) / math.sqrt(length)
            edge = [piece[2][:, : piece[1].shape[0]] for piece in given + kept]
            edge = jnp.concatenate(edge, axis=1)
            edge = jnp.einsum("ba,bk->ak", edge / math.sqrt(length), table_cols, precision=HIGH)
            edge = edge + jnp.concatenate([alternate, edge[:, half:]], axis=1)
            rim = jnp.einsum("aj,ak->jk", ordered_rows[:, :half], edge[:, :half], precision=HIGH)
            corner = 2.0 * jnp.einsum("a,ak->k", ordered_rows[:, half], edge, precision=HIGH)
            corner = corner + jnp.einsum("aj,a->j", ordered_rows, edge[:, half], precision=HIGH)
            corner = jnp.pad(corner, (0, width - half - 1))

        *packed, side = packed_section(
            col, held, got, table_pair, kept_rows[parts[c]], marks,
            rim, corner, side, offsets, (gx, gy), closing,
        )
    lines = sent_lines(exchanged(packed), counts[-1], lines)
    values = values + first_axis(lines, table_parts[-1])
    side = jnp.sum(lines[:, :, 2 * counts[-1] :], axis=0) / 6.0
    turned = values.reshape(own, blocks, own, devices, width)
    turned = jnp.transpose(turned, (3, 1, 2, 0, 4))
    turned = [turned[:, b, :, :, : offsets[b + 1]] for b in range(blocks)]
    turned = lax.all_to_all(jnp.concatenate(turned, axis=3), ("gy", "gx"), 0, 0, tiled=True)
    turned = jnp.transpose(turned, (1, 2, 0, 3)).reshape(own, block, -1)

    slab = jnp.minimum(row, gx - 1 - row)
    far_row, far_col = row >= slabs, col >= gy // 2
    pick_rows = jnp.arange(rows)
    pick_rows = slab * rows + jnp.where(far_row, rows - pick_rows, pick_rows)
    pick_cols = jnp.arange(cols)
    pick_cols = jnp.where(far_col, (gy - col) * cols - pick_cols, col * cols + pick_cols)

    if rows == block:
        got, piece = [], None
        for messages in slab_messages(values, turned, side, offsets, slabs):
            if piece is not None:
                messages, piece = lax.optimization_barrier((messages, piece))
                got.append(gathered(piece, gy, got[-1] if got else None))
            piece = lax.all_to_all(messages, "gx", 0, 0, tiled=True)
        got.append(gathered(piece, gy, got[-1] if got else None))
        tiles = width // 128
        start = tile_groups(tiles)[0].stop * own * block
        side = jnp.stack([piece[:, start : start + 3 * own * tiles] for piece in got[0]])
        bit = gy // 2
        while bit:
            paired = side.reshape((-1, 2, bit) + side.shape[1:])
            side = jnp.where((col & bit) == 0, paired, paired[:, ::-1]).reshape(side.shape)
            bit //= 2
        side = side.reshape(devices, own, 3, width)
        side = jnp.transpose(side, (2, 1, 0, 3)).reshape(3, block, width)
        next_plane, across = side[0], rim_rows(side[1:], offsets, pick_rows)
        rim_col = col == gy // 2
        rim = across[:, pick_cols]
        return result_block(
            got, next_plane, across, rim, pick_cols, slab, far_row, rim_col, col, offsets
        )

    side = lax.all_gather(side, ("gy", "gx"), axis=0)
    side = jnp.transpose(side, (2, 1, 0, 3)).reshape(slabs + 1, block, width)
    across = rim_rows(side[slabs - 1 :], offsets, pick_rows)
    next_plane = lax.dynamic_index_in_dim(side, slab, 0, keepdims=False)
    sums = axis_order_sums(values, turned, offsets, block)
    messages = []
    for s in range(slabs):
        base, first = s * rows // block, s * rows
        units = []
        for b in range(blocks):
            size = (b + 1) * block
            near = jnp.zeros((own, rows, size))
            far = jnp.zeros((own, block, size))
            if b >= base:
                near = jnp.stack([sums[b][e][first : first + rows, :size] for e in range(own)])
            else:
                far = jnp.stack([sums[base][e][b * block : size, :size] for e in range(own)])
            units.append(jnp.concatenate([near, far], axis=1))
        messages.append(jnp.concatenate(units, axis=2))
    messages = jnp.stack(messages + messages[::-1])
    got = lax.all_to_all(messages, "gx", 0, 0, tiled=True)
    got = lax.all_gather(got, "gy", axis=0, tiled=True)
    got = jnp.swapaxes(got, 0, 1).reshape(block, rows + block, width)
    base = slab * rows // block
    lower = []
    for b in range(blocks):
        lanes = slice(offsets[b], offsets[b + 1])
        near = jnp.swapaxes(got[:, :rows, lanes], 0, 1)
        far = lax.dynamic_slice_in_dim(got[:, rows:, lanes], lax.rem(slab * rows, block), rows, 0)
        lower.append(jnp.where(b >= base, near, far))
    lower = jnp.concatenate(lower, axis=2)
    lower = jnp.concatenate([lower, next_plane[None]], axis=0)
    body = square([lower[:, :, offsets[b] : offsets[b + 1]] for b in range(blocks)], block)
    body = body[pick_rows - slab * rows]
    body = jnp.concatenate([body, across[:, None, :half]], axis=1)[:, pick_cols]
    body = jnp.concatenate([body, across[:, pick_cols][:, :, None]], axis=2)
    return jnp.concatenate([body, jnp.flip(body[:, :, 1:half], 2)], axis=2)


def rim_rows(side, offsets, pick_rows):
    blocks, block = len(offsets) - 1, offsets[1]
    half = blocks * block
    last = square([side[0][:, offsets[b] : offsets[b + 1]] for b in range(blocks)], block)
    rim = side[1, 0, : half + 1]
    last = jnp.concatenate([last, rim[None, :half]], axis=0)
    return jnp.concatenate([last, rim[:, None]], axis=1)[pick_rows]


def axis_order_sums(values, turned, offsets, block):
    start = 0
    sums = []
    for top in range(len(offsets) - 1):
        size = (top + 1) * block
        parts = []
        for e in range(values.shape[0]):
            part = values[e, :size, offsets[top] : offsets[top] + size]
            lower = [turned[e, :, start + offsets[b] : start + offsets[b + 1]] for b in range(top + 1)]
            parts.append(part + part.T + square(lower, block))
        sums.append(parts)
        start += offsets[top + 1]
    return sums


def message_kernel(offsets, slabs, values, turned, side, *messages):
    blocks, block = len(offsets) - 1, offsets[1]
    values, turned = values[...], turned[...]
    own = values.shape[0]
    sums = axis_order_sums(values, turned, offsets, block)
    groups = tile_groups(offsets[-1] // 128)
    side_start = groups[0].stop * own * block
    messages[0][:, side_start:] = jnp.zeros_like(messages[0][:, side_start:])
    for s in range(slabs):
        places = s, 2 * slabs - 1 - s
        for e in range(own):
            units = []
            for b in range(blocks):
                size = (b + 1) * block
                if b >= s:
                    units.append(sums[b][e][s * block : (s + 1) * block, :size])
                else:
                    units.append(sums[s][e][b * block : size, :size])
            line = jnp.concatenate(units, axis=1)
            for group, out in zip(groups, messages):
                for tile in range(group.start, group.stop):
                    start = ((tile - group.start) * own + e) * block
                    for place in places:
                        out[place, start : start + block] = line[:, tile * 128 : (tile + 1) * 128]
            row = side_start + 3 * e * groups[-1].stop
            for plane in (s, slabs - 1, slabs):
                for tile in range(groups[-1].stop):
                    part = side[e, plane : plane + 1, tile * 128 : (tile + 1) * 128]
                    for place in places:
                        messages[0][place, row : row + 1] = part
                    row += 1


def slab_messages(values, turned, side, offsets, slabs):
    own, block, tiles = values.shape[0], offsets[1], offsets[-1] // 128
    sizes = [(group.stop - group.start) * own * block for group in tile_groups(tiles)]
    sizes[0] += -(-3 * own * tiles // 8) * 8
    return pl.pallas_call(
        lambda *refs: message_kernel(offsets, slabs, *refs),
        in_specs=[pl.BlockSpec(memory_space=pltpu.VMEM)] * 3,
        out_specs=[pl.BlockSpec(memory_space=pltpu.VMEM)] * len(sizes),
        out_shape=[jax.ShapeDtypeStruct((2 * slabs, size, 128), jnp.float32) for size in sizes],
        compiler_params=pltpu.CompilerParams(vmem_limit_bytes=VMEM_BYTES),
    )(values, turned, side)


def result_kernel(
    offsets, own, devices, groups, places, next_plane, across, rim, pick, flip, *refs
):
    blocks, block = len(offsets) - 1, offsets[1]
    tiles = offsets[-1] // 128
    peers = (len(refs) - 2) // len(groups) - 1
    pieces, out = refs[: peers * len(groups)], refs[peers * len(groups)]
    held, sems = refs[peers * len(groups) + 1 : -1], refs[-1]
    step_rows, cols, length = out.shape
    half = length // 2
    slab, far_row, rim_col, me = places[0], places[1], places[2], places[3]
    lane = lax.broadcasted_iota(jnp.int32, (block, 128), 1)
    at_rim = lax.broadcasted_iota(jnp.int32, (cols, half), 0) + (1 - rim_col) == 0
    rim_lane = lax.broadcasted_iota(jnp.int32, rim.shape, 1)
    first_lane = lax.broadcasted_iota(jnp.int32, (cols, half), 1) == 0

    @pl.when(pl.program_id(0) == 0)
    def _():
        copies = []
        for g in range(len(groups)):
            for peer in range(peers):
                piece = pieces[g * peers + peer]
                size = piece.shape[0]
                spot = pl.ds(pl.multiple_of((me ^ peer) * size, size), size)
                copies.append(pltpu.make_async_copy(piece, held[g].at[spot], sems.at[g, peer]))
        for copy in copies:
            copy.start()
        for copy in copies:
            copy.wait()

    def left_half(r):
        t = pl.program_id(0) * step_rows + r
        i = jnp.where(far_row == 1, block - t, t)
        inside = (jnp.zeros((block, 128), jnp.int32) + i) < block
        i = jnp.minimum(i, block - 1)
        source = lax.div(i, devices), lax.rem(i, devices)
        parts = []
        for g, group in enumerate(groups):
            stride = held[g].shape[0] // devices
            for tile in range(group.start, group.stop):
                start = (tile - group.start) * own * block
                near = [
                    held[g][pl.ds(start + e * block + i, devices, stride=stride), :]
                    for e in range(own)
                ]
                near = jnp.concatenate(near, axis=0)
                far = pl.multiple_of(source[1] * stride + start + source[0] * block, 8)
                far = held[g][pl.ds(far, block), :]
                kind = jnp.zeros((block, 128), jnp.int32)
                for b in range(1, blocks):
                    kind += (lane + tile * 128 >= offsets[b]).astype(jnp.int32)
                line = jnp.where(kind >= slab, near, far)
                line = jnp.where(inside, line, next_plane[:, pl.ds(tile * 128, 128)])
                parts.append(line)
        line = jnp.concatenate(parts, axis=1)
        plane = square([line[:, offsets[b] : offsets[b + 1]] for b in range(blocks)], block)
        high, low = split(plane)
        left = jnp.dot(pick[...], high, preferred_element_type=jnp.float32)
        left += jnp.dot(pick[...], low, preferred_element_type=jnp.float32)
        left = jnp.where(at_rim, across[pl.ds(t, 1), :], left)
        out[r, :, pl.ds(0, half)] = left
        return left

    together = 4

    @pl.loop(0, step_rows // together)
    def _(c):
        left = [left_half(c * together + n) for n in range(together)]
        high, low = split(jnp.concatenate(left, axis=0))
        right = jnp.dot(high, flip[...], preferred_element_type=jnp.float32)
        right += jnp.dot(low, flip[...], preferred_element_type=jnp.float32)
        for n in range(together):
            r = c * together + n
            t = pl.program_id(0) * step_rows + r
            edge = jnp.sum(jnp.where(rim_lane == t, rim[...], 0.0), axis=1, keepdims=True)
            part = right[n * cols : (n + 1) * cols]
            out[r, :, pl.ds(half, half)] = jnp.where(first_lane, edge, part)


def result_block(got, next_plane, across, rim, pick_cols, slab, far_row, rim_col, col, offsets):
    block = offsets[1]
    gx = got[0][0].shape[0]
    groups = tile_groups(offsets[-1] // 128)
    devices = gx * len(got[0])
    own = block // devices
    rows, half = across.shape[0], across.shape[1] - 1
    cols = pick_cols.shape[0]
    step_rows = 8
    places = jnp.stack([slab, far_row.astype(jnp.int32), rim_col.astype(jnp.int32), col])
    cell = jnp.arange(half)
    pick = (pick_cols[:, None] == cell[None, :]).astype(jnp.bfloat16)
    flip = (cell[:, None] + cell[None, :] == half).astype(jnp.bfloat16)
    rim = jnp.pad(rim.T, ((0, 0), (0, 128 - rows)))
    whole = lambda array: pl.BlockSpec(array.shape, lambda i: (0,) * array.ndim)
    arrays = (next_plane, across[:, :half], rim, pick, flip)
    pieces = [piece.reshape(-1, 128) for group in got for piece in group]
    return pl.pallas_call(
        lambda *refs: result_kernel(offsets, own, devices, groups, *refs),
        grid=(rows // step_rows,),
        in_specs=[pl.BlockSpec(memory_space=pltpu.SMEM)] + [whole(array) for array in arrays]
        + [pl.BlockSpec(memory_space=pl.ANY)] * len(pieces),
        out_specs=pl.BlockSpec((step_rows, cols, 2 * half), lambda i: (i, 0, 0)),
        out_shape=jax.ShapeDtypeStruct((rows, cols, 2 * half), jnp.float32),
        scratch_shapes=[
            pltpu.VMEM((devices * group[0].shape[1], 128), jnp.float32) for group in got
        ] + [pltpu.SemaphoreType.DMA((len(groups), len(got[0])))],
        compiler_params=pltpu.CompilerParams(vmem_limit_bytes=VMEM_BYTES),
    )(places, *arrays, *pieces)


def tile_groups(tiles):
    return [slice(tile, min(tile + 2, tiles)) for tile in range(0, tiles, 2)]


def swap(peers, bit):
    return [(q, q ^ bit) for q in range(peers)]


def gathered(piece, peers, after):
    if after is not None:
        piece, first_hops = lax.optimization_barrier((piece, after[1:3]))
        after[1:3] = first_hops
    pieces, bit = {0: piece}, peers // 2
    while bit:
        for place in list(pieces):
            pieces[place ^ bit] = lax.ppermute(pieces[place], "gy", swap(peers, bit))
        bit //= 2
    return [pieces[place] for place in range(peers)]


def exchanged(packed):
    gy = len(packed)
    return [packed[0]] + [lax.ppermute(packed[p], "gy", swap(gy, p)) for p in range(1, gy)]


def sent_lines(got, count, after):
    gy = len(got)
    lines = [sum(got[p][:count] for p in range(first, gy, 2)) for first in range(2)]
    lines = jnp.concatenate(lines + [sum(piece[count:] for piece in got)], axis=0)
    lines = jnp.transpose(lines, (2, 1, 0, 3))
    if after is not None:
        lines, _ = lax.optimization_barrier((lines, after))
    return lax.all_to_all(lines, "gx", 0, 0, tiled=True)


def first_axis(lines, table):
    gx, _, count, half = table.shape
    table = table.reshape(gx, 2 * count, half)
    return jnp.einsum("geaw,gai->eiw", lines[:, :, : 2 * count], table, precision=HIGH)


def row_parts(rows):
    if rows < 4 * PART_STEP:
        return [slice(0, rows)]
    return [slice(PART_STEP, rows - PART_STEP), slice(0, PART_STEP), slice(rows - PART_STEP, rows)]


def square(lower, block):
    lines = []
    for b in range(len(lower)):
        parts = [lower[b]]
        for c in range(b + 1, len(lower)):
            part = lower[c][..., b * block : (b + 1) * block]
            parts.append(jnp.swapaxes(part, -1, -2))
        lines.append(jnp.concatenate(parts, axis=-1))
    return jnp.concatenate(lines, axis=-2)


def solution(mesh):
    placed = (P("gx", "gy", None), P())
    return jax.shard_map(
        on_device, mesh=mesh, in_specs=placed, out_specs=P("gx", "gy", None), check_vma=False
    )
```

```python
import math

import jax
import jax.numpy as jnp
import numpy as np
from jax import lax
from jax.experimental import pallas as pl
from jax.experimental.pallas import tpu as pltpu
from jax.sharding import PartitionSpec as P

SWEEPS = 2

AXIS_ORDERS = ((0, 1, 2), (0, 2, 1), (1, 0, 2), (1, 2, 0), (2, 0, 1), (2, 1, 0))

HIGH = lax.Precision.HIGH


def ring(axis):
    peers = lax.axis_size(axis)
    up = [(i, (i + 1) % peers) for i in range(peers)]
    return up, [(j, i) for i, j in up]


FREE = ((8 - SWEEPS, 8 - SWEEPS), (0, 0))


def side_faces(block):
    cols = block.shape[1]
    right, left = ring("gy")
    before = lax.ppermute(block[:, cols - SWEEPS :], "gy", right)
    after = lax.ppermute(block[:, :SWEEPS], "gy", left)
    return jnp.concatenate([before, after], axis=1)


def end_faces(block, sides):
    rows, cols, _ = block.shape
    up, down = ring("gx")
    last = jnp.concatenate([block[rows - SWEEPS :], sides[rows - SWEEPS :]], axis=1)
    first = jnp.concatenate([block[:SWEEPS], sides[:SWEEPS]], axis=1)
    above, below = lax.ppermute(last, "gx", up), lax.ppermute(first, "gx", down)
    whole = jnp.concatenate([above[:, cols:], sides, below[:, cols:]], axis=0)
    return above[:, :cols], below[:, :cols], jnp.pad(whole, ((0, 0),) + FREE)


def mirror(values, axis):
    return jnp.roll(jnp.flip(values, axis), 1, axis)


def symmetric_marks(marks):
    for flip_axis in range(3):
        marks = jnp.maximum(marks, mirror(marks, flip_axis))
    united = marks
    for axis_order in AXIS_ORDERS[1:]:
        united = jnp.maximum(united, jnp.transpose(marks, axis_order))
    return united


def cosine_table(length):
    position = np.arange(length)
    phases = np.mod(position[:, None] * position[None, : length // 2 + 1], length)
    return (np.cos(phases * (2.0 * math.pi / length)) / math.sqrt(length)).astype(np.float32)


MARGIN = 16
CHUNK = 16
STEP_ROWS = 16
PART_STEP = 8
VMEM_BYTES = 56 * 1024 * 1024


def split(values):
    high = values.astype(jnp.bfloat16)
    low = (values - high.astype(jnp.float32)).astype(jnp.bfloat16)
    return high, low


def fill_kernel(
    base, here, above, below, top, bottom, sides, marks, table_high, table_low,
    spectrum, alternate, edge, punched, once, high, low, folded,
):
    step_rows, cols, length = here.shape
    step = pl.program_id(0) + base[0]
    first_row = step * step_rows
    local_row = pl.program_id(0) * step_rows
    period = marks.shape[0]
    lane = lax.broadcasted_iota(jnp.int32, (128, 128), 1)
    signs = jnp.where(lax.broadcasted_iota(jnp.int32, (128, 128), 0) % 2 == 0, 1.0, -1.0)

    @pl.when(pl.program_id(0) == 0)
    def _():
        edge[...] = jnp.zeros_like(edge)

    def holes(row, start, size):
        row = lax.rem(first_row + row, period)
        start = start % period
        if start + size <= period:
            part = marks[row, pl.ds(start, size), :]
        else:
            part = jnp.concatenate(
                [marks[row, pl.ds(start, period - start), :], marks[row, pl.ds(0, start + size - period), :]],
                axis=0,
            )
        return jnp.concatenate([part] * (length // 128), axis=1)

    def punch(row, start, values):
        kept = jnp.where(holes(row, start, values.shape[0]) > 0.0, 0.0, values)
        punched[row, pl.ds(start, values.shape[0]), :] = kept

    def punch_row(row, source, index):
        full = first_row + row
        punch(row, MARGIN - 8, sides[full, pl.ds(0, 8), :])
        punch(row, MARGIN + cols, sides[full, pl.ds(8, 8), :])
        for c in range(0, cols, CHUNK):
            punch(row, MARGIN + c, source[index, pl.ds(c, CHUNK), :])

    def neighbours(ref, row, start):
        middle = ref[row, pl.ds(start, CHUNK), :]
        total = ref[row - 1, pl.ds(start, CHUNK), :] + ref[row + 1, pl.ds(start, CHUNK), :]
        total += ref[row, pl.ds(start - 1, CHUNK), :] + ref[row, pl.ds(start + 1, CHUNK), :]
        return total + pltpu.roll(middle, 1, 1) + pltpu.roll(middle, length - 1, 1)

    last = (sides.shape[0] - 2 * SWEEPS) // step_rows - 1
    for edge_rows, inside, offset, outer in (
        (above, step > 0, 0, top),
        (below, step < last, step_rows + SWEEPS, bottom),
    ):
        @pl.when(inside)
        def _():
            for r in range(SWEEPS):
                punch_row(offset + r, edge_rows, r)

        @pl.when(jnp.logical_not(inside))
        def _():
            for r in range(SWEEPS):
                punch_row(offset + r, outer, r)

    @pl.loop(0, step_rows)
    def _(r):
        punch_row(r + SWEEPS, here, r)

    @pl.loop(1, step_rows + 2 * SWEEPS - 1, unroll=2)
    def _(r):
        for start in range(MARGIN - 8, MARGIN + cols + 8, CHUNK):
            total = neighbours(punched, r, start) * holes(r, start, CHUNK)
            once[r, pl.ds(start, CHUNK), :] = punched[r, pl.ds(start, CHUNK), :] + total

    @pl.loop(0, step_rows)
    def _(r):
        for c in range(0, cols, CHUNK):
            start = MARGIN + c
            total = neighbours(once, r + SWEEPS, start) * holes(r + SWEEPS, start, CHUNK)
            filled = punched[r + SWEEPS, pl.ds(start, CHUNK), :] + total
            first, second = split(filled)
            spot = pl.ds(pl.multiple_of(r * cols + c, CHUNK), CHUNK)
            high[spot, :] = first
            low[spot, :] = second
            wrapped = filled[:, :128]
            for tile in range(1, length // 128):
                wrapped += filled[:, tile * 128 : (tile + 1) * 128]
            folded[pl.ds(c, CHUNK), :] = wrapped
        column = jnp.where(lane == local_row + r, signs, 0.0).astype(jnp.bfloat16)
        first, second = split(folded[...])
        total = jnp.dot(first, column, preferred_element_type=jnp.float32)
        total += jnp.dot(second, column, preferred_element_type=jnp.float32)
        edge[...] += total

    rows_each = 8
    half = spectrum.shape[2]
    order = lax.broadcasted_iota(jnp.int32, (rows_each, cols, half), 1)

    @pl.loop(0, step_rows // rows_each)
    def _(r):
        spot = pl.ds(pl.multiple_of(r * rows_each * cols, CHUNK), rows_each * cols)
        first, second = high[spot, :], low[spot, :]
        total = jnp.dot(first, table_low[...], preferred_element_type=jnp.float32)
        total += jnp.dot(second, table_high[...], preferred_element_type=jnp.float32)
        total += jnp.dot(first, table_high[...], preferred_element_type=jnp.float32)
        total = total.reshape(rows_each, cols, half)
        spectrum[pl.ds(r * rows_each, rows_each)] = total
        signed = jnp.sum(jnp.where(order % 2 == 0, total, -total), axis=1)
        alternate[pl.ds(pl.multiple_of(r * rows_each, rows_each), rows_each), :] = signed


def rounded_parts(table):
    rounded = lax.reduce_precision(table, 8, 7)
    return rounded.astype(jnp.bfloat16), (table - rounded).astype(jnp.bfloat16)


def marks_kernel(shifts, template, out, held):
    period = template.shape[0]
    repeats = held.shape[1] // period
    line = lax.broadcasted_iota(jnp.int32, (period, period), 0)
    across = lax.broadcasted_iota(jnp.int32, (period, period), 1)
    flip = jnp.where((line + across) % period == 0, 1.0, 0.0)
    for i in range(period):
        plane = jnp.maximum(template[i], template[-i % period]).astype(jnp.float32)
        plane = jnp.maximum(plane, jnp.dot(flip, plane, preferred_element_type=jnp.float32))
        plane = jnp.maximum(plane, jnp.dot(plane, flip, preferred_element_type=jnp.float32))
        plane = jnp.maximum(plane, plane.T)
        held[i * period : (i + 1) * period, :] = jnp.concatenate([plane] * repeats, axis=1)
    for i in range(period):
        plane = held[i * period : (i + 1) * period, :]
        turned = held[pl.ds(i, period, stride=period), :]
        back = turned[:, :period].T
        plane = jnp.maximum(jnp.maximum(plane, turned), jnp.concatenate([back] * repeats, axis=1))
        plane = jnp.where(plane == 1.0, 1.0 / 6.0, 0.0)
        shift = shifts[1]
        out[(i - shifts[0]) % period] = jnp.concatenate([plane[shift:], plane[:shift]], axis=0)


def hole_marks(template, row, col, rows, cols):
    period = template.shape[0]
    shape = (period, period, 128)
    if rows % period == 0 and cols % period == 0:
        shifts = (-SWEEPS % period, -MARGIN % period)
        return pl.pallas_call(
            lambda *refs: marks_kernel(shifts, *refs),
            in_specs=[pl.BlockSpec(memory_space=pltpu.VMEM)],
            out_specs=pl.BlockSpec(memory_space=pltpu.VMEM),
            out_shape=jax.ShapeDtypeStruct(shape, jnp.float32),
            scratch_shapes=[pltpu.VMEM((period * period, 128), jnp.float32)],
        )(template)
    shifts = (jnp.mod(row * rows - SWEEPS, period), jnp.mod(col * cols - MARGIN, period))
    marks = jnp.roll(symmetric_marks(template), (-shifts[0], -shifts[1]), (0, 1))
    return jnp.tile(marks.astype(jnp.float32) / 6.0, (1, 1, 128 // period))


def fill_constants(intensity, template, row, col, main):
    rows, cols, _ = intensity.shape
    high = main.astype(jnp.bfloat16)
    low = (main - high.astype(np.float32)).astype(jnp.bfloat16)
    return hole_marks(template, row, col, rows, cols), jnp.asarray(high), jnp.asarray(low)


def filled_spectrum(intensity, arrays, first, part):
    rows, cols, length = intensity.shape
    half, count = length // 2, part.stop - part.start
    step_rows = STEP_ROWS if part.start % STEP_ROWS == 0 and count % STEP_ROWS == 0 else PART_STEP
    pairs = step_rows // SWEEPS
    last = rows // SWEEPS - 1
    whole = lambda array: pl.BlockSpec(array.shape, lambda i, b: (0,) * array.ndim)
    before = lambda i, b: (jnp.maximum((i + b[0]) * pairs - 1, 0), 0, 0)
    after = lambda i, b: (jnp.minimum((i + b[0] + 1) * pairs, last), 0, 0)
    padded = (step_rows + 2 * SWEEPS, cols + 2 * MARGIN, length)
    return pl.pallas_call(
        fill_kernel,
        grid_spec=pltpu.PrefetchScalarGridSpec(
            num_scalar_prefetch=1,
            grid=(count // step_rows,),
            in_specs=[
                pl.BlockSpec((step_rows, cols, length), lambda i, b: (i + b[0], 0, 0)),
                pl.BlockSpec((SWEEPS, cols, length), before),
                pl.BlockSpec((SWEEPS, cols, length), after),
            ] + [whole(array) for array in arrays],
            out_specs=[
                pl.BlockSpec((step_rows, cols, half), lambda i, b: (i, 0, 0)),
                pl.BlockSpec((step_rows, half), lambda i, b: (i, 0)),
                pl.BlockSpec((cols, 128), lambda i, b: (0, 0)),
            ],
            scratch_shapes=[
                pltpu.VMEM(padded, jnp.float32),
                pltpu.VMEM(padded, jnp.float32),
                pltpu.VMEM((step_rows * cols, length), jnp.bfloat16),
                pltpu.VMEM((step_rows * cols, length), jnp.bfloat16),
                pltpu.VMEM((cols, 128), jnp.float32),
            ],
        ),
        out_shape=[
            jax.ShapeDtypeStruct((count, cols, half), jnp.float32),
            jax.ShapeDtypeStruct((count, half), jnp.float32),
            jax.ShapeDtypeStruct((cols, 128), jnp.float32),
        ],
        compiler_params=pltpu.CompilerParams(vmem_limit_bytes=VMEM_BYTES),
        cost_estimate=pl.CostEstimate(
            flops=count * cols * length * half * 6,
            bytes_accessed=count * cols * (length + half) * 4,
            transcendentals=0,
        ),
    )((first // step_rows).reshape(1), intensity, intensity, intensity, *arrays)


def pack(section, offsets):
    block = offsets[1]
    units = [section[b * block : (b + 1) * block, : (b + 1) * block] for b in range(len(offsets) - 1)]
    return jnp.concatenate(units, axis=1)


def three_dots(left, right):
    total = jnp.dot(left[1], right[0], preferred_element_type=jnp.float32)
    total += jnp.dot(left[0], right[1], preferred_element_type=jnp.float32)
    return total + jnp.dot(left[0], right[0], preferred_element_type=jnp.float32)


def section_kernel(
    offsets, closing, me, weights, kept, got, cols_high, cols_low, rows_high, rows_low,
    rim, corner, before, *refs
):
    step, steps = pl.program_id(0), pl.num_programs(0)
    step_rows = kept.shape[0]
    half, count = rows_high.shape
    planes, block, width = before.shape
    *outs, total, lines, packed = refs
    gy, (_, own, gx, _) = len(outs), outs[0].shape

    def place(layer, values, slot=0):
        packed[slot] = values
        for e in range(own):
            for p in range(gy):
                start = pl.multiple_of((e * gy + (p ^ me[0])) * gx, gx)
                outs[p][layer, e] = packed[slot, pl.ds(start, gx), :]

    @pl.when(step == 0)
    def _():
        total[...] = before[...]

    for r in range(step_rows):
        layer = step * step_rows + r
        values = jnp.concatenate([kept[r], got[r]], axis=0)
        section = three_dots((cols_high[...], cols_low[...]), split(values))
        section = section + section.T
        line = pack(section, offsets)
        place(layer, line, r)
        for m in range(planes):
            total[m] += weights[m, layer] * line
        for m in range(planes - 1):
            row = (m + 1) * (half // planes)
            lines[m, pl.ds(layer, 1), :] = section[row : row + 1]

    @pl.when(step == steps - 1)
    def _():
        for m in range(planes - 1):
            plane = three_dots((rows_high[...], rows_low[...]), split(lines[m]))
            total[m] += pack(plane + plane.T, offsets)
        if closing:
            total[planes - 1] += pack(rim[...] + rim[...].T, offsets)
            for m in range(planes):
                place(count + m, total[m])
            place(count + planes, jnp.zeros((block, width), jnp.float32) + corner[...])


def packed_section(col, kept, got, table_pair, table_rows, marks, rim, corner, before, offsets, shape, closing):
    count, cols, half = kept.shape
    planes, block, width = before.shape
    gx, gy = shape
    step_rows = 4
    layers = count + (planes + 1 if closing else 0)
    whole = lambda array: pl.BlockSpec(array.shape, lambda i: (0,) * array.ndim)
    weights = jnp.stack([table_rows[:, m] for m in marks])
    arrays = rounded_parts(table_pair.T) + rounded_parts(table_rows[:, :half].T)
    arrays += (rim, corner[None], before)
    out = jax.ShapeDtypeStruct((layers, block // (gx * gy), gx, width), jnp.float32)
    outs = [out] * gy + [jax.ShapeDtypeStruct(before.shape, jnp.float32)]
    rows_spec = pl.BlockSpec((step_rows, cols, half), lambda i: (i, 0, 0))
    return pl.pallas_call(
        lambda *refs: section_kernel(offsets, closing, *refs),
        grid=(count // step_rows,),
        in_specs=[pl.BlockSpec(memory_space=pltpu.SMEM)] * 2 + [rows_spec, rows_spec]
        + [whole(array) for array in arrays],
        out_specs=[whole(out) for out in outs],
        out_shape=outs,
        scratch_shapes=[
            pltpu.VMEM((planes, count, half), jnp.float32),
            pltpu.VMEM((step_rows, block, width), jnp.float32),
        ],
        compiler_params=pltpu.CompilerParams(vmem_limit_bytes=VMEM_BYTES),
        cost_estimate=pl.CostEstimate(
            flops=count * 12 * cols * half * half,
            bytes_accessed=count * cols * half * 16,
            transcendentals=0,
        ),
    )(col.reshape(1), weights, kept, got, *arrays)


def on_device(intensity, template):
    rows, cols, length = intensity.shape
    gx, gy = lax.axis_size("gx"), lax.axis_size("gy")
    row, col = lax.axis_index("gx"), lax.axis_index("gy")
    devices, half = gx * gy, length // 2
    block = max(devices, rows)
    blocks, own, slabs = half // block, block // devices, gx // 2
    offsets = [block * b * (b + 1) // 2 for b in range(blocks + 1)]
    width = offsets[blocks]
    table = jnp.asarray(cosine_table(length))
    main = table[:, :half]

    pair_rows = rows // 2
    parts = row_parts(pair_rows)
    counts = [part.stop - part.start for part in parts]
    core = lax.rem(col, 2)
    constants = fill_constants(intensity, template, row, col, cosine_table(length)[:, :half])
    sides = side_faces(intensity)
    given_first, kept_first = (1 - core) * pair_rows, core * pair_rows
    given, kept = [], []
    blank = intensity[:SWEEPS]
    inner_faces = blank, blank, jnp.pad(sides, ((SWEEPS, SWEEPS),) + FREE)
    outer_faces = []

    def fill(c, start):
        part = parts[c]
        inner = part.start >= SWEEPS and part.stop <= pair_rows - SWEEPS
        use = (inner_faces if inner else tuple(outer_faces)) + constants
        return list(filled_spectrum(intensity, use, start + part.start, part))

    if not (parts[0].start >= SWEEPS and parts[0].stop <= pair_rows - SWEEPS):
        outer_faces.extend(end_faces(intensity, sides))
    given.append(fill(0, given_first))
    if not outer_faces:
        given[0], late_sides = lax.optimization_barrier((given[0], sides))
        outer_faces.extend(end_faces(intensity, late_sides))
    kept.append(fill(0, kept_first))

    table_cols = lax.dynamic_slice_in_dim(table, col * cols, cols, 0)
    kept_rows = lax.dynamic_slice_in_dim(table, row * rows + kept_first, pair_rows, 0)
    marks = [rows * (m + 1) for m in range(slabs)]
    mates = lax.dynamic_slice_in_dim(main, (col + 1 - 2 * core) * cols, cols, 0)
    table_pair = jnp.concatenate([table_cols[:, :half], mates], axis=0)
    table_parts = main.reshape(gx, 2, pair_rows, half) / 6.0
    table_parts = jnp.where(core == 0, table_parts, table_parts[:, ::-1])
    table_parts = [table_parts[:, :, part] for part in parts]
    side = jnp.zeros((slabs, block, width), jnp.float32)
    rim, corner = jnp.zeros((half, half), jnp.float32), jnp.zeros((width,), jnp.float32)
    values, packed, lines = 0.0, None, None
    for c, count in enumerate(counts):
        closing = c == len(counts) - 1
        if c == 1:
            start, packed = lax.optimization_barrier((given_first, packed))
            given.extend(fill(later, start) for later in range(1, len(counts)))
        sent = given[c][0]
        if c > 0:
            got_lines = exchanged(packed)
        if c == 1:
            start, got_lines = lax.optimization_barrier((kept_first, got_lines))
            kept.extend(fill(later, start) for later in range(1, len(counts)))
        held = kept[c][0]
        if c > 0:
            sent, held = lax.optimization_barrier((sent, held))
        got = lax.ppermute(sent, "gy", swap(gy, 1))
        if c > 0:
            held, *later = lax.optimization_barrier([held] + [piece[0] for piece in kept[c + 1 :]])
            for n, spectrum in enumerate(later):
                kept[c + 1 + n][0] = spectrum
            lines = sent_lines(got_lines, counts[c - 1], lines)
            values = values + first_axis(lines, table_parts[c - 1])
        if closing:
            given_rows = lax.dynamic_slice_in_dim(table, row * rows + given_first, pair_rows, 0)
            ordered_rows = [held_rows[part] for held_rows in (given_rows, kept_rows) for part in parts]
            ordered_rows = jnp.concatenate(ordered_rows, axis=0)
            alternate = jnp.concatenate([piece[1] for piece in given + kept], axis=0) / math.sqrt(length)
            edge = [piece[2][:, : piece[1].shape[0]] for piece in given + kept]
            edge = jnp.concatenate(edge, axis=1)
            edge = jnp.einsum("ba,bk->ak", edge / math.sqrt(length), table_cols, precision=HIGH)
            edge = edge + jnp.concatenate([alternate, edge[:, half:]], axis=1)
            rim = jnp.einsum("aj,ak->jk", ordered_rows[:, :half], edge[:, :half], precision=HIGH)
            corner = 2.0 * jnp.einsum("a,ak->k", ordered_rows[:, half], edge, precision=HIGH)
            corner = corner + jnp.einsum("aj,a->j", ordered_rows, edge[:, half], precision=HIGH)
            corner = jnp.pad(corner, (0, width - half - 1))

        *packed, side = packed_section(
            col, held, got, table_pair, kept_rows[parts[c]], marks,
            rim, corner, side, offsets, (gx, gy), closing,
        )
    lines = sent_lines(exchanged(packed), counts[-1], lines)
    values = values + first_axis(lines, table_parts[-1])
    side = jnp.sum(lines[:, :, 2 * counts[-1] :], axis=0) / 6.0
    turned = values.reshape(own, blocks, own, devices, width)
    turned = jnp.transpose(turned, (3, 1, 2, 0, 4))
    turned = [turned[:, b, :, :, : offsets[b + 1]] for b in range(blocks)]
    turned = lax.all_to_all(jnp.concatenate(turned, axis=3), ("gy", "gx"), 0, 0, tiled=True)
    turned = jnp.transpose(turned, (1, 2, 0, 3)).reshape(own, block, -1)

    slab = jnp.minimum(row, gx - 1 - row)
    far_row, far_col = row >= slabs, col >= gy // 2
    pick_rows = jnp.arange(rows)
    pick_rows = slab * rows + jnp.where(far_row, rows - pick_rows, pick_rows)
    pick_cols = jnp.arange(cols)
    pick_cols = jnp.where(far_col, (gy - col) * cols - pick_cols, col * cols + pick_cols)

    if rows == block:
        got, piece = [], None
        for messages in slab_messages(values, turned, side, offsets, slabs):
            if piece is not None:
                messages, piece = lax.optimization_barrier((messages, piece))
                got.append(gathered(piece, gy, got[-1] if got else None))
            piece = lax.all_to_all(messages, "gx", 0, 0, tiled=True)
        got.append(gathered(piece, gy, got[-1] if got else None))
        tiles = width // 128
        start = tile_groups(tiles)[0].stop * own * block
        side = jnp.stack([piece[:, start : start + 3 * own * tiles] for piece in got[0]])
        bit = gy // 2
        while bit:
            paired = side.reshape((-1, 2, bit) + side.shape[1:])
            side = jnp.where((col & bit) == 0, paired, paired[:, ::-1]).reshape(side.shape)
            bit //= 2
        side = side.reshape(devices, own, 3, width)
        side = jnp.transpose(side, (2, 1, 0, 3)).reshape(3, block, width)
        next_plane, across = side[0], rim_rows(side[1:], offsets, pick_rows)
        rim_col = col == gy // 2
        rim = across[:, pick_cols]
        return result_block(
            got, next_plane, across, rim, pick_cols, slab, far_row, rim_col, col, offsets
        )

    side = lax.all_gather(side, ("gy", "gx"), axis=0)
    side = jnp.transpose(side, (2, 1, 0, 3)).reshape(slabs + 1, block, width)
    across = rim_rows(side[slabs - 1 :], offsets, pick_rows)
    next_plane = lax.dynamic_index_in_dim(side, slab, 0, keepdims=False)
    sums = axis_order_sums(values, turned, offsets, block)
    messages = []
    for s in range(slabs):
        base, first = s * rows // block, s * rows
        units = []
        for b in range(blocks):
            size = (b + 1) * block
            near = jnp.zeros((own, rows, size))
            far = jnp.zeros((own, block, size))
            if b >= base:
                near = jnp.stack([sums[b][e][first : first + rows, :size] for e in range(own)])
            else:
                far = jnp.stack([sums[base][e][b * block : size, :size] for e in range(own)])
            units.append(jnp.concatenate([near, far], axis=1))
        messages.append(jnp.concatenate(units, axis=2))
    messages = jnp.stack(messages + messages[::-1])
    got = lax.all_to_all(messages, "gx", 0, 0, tiled=True)
    got = lax.all_gather(got, "gy", axis=0, tiled=True)
    got = jnp.swapaxes(got, 0, 1).reshape(block, rows + block, width)
    base = slab * rows // block
    lower = []
    for b in range(blocks):
        lanes = slice(offsets[b], offsets[b + 1])
        near = jnp.swapaxes(got[:, :rows, lanes], 0, 1)
        far = lax.dynamic_slice_in_dim(got[:, rows:, lanes], lax.rem(slab * rows, block), rows, 0)
        lower.append(jnp.where(b >= base, near, far))
    lower = jnp.concatenate(lower, axis=2)
    lower = jnp.concatenate([lower, next_plane[None]], axis=0)
    body = square([lower[:, :, offsets[b] : offsets[b + 1]] for b in range(blocks)], block)
    body = body[pick_rows - slab * rows]
    body = jnp.concatenate([body, across[:, None, :half]], axis=1)[:, pick_cols]
    body = jnp.concatenate([body, across[:, pick_cols][:, :, None]], axis=2)
    return jnp.concatenate([body, jnp.flip(body[:, :, 1:half], 2)], axis=2)


def rim_rows(side, offsets, pick_rows):
    blocks, block = len(offsets) - 1, offsets[1]
    half = blocks * block
    last = square([side[0][:, offsets[b] : offsets[b + 1]] for b in range(blocks)], block)
    rim = side[1, 0, : half + 1]
    last = jnp.concatenate([last, rim[None, :half]], axis=0)
    return jnp.concatenate([last, rim[:, None]], axis=1)[pick_rows]


def axis_order_sums(values, turned, offsets, block):
    start = 0
    sums = []
    for top in range(len(offsets) - 1):
        size = (top + 1) * block
        parts = []
        for e in range(values.shape[0]):
            part = values[e, :size, offsets[top] : offsets[top] + size]
            lower = [turned[e, :, start + offsets[b] : start + offsets[b + 1]] for b in range(top + 1)]
            parts.append(part + part.T + square(lower, block))
        sums.append(parts)
        start += offsets[top + 1]
    return sums


def message_kernel(offsets, slabs, values, turned, side, *messages):
    blocks, block = len(offsets) - 1, offsets[1]
    values, turned = values[...], turned[...]
    own = values.shape[0]
    sums = axis_order_sums(values, turned, offsets, block)
    groups = tile_groups(offsets[-1] // 128)
    side_start = groups[0].stop * own * block
    messages[0][:, side_start:] = jnp.zeros_like(messages[0][:, side_start:])
    for s in range(slabs):
        places = s, 2 * slabs - 1 - s
        for e in range(own):
            units = []
            for b in range(blocks):
                size = (b + 1) * block
                if b >= s:
                    units.append(sums[b][e][s * block : (s + 1) * block, :size])
                else:
                    units.append(sums[s][e][b * block : size, :size])
            line = jnp.concatenate(units, axis=1)
            for group, out in zip(groups, messages):
                for tile in range(group.start, group.stop):
                    start = ((tile - group.start) * own + e) * block
                    for place in places:
                        out[place, start : start + block] = line[:, tile * 128 : (tile + 1) * 128]
            row = side_start + 3 * e * groups[-1].stop
            for plane in (s, slabs - 1, slabs):
                for tile in range(groups[-1].stop):
                    part = side[e, plane : plane + 1, tile * 128 : (tile + 1) * 128]
                    for place in places:
                        messages[0][place, row : row + 1] = part
                    row += 1


def slab_messages(values, turned, side, offsets, slabs):
    own, block, tiles = values.shape[0], offsets[1], offsets[-1] // 128
    sizes = [(group.stop - group.start) * own * block for group in tile_groups(tiles)]
    sizes[0] += -(-3 * own * tiles // 8) * 8
    return pl.pallas_call(
        lambda *refs: message_kernel(offsets, slabs, *refs),
        in_specs=[pl.BlockSpec(memory_space=pltpu.VMEM)] * 3,
        out_specs=[pl.BlockSpec(memory_space=pltpu.VMEM)] * len(sizes),
        out_shape=[jax.ShapeDtypeStruct((2 * slabs, size, 128), jnp.float32) for size in sizes],
        compiler_params=pltpu.CompilerParams(vmem_limit_bytes=VMEM_BYTES),
    )(values, turned, side)


def result_kernel(
    offsets, own, devices, groups, places, next_plane, across, rim, pick, flip, *refs
):
    blocks, block = len(offsets) - 1, offsets[1]
    tiles = offsets[-1] // 128
    peers = (len(refs) - 2) // len(groups) - 1
    pieces, out = refs[: peers * len(groups)], refs[peers * len(groups)]
    held, sems = refs[peers * len(groups) + 1 : -1], refs[-1]
    step_rows, cols, length = out.shape
    half = length // 2
    slab, far_row, rim_col, me = places[0], places[1], places[2], places[3]
    lane = lax.broadcasted_iota(jnp.int32, (block, 128), 1)
    at_rim = lax.broadcasted_iota(jnp.int32, (cols, half), 0) + (1 - rim_col) == 0
    rim_lane = lax.broadcasted_iota(jnp.int32, rim.shape, 1)
    first_lane = lax.broadcasted_iota(jnp.int32, (cols, half), 1) == 0

    @pl.when(pl.program_id(0) == 0)
    def _():
        copies = []
        for g in range(len(groups)):
            for peer in range(peers):
                piece = pieces[g * peers + peer]
                size = piece.shape[0]
                spot = pl.ds(pl.multiple_of((me ^ peer) * size, size), size)
                copies.append(pltpu.make_async_copy(piece, held[g].at[spot], sems.at[g, peer]))
        for copy in copies:
            copy.start()
        for copy in copies:
            copy.wait()

    def left_half(r):
        t = pl.program_id(0) * step_rows + r
        i = jnp.where(far_row == 1, block - t, t)
        inside = (jnp.zeros((block, 128), jnp.int32) + i) < block
        i = jnp.minimum(i, block - 1)
        source = lax.div(i, devices), lax.rem(i, devices)
        parts = []
        for g, group in enumerate(groups):
            stride = held[g].shape[0] // devices
            for tile in range(group.start, group.stop):
                start = (tile - group.start) * own * block
                near = [
                    held[g][pl.ds(start + e * block + i, devices, stride=stride), :]
                    for e in range(own)
                ]
                near = jnp.concatenate(near, axis=0)
                far = pl.multiple_of(source[1] * stride + start + source[0] * block, 8)
                far = held[g][pl.ds(far, block), :]
                kind = jnp.zeros((block, 128), jnp.int32)
                for b in range(1, blocks):
                    kind += (lane + tile * 128 >= offsets[b]).astype(jnp.int32)
                line = jnp.where(kind >= slab, near, far)
                line = jnp.where(inside, line, next_plane[:, pl.ds(tile * 128, 128)])
                parts.append(line)
        line = jnp.concatenate(parts, axis=1)
        plane = square([line[:, offsets[b] : offsets[b + 1]] for b in range(blocks)], block)
        high, low = split(plane)
        left = jnp.dot(pick[...], high, preferred_element_type=jnp.float32)
        left += jnp.dot(pick[...], low, preferred_element_type=jnp.float32)
        left = jnp.where(at_rim, across[pl.ds(t, 1), :], left)
        out[r, :, pl.ds(0, half)] = left
        return left

    together = 4

    @pl.loop(0, step_rows // together)
    def _(c):
        left = [left_half(c * together + n) for n in range(together)]
        high, low = split(jnp.concatenate(left, axis=0))
        right = jnp.dot(high, flip[...], preferred_element_type=jnp.float32)
        right += jnp.dot(low, flip[...], preferred_element_type=jnp.float32)
        for n in range(together):
            r = c * together + n
            t = pl.program_id(0) * step_rows + r
            edge = jnp.sum(jnp.where(rim_lane == t, rim[...], 0.0), axis=1, keepdims=True)
            part = right[n * cols : (n + 1) * cols]
            out[r, :, pl.ds(half, half)] = jnp.where(first_lane, edge, part)


def result_block(got, next_plane, across, rim, pick_cols, slab, far_row, rim_col, col, offsets):
    block = offsets[1]
    gx = got[0][0].shape[0]
    groups = tile_groups(offsets[-1] // 128)
    devices = gx * len(got[0])
    own = block // devices
    rows, half = across.shape[0], across.shape[1] - 1
    cols = pick_cols.shape[0]
    step_rows = 8
    places = jnp.stack([slab, far_row.astype(jnp.int32), rim_col.astype(jnp.int32), col])
    cell = jnp.arange(half)
    pick = (pick_cols[:, None] == cell[None, :]).astype(jnp.bfloat16)
    flip = (cell[:, None] + cell[None, :] == half).astype(jnp.bfloat16)
    rim = jnp.pad(rim.T, ((0, 0), (0, 128 - rows)))
    whole = lambda array: pl.BlockSpec(array.shape, lambda i: (0,) * array.ndim)
    arrays = (next_plane, across[:, :half], rim, pick, flip)
    pieces = [piece.reshape(-1, 128) for group in got for piece in group]
    return pl.pallas_call(
        lambda *refs: result_kernel(offsets, own, devices, groups, *refs),
        grid=(rows // step_rows,),
        in_specs=[pl.BlockSpec(memory_space=pltpu.SMEM)] + [whole(array) for array in arrays]
        + [pl.BlockSpec(memory_space=pl.ANY)] * len(pieces),
        out_specs=pl.BlockSpec((step_rows, cols, 2 * half), lambda i: (i, 0, 0)),
        out_shape=jax.ShapeDtypeStruct((rows, cols, 2 * half), jnp.float32),
        scratch_shapes=[
            pltpu.VMEM((devices * group[0].shape[1], 128), jnp.float32) for group in got
        ] + [pltpu.SemaphoreType.DMA((len(groups), len(got[0])))],
        compiler_params=pltpu.CompilerParams(vmem_limit_bytes=VMEM_BYTES),
    )(places, *arrays, *pieces)


def tile_groups(tiles):
    return [slice(tile, min(tile + 2, tiles)) for tile in range(0, tiles, 2)]


def swap(peers, bit):
    return [(q, q ^ bit) for q in range(peers)]


def gathered(piece, peers, after):
    if after is not None:
        piece, first_hops = lax.optimization_barrier((piece, after[1:3]))
        after[1:3] = first_hops
    pieces, bit = {0: piece}, peers // 2
    while bit:
        for place in list(pieces):
            pieces[place ^ bit] = lax.ppermute(pieces[place], "gy", swap(peers, bit))
        bit //= 2
    return [pieces[place] for place in range(peers)]


def exchanged(packed):
    gy = len(packed)
    return [packed[0]] + [lax.ppermute(packed[p], "gy", swap(gy, p)) for p in range(1, gy)]


def sent_lines(got, count, after):
    gy = len(got)
    lines = [sum(got[p][:count] for p in range(first, gy, 2)) for first in range(2)]
    lines = jnp.concatenate(lines + [sum(piece[count:] for piece in got)], axis=0)
    lines = jnp.transpose(lines, (2, 1, 0, 3))
    if after is not None:
        lines, _ = lax.optimization_barrier((lines, after))
    return lax.all_to_all(lines, "gx", 0, 0, tiled=True)


def first_axis(lines, table):
    gx, _, count, half = table.shape
    table = table.reshape(gx, 2 * count, half)
    return jnp.einsum("geaw,gai->eiw", lines[:, :, : 2 * count], table, precision=HIGH)


def row_parts(rows):
    if rows < 4 * PART_STEP:
        return [slice(0, rows)]
    return [slice(PART_STEP, rows - PART_STEP), slice(0, PART_STEP), slice(rows - PART_STEP, rows)]


def square(lower, block):
    lines = []
    for b in range(len(lower)):
        parts = [lower[b]]
        for c in range(b + 1, len(lower)):
            part = lower[c][..., b * block : (b + 1) * block]
            parts.append(jnp.swapaxes(part, -1, -2))
        lines.append(jnp.concatenate(parts, axis=-1))
    return jnp.concatenate(lines, axis=-2)


def solution(mesh):
    placed = (P("gx", "gy", None), P())
    return jax.shard_map(
        on_device, mesh=mesh, in_specs=placed, out_specs=P("gx", "gy", None), check_vma=False
    )
```

```python
import math

import jax
import jax.numpy as jnp
import numpy as np
from jax import lax
from jax.experimental import pallas as pl
from jax.experimental.pallas import tpu as pltpu
from jax.sharding import PartitionSpec as P

SWEEPS = 2

AXIS_ORDERS = ((0, 1, 2), (0, 2, 1), (1, 0, 2), (1, 2, 0), (2, 0, 1), (2, 1, 0))

HIGH = lax.Precision.HIGH


def ring(axis):
    peers = lax.axis_size(axis)
    up = [(i, (i + 1) % peers) for i in range(peers)]
    return up, [(j, i) for i, j in up]


FREE = ((8 - SWEEPS, 8 - SWEEPS), (0, 0))


def side_faces(block):
    cols = block.shape[1]
    right, left = ring("gy")
    before = lax.ppermute(block[:, cols - SWEEPS :], "gy", right)
    after = lax.ppermute(block[:, :SWEEPS], "gy", left)
    return jnp.concatenate([before, after], axis=1)


def end_faces(block, sides):
    rows = block.shape[0]
    up, down = ring("gx")
    last = jnp.concatenate([block[rows - SWEEPS :], sides[rows - SWEEPS :]], axis=1)
    first = jnp.concatenate([block[:SWEEPS], sides[:SWEEPS]], axis=1)
    return lax.ppermute(last, "gx", up), lax.ppermute(first, "gx", down)


def mirror(values, axis):
    return jnp.roll(jnp.flip(values, axis), 1, axis)


def symmetric_marks(marks):
    for flip_axis in range(3):
        marks = jnp.maximum(marks, mirror(marks, flip_axis))
    united = marks
    for axis_order in AXIS_ORDERS[1:]:
        united = jnp.maximum(united, jnp.transpose(marks, axis_order))
    return united


def cosine_table(length):
    position = np.arange(length)
    phases = np.mod(position[:, None] * position[None, : length // 2 + 1], length)
    return (np.cos(phases * (2.0 * math.pi / length)) / math.sqrt(length)).astype(np.float32)


MARGIN = 16
CHUNK = 16
STEP_ROWS = 16
PART_STEP = 8
VMEM_BYTES = 56 * 1024 * 1024


def split(values):
    high = values.astype(jnp.bfloat16)
    low = (values - high.astype(jnp.float32)).astype(jnp.bfloat16)
    return high, low


def fill_kernel(
    base, here, above, below, top, bottom, sides, marks, table_high, table_low,
    spectrum, alternate, edge, punched, once, high, low, folded,
):
    step_rows, cols, length = here.shape
    step = base[pl.program_id(0)]
    first_row = step * step_rows
    local_row = pl.program_id(0) * step_rows
    period = marks.shape[0]
    lane = lax.broadcasted_iota(jnp.int32, (128, 128), 1)
    signs = jnp.where(lax.broadcasted_iota(jnp.int32, (128, 128), 0) % 2 == 0, 1.0, -1.0)

    @pl.when(pl.program_id(0) == 0)
    def _():
        edge[...] = jnp.zeros_like(edge)

    def holes(row, start, size):
        row = lax.rem(first_row + row, period)
        start = start % period
        if start + size <= period:
            part = marks[row, pl.ds(start, size), :]
        else:
            part = jnp.concatenate(
                [marks[row, pl.ds(start, period - start), :], marks[row, pl.ds(0, start + size - period), :]],
                axis=0,
            )
        return jnp.concatenate([part] * (length // 128), axis=1)

    def punch(row, start, values):
        kept = jnp.where(holes(row, start, values.shape[0]) > 0.0, 0.0, values)
        punched[row, pl.ds(start, values.shape[0]), :] = kept

    def punch_row(row, source, index):
        for c in range(0, cols, CHUNK):
            punch(row, MARGIN + c, source[index, pl.ds(c, CHUNK), :])

    def punch_sides(row):
        full = first_row + row - SWEEPS
        punch(row, MARGIN - 8, sides[full, pl.ds(0, 8), :])
        punch(row, MARGIN + cols, sides[full, pl.ds(8, 8), :])

    def neighbours(ref, row, start):
        middle = ref[row, pl.ds(start, CHUNK), :]
        total = ref[row - 1, pl.ds(start, CHUNK), :] + ref[row + 1, pl.ds(start, CHUNK), :]
        total += ref[row, pl.ds(start - 1, CHUNK), :] + ref[row, pl.ds(start + 1, CHUNK), :]
        return total + pltpu.roll(middle, 1, 1) + pltpu.roll(middle, length - 1, 1)

    last = sides.shape[0] // step_rows - 1
    for edge_rows, inside, offset, outer in (
        (above, step > 0, 0, top),
        (below, step < last, step_rows + SWEEPS, bottom),
    ):
        @pl.when(inside)
        def _():
            for r in range(SWEEPS):
                punch_row(offset + r, edge_rows, r)
                punch_sides(offset + r)

        @pl.when(jnp.logical_not(inside))
        def _():
            for r in range(SWEEPS):
                punch_row(offset + r, outer, r)
                punch(offset + r, MARGIN - SWEEPS, outer[r, pl.ds(cols, SWEEPS), :])
                punch(offset + r, MARGIN + cols, outer[r, pl.ds(cols + SWEEPS, SWEEPS), :])

    @pl.loop(0, step_rows)
    def _(r):
        punch_row(r + SWEEPS, here, r)
        punch_sides(r + SWEEPS)

    @pl.loop(1, step_rows + 2 * SWEEPS - 1, unroll=2)
    def _(r):
        for start in range(MARGIN - 8, MARGIN + cols + 8, CHUNK):
            total = neighbours(punched, r, start) * holes(r, start, CHUNK)
            once[r, pl.ds(start, CHUNK), :] = punched[r, pl.ds(start, CHUNK), :] + total

    @pl.loop(0, step_rows)
    def _(r):
        for c in range(0, cols, CHUNK):
            start = MARGIN + c
            total = neighbours(once, r + SWEEPS, start) * holes(r + SWEEPS, start, CHUNK)
            filled = punched[r + SWEEPS, pl.ds(start, CHUNK), :] + total
            first, second = split(filled)
            spot = pl.ds(pl.multiple_of(r * cols + c, CHUNK), CHUNK)
            high[spot, :] = first
            low[spot, :] = second
            wrapped = filled[:, :128]
            for tile in range(1, length // 128):
                wrapped += filled[:, tile * 128 : (tile + 1) * 128]
            folded[pl.ds(c, CHUNK), :] = wrapped
        column = jnp.where(lane == local_row + r, signs, 0.0).astype(jnp.bfloat16)
        first, second = split(folded[...])
        total = jnp.dot(first, column, preferred_element_type=jnp.float32)
        total += jnp.dot(second, column, preferred_element_type=jnp.float32)
        edge[...] += total

    rows_each = 8
    half = spectrum.shape[2]
    order = lax.broadcasted_iota(jnp.int32, (rows_each, cols, half), 1)

    @pl.loop(0, step_rows // rows_each)
    def _(r):
        spot = pl.ds(pl.multiple_of(r * rows_each * cols, CHUNK), rows_each * cols)
        first, second = high[spot, :], low[spot, :]
        total = jnp.dot(first, table_low[...], preferred_element_type=jnp.float32)
        total += jnp.dot(second, table_high[...], preferred_element_type=jnp.float32)
        total += jnp.dot(first, table_high[...], preferred_element_type=jnp.float32)
        total = total.reshape(rows_each, cols, half)
        spectrum[pl.ds(r * rows_each, rows_each)] = total
        signed = jnp.sum(jnp.where(order % 2 == 0, total, -total), axis=1)
        alternate[pl.ds(pl.multiple_of(r * rows_each, rows_each), rows_each), :] = signed


def rounded_parts(table):
    rounded = lax.reduce_precision(table, 8, 7)
    return rounded.astype(jnp.bfloat16), (table - rounded).astype(jnp.bfloat16)


def marks_kernel(shifts, template, out, held):
    period = template.shape[0]
    repeats = held.shape[1] // period
    line = lax.broadcasted_iota(jnp.int32, (period, period), 0)
    across = lax.broadcasted_iota(jnp.int32, (period, period), 1)
    flip = jnp.where((line + across) % period == 0, 1.0, 0.0)
    for i in range(period):
        plane = jnp.maximum(template[i], template[-i % period]).astype(jnp.float32)
        plane = jnp.maximum(plane, jnp.dot(flip, plane, preferred_element_type=jnp.float32))
        plane = jnp.maximum(plane, jnp.dot(plane, flip, preferred_element_type=jnp.float32))
        plane = jnp.maximum(plane, plane.T)
        held[i * period : (i + 1) * period, :] = jnp.concatenate([plane] * repeats, axis=1)
    for i in range(period):
        plane = held[i * period : (i + 1) * period, :]
        turned = held[pl.ds(i, period, stride=period), :]
        back = turned[:, :period].T
        plane = jnp.maximum(jnp.maximum(plane, turned), jnp.concatenate([back] * repeats, axis=1))
        plane = jnp.where(plane == 1.0, 1.0 / 6.0, 0.0)
        shift = shifts[1]
        out[(i - shifts[0]) % period] = jnp.concatenate([plane[shift:], plane[:shift]], axis=0)


def hole_marks(template, row, col, rows, cols):
    period = template.shape[0]
    shape = (period, period, 128)
    if rows % period == 0 and cols % period == 0:
        shifts = (-SWEEPS % period, -MARGIN % period)
        return pl.pallas_call(
            lambda *refs: marks_kernel(shifts, *refs),
            in_specs=[pl.BlockSpec(memory_space=pltpu.VMEM)],
            out_specs=pl.BlockSpec(memory_space=pltpu.VMEM),
            out_shape=jax.ShapeDtypeStruct(shape, jnp.float32),
            scratch_shapes=[pltpu.VMEM((period * period, 128), jnp.float32)],
        )(template)
    shifts = (jnp.mod(row * rows - SWEEPS, period), jnp.mod(col * cols - MARGIN, period))
    marks = jnp.roll(symmetric_marks(template), (-shifts[0], -shifts[1]), (0, 1))
    return jnp.tile(marks.astype(jnp.float32) / 6.0, (1, 1, 128 // period))


def fill_constants(intensity, template, row, col, main):
    rows, cols, _ = intensity.shape
    high = main.astype(jnp.bfloat16)
    low = (main - high.astype(np.float32)).astype(jnp.bfloat16)
    return hole_marks(template, row, col, rows, cols), jnp.asarray(high), jnp.asarray(low)


def filled_spectrum(intensity, arrays, first, parts):
    rows, cols, length = intensity.shape
    half = length // 2
    aligned = all(edge % STEP_ROWS == 0 for part in parts for edge in (part.start, part.stop))
    step_rows = STEP_ROWS if aligned else PART_STEP
    starts = [start for part in parts for start in range(part.start, part.stop, step_rows)]
    count = step_rows * len(starts)
    steps = jnp.stack([(first + start) // step_rows for start in starts])
    pairs = step_rows // SWEEPS
    last = rows // SWEEPS - 1
    whole = lambda array: pl.BlockSpec(array.shape, lambda i, b: (0,) * array.ndim)
    before = lambda i, b: (jnp.maximum(b[i] * pairs - 1, 0), 0, 0)
    after = lambda i, b: (jnp.minimum((b[i] + 1) * pairs, last), 0, 0)
    padded = (step_rows + 2 * SWEEPS, cols + 2 * MARGIN, length)
    return pl.pallas_call(
        fill_kernel,
        grid_spec=pltpu.PrefetchScalarGridSpec(
            num_scalar_prefetch=1,
            grid=(len(starts),),
            in_specs=[
                pl.BlockSpec((step_rows, cols, length), lambda i, b: (b[i], 0, 0)),
                pl.BlockSpec((SWEEPS, cols, length), before),
                pl.BlockSpec((SWEEPS, cols, length), after),
            ] + [whole(array) for array in arrays],
            out_specs=[
                pl.BlockSpec((step_rows, cols, half), lambda i, b: (i, 0, 0)),
                pl.BlockSpec((step_rows, half), lambda i, b: (i, 0)),
                pl.BlockSpec((cols, 128), lambda i, b: (0, 0)),
            ],
            scratch_shapes=[
                pltpu.VMEM(padded, jnp.float32),
                pltpu.VMEM(padded, jnp.float32),
                pltpu.VMEM((step_rows * cols, length), jnp.bfloat16),
                pltpu.VMEM((step_rows * cols, length), jnp.bfloat16),
                pltpu.VMEM((cols, 128), jnp.float32),
            ],
        ),
        out_shape=[
            jax.ShapeDtypeStruct((count, cols, half), jnp.float32),
            jax.ShapeDtypeStruct((count, half), jnp.float32),
            jax.ShapeDtypeStruct((cols, 128), jnp.float32),
        ],
        compiler_params=pltpu.CompilerParams(vmem_limit_bytes=VMEM_BYTES),
        cost_estimate=pl.CostEstimate(
            flops=count * cols * length * half * 6,
            bytes_accessed=count * cols * (length + half) * 4,
            transcendentals=0,
        ),
    )(steps, intensity, intensity, intensity, *arrays)


def pack(section, offsets):
    block = offsets[1]
    units = [section[b * block : (b + 1) * block, : (b + 1) * block] for b in range(len(offsets) - 1)]
    return jnp.concatenate(units, axis=1)


def three_dots(left, right):
    total = jnp.dot(left[1], right[0], preferred_element_type=jnp.float32)
    total += jnp.dot(left[0], right[1], preferred_element_type=jnp.float32)
    return total + jnp.dot(left[0], right[0], preferred_element_type=jnp.float32)


def section_kernel(
    offsets, closing, me, weights, kept, got, cols_high, cols_low, rows_high, rows_low,
    rim, corner, before, *refs
):
    step, steps = pl.program_id(0), pl.num_programs(0)
    step_rows = kept.shape[0]
    half, count = rows_high.shape
    planes, block, width = before.shape
    *outs, total, lines, packed = refs
    gy, (_, own, gx, _) = len(outs), outs[0].shape

    def place(layer, values, slot=0):
        packed[slot] = values
        for e in range(own):
            for p in range(gy):
                start = pl.multiple_of((e * gy + (p ^ me[0])) * gx, gx)
                outs[p][layer, e] = packed[slot, pl.ds(start, gx), :]

    @pl.when(step == 0)
    def _():
        total[...] = before[...]

    for r in range(step_rows):
        layer = step * step_rows + r
        values = jnp.concatenate([kept[r], got[r]], axis=0)
        section = three_dots((cols_high[...], cols_low[...]), split(values))
        section = section + section.T
        line = pack(section, offsets)
        place(layer, line, r)
        for m in range(planes):
            total[m] += weights[m, layer] * line
        for m in range(planes - 1):
            row = (m + 1) * (half // planes)
            lines[m, pl.ds(layer, 1), :] = section[row : row + 1]

    @pl.when(step == steps - 1)
    def _():
        for m in range(planes - 1):
            plane = three_dots((rows_high[...], rows_low[...]), split(lines[m]))
            total[m] += pack(plane + plane.T, offsets)
        if closing:
            total[planes - 1] += pack(rim[...] + rim[...].T, offsets)
            for m in range(planes):
                place(count + m, total[m])
            place(count + planes, jnp.zeros((block, width), jnp.float32) + corner[...])


def packed_section(col, kept, got, first, table_pair, table_rows, marks, rim, corner, before, offsets, shape, closing):
    _, cols, half = kept.shape
    count = table_rows.shape[0]
    planes, block, width = before.shape
    gx, gy = shape
    step_rows = 4
    layers = count + (planes + 1 if closing else 0)
    whole = lambda array: pl.BlockSpec(array.shape, lambda i: (0,) * array.ndim)
    weights = jnp.stack([table_rows[:, m] for m in marks])
    arrays = rounded_parts(table_pair.T) + rounded_parts(table_rows[:, :half].T)
    arrays += (rim, corner[None], before)
    out = jax.ShapeDtypeStruct((layers, block // (gx * gy), gx, width), jnp.float32)
    outs = [out] * gy + [jax.ShapeDtypeStruct(before.shape, jnp.float32)]
    rows_spec = pl.BlockSpec((step_rows, cols, half), lambda i: (i + first // step_rows, 0, 0))
    return pl.pallas_call(
        lambda *refs: section_kernel(offsets, closing, *refs),
        grid=(count // step_rows,),
        in_specs=[pl.BlockSpec(memory_space=pltpu.SMEM)] * 2 + [rows_spec, rows_spec]
        + [whole(array) for array in arrays],
        out_specs=[whole(out) for out in outs],
        out_shape=outs,
        scratch_shapes=[
            pltpu.VMEM((planes, count, half), jnp.float32),
            pltpu.VMEM((step_rows, block, width), jnp.float32),
        ],
        compiler_params=pltpu.CompilerParams(vmem_limit_bytes=VMEM_BYTES),
        cost_estimate=pl.CostEstimate(
            flops=count * 12 * cols * half * half,
            bytes_accessed=count * cols * half * 16,
            transcendentals=0,
        ),
    )(col.reshape(1), weights, kept, got, *arrays)


def on_device(intensity, template):
    rows, cols, length = intensity.shape
    gx, gy = lax.axis_size("gx"), lax.axis_size("gy")
    row, col = lax.axis_index("gx"), lax.axis_index("gy")
    devices, half = gx * gy, length // 2
    block = max(devices, rows)
    blocks, own, slabs = half // block, block // devices, gx // 2
    offsets = [block * b * (b + 1) // 2 for b in range(blocks + 1)]
    width = offsets[blocks]
    table = jnp.asarray(cosine_table(length))
    main = table[:, :half]

    pair_rows = rows // 2
    parts = row_parts(pair_rows)
    counts = [part.stop - part.start for part in parts]
    core = lax.rem(col, 2)
    constants = fill_constants(intensity, template, row, col, cosine_table(length)[:, :half])
    sides = side_faces(intensity)
    given_first, kept_first = (1 - core) * pair_rows, core * pair_rows
    inner = parts[0].start >= SWEEPS and parts[0].stop <= pair_rows - SWEEPS
    side_columns = jnp.pad(sides, ((0, 0),) + FREE)
    blank = jnp.zeros((SWEEPS, cols + 2 * SWEEPS, length), jnp.float32)
    ends = (blank, blank) if inner else end_faces(intensity, sides)

    def fill(some, start):
        arrays = tuple(ends) + (side_columns,) + constants
        return list(filled_spectrum(intensity, arrays, start, some))

    given, kept = [fill(parts[:1], given_first)], []
    outer = ends
    if inner:
        given[0], late_sides = lax.optimization_barrier((given[0], sides))
        outer = end_faces(intensity, late_sides)
    kept.append(fill(parts[:1], kept_first))
    ends = outer

    table_cols = lax.dynamic_slice_in_dim(table, col * cols, cols, 0)
    kept_rows = lax.dynamic_slice_in_dim(table, row * rows + kept_first, pair_rows, 0)
    marks = [rows * (m + 1) for m in range(slabs)]
    mates = lax.dynamic_slice_in_dim(main, (col + 1 - 2 * core) * cols, cols, 0)
    table_pair = jnp.concatenate([table_cols[:, :half], mates], axis=0)
    table_parts = main.reshape(gx, 2, pair_rows, half) / 6.0
    table_parts = jnp.where(core == 0, table_parts, table_parts[:, ::-1])
    table_parts = [table_parts[:, :, part] for part in parts]
    side = jnp.zeros((slabs, block, width), jnp.float32)
    rim, corner = jnp.zeros((half, half), jnp.float32), jnp.zeros((width,), jnp.float32)
    values, packed, lines = 0.0, None, None
    for c, count in enumerate(counts):
        closing = c == len(counts) - 1
        if c > 0:
            if c == 1:
                start, packed = lax.optimization_barrier((given_first, packed))
                given.append(fill(parts[1:], start))
            got_lines = exchanged(packed)
            if c == 1:
                behind = kept_first, got_lines, given[1][0]
                start, got_lines, given[1][0] = lax.optimization_barrier(behind)
                kept.append(fill(parts[1:], start))
        if c < 2:
            got = lax.ppermute(given[c][0], "gy", swap(gy, 1))
            held = kept[c][0]
        if c > 0:
            lines = sent_lines(got_lines, counts[c - 1], lines)
            values = values + first_axis(lines, table_parts[c - 1])
        if closing:
            given_rows = lax.dynamic_slice_in_dim(table, row * rows + given_first, pair_rows, 0)
            ordered_rows = [held_rows[part] for held_rows in (given_rows, kept_rows) for part in parts]
            ordered_rows = jnp.concatenate(ordered_rows, axis=0)
            alternate = jnp.concatenate([piece[1] for piece in given + kept], axis=0) / math.sqrt(length)
            edge = [piece[2][:, : piece[1].shape[0]] for piece in given + kept]
            edge = jnp.concatenate(edge, axis=1)
            edge = jnp.einsum("ba,bk->ak", edge / math.sqrt(length), table_cols, precision=HIGH)
            edge = edge + jnp.concatenate([alternate, edge[:, half:]], axis=1)
            rim = jnp.einsum("aj,ak->jk", ordered_rows[:, :half], edge[:, :half], precision=HIGH)
            corner = 2.0 * jnp.einsum("a,ak->k", ordered_rows[:, half], edge, precision=HIGH)
            corner = corner + jnp.einsum("aj,a->j", ordered_rows, edge[:, half], precision=HIGH)
            corner = jnp.pad(corner, (0, width - half - 1))

        *packed, side = packed_section(
            col, held, got, sum(counts[1:c]), table_pair, kept_rows[parts[c]], marks,
            rim, corner, side, offsets, (gx, gy), closing,
        )
    lines = sent_lines(exchanged(packed), counts[-1], lines)
    values = values + first_axis(lines, table_parts[-1])
    side = jnp.sum(lines[:, :, 2 * counts[-1] :], axis=0) / 6.0
    turned = values.reshape(own, blocks, own, devices, width)
    turned = jnp.transpose(turned, (3, 1, 2, 0, 4))
    turned = [turned[:, b, :, :, : offsets[b + 1]] for b in range(blocks)]
    turned = lax.all_to_all(jnp.concatenate(turned, axis=3), ("gy", "gx"), 0, 0, tiled=True)
    turned = jnp.transpose(turned, (1, 2, 0, 3)).reshape(own, block, -1)

    slab = jnp.minimum(row, gx - 1 - row)
    far_row, far_col = row >= slabs, col >= gy // 2
    pick_rows = jnp.arange(rows)
    pick_rows = slab * rows + jnp.where(far_row, rows - pick_rows, pick_rows)
    pick_cols = jnp.arange(cols)
    pick_cols = jnp.where(far_col, (gy - col) * cols - pick_cols, col * cols + pick_cols)

    if rows == block:
        got, piece = [], None
        for messages in slab_messages(values, turned, side, offsets, slabs):
            if piece is not None:
                messages, piece = lax.optimization_barrier((messages, piece))
                got.append(gathered(piece, gy, got[-1] if got else None))
            piece = lax.all_to_all(messages, "gx", 0, 0, tiled=True)
        got.append(gathered(piece, gy, got[-1] if got else None))
        tiles = width // 128
        start = tile_groups(tiles)[0].stop * own * block
        side = jnp.stack([piece[:, start : start + 3 * own * tiles] for piece in got[0]])
        bit = gy // 2
        while bit:
            paired = side.reshape((-1, 2, bit) + side.shape[1:])
            side = jnp.where((col & bit) == 0, paired, paired[:, ::-1]).reshape(side.shape)
            bit //= 2
        side = side.reshape(devices, own, 3, width)
        side = jnp.transpose(side, (2, 1, 0, 3)).reshape(3, block, width)
        next_plane, across = side[0], rim_rows(side[1:], offsets, pick_rows)
        rim_col = col == gy // 2
        rim = across[:, pick_cols]
        return result_block(
            got, next_plane, across, rim, pick_cols, slab, far_row, rim_col, col, offsets
        )

    side = lax.all_gather(side, ("gy", "gx"), axis=0)
    side = jnp.transpose(side, (2, 1, 0, 3)).reshape(slabs + 1, block, width)
    across = rim_rows(side[slabs - 1 :], offsets, pick_rows)
    next_plane = lax.dynamic_index_in_dim(side, slab, 0, keepdims=False)
    sums = axis_order_sums(values, turned, offsets, block)
    messages = []
    for s in range(slabs):
        base, first = s * rows // block, s * rows
        units = []
        for b in range(blocks):
            size = (b + 1) * block
            near = jnp.zeros((own, rows, size))
            far = jnp.zeros((own, block, size))
            if b >= base:
                near = jnp.stack([sums[b][e][first : first + rows, :size] for e in range(own)])
            else:
                far = jnp.stack([sums[base][e][b * block : size, :size] for e in range(own)])
            units.append(jnp.concatenate([near, far], axis=1))
        messages.append(jnp.concatenate(units, axis=2))
    messages = jnp.stack(messages + messages[::-1])
    got = lax.all_to_all(messages, "gx", 0, 0, tiled=True)
    got = lax.all_gather(got, "gy", axis=0, tiled=True)
    got = jnp.swapaxes(got, 0, 1).reshape(block, rows + block, width)
    base = slab * rows // block
    lower = []
    for b in range(blocks):
        lanes = slice(offsets[b], offsets[b + 1])
        near = jnp.swapaxes(got[:, :rows, lanes], 0, 1)
        far = lax.dynamic_slice_in_dim(got[:, rows:, lanes], lax.rem(slab * rows, block), rows, 0)
        lower.append(jnp.where(b >= base, near, far))
    lower = jnp.concatenate(lower, axis=2)
    lower = jnp.concatenate([lower, next_plane[None]], axis=0)
    body = square([lower[:, :, offsets[b] : offsets[b + 1]] for b in range(blocks)], block)
    body = body[pick_rows - slab * rows]
    body = jnp.concatenate([body, across[:, None, :half]], axis=1)[:, pick_cols]
    body = jnp.concatenate([body, across[:, pick_cols][:, :, None]], axis=2)
    return jnp.concatenate([body, jnp.flip(body[:, :, 1:half], 2)], axis=2)


def rim_rows(side, offsets, pick_rows):
    blocks, block = len(offsets) - 1, offsets[1]
    half = blocks * block
    last = square([side[0][:, offsets[b] : offsets[b + 1]] for b in range(blocks)], block)
    rim = side[1, 0, : half + 1]
    last = jnp.concatenate([last, rim[None, :half]], axis=0)
    return jnp.concatenate([last, rim[:, None]], axis=1)[pick_rows]


def axis_order_sums(values, turned, offsets, block):
    start = 0
    sums = []
    for top in range(len(offsets) - 1):
        size = (top + 1) * block
        parts = []
        for e in range(values.shape[0]):
            part = values[e, :size, offsets[top] : offsets[top] + size]
            lower = [turned[e, :, start + offsets[b] : start + offsets[b + 1]] for b in range(top + 1)]
            parts.append(part + part.T + square(lower, block))
        sums.append(parts)
        start += offsets[top + 1]
    return sums


def message_kernel(offsets, slabs, values, turned, side, *messages):
    blocks, block = len(offsets) - 1, offsets[1]
    values, turned = values[...], turned[...]
    own = values.shape[0]
    sums = axis_order_sums(values, turned, offsets, block)
    groups = tile_groups(offsets[-1] // 128)
    side_start = groups[0].stop * own * block
    messages[0][:, side_start:] = jnp.zeros_like(messages[0][:, side_start:])
    for s in range(slabs):
        places = s, 2 * slabs - 1 - s
        for e in range(own):
            units = []
            for b in range(blocks):
                size = (b + 1) * block
                if b >= s:
                    units.append(sums[b][e][s * block : (s + 1) * block, :size])
                else:
                    units.append(sums[s][e][b * block : size, :size])
            line = jnp.concatenate(units, axis=1)
            for group, out in zip(groups, messages):
                for tile in range(group.start, group.stop):
                    start = ((tile - group.start) * own + e) * block
                    for place in places:
                        out[place, start : start + block] = line[:, tile * 128 : (tile + 1) * 128]
            row = side_start + 3 * e * groups[-1].stop
            for plane in (s, slabs - 1, slabs):
                for tile in range(groups[-1].stop):
                    part = side[e, plane : plane + 1, tile * 128 : (tile + 1) * 128]
                    for place in places:
                        messages[0][place, row : row + 1] = part
                    row += 1


def slab_messages(values, turned, side, offsets, slabs):
    own, block, tiles = values.shape[0], offsets[1], offsets[-1] // 128
    sizes = [(group.stop - group.start) * own * block for group in tile_groups(tiles)]
    sizes[0] += -(-3 * own * tiles // 8) * 8
    return pl.pallas_call(
        lambda *refs: message_kernel(offsets, slabs, *refs),
        in_specs=[pl.BlockSpec(memory_space=pltpu.VMEM)] * 3,
        out_specs=[pl.BlockSpec(memory_space=pltpu.VMEM)] * len(sizes),
        out_shape=[jax.ShapeDtypeStruct((2 * slabs, size, 128), jnp.float32) for size in sizes],
        compiler_params=pltpu.CompilerParams(vmem_limit_bytes=VMEM_BYTES),
    )(values, turned, side)


def result_kernel(
    offsets, own, devices, groups, places, next_plane, across, rim, pick, flip, *refs
):
    blocks, block = len(offsets) - 1, offsets[1]
    tiles = offsets[-1] // 128
    peers = (len(refs) - 2) // len(groups) - 1
    pieces, out = refs[: peers * len(groups)], refs[peers * len(groups)]
    held, sems = refs[peers * len(groups) + 1 : -1], refs[-1]
    step_rows, cols, length = out.shape
    half = length // 2
    slab, far_row, rim_col, me = places[0], places[1], places[2], places[3]
    lane = lax.broadcasted_iota(jnp.int32, (block, 128), 1)
    at_rim = lax.broadcasted_iota(jnp.int32, (cols, half), 0) + (1 - rim_col) == 0
    rim_lane = lax.broadcasted_iota(jnp.int32, rim.shape, 1)
    first_lane = lax.broadcasted_iota(jnp.int32, (cols, half), 1) == 0

    @pl.when(pl.program_id(0) == 0)
    def _():
        copies = []
        for g in range(len(groups)):
            for peer in range(peers):
                piece = pieces[g * peers + peer]
                size = piece.shape[0]
                spot = pl.ds(pl.multiple_of((me ^ peer) * size, size), size)
                copies.append(pltpu.make_async_copy(piece, held[g].at[spot], sems.at[g, peer]))
        for copy in copies:
            copy.start()
        for copy in copies:
            copy.wait()

    def left_half(r):
        t = pl.program_id(0) * step_rows + r
        i = jnp.where(far_row == 1, block - t, t)
        inside = (jnp.zeros((block, 128), jnp.int32) + i) < block
        i = jnp.minimum(i, block - 1)
        source = lax.div(i, devices), lax.rem(i, devices)
        parts = []
        for g, group in enumerate(groups):
            stride = held[g].shape[0] // devices
            for tile in range(group.start, group.stop):
                start = (tile - group.start) * own * block
                near = [
                    held[g][pl.ds(start + e * block + i, devices, stride=stride), :]
                    for e in range(own)
                ]
                near = jnp.concatenate(near, axis=0)
                far = pl.multiple_of(source[1] * stride + start + source[0] * block, 8)
                far = held[g][pl.ds(far, block), :]
                kind = jnp.zeros((block, 128), jnp.int32)
                for b in range(1, blocks):
                    kind += (lane + tile * 128 >= offsets[b]).astype(jnp.int32)
                line = jnp.where(kind >= slab, near, far)
                line = jnp.where(inside, line, next_plane[:, pl.ds(tile * 128, 128)])
                parts.append(line)
        line = jnp.concatenate(parts, axis=1)
        plane = square([line[:, offsets[b] : offsets[b + 1]] for b in range(blocks)], block)
        high, low = split(plane)
        left = jnp.dot(pick[...], high, preferred_element_type=jnp.float32)
        left += jnp.dot(pick[...], low, preferred_element_type=jnp.float32)
        left = jnp.where(at_rim, across[pl.ds(t, 1), :], left)
        out[r, :, pl.ds(0, half)] = left
        return left

    together = 4

    @pl.loop(0, step_rows // together)
    def _(c):
        left = [left_half(c * together + n) for n in range(together)]
        high, low = split(jnp.concatenate(left, axis=0))
        right = jnp.dot(high, flip[...], preferred_element_type=jnp.float32)
        right += jnp.dot(low, flip[...], preferred_element_type=jnp.float32)
        for n in range(together):
            r = c * together + n
            t = pl.program_id(0) * step_rows + r
            edge = jnp.sum(jnp.where(rim_lane == t, rim[...], 0.0), axis=1, keepdims=True)
            part = right[n * cols : (n + 1) * cols]
            out[r, :, pl.ds(half, half)] = jnp.where(first_lane, edge, part)


def result_block(got, next_plane, across, rim, pick_cols, slab, far_row, rim_col, col, offsets):
    block = offsets[1]
    gx = got[0][0].shape[0]
    groups = tile_groups(offsets[-1] // 128)
    devices = gx * len(got[0])
    own = block // devices
    rows, half = across.shape[0], across.shape[1] - 1
    cols = pick_cols.shape[0]
    step_rows = 8
    places = jnp.stack([slab, far_row.astype(jnp.int32), rim_col.astype(jnp.int32), col])
    cell = jnp.arange(half)
    pick = (pick_cols[:, None] == cell[None, :]).astype(jnp.bfloat16)
    flip = (cell[:, None] + cell[None, :] == half).astype(jnp.bfloat16)
    rim = jnp.pad(rim.T, ((0, 0), (0, 128 - rows)))
    whole = lambda array: pl.BlockSpec(array.shape, lambda i: (0,) * array.ndim)
    arrays = (next_plane, across[:, :half], rim, pick, flip)
    pieces = [piece.reshape(-1, 128) for group in got for piece in group]
    return pl.pallas_call(
        lambda *refs: result_kernel(offsets, own, devices, groups, *refs),
        grid=(rows // step_rows,),
        in_specs=[pl.BlockSpec(memory_space=pltpu.SMEM)] + [whole(array) for array in arrays]
        + [pl.BlockSpec(memory_space=pl.ANY)] * len(pieces),
        out_specs=pl.BlockSpec((step_rows, cols, 2 * half), lambda i: (i, 0, 0)),
        out_shape=jax.ShapeDtypeStruct((rows, cols, 2 * half), jnp.float32),
        scratch_shapes=[
            pltpu.VMEM((devices * group[0].shape[1], 128), jnp.float32) for group in got
        ] + [pltpu.SemaphoreType.DMA((len(groups), len(got[0])))],
        compiler_params=pltpu.CompilerParams(vmem_limit_bytes=VMEM_BYTES),
    )(places, *arrays, *pieces)


def tile_groups(tiles):
    return [slice(tile, min(tile + 2, tiles)) for tile in range(0, tiles, 2)]


def swap(peers, bit):
    return [(q, q ^ bit) for q in range(peers)]


def gathered(piece, peers, after):
    if after is not None:
        piece, first_hops = lax.optimization_barrier((piece, after[1:3]))
        after[1:3] = first_hops
    pieces, bit = {0: piece}, peers // 2
    while bit:
        for place in list(pieces):
            pieces[place ^ bit] = lax.ppermute(pieces[place], "gy", swap(peers, bit))
        bit //= 2
    return [pieces[place] for place in range(peers)]


def exchanged(packed):
    gy = len(packed)
    return [packed[0]] + [lax.ppermute(packed[p], "gy", swap(gy, p)) for p in range(1, gy)]


def sent_lines(got, count, after):
    gy = len(got)
    lines = [sum(got[p][:count] for p in range(first, gy, 2)) for first in range(2)]
    lines = jnp.concatenate(lines + [sum(piece[count:] for piece in got)], axis=0)
    lines = jnp.transpose(lines, (2, 1, 0, 3))
    if after is not None:
        lines, _ = lax.optimization_barrier((lines, after))
    return lax.all_to_all(lines, "gx", 0, 0, tiled=True)


def first_axis(lines, table):
    gx, _, count, half = table.shape
    table = table.reshape(gx, 2 * count, half)
    return jnp.einsum("geaw,gai->eiw", lines[:, :, : 2 * count], table, precision=HIGH)


def row_parts(rows):
    if rows < 4 * PART_STEP:
        return [slice(0, rows)]
    return [slice(PART_STEP, rows - PART_STEP), slice(0, PART_STEP), slice(rows - PART_STEP, rows)]


def square(lower, block):
    if len(lower) == 1:
        return lower[0]
    split_at = len(lower) // 2
    size = split_at * block
    first = square(lower[:split_at], block)
    corner = jnp.concatenate([line[..., :size] for line in lower[split_at:]], axis=-2)
    last = square([line[..., size:] for line in lower[split_at:]], block)
    top = jnp.concatenate([first, jnp.swapaxes(corner, -1, -2)], axis=-1)
    return jnp.concatenate([top, jnp.concatenate([corner, last], axis=-1)], axis=-2)


def solution(mesh):
    placed = (P("gx", "gy", None), P())
    return jax.shard_map(
        on_device, mesh=mesh, in_specs=placed, out_specs=P("gx", "gy", None), check_vma=False
    )
```

```python
import math

import jax
import jax.numpy as jnp
import numpy as np
from jax import lax
from jax.experimental import pallas as pl
from jax.experimental.pallas import tpu as pltpu
from jax.sharding import PartitionSpec as P

SWEEPS = 2

AXIS_ORDERS = ((0, 1, 2), (0, 2, 1), (1, 0, 2), (1, 2, 0), (2, 0, 1), (2, 1, 0))

HIGH = lax.Precision.HIGH


def ring(axis):
    peers = lax.axis_size(axis)
    up = [(i, (i + 1) % peers) for i in range(peers)]
    return up, [(j, i) for i, j in up]


FREE = ((8 - SWEEPS, 8 - SWEEPS), (0, 0))


def side_faces(block):
    cols = block.shape[1]
    right, left = ring("gy")
    before = lax.ppermute(block[:, cols - SWEEPS :], "gy", right)
    after = lax.ppermute(block[:, :SWEEPS], "gy", left)
    return jnp.concatenate([before, after], axis=1)


def end_faces(block, sides):
    rows = block.shape[0]
    up, down = ring("gx")
    last = jnp.concatenate([block[rows - SWEEPS :], sides[rows - SWEEPS :]], axis=1)
    first = jnp.concatenate([block[:SWEEPS], sides[:SWEEPS]], axis=1)
    return lax.ppermute(last, "gx", up), lax.ppermute(first, "gx", down)


def mirror(values, axis):
    return jnp.roll(jnp.flip(values, axis), 1, axis)


def symmetric_marks(marks):
    for flip_axis in range(3):
        marks = jnp.maximum(marks, mirror(marks, flip_axis))
    united = marks
    for axis_order in AXIS_ORDERS[1:]:
        united = jnp.maximum(united, jnp.transpose(marks, axis_order))
    return united


def cosine_table(length):
    position = np.arange(length)
    phases = np.mod(position[:, None] * position[None, : length // 2 + 1], length)
    return (np.cos(phases * (2.0 * math.pi / length)) / math.sqrt(length)).astype(np.float32)


MARGIN = 16
CHUNK = 16
STEP_ROWS = 16
PART_STEP = 8
VMEM_BYTES = 56 * 1024 * 1024


def split(values):
    high = values.astype(jnp.bfloat16)
    low = (values - high.astype(jnp.float32)).astype(jnp.bfloat16)
    return high, low


def fill_kernel(
    base, here, above, below, top, bottom, sides, marks, table_high, table_low,
    spectrum, alternate, edge, punched, once, high, low, folded,
):
    step_rows, cols, length = here.shape
    step = base[pl.program_id(0)]
    first_row = step * step_rows
    local_row = pl.program_id(0) * step_rows
    period = marks.shape[0]
    lane = lax.broadcasted_iota(jnp.int32, (128, 128), 1)
    signs = jnp.where(lax.broadcasted_iota(jnp.int32, (128, 128), 0) % 2 == 0, 1.0, -1.0)

    @pl.when(pl.program_id(0) == 0)
    def _():
        edge[...] = jnp.zeros_like(edge)

    def holes(row, start, size):
        row = lax.rem(first_row + row, period)
        start = start % period
        if start + size <= period:
            part = marks[row, pl.ds(start, size), :]
        else:
            part = jnp.concatenate(
                [marks[row, pl.ds(start, period - start), :], marks[row, pl.ds(0, start + size - period), :]],
                axis=0,
            )
        return jnp.concatenate([part] * (length // 128), axis=1)

    def punch(row, start, values):
        kept = jnp.where(holes(row, start, values.shape[0]) > 0.0, 0.0, values)
        punched[row, pl.ds(start, values.shape[0]), :] = kept

    def punch_row(row, source, index):
        for c in range(0, cols, CHUNK):
            punch(row, MARGIN + c, source[index, pl.ds(c, CHUNK), :])

    def punch_sides(row):
        full = first_row + row - SWEEPS
        punch(row, MARGIN - 8, sides[full, pl.ds(0, 8), :])
        punch(row, MARGIN + cols, sides[full, pl.ds(8, 8), :])

    def neighbours(ref, row, start):
        middle = ref[row, pl.ds(start, CHUNK), :]
        total = ref[row - 1, pl.ds(start, CHUNK), :] + ref[row + 1, pl.ds(start, CHUNK), :]
        total += ref[row, pl.ds(start - 1, CHUNK), :] + ref[row, pl.ds(start + 1, CHUNK), :]
        return total + pltpu.roll(middle, 1, 1) + pltpu.roll(middle, length - 1, 1)

    last = sides.shape[0] // step_rows - 1
    for edge_rows, inside, offset, outer in (
        (above, step > 0, 0, top),
        (below, step < last, step_rows + SWEEPS, bottom),
    ):
        @pl.when(inside)
        def _():
            for r in range(SWEEPS):
                punch_row(offset + r, edge_rows, r)
                punch_sides(offset + r)

        @pl.when(jnp.logical_not(inside))
        def _():
            for r in range(SWEEPS):
                punch_row(offset + r, outer, r)
                punch(offset + r, MARGIN - SWEEPS, outer[r, pl.ds(cols, SWEEPS), :])
                punch(offset + r, MARGIN + cols, outer[r, pl.ds(cols + SWEEPS, SWEEPS), :])

    @pl.loop(0, step_rows)
    def _(r):
        punch_row(r + SWEEPS, here, r)
        punch_sides(r + SWEEPS)

    @pl.loop(1, step_rows + 2 * SWEEPS - 1, unroll=2)
    def _(r):
        for start in range(MARGIN - 8, MARGIN + cols + 8, CHUNK):
            total = neighbours(punched, r, start) * holes(r, start, CHUNK)
            once[r, pl.ds(start, CHUNK), :] = punched[r, pl.ds(start, CHUNK), :] + total

    @pl.loop(0, step_rows)
    def _(r):
        for c in range(0, cols, CHUNK):
            start = MARGIN + c
            total = neighbours(once, r + SWEEPS, start) * holes(r + SWEEPS, start, CHUNK)
            filled = punched[r + SWEEPS, pl.ds(start, CHUNK), :] + total
            first, second = split(filled)
            spot = pl.ds(pl.multiple_of(r * cols + c, CHUNK), CHUNK)
            high[spot, :] = first
            low[spot, :] = second
            wrapped = filled[:, :128]
            for tile in range(1, length // 128):
                wrapped += filled[:, tile * 128 : (tile + 1) * 128]
            folded[pl.ds(c, CHUNK), :] = wrapped
        column = jnp.where(lane == local_row + r, signs, 0.0).astype(jnp.bfloat16)
        first, second = split(folded[...])
        total = jnp.dot(first, column, preferred_element_type=jnp.float32)
        total += jnp.dot(second, column, preferred_element_type=jnp.float32)
        edge[...] += total

    rows_each = 8
    half = spectrum.shape[2]
    order = lax.broadcasted_iota(jnp.int32, (rows_each, cols, half), 1)

    @pl.loop(0, step_rows // rows_each)
    def _(r):
        spot = pl.ds(pl.multiple_of(r * rows_each * cols, CHUNK), rows_each * cols)
        first, second = high[spot, :], low[spot, :]
        total = jnp.dot(first, table_low[...], preferred_element_type=jnp.float32)
        total += jnp.dot(second, table_high[...], preferred_element_type=jnp.float32)
        total += jnp.dot(first, table_high[...], preferred_element_type=jnp.float32)
        total = total.reshape(rows_each, cols, half)
        spectrum[pl.ds(r * rows_each, rows_each)] = total
        signed = jnp.sum(jnp.where(order % 2 == 0, total, -total), axis=1)
        alternate[pl.ds(pl.multiple_of(r * rows_each, rows_each), rows_each), :] = signed


def rounded_parts(table):
    rounded = lax.reduce_precision(table, 8, 7)
    return rounded.astype(jnp.bfloat16), (table - rounded).astype(jnp.bfloat16)


def marks_kernel(shifts, template, out, held):
    period = template.shape[0]
    repeats = held.shape[1] // period
    line = lax.broadcasted_iota(jnp.int32, (period, period), 0)
    across = lax.broadcasted_iota(jnp.int32, (period, period), 1)
    flip = jnp.where((line + across) % period == 0, 1.0, 0.0)
    for i in range(period):
        plane = jnp.maximum(template[i], template[-i % period]).astype(jnp.float32)
        plane = jnp.maximum(plane, jnp.dot(flip, plane, preferred_element_type=jnp.float32))
        plane = jnp.maximum(plane, jnp.dot(plane, flip, preferred_element_type=jnp.float32))
        plane = jnp.maximum(plane, plane.T)
        held[i * period : (i + 1) * period, :] = jnp.concatenate([plane] * repeats, axis=1)
    for i in range(period):
        plane = held[i * period : (i + 1) * period, :]
        turned = held[pl.ds(i, period, stride=period), :]
        back = turned[:, :period].T
        plane = jnp.maximum(jnp.maximum(plane, turned), jnp.concatenate([back] * repeats, axis=1))
        plane = jnp.where(plane == 1.0, 1.0 / 6.0, 0.0)
        shift = shifts[1]
        out[(i - shifts[0]) % period] = jnp.concatenate([plane[shift:], plane[:shift]], axis=0)


def hole_marks(template, row, col, rows, cols):
    period = template.shape[0]
    shape = (period, period, 128)
    if rows % period == 0 and cols % period == 0:
        shifts = (-SWEEPS % period, -MARGIN % period)
        return pl.pallas_call(
            lambda *refs: marks_kernel(shifts, *refs),
            in_specs=[pl.BlockSpec(memory_space=pltpu.VMEM)],
            out_specs=pl.BlockSpec(memory_space=pltpu.VMEM),
            out_shape=jax.ShapeDtypeStruct(shape, jnp.float32),
            scratch_shapes=[pltpu.VMEM((period * period, 128), jnp.float32)],
        )(template)
    shifts = (jnp.mod(row * rows - SWEEPS, period), jnp.mod(col * cols - MARGIN, period))
    marks = jnp.roll(symmetric_marks(template), (-shifts[0], -shifts[1]), (0, 1))
    return jnp.tile(marks.astype(jnp.float32) / 6.0, (1, 1, 128 // period))


def fill_constants(intensity, template, row, col, main):
    rows, cols, _ = intensity.shape
    high = main.astype(jnp.bfloat16)
    low = (main - high.astype(np.float32)).astype(jnp.bfloat16)
    return hole_marks(template, row, col, rows, cols), jnp.asarray(high), jnp.asarray(low)


def filled_spectrum(intensity, arrays, first, parts):
    rows, cols, length = intensity.shape
    half = length // 2
    aligned = all(edge % STEP_ROWS == 0 for part in parts for edge in (part.start, part.stop))
    step_rows = STEP_ROWS if aligned else PART_STEP
    starts = [start for part in parts for start in range(part.start, part.stop, step_rows)]
    count = step_rows * len(starts)
    steps = jnp.stack([(first + start) // step_rows for start in starts])
    pairs = step_rows // SWEEPS
    last = rows // SWEEPS - 1
    whole = lambda array: pl.BlockSpec(array.shape, lambda i, b: (0,) * array.ndim)
    before = lambda i, b: (jnp.maximum(b[i] * pairs - 1, 0), 0, 0)
    after = lambda i, b: (jnp.minimum((b[i] + 1) * pairs, last), 0, 0)
    padded = (step_rows + 2 * SWEEPS, cols + 2 * MARGIN, length)
    return pl.pallas_call(
        fill_kernel,
        grid_spec=pltpu.PrefetchScalarGridSpec(
            num_scalar_prefetch=1,
            grid=(len(starts),),
            in_specs=[
                pl.BlockSpec((step_rows, cols, length), lambda i, b: (b[i], 0, 0)),
                pl.BlockSpec((SWEEPS, cols, length), before),
                pl.BlockSpec((SWEEPS, cols, length), after),
            ] + [whole(array) for array in arrays],
            out_specs=[
                pl.BlockSpec((step_rows, cols, half), lambda i, b: (i, 0, 0)),
                pl.BlockSpec((step_rows, half), lambda i, b: (i, 0)),
                pl.BlockSpec((cols, 128), lambda i, b: (0, 0)),
            ],
            scratch_shapes=[
                pltpu.VMEM(padded, jnp.float32),
                pltpu.VMEM(padded, jnp.float32),
                pltpu.VMEM((step_rows * cols, length), jnp.bfloat16),
                pltpu.VMEM((step_rows * cols, length), jnp.bfloat16),
                pltpu.VMEM((cols, 128), jnp.float32),
            ],
        ),
        out_shape=[
            jax.ShapeDtypeStruct((count, cols, half), jnp.float32),
            jax.ShapeDtypeStruct((count, half), jnp.float32),
            jax.ShapeDtypeStruct((cols, 128), jnp.float32),
        ],
        compiler_params=pltpu.CompilerParams(vmem_limit_bytes=VMEM_BYTES),
        cost_estimate=pl.CostEstimate(
            flops=count * cols * length * half * 6,
            bytes_accessed=count * cols * (length + half) * 4,
            transcendentals=0,
        ),
    )(steps, intensity, intensity, intensity, *arrays)


def pack(section, offsets):
    block = offsets[1]
    units = [section[b * block : (b + 1) * block, : (b + 1) * block] for b in range(len(offsets) - 1)]
    return jnp.concatenate(units, axis=1)


def three_dots(left, right):
    total = jnp.dot(left[1], right[0], preferred_element_type=jnp.float32)
    total += jnp.dot(left[0], right[1], preferred_element_type=jnp.float32)
    return total + jnp.dot(left[0], right[0], preferred_element_type=jnp.float32)


def section_kernel(
    offsets, closing, me, weights, kept, got, cols_high, cols_low, rows_high, rows_low,
    rim, corner, before, *refs
):
    step, steps = pl.program_id(0), pl.num_programs(0)
    step_rows = kept.shape[0]
    half, count = rows_high.shape
    planes, block, width = before.shape
    *outs, total, lines, packed = refs
    gy, (_, own, gx, _) = len(outs), outs[0].shape

    def place(layer, values, slot=0):
        packed[slot] = values
        for e in range(own):
            for p in range(gy):
                start = pl.multiple_of((e * gy + (p ^ me[0])) * gx, gx)
                outs[p][layer, e] = packed[slot, pl.ds(start, gx), :]

    @pl.when(step == 0)
    def _():
        total[...] = before[...]

    for r in range(step_rows):
        layer = step * step_rows + r
        values = jnp.concatenate([kept[r], got[r]], axis=0)
        section = three_dots((cols_high[...], cols_low[...]), split(values))
        section = section + section.T
        line = pack(section, offsets)
        place(layer, line, r)
        for m in range(planes):
            total[m] += weights[m, layer] * line
        for m in range(planes - 1):
            row = (m + 1) * (half // planes)
            lines[m, pl.ds(layer, 1), :] = section[row : row + 1]

    @pl.when(step == steps - 1)
    def _():
        for m in range(planes - 1):
            plane = three_dots((rows_high[...], rows_low[...]), split(lines[m]))
            total[m] += pack(plane + plane.T, offsets)
        if closing:
            total[planes - 1] += pack(rim[...] + rim[...].T, offsets)
            for m in range(planes):
                place(count + m, total[m])
            place(count + planes, jnp.zeros((block, width), jnp.float32) + corner[...])


def packed_section(col, kept, got, first, table_pair, table_rows, marks, rim, corner, before, offsets, shape, closing):
    _, cols, half = kept.shape
    count = table_rows.shape[0]
    planes, block, width = before.shape
    gx, gy = shape
    step_rows = 4
    layers = count + (planes + 1 if closing else 0)
    whole = lambda array: pl.BlockSpec(array.shape, lambda i: (0,) * array.ndim)
    weights = jnp.stack([table_rows[:, m] for m in marks])
    arrays = rounded_parts(table_pair.T) + rounded_parts(table_rows[:, :half].T)
    arrays += (rim, corner[None], before)
    out = jax.ShapeDtypeStruct((layers, block // (gx * gy), gx, width), jnp.float32)
    outs = [out] * gy + [jax.ShapeDtypeStruct(before.shape, jnp.float32)]
    rows_spec = pl.BlockSpec((step_rows, cols, half), lambda i: (i + first // step_rows, 0, 0))
    return pl.pallas_call(
        lambda *refs: section_kernel(offsets, closing, *refs),
        grid=(count // step_rows,),
        in_specs=[pl.BlockSpec(memory_space=pltpu.SMEM)] * 2 + [rows_spec, rows_spec]
        + [whole(array) for array in arrays],
        out_specs=[whole(out) for out in outs],
        out_shape=outs,
        scratch_shapes=[
            pltpu.VMEM((planes, count, half), jnp.float32),
            pltpu.VMEM((step_rows, block, width), jnp.float32),
        ],
        compiler_params=pltpu.CompilerParams(vmem_limit_bytes=VMEM_BYTES),
        cost_estimate=pl.CostEstimate(
            flops=count * 12 * cols * half * half,
            bytes_accessed=count * cols * half * 16,
            transcendentals=0,
        ),
    )(col.reshape(1), weights, kept, got, *arrays)


def on_device(intensity, template):
    rows, cols, length = intensity.shape
    gx, gy = lax.axis_size("gx"), lax.axis_size("gy")
    row, col = lax.axis_index("gx"), lax.axis_index("gy")
    devices, half = gx * gy, length // 2
    block = max(devices, rows)
    blocks, own, slabs = half // block, block // devices, gx // 2
    offsets = [block * b * (b + 1) // 2 for b in range(blocks + 1)]
    width = offsets[blocks]
    table = jnp.asarray(cosine_table(length))
    main = table[:, :half]

    pair_rows = rows // 2
    parts = row_parts(pair_rows)
    counts = [part.stop - part.start for part in parts]
    core = lax.rem(col, 2)
    constants = fill_constants(intensity, template, row, col, cosine_table(length)[:, :half])
    sides = side_faces(intensity)
    given_first, kept_first = (1 - core) * pair_rows, core * pair_rows
    inner = parts[0].start >= SWEEPS and parts[0].stop <= pair_rows - SWEEPS
    side_columns = jnp.pad(sides, ((0, 0),) + FREE)
    blank = jnp.zeros((SWEEPS, cols + 2 * SWEEPS, length), jnp.float32)
    ends = (blank, blank) if inner else end_faces(intensity, sides)

    def fill(some, start):
        arrays = tuple(ends) + (side_columns,) + constants
        return list(filled_spectrum(intensity, arrays, start, some))

    given, kept = [fill(parts[:1], given_first)], []
    outer = ends
    if inner:
        given[0], late_sides = lax.optimization_barrier((given[0], sides))
        outer = end_faces(intensity, late_sides)
    kept.append(fill(parts[:1], kept_first))
    ends = outer

    table_cols = lax.dynamic_slice_in_dim(table, col * cols, cols, 0)
    kept_rows = lax.dynamic_slice_in_dim(table, row * rows + kept_first, pair_rows, 0)
    marks = [rows * (m + 1) for m in range(slabs)]
    mates = lax.dynamic_slice_in_dim(main, (col + 1 - 2 * core) * cols, cols, 0)
    table_pair = jnp.concatenate([table_cols[:, :half], mates], axis=0)
    table_parts = main.reshape(gx, 2, pair_rows, half) / 6.0
    table_parts = jnp.where(core == 0, table_parts, table_parts[:, ::-1])
    table_parts = [table_parts[:, :, part] for part in parts]
    side = jnp.zeros((slabs, block, width), jnp.float32)
    rim, corner = jnp.zeros((half, half), jnp.float32), jnp.zeros((width,), jnp.float32)
    values, packed, lines = 0.0, None, None
    for c, count in enumerate(counts):
        closing = c == len(counts) - 1
        if c == 1:
            behind = (given_first, kept_first), packed
            starts, packed = lax.optimization_barrier(behind)
            given.append(fill(parts[1:], starts[0]))
            kept.append(fill(parts[1:], starts[1]))
            behind = given[1][0], kept[1][0]
            given[1][0], kept[1][0] = lax.optimization_barrier(behind)
        if c < 2:
            got = lax.ppermute(given[c][0], "gy", swap(gy, 1))
            held = kept[c][0]
        flanks = [piece[1:] for piece in given + kept]
        if c > 1:
            flanks, packed = lax.optimization_barrier((flanks, packed))
        if c > 0:
            got_lines = exchanged(packed)
            if c == 1:
                held, got_lines = lax.optimization_barrier((held, got_lines))
            lines = sent_lines(got_lines, counts[c - 1], lines)
            values = values + first_axis(lines, table_parts[c - 1])
        if closing:
            given_rows = lax.dynamic_slice_in_dim(table, row * rows + given_first, pair_rows, 0)
            ordered_rows = [held_rows[part] for held_rows in (given_rows, kept_rows) for part in parts]
            ordered_rows = jnp.concatenate(ordered_rows, axis=0)
            alternate = jnp.concatenate([piece[0] for piece in flanks], axis=0) / math.sqrt(length)
            edge = [piece[1][:, : piece[0].shape[0]] for piece in flanks]
            edge = jnp.concatenate(edge, axis=1)
            edge = jnp.einsum("ba,bk->ak", edge / math.sqrt(length), table_cols, precision=HIGH)
            edge = edge + jnp.concatenate([alternate, edge[:, half:]], axis=1)
            rim = jnp.einsum("aj,ak->jk", ordered_rows[:, :half], edge[:, :half], precision=HIGH)
            corner = 2.0 * jnp.einsum("a,ak->k", ordered_rows[:, half], edge, precision=HIGH)
            corner = corner + jnp.einsum("aj,a->j", ordered_rows, edge[:, half], precision=HIGH)
            corner = jnp.pad(corner, (0, width - half - 1))

        *packed, side = packed_section(
            col, held, got, sum(counts[1:c]), table_pair, kept_rows[parts[c]], marks,
            rim, corner, side, offsets, (gx, gy), closing,
        )
    lines = sent_lines(exchanged(packed), counts[-1], lines)
    values = values + first_axis(lines, table_parts[-1])
    side = jnp.sum(lines[:, :, 2 * counts[-1] :], axis=0) / 6.0
    turned = values.reshape(own, blocks, own, devices, width)
    turned = jnp.transpose(turned, (3, 1, 2, 0, 4))
    turned = [turned[:, b, :, :, : offsets[b + 1]] for b in range(blocks)]
    turned = lax.all_to_all(jnp.concatenate(turned, axis=3), ("gy", "gx"), 0, 0, tiled=True)
    turned = jnp.transpose(turned, (1, 2, 0, 3)).reshape(own, block, -1)

    slab = jnp.minimum(row, gx - 1 - row)
    far_row, far_col = row >= slabs, col >= gy // 2
    pick_rows = jnp.arange(rows)
    pick_rows = slab * rows + jnp.where(far_row, rows - pick_rows, pick_rows)
    pick_cols = jnp.arange(cols)
    pick_cols = jnp.where(far_col, (gy - col) * cols - pick_cols, col * cols + pick_cols)

    if rows == block:
        got, piece = [], None
        for messages in slab_messages(values, turned, side, offsets, slabs):
            if piece is not None:
                messages, piece = lax.optimization_barrier((messages, piece))
                got.append(gathered(piece, gy, got[-1] if got else None))
            piece = lax.all_to_all(messages, "gx", 0, 0, tiled=True)
        got.append(gathered(piece, gy, got[-1] if got else None))
        tiles = width // 128
        start = tile_groups(tiles)[0].stop * own * block
        side = jnp.stack([piece[:, start : start + 3 * own * tiles] for piece in got[0]])
        bit = gy // 2
        while bit:
            paired = side.reshape((-1, 2, bit) + side.shape[1:])
            side = jnp.where((col & bit) == 0, paired, paired[:, ::-1]).reshape(side.shape)
            bit //= 2
        side = side.reshape(devices, own, 3, width)
        side = jnp.transpose(side, (2, 1, 0, 3)).reshape(3, block, width)
        next_plane, across = side[0], rim_rows(side[1:], offsets, pick_rows)
        rim_col = col == gy // 2
        rim = across[:, pick_cols]
        return result_block(
            got, next_plane, across, rim, pick_cols, slab, far_row, rim_col, col, offsets
        )

    side = lax.all_gather(side, ("gy", "gx"), axis=0)
    side = jnp.transpose(side, (2, 1, 0, 3)).reshape(slabs + 1, block, width)
    across = rim_rows(side[slabs - 1 :], offsets, pick_rows)
    next_plane = lax.dynamic_index_in_dim(side, slab, 0, keepdims=False)
    sums = axis_order_sums(values, turned, offsets, block)
    messages = []
    for s in range(slabs):
        base, first = s * rows // block, s * rows
        units = []
        for b in range(blocks):
            size = (b + 1) * block
            near = jnp.zeros((own, rows, size))
            far = jnp.zeros((own, block, size))
            if b >= base:
                near = jnp.stack([sums[b][e][first : first + rows, :size] for e in range(own)])
            else:
                far = jnp.stack([sums[base][e][b * block : size, :size] for e in range(own)])
            units.append(jnp.concatenate([near, far], axis=1))
        messages.append(jnp.concatenate(units, axis=2))
    messages = jnp.stack(messages + messages[::-1])
    got = lax.all_to_all(messages, "gx", 0, 0, tiled=True)
    got = lax.all_gather(got, "gy", axis=0, tiled=True)
    got = jnp.swapaxes(got, 0, 1).reshape(block, rows + block, width)
    base = slab * rows // block
    lower = []
    for b in range(blocks):
        lanes = slice(offsets[b], offsets[b + 1])
        near = jnp.swapaxes(got[:, :rows, lanes], 0, 1)
        far = lax.dynamic_slice_in_dim(got[:, rows:, lanes], lax.rem(slab * rows, block), rows, 0)
        lower.append(jnp.where(b >= base, near, far))
    lower = jnp.concatenate(lower, axis=2)
    lower = jnp.concatenate([lower, next_plane[None]], axis=0)
    body = square([lower[:, :, offsets[b] : offsets[b + 1]] for b in range(blocks)], block)
    body = body[pick_rows - slab * rows]
    body = jnp.concatenate([body, across[:, None, :half]], axis=1)[:, pick_cols]
    body = jnp.concatenate([body, across[:, pick_cols][:, :, None]], axis=2)
    return jnp.concatenate([body, jnp.flip(body[:, :, 1:half], 2)], axis=2)


def rim_rows(side, offsets, pick_rows):
    blocks, block = len(offsets) - 1, offsets[1]
    half = blocks * block
    last = square([side[0][:, offsets[b] : offsets[b + 1]] for b in range(blocks)], block)
    rim = side[1, 0, : half + 1]
    last = jnp.concatenate([last, rim[None, :half]], axis=0)
    return jnp.concatenate([last, rim[:, None]], axis=1)[pick_rows]


def axis_order_sums(values, turned, offsets, block):
    start = 0
    sums = []
    for top in range(len(offsets) - 1):
        size = (top + 1) * block
        parts = []
        for e in range(values.shape[0]):
            part = values[e, :size, offsets[top] : offsets[top] + size]
            lower = [turned[e, :, start + offsets[b] : start + offsets[b + 1]] for b in range(top + 1)]
            parts.append(part + part.T + square(lower, block))
        sums.append(parts)
        start += offsets[top + 1]
    return sums


def message_kernel(offsets, slabs, values, turned, side, *messages):
    blocks, block = len(offsets) - 1, offsets[1]
    values, turned = values[...], turned[...]
    own = values.shape[0]
    sums = axis_order_sums(values, turned, offsets, block)
    groups = tile_groups(offsets[-1] // 128)
    side_start = groups[0].stop * own * block
    messages[0][:, side_start:] = jnp.zeros_like(messages[0][:, side_start:])
    for s in range(slabs):
        places = s, 2 * slabs - 1 - s
        for e in range(own):
            units = []
            for b in range(blocks):
                size = (b + 1) * block
                if b >= s:
                    units.append(sums[b][e][s * block : (s + 1) * block, :size])
                else:
                    units.append(sums[s][e][b * block : size, :size])
            line = jnp.concatenate(units, axis=1)
            for group, out in zip(groups, messages):
                for tile in range(group.start, group.stop):
                    start = ((tile - group.start) * own + e) * block
                    for place in places:
                        out[place, start : start + block] = line[:, tile * 128 : (tile + 1) * 128]
            row = side_start + 3 * e * groups[-1].stop
            for plane in (s, slabs - 1, slabs):
                for tile in range(groups[-1].stop):
                    part = side[e, plane : plane + 1, tile * 128 : (tile + 1) * 128]
                    for place in places:
                        messages[0][place, row : row + 1] = part
                    row += 1


def slab_messages(values, turned, side, offsets, slabs):
    own, block, tiles = values.shape[0], offsets[1], offsets[-1] // 128
    sizes = [(group.stop - group.start) * own * block for group in tile_groups(tiles)]
    sizes[0] += -(-3 * own * tiles // 8) * 8
    return pl.pallas_call(
        lambda *refs: message_kernel(offsets, slabs, *refs),
        in_specs=[pl.BlockSpec(memory_space=pltpu.VMEM)] * 3,
        out_specs=[pl.BlockSpec(memory_space=pltpu.VMEM)] * len(sizes),
        out_shape=[jax.ShapeDtypeStruct((2 * slabs, size, 128), jnp.float32) for size in sizes],
        compiler_params=pltpu.CompilerParams(vmem_limit_bytes=VMEM_BYTES),
    )(values, turned, side)


def result_kernel(
    offsets, own, devices, groups, places, next_plane, across, rim, pick, flip, *refs
):
    blocks, block = len(offsets) - 1, offsets[1]
    tiles = offsets[-1] // 128
    peers = (len(refs) - 2) // len(groups) - 1
    pieces, out = refs[: peers * len(groups)], refs[peers * len(groups)]
    held, sems = refs[peers * len(groups) + 1 : -1], refs[-1]
    step_rows, cols, length = out.shape
    half = length // 2
    slab, far_row, rim_col, me = places[0], places[1], places[2], places[3]
    lane = lax.broadcasted_iota(jnp.int32, (block, 128), 1)
    at_rim = lax.broadcasted_iota(jnp.int32, (cols, half), 0) + (1 - rim_col) == 0
    rim_lane = lax.broadcasted_iota(jnp.int32, rim.shape, 1)
    first_lane = lax.broadcasted_iota(jnp.int32, (cols, half), 1) == 0

    @pl.when(pl.program_id(0) == 0)
    def _():
        copies = []
        for g in range(len(groups)):
            for peer in range(peers):
                piece = pieces[g * peers + peer]
                size = piece.shape[0]
                spot = pl.ds(pl.multiple_of((me ^ peer) * size, size), size)
                copies.append(pltpu.make_async_copy(piece, held[g].at[spot], sems.at[g, peer]))
        for copy in copies:
            copy.start()
        for copy in copies:
            copy.wait()

    def left_half(r):
        t = pl.program_id(0) * step_rows + r
        i = jnp.where(far_row == 1, block - t, t)
        inside = (jnp.zeros((block, 128), jnp.int32) + i) < block
        i = jnp.minimum(i, block - 1)
        source = lax.div(i, devices), lax.rem(i, devices)
        parts = []
        for g, group in enumerate(groups):
            stride = held[g].shape[0] // devices
            for tile in range(group.start, group.stop):
                start = (tile - group.start) * own * block
                near = [
                    held[g][pl.ds(start + e * block + i, devices, stride=stride), :]
                    for e in range(own)
                ]
                near = jnp.concatenate(near, axis=0)
                far = pl.multiple_of(source[1] * stride + start + source[0] * block, 8)
                far = held[g][pl.ds(far, block), :]
                kind = jnp.zeros((block, 128), jnp.int32)
                for b in range(1, blocks):
                    kind += (lane + tile * 128 >= offsets[b]).astype(jnp.int32)
                line = jnp.where(kind >= slab, near, far)
                line = jnp.where(inside, line, next_plane[:, pl.ds(tile * 128, 128)])
                parts.append(line)
        line = jnp.concatenate(parts, axis=1)
        plane = square([line[:, offsets[b] : offsets[b + 1]] for b in range(blocks)], block)
        high, low = split(plane)
        left = jnp.dot(pick[...], high, preferred_element_type=jnp.float32)
        left += jnp.dot(pick[...], low, preferred_element_type=jnp.float32)
        left = jnp.where(at_rim, across[pl.ds(t, 1), :], left)
        out[r, :, pl.ds(0, half)] = left
        return left

    together = 4

    @pl.loop(0, step_rows // together)
    def _(c):
        left = [left_half(c * together + n) for n in range(together)]
        high, low = split(jnp.concatenate(left, axis=0))
        right = jnp.dot(high, flip[...], preferred_element_type=jnp.float32)
        right += jnp.dot(low, flip[...], preferred_element_type=jnp.float32)
        for n in range(together):
            r = c * together + n
            t = pl.program_id(0) * step_rows + r
            edge = jnp.sum(jnp.where(rim_lane == t, rim[...], 0.0), axis=1, keepdims=True)
            part = right[n * cols : (n + 1) * cols]
            out[r, :, pl.ds(half, half)] = jnp.where(first_lane, edge, part)


def result_block(got, next_plane, across, rim, pick_cols, slab, far_row, rim_col, col, offsets):
    block = offsets[1]
    gx = got[0][0].shape[0]
    groups = tile_groups(offsets[-1] // 128)
    devices = gx * len(got[0])
    own = block // devices
    rows, half = across.shape[0], across.shape[1] - 1
    cols = pick_cols.shape[0]
    step_rows = 8
    places = jnp.stack([slab, far_row.astype(jnp.int32), rim_col.astype(jnp.int32), col])
    cell = jnp.arange(half)
    pick = (pick_cols[:, None] == cell[None, :]).astype(jnp.bfloat16)
    flip = (cell[:, None] + cell[None, :] == half).astype(jnp.bfloat16)
    rim = jnp.pad(rim.T, ((0, 0), (0, 128 - rows)))
    whole = lambda array: pl.BlockSpec(array.shape, lambda i: (0,) * array.ndim)
    arrays = (next_plane, across[:, :half], rim, pick, flip)
    pieces = [piece.reshape(-1, 128) for group in got for piece in group]
    return pl.pallas_call(
        lambda *refs: result_kernel(offsets, own, devices, groups, *refs),
        grid=(rows // step_rows,),
        in_specs=[pl.BlockSpec(memory_space=pltpu.SMEM)] + [whole(array) for array in arrays]
        + [pl.BlockSpec(memory_space=pl.ANY)] * len(pieces),
        out_specs=pl.BlockSpec((step_rows, cols, 2 * half), lambda i: (i, 0, 0)),
        out_shape=jax.ShapeDtypeStruct((rows, cols, 2 * half), jnp.float32),
        scratch_shapes=[
            pltpu.VMEM((devices * group[0].shape[1], 128), jnp.float32) for group in got
        ] + [pltpu.SemaphoreType.DMA((len(groups), len(got[0])))],
        compiler_params=pltpu.CompilerParams(vmem_limit_bytes=VMEM_BYTES),
    )(places, *arrays, *pieces)


def tile_groups(tiles):
    return [slice(tile, min(tile + 2, tiles)) for tile in range(0, tiles, 2)]


def swap(peers, bit):
    return [(q, q ^ bit) for q in range(peers)]


def gathered(piece, peers, after):
    if after is not None:
        piece, first_hops = lax.optimization_barrier((piece, after[1:3]))
        after[1:3] = first_hops
    pieces, bit = {0: piece}, peers // 2
    while bit:
        for place in list(pieces):
            pieces[place ^ bit] = lax.ppermute(pieces[place], "gy", swap(peers, bit))
        bit //= 2
    return [pieces[place] for place in range(peers)]


def exchanged(packed):
    gy = len(packed)
    return [packed[0]] + [lax.ppermute(packed[p], "gy", swap(gy, p)) for p in range(1, gy)]


def sent_lines(got, count, after):
    gy = len(got)
    lines = [sum(got[p][:count] for p in range(first, gy, 2)) for first in range(2)]
    lines = jnp.concatenate(lines + [sum(piece[count:] for piece in got)], axis=0)
    lines = jnp.transpose(lines, (2, 1, 0, 3))
    if after is not None:
        lines, _ = lax.optimization_barrier((lines, after))
    return lax.all_to_all(lines, "gx", 0, 0, tiled=True)


def first_axis(lines, table):
    gx, _, count, half = table.shape
    table = table.reshape(gx, 2 * count, half)
    return jnp.einsum("geaw,gai->eiw", lines[:, :, : 2 * count], table, precision=HIGH)


def row_parts(rows):
    if rows < 4 * PART_STEP:
        return [slice(0, rows)]
    return [slice(PART_STEP, rows - PART_STEP), slice(0, PART_STEP), slice(rows - PART_STEP, rows)]


def square(lower, block):
    if len(lower) == 1:
        return lower[0]
    split_at = len(lower) // 2
    size = split_at * block
    first = square(lower[:split_at], block)
    corner = jnp.concatenate([line[..., :size] for line in lower[split_at:]], axis=-2)
    last = square([line[..., size:] for line in lower[split_at:]], block)
    top = jnp.concatenate([first, jnp.swapaxes(corner, -1, -2)], axis=-1)
    return jnp.concatenate([top, jnp.concatenate([corner, last], axis=-1)], axis=-2)


def solution(mesh):
    placed = (P("gx", "gy", None), P())
    return jax.shard_map(
        on_device, mesh=mesh, in_specs=placed, out_specs=P("gx", "gy", None), check_vma=False
    )
```

```python
import math

import jax
import jax.numpy as jnp
import numpy as np
from jax import lax
from jax.experimental import pallas as pl
from jax.experimental.pallas import tpu as pltpu
from jax.sharding import PartitionSpec as P

SWEEPS = 2

AXIS_ORDERS = ((0, 1, 2), (0, 2, 1), (1, 0, 2), (1, 2, 0), (2, 0, 1), (2, 1, 0))

HIGH = lax.Precision.HIGH


def ring(axis):
    peers = lax.axis_size(axis)
    up = [(i, (i + 1) % peers) for i in range(peers)]
    return up, [(j, i) for i, j in up]


FREE = ((8 - SWEEPS, 8 - SWEEPS), (0, 0))


def side_faces(block):
    cols = block.shape[1]
    right, left = ring("gy")
    before = lax.ppermute(block[:, cols - SWEEPS :], "gy", right)
    after = lax.ppermute(block[:, :SWEEPS], "gy", left)
    return jnp.concatenate([before, after], axis=1)


def end_faces(block, sides):
    rows = block.shape[0]
    up, down = ring("gx")
    last = jnp.concatenate([block[rows - SWEEPS :], sides[rows - SWEEPS :]], axis=1)
    first = jnp.concatenate([block[:SWEEPS], sides[:SWEEPS]], axis=1)
    return lax.ppermute(last, "gx", up), lax.ppermute(first, "gx", down)


def mirror(values, axis):
    return jnp.roll(jnp.flip(values, axis), 1, axis)


def symmetric_marks(marks):
    for flip_axis in range(3):
        marks = jnp.maximum(marks, mirror(marks, flip_axis))
    united = marks
    for axis_order in AXIS_ORDERS[1:]:
        united = jnp.maximum(united, jnp.transpose(marks, axis_order))
    return united


def cosine_table(length):
    position = np.arange(length)
    phases = np.mod(position[:, None] * position[None, : length // 2 + 1], length)
    return (np.cos(phases * (2.0 * math.pi / length)) / math.sqrt(length)).astype(np.float32)


MARGIN = 16
CHUNK = 16
STEP_ROWS = 16
PART_STEP = 8
VMEM_BYTES = 56 * 1024 * 1024


def split(values):
    high = values.astype(jnp.bfloat16)
    low = (values - high.astype(jnp.float32)).astype(jnp.bfloat16)
    return high, low


def fill_kernel(
    base, here, above, below, top, bottom, sides, marks, table_high, table_low,
    spectrum, alternate, edge, punched, once, high, low, folded,
):
    step_rows, cols, length = here.shape
    step = base[pl.program_id(0)]
    first_row = step * step_rows
    local_row = pl.program_id(0) * step_rows
    period = marks.shape[0]
    lane = lax.broadcasted_iota(jnp.int32, (128, 128), 1)
    signs = jnp.where(lax.broadcasted_iota(jnp.int32, (128, 128), 0) % 2 == 0, 1.0, -1.0)

    @pl.when(pl.program_id(0) == 0)
    def _():
        edge[...] = jnp.zeros_like(edge)

    def holes(row, start, size):
        row = lax.rem(first_row + row, period)
        start = start % period
        if start + size <= period:
            part = marks[row, pl.ds(start, size), :]
        else:
            part = jnp.concatenate(
                [marks[row, pl.ds(start, period - start), :], marks[row, pl.ds(0, start + size - period), :]],
                axis=0,
            )
        return jnp.concatenate([part] * (length // 128), axis=1)

    def punch(row, start, values):
        kept = jnp.where(holes(row, start, values.shape[0]) > 0.0, 0.0, values)
        punched[row, pl.ds(start, values.shape[0]), :] = kept

    def punch_row(row, source, index):
        for c in range(0, cols, CHUNK):
            punch(row, MARGIN + c, source[index, pl.ds(c, CHUNK), :])

    def punch_sides(row):
        full = first_row + row - SWEEPS
        punch(row, MARGIN - 8, sides[full, pl.ds(0, 8), :])
        punch(row, MARGIN + cols, sides[full, pl.ds(8, 8), :])

    def neighbours(ref, row, start):
        middle = ref[row, pl.ds(start, CHUNK), :]
        total = ref[row - 1, pl.ds(start, CHUNK), :] + ref[row + 1, pl.ds(start, CHUNK), :]
        total += ref[row, pl.ds(start - 1, CHUNK), :] + ref[row, pl.ds(start + 1, CHUNK), :]
        return total + pltpu.roll(middle, 1, 1) + pltpu.roll(middle, length - 1, 1)

    last = sides.shape[0] // step_rows - 1
    for edge_rows, inside, offset, outer in (
        (above, step > 0, 0, top),
        (below, step < last, step_rows + SWEEPS, bottom),
    ):
        @pl.when(inside)
        def _():
            for r in range(SWEEPS):
                punch_row(offset + r, edge_rows, r)
                punch_sides(offset + r)

        @pl.when(jnp.logical_not(inside))
        def _():
            for r in range(SWEEPS):
                punch_row(offset + r, outer, r)
                punch(offset + r, MARGIN - SWEEPS, outer[r, pl.ds(cols, SWEEPS), :])
                punch(offset + r, MARGIN + cols, outer[r, pl.ds(cols + SWEEPS, SWEEPS), :])

    @pl.loop(0, step_rows)
    def _(r):
        punch_row(r + SWEEPS, here, r)
        punch_sides(r + SWEEPS)

    @pl.loop(1, step_rows + 2 * SWEEPS - 1, unroll=2)
    def _(r):
        for start in range(MARGIN - 8, MARGIN + cols + 8, CHUNK):
            total = neighbours(punched, r, start) * holes(r, start, CHUNK)
            once[r, pl.ds(start, CHUNK), :] = punched[r, pl.ds(start, CHUNK), :] + total

    @pl.loop(0, step_rows)
    def _(r):
        for c in range(0, cols, CHUNK):
            start = MARGIN + c
            total = neighbours(once, r + SWEEPS, start) * holes(r + SWEEPS, start, CHUNK)
            filled = punched[r + SWEEPS, pl.ds(start, CHUNK), :] + total
            first, second = split(filled)
            spot = pl.ds(pl.multiple_of(r * cols + c, CHUNK), CHUNK)
            high[spot, :] = first
            low[spot, :] = second
            wrapped = filled[:, :128]
            for tile in range(1, length // 128):
                wrapped += filled[:, tile * 128 : (tile + 1) * 128]
            folded[pl.ds(c, CHUNK), :] = wrapped
        column = jnp.where(lane == local_row + r, signs, 0.0).astype(jnp.bfloat16)
        first, second = split(folded[...])
        total = jnp.dot(first, column, preferred_element_type=jnp.float32)
        total += jnp.dot(second, column, preferred_element_type=jnp.float32)
        edge[...] += total

    rows_each = 8
    half = spectrum.shape[2]
    order = lax.broadcasted_iota(jnp.int32, (rows_each, cols, half), 1)

    @pl.loop(0, step_rows // rows_each)
    def _(r):
        spot = pl.ds(pl.multiple_of(r * rows_each * cols, CHUNK), rows_each * cols)
        first, second = high[spot, :], low[spot, :]
        total = jnp.dot(first, table_low[...], preferred_element_type=jnp.float32)
        total += jnp.dot(second, table_high[...], preferred_element_type=jnp.float32)
        total += jnp.dot(first, table_high[...], preferred_element_type=jnp.float32)
        total = total.reshape(rows_each, cols, half)
        spectrum[pl.ds(r * rows_each, rows_each)] = total
        signed = jnp.sum(jnp.where(order % 2 == 0, total, -total), axis=1)
        alternate[pl.ds(pl.multiple_of(r * rows_each, rows_each), rows_each), :] = signed


def rounded_parts(table):
    rounded = lax.reduce_precision(table, 8, 7)
    return rounded.astype(jnp.bfloat16), (table - rounded).astype(jnp.bfloat16)


def marks_kernel(shifts, template, out, held):
    period = template.shape[0]
    repeats = held.shape[1] // period
    line = lax.broadcasted_iota(jnp.int32, (period, period), 0)
    across = lax.broadcasted_iota(jnp.int32, (period, period), 1)
    flip = jnp.where((line + across) % period == 0, 1.0, 0.0)
    for i in range(period):
        plane = jnp.maximum(template[i], template[-i % period]).astype(jnp.float32)
        plane = jnp.maximum(plane, jnp.dot(flip, plane, preferred_element_type=jnp.float32))
        plane = jnp.maximum(plane, jnp.dot(plane, flip, preferred_element_type=jnp.float32))
        plane = jnp.maximum(plane, plane.T)
        held[i * period : (i + 1) * period, :] = jnp.concatenate([plane] * repeats, axis=1)
    for i in range(period):
        plane = held[i * period : (i + 1) * period, :]
        turned = held[pl.ds(i, period, stride=period), :]
        back = turned[:, :period].T
        plane = jnp.maximum(jnp.maximum(plane, turned), jnp.concatenate([back] * repeats, axis=1))
        plane = jnp.where(plane == 1.0, 1.0 / 6.0, 0.0)
        shift = shifts[1]
        out[(i - shifts[0]) % period] = jnp.concatenate([plane[shift:], plane[:shift]], axis=0)


def hole_marks(template, row, col, rows, cols):
    period = template.shape[0]
    shape = (period, period, 128)
    if rows % period == 0 and cols % period == 0:
        shifts = (-SWEEPS % period, -MARGIN % period)
        return pl.pallas_call(
            lambda *refs: marks_kernel(shifts, *refs),
            in_specs=[pl.BlockSpec(memory_space=pltpu.VMEM)],
            out_specs=pl.BlockSpec(memory_space=pltpu.VMEM),
            out_shape=jax.ShapeDtypeStruct(shape, jnp.float32),
            scratch_shapes=[pltpu.VMEM((period * period, 128), jnp.float32)],
        )(template)
    shifts = (jnp.mod(row * rows - SWEEPS, period), jnp.mod(col * cols - MARGIN, period))
    marks = jnp.roll(symmetric_marks(template), (-shifts[0], -shifts[1]), (0, 1))
    return jnp.tile(marks.astype(jnp.float32) / 6.0, (1, 1, 128 // period))


def fill_constants(intensity, template, row, col, main):
    rows, cols, _ = intensity.shape
    high = main.astype(jnp.bfloat16)
    low = (main - high.astype(np.float32)).astype(jnp.bfloat16)
    return hole_marks(template, row, col, rows, cols), jnp.asarray(high), jnp.asarray(low)


def filled_spectrum(intensity, arrays, first, parts):
    rows, cols, length = intensity.shape
    half = length // 2
    aligned = all(edge % STEP_ROWS == 0 for part in parts for edge in (part.start, part.stop))
    step_rows = STEP_ROWS if aligned else PART_STEP
    starts = [start for part in parts for start in range(part.start, part.stop, step_rows)]
    count = step_rows * len(starts)
    steps = jnp.stack([(first + start) // step_rows for start in starts])
    pairs = step_rows // SWEEPS
    last = rows // SWEEPS - 1
    whole = lambda array: pl.BlockSpec(array.shape, lambda i, b: (0,) * array.ndim)
    before = lambda i, b: (jnp.maximum(b[i] * pairs - 1, 0), 0, 0)
    after = lambda i, b: (jnp.minimum((b[i] + 1) * pairs, last), 0, 0)
    padded = (step_rows + 2 * SWEEPS, cols + 2 * MARGIN, length)
    return pl.pallas_call(
        fill_kernel,
        grid_spec=pltpu.PrefetchScalarGridSpec(
            num_scalar_prefetch=1,
            grid=(len(starts),),
            in_specs=[
                pl.BlockSpec((step_rows, cols, length), lambda i, b: (b[i], 0, 0)),
                pl.BlockSpec((SWEEPS, cols, length), before),
                pl.BlockSpec((SWEEPS, cols, length), after),
            ] + [whole(array) for array in arrays],
            out_specs=[
                pl.BlockSpec((step_rows, cols, half), lambda i, b: (i, 0, 0)),
                pl.BlockSpec((step_rows, half), lambda i, b: (i, 0)),
                pl.BlockSpec((cols, 128), lambda i, b: (0, 0)),
            ],
            scratch_shapes=[
                pltpu.VMEM(padded, jnp.float32),
                pltpu.VMEM(padded, jnp.float32),
                pltpu.VMEM((step_rows * cols, length), jnp.bfloat16),
                pltpu.VMEM((step_rows * cols, length), jnp.bfloat16),
                pltpu.VMEM((cols, 128), jnp.float32),
            ],
        ),
        out_shape=[
            jax.ShapeDtypeStruct((count, cols, half), jnp.float32),
            jax.ShapeDtypeStruct((count, half), jnp.float32),
            jax.ShapeDtypeStruct((cols, 128), jnp.float32),
        ],
        compiler_params=pltpu.CompilerParams(vmem_limit_bytes=VMEM_BYTES),
        cost_estimate=pl.CostEstimate(
            flops=count * cols * length * half * 6,
            bytes_accessed=count * cols * (length + half) * 4,
            transcendentals=0,
        ),
    )(steps, intensity, intensity, intensity, *arrays)


def pack(section, offsets):
    block = offsets[1]
    units = [section[b * block : (b + 1) * block, : (b + 1) * block] for b in range(len(offsets) - 1)]
    return jnp.concatenate(units, axis=1)


def three_dots(left, right):
    total = jnp.dot(left[1], right[0], preferred_element_type=jnp.float32)
    total += jnp.dot(left[0], right[1], preferred_element_type=jnp.float32)
    return total + jnp.dot(left[0], right[0], preferred_element_type=jnp.float32)


def section_kernel(
    offsets, closing, me, weights, kept, got, cols_high, cols_low, rows_high, rows_low,
    rim, corner, before, *refs
):
    step, steps = pl.program_id(0), pl.num_programs(0)
    step_rows = kept.shape[0]
    half, count = rows_high.shape
    planes, block, width = before.shape
    *outs, total, lines, packed = refs
    gy, (_, own, gx, _) = len(outs), outs[0].shape

    def place(layer, values, slot=0):
        packed[slot] = values
        for e in range(own):
            for p in range(gy):
                start = pl.multiple_of((e * gy + (p ^ me[0])) * gx, gx)
                outs[p][layer, e] = packed[slot, pl.ds(start, gx), :]

    @pl.when(step == 0)
    def _():
        total[...] = before[...]

    for r in range(step_rows):
        layer = step * step_rows + r
        values = jnp.concatenate([kept[r], got[r]], axis=0)
        section = three_dots((cols_high[...], cols_low[...]), split(values))
        section = section + section.T
        line = pack(section, offsets)
        place(layer, line, r)
        for m in range(planes):
            total[m] += weights[m, layer] * line
        for m in range(planes - 1):
            row = (m + 1) * (half // planes)
            lines[m, pl.ds(layer, 1), :] = section[row : row + 1]

    @pl.when(step == steps - 1)
    def _():
        for m in range(planes - 1):
            plane = three_dots((rows_high[...], rows_low[...]), split(lines[m]))
            total[m] += pack(plane + plane.T, offsets)
        if closing:
            total[planes - 1] += pack(rim[...] + rim[...].T, offsets)
            for m in range(planes):
                place(count + m, total[m])
            place(count + planes, jnp.zeros((block, width), jnp.float32) + corner[...])


def packed_section(col, kept, got, first, table_pair, table_rows, marks, rim, corner, before, offsets, shape, closing):
    _, cols, half = kept.shape
    count = table_rows.shape[0]
    planes, block, width = before.shape
    gx, gy = shape
    step_rows = 4
    layers = count + (planes + 1 if closing else 0)
    whole = lambda array: pl.BlockSpec(array.shape, lambda i: (0,) * array.ndim)
    weights = jnp.stack([table_rows[:, m] for m in marks])
    arrays = rounded_parts(table_pair.T) + rounded_parts(table_rows[:, :half].T)
    arrays += (rim, corner[None], before)
    out = jax.ShapeDtypeStruct((layers, block // (gx * gy), gx, width), jnp.float32)
    outs = [out] * gy + [jax.ShapeDtypeStruct(before.shape, jnp.float32)]
    rows_spec = pl.BlockSpec((step_rows, cols, half), lambda i: (i + first // step_rows, 0, 0))
    return pl.pallas_call(
        lambda *refs: section_kernel(offsets, closing, *refs),
        grid=(count // step_rows,),
        in_specs=[pl.BlockSpec(memory_space=pltpu.SMEM)] * 2 + [rows_spec, rows_spec]
        + [whole(array) for array in arrays],
        out_specs=[whole(out) for out in outs],
        out_shape=outs,
        scratch_shapes=[
            pltpu.VMEM((planes, count, half), jnp.float32),
            pltpu.VMEM((step_rows, block, width), jnp.float32),
        ],
        compiler_params=pltpu.CompilerParams(vmem_limit_bytes=VMEM_BYTES),
        cost_estimate=pl.CostEstimate(
            flops=count * 12 * cols * half * half,
            bytes_accessed=count * cols * half * 16,
            transcendentals=0,
        ),
    )(col.reshape(1), weights, kept, got, *arrays)


def on_device(intensity, template):
    rows, cols, length = intensity.shape
    gx, gy = lax.axis_size("gx"), lax.axis_size("gy")
    row, col = lax.axis_index("gx"), lax.axis_index("gy")
    devices, half = gx * gy, length // 2
    block = max(devices, rows)
    blocks, own, slabs = half // block, block // devices, gx // 2
    offsets = [block * b * (b + 1) // 2 for b in range(blocks + 1)]
    width = offsets[blocks]
    table = jnp.asarray(cosine_table(length))
    main = table[:, :half]

    pair_rows = rows // 2
    parts = row_parts(pair_rows)
    counts = [part.stop - part.start for part in parts]
    core = lax.rem(col, 2)
    constants = fill_constants(intensity, template, row, col, cosine_table(length)[:, :half])
    sides = side_faces(intensity)
    given_first, kept_first = (1 - core) * pair_rows, core * pair_rows
    inner = parts[0].start >= SWEEPS and parts[0].stop <= pair_rows - SWEEPS
    side_columns = jnp.pad(sides, ((0, 0),) + FREE)
    blank = jnp.zeros((SWEEPS, cols + 2 * SWEEPS, length), jnp.float32)
    ends = (blank, blank) if inner else end_faces(intensity, sides)

    def fill(some, start):
        arrays = tuple(ends) + (side_columns,) + constants
        return list(filled_spectrum(intensity, arrays, start, some))

    given, kept = [fill(parts[:1], given_first)], []
    outer = ends
    if inner:
        given[0], late_sides = lax.optimization_barrier((given[0], sides))
        outer = end_faces(intensity, late_sides)
    kept.append(fill(parts[:1], kept_first))
    ends = outer

    table_cols = lax.dynamic_slice_in_dim(table, col * cols, cols, 0)
    kept_rows = lax.dynamic_slice_in_dim(table, row * rows + kept_first, pair_rows, 0)
    marks = [rows * (m + 1) for m in range(slabs)]
    mates = lax.dynamic_slice_in_dim(main, (col + 1 - 2 * core) * cols, cols, 0)
    table_pair = jnp.concatenate([table_cols[:, :half], mates], axis=0)
    table_parts = main.reshape(gx, 2, pair_rows, half) / 6.0
    table_parts = jnp.where(core == 0, table_parts, table_parts[:, ::-1])
    table_parts = [table_parts[:, :, part] for part in parts]
    side = jnp.zeros((slabs, block, width), jnp.float32)
    rim, corner = jnp.zeros((half, half), jnp.float32), jnp.zeros((width,), jnp.float32)
    values, packed, lines = 0.0, None, None
    for c, count in enumerate(counts):
        closing = c == len(counts) - 1
        if c == 1:
            behind = (given_first, kept_first), packed
            starts, packed = lax.optimization_barrier(behind)
            given.append(fill(parts[1:], starts[0]))
            kept.append(fill(parts[1:], starts[1]))
        flanks = [piece[1:] for piece in given + kept]
        if c > 1:
            flanks, packed = lax.optimization_barrier((flanks, packed))
        if c > 0:
            got_lines = exchanged(packed)
        if c == 1:
            behind = given[1][0], kept[1][0], got_lines
            given[1][0], kept[1][0], got_lines = lax.optimization_barrier(behind)
        if c < 2:
            got = lax.ppermute(given[c][0], "gy", swap(gy, 1))
            held = kept[c][0]
        if c > 0:
            lines = sent_lines(got_lines, counts[c - 1], lines)
            values = values + first_axis(lines, table_parts[c - 1])
        if closing:
            given_rows = lax.dynamic_slice_in_dim(table, row * rows + given_first, pair_rows, 0)
            ordered_rows = [held_rows[part] for held_rows in (given_rows, kept_rows) for part in parts]
            ordered_rows = jnp.concatenate(ordered_rows, axis=0)
            alternate = jnp.concatenate([piece[0] for piece in flanks], axis=0) / math.sqrt(length)
            edge = [piece[1][:, : piece[0].shape[0]] for piece in flanks]
            edge = jnp.concatenate(edge, axis=1)
            edge = jnp.einsum("ba,bk->ak", edge / math.sqrt(length), table_cols, precision=HIGH)
            edge = edge + jnp.concatenate([alternate, edge[:, half:]], axis=1)
            rim = jnp.einsum("aj,ak->jk", ordered_rows[:, :half], edge[:, :half], precision=HIGH)
            corner = 2.0 * jnp.einsum("a,ak->k", ordered_rows[:, half], edge, precision=HIGH)
            corner = corner + jnp.einsum("aj,a->j", ordered_rows, edge[:, half], precision=HIGH)
            corner = jnp.pad(corner, (0, width - half - 1))

        *packed, side = packed_section(
            col, held, got, sum(counts[1:c]), table_pair, kept_rows[parts[c]], marks,
            rim, corner, side, offsets, (gx, gy), closing,
        )
    lines = sent_lines(exchanged(packed), counts[-1], lines)
    values = values + first_axis(lines, table_parts[-1])
    side = jnp.sum(lines[:, :, 2 * counts[-1] :], axis=0) / 6.0
    turned = values.reshape(own, blocks, own, devices, width)
    turned = jnp.transpose(turned, (3, 1, 2, 0, 4))
    turned = [turned[:, b, :, :, : offsets[b + 1]] for b in range(blocks)]
    turned = lax.all_to_all(jnp.concatenate(turned, axis=3), ("gy", "gx"), 0, 0, tiled=True)
    turned = jnp.transpose(turned, (1, 2, 0, 3)).reshape(own, block, -1)

    slab = jnp.minimum(row, gx - 1 - row)
    far_row, far_col = row >= slabs, col >= gy // 2
    pick_rows = jnp.arange(rows)
    pick_rows = slab * rows + jnp.where(far_row, rows - pick_rows, pick_rows)
    pick_cols = jnp.arange(cols)
    pick_cols = jnp.where(far_col, (gy - col) * cols - pick_cols, col * cols + pick_cols)

    if rows == block:
        got, piece = [], None
        for messages in slab_messages(values, turned, side, offsets, slabs):
            if piece is not None:
                messages, piece = lax.optimization_barrier((messages, piece))
                got.append(gathered(piece, gy, got[-1] if got else None))
            piece = lax.all_to_all(messages, "gx", 0, 0, tiled=True)
        got.append(gathered(piece, gy, got[-1] if got else None))
        tiles = width // 128
        start = tile_groups(tiles)[0].stop * own * block
        side = jnp.stack([piece[:, start : start + 3 * own * tiles] for piece in got[0]])
        bit = gy // 2
        while bit:
            paired = side.reshape((-1, 2, bit) + side.shape[1:])
            side = jnp.where((col & bit) == 0, paired, paired[:, ::-1]).reshape(side.shape)
            bit //= 2
        side = side.reshape(devices, own, 3, width)
        side = jnp.transpose(side, (2, 1, 0, 3)).reshape(3, block, width)
        next_plane, across = side[0], rim_rows(side[1:], offsets, pick_rows)
        rim_col = col == gy // 2
        rim = across[:, pick_cols]
        return result_block(
            got, next_plane, across, rim, pick_cols, slab, far_row, rim_col, col, offsets
        )

    side = lax.all_gather(side, ("gy", "gx"), axis=0)
    side = jnp.transpose(side, (2, 1, 0, 3)).reshape(slabs + 1, block, width)
    across = rim_rows(side[slabs - 1 :], offsets, pick_rows)
    next_plane = lax.dynamic_index_in_dim(side, slab, 0, keepdims=False)
    sums = axis_order_sums(values, turned, offsets, block)
    messages = []
    for s in range(slabs):
        base, first = s * rows // block, s * rows
        units = []
        for b in range(blocks):
            size = (b + 1) * block
            near = jnp.zeros((own, rows, size))
            far = jnp.zeros((own, block, size))
            if b >= base:
                near = jnp.stack([sums[b][e][first : first + rows, :size] for e in range(own)])
            else:
                far = jnp.stack([sums[base][e][b * block : size, :size] for e in range(own)])
            units.append(jnp.concatenate([near, far], axis=1))
        messages.append(jnp.concatenate(units, axis=2))
    messages = jnp.stack(messages + messages[::-1])
    got = lax.all_to_all(messages, "gx", 0, 0, tiled=True)
    got = lax.all_gather(got, "gy", axis=0, tiled=True)
    got = jnp.swapaxes(got, 0, 1).reshape(block, rows + block, width)
    base = slab * rows // block
    lower = []
    for b in range(blocks):
        lanes = slice(offsets[b], offsets[b + 1])
        near = jnp.swapaxes(got[:, :rows, lanes], 0, 1)
        far = lax.dynamic_slice_in_dim(got[:, rows:, lanes], lax.rem(slab * rows, block), rows, 0)
        lower.append(jnp.where(b >= base, near, far))
    lower = jnp.concatenate(lower, axis=2)
    lower = jnp.concatenate([lower, next_plane[None]], axis=0)
    body = square([lower[:, :, offsets[b] : offsets[b + 1]] for b in range(blocks)], block)
    body = body[pick_rows - slab * rows]
    body = jnp.concatenate([body, across[:, None, :half]], axis=1)[:, pick_cols]
    body = jnp.concatenate([body, across[:, pick_cols][:, :, None]], axis=2)
    return jnp.concatenate([body, jnp.flip(body[:, :, 1:half], 2)], axis=2)


def rim_rows(side, offsets, pick_rows):
    blocks, block = len(offsets) - 1, offsets[1]
    half = blocks * block
    last = square([side[0][:, offsets[b] : offsets[b + 1]] for b in range(blocks)], block)
    rim = side[1, 0, : half + 1]
    last = jnp.concatenate([last, rim[None, :half]], axis=0)
    return jnp.concatenate([last, rim[:, None]], axis=1)[pick_rows]


def axis_order_sums(values, turned, offsets, block):
    start = 0
    sums = []
    for top in range(len(offsets) - 1):
        size = (top + 1) * block
        parts = []
        for e in range(values.shape[0]):
            part = values[e, :size, offsets[top] : offsets[top] + size]
            lower = [turned[e, :, start + offsets[b] : start + offsets[b + 1]] for b in range(top + 1)]
            parts.append(part + part.T + square(lower, block))
        sums.append(parts)
        start += offsets[top + 1]
    return sums


def message_kernel(offsets, slabs, values, turned, side, *messages):
    blocks, block = len(offsets) - 1, offsets[1]
    values, turned = values[...], turned[...]
    own = values.shape[0]
    sums = axis_order_sums(values, turned, offsets, block)
    groups = tile_groups(offsets[-1] // 128)
    side_start = groups[0].stop * own * block
    messages[0][:, side_start:] = jnp.zeros_like(messages[0][:, side_start:])
    for s in range(slabs):
        places = s, 2 * slabs - 1 - s
        for e in range(own):
            units = []
            for b in range(blocks):
                size = (b + 1) * block
                if b >= s:
                    units.append(sums[b][e][s * block : (s + 1) * block, :size])
                else:
                    units.append(sums[s][e][b * block : size, :size])
            line = jnp.concatenate(units, axis=1)
            for group, out in zip(groups, messages):
                for tile in range(group.start, group.stop):
                    start = ((tile - group.start) * own + e) * block
                    for place in places:
                        out[place, start : start + block] = line[:, tile * 128 : (tile + 1) * 128]
            row = side_start + 3 * e * groups[-1].stop
            for plane in (s, slabs - 1, slabs):
                for tile in range(groups[-1].stop):
                    part = side[e, plane : plane + 1, tile * 128 : (tile + 1) * 128]
                    for place in places:
                        messages[0][place, row : row + 1] = part
                    row += 1


def slab_messages(values, turned, side, offsets, slabs):
    own, block, tiles = values.shape[0], offsets[1], offsets[-1] // 128
    sizes = [(group.stop - group.start) * own * block for group in tile_groups(tiles)]
    sizes[0] += -(-3 * own * tiles // 8) * 8
    return pl.pallas_call(
        lambda *refs: message_kernel(offsets, slabs, *refs),
        in_specs=[pl.BlockSpec(memory_space=pltpu.VMEM)] * 3,
        out_specs=[pl.BlockSpec(memory_space=pltpu.VMEM)] * len(sizes),
        out_shape=[jax.ShapeDtypeStruct((2 * slabs, size, 128), jnp.float32) for size in sizes],
        compiler_params=pltpu.CompilerParams(vmem_limit_bytes=VMEM_BYTES),
    )(values, turned, side)


def result_kernel(
    offsets, own, devices, groups, places, next_plane, across, rim, pick, flip, *refs
):
    blocks, block = len(offsets) - 1, offsets[1]
    tiles = offsets[-1] // 128
    peers = (len(refs) - 2) // len(groups) - 1
    pieces, out = refs[: peers * len(groups)], refs[peers * len(groups)]
    held, sems = refs[peers * len(groups) + 1 : -1], refs[-1]
    step_rows, cols, length = out.shape
    half = length // 2
    slab, far_row, rim_col, me = places[0], places[1], places[2], places[3]
    lane = lax.broadcasted_iota(jnp.int32, (block, 128), 1)
    at_rim = lax.broadcasted_iota(jnp.int32, (cols, half), 0) + (1 - rim_col) == 0
    rim_lane = lax.broadcasted_iota(jnp.int32, rim.shape, 1)
    first_lane = lax.broadcasted_iota(jnp.int32, (cols, half), 1) == 0

    @pl.when(pl.program_id(0) == 0)
    def _():
        copies = []
        for g in range(len(groups)):
            for peer in range(peers):
                piece = pieces[g * peers + peer]
                size = piece.shape[0]
                spot = pl.ds(pl.multiple_of((me ^ peer) * size, size), size)
                copies.append(pltpu.make_async_copy(piece, held[g].at[spot], sems.at[g, peer]))
        for copy in copies:
            copy.start()
        for copy in copies:
            copy.wait()

    def left_half(r):
        t = pl.program_id(0) * step_rows + r
        i = jnp.where(far_row == 1, block - t, t)
        inside = (jnp.zeros((block, 128), jnp.int32) + i) < block
        i = jnp.minimum(i, block - 1)
        source = lax.div(i, devices), lax.rem(i, devices)
        parts = []
        for g, group in enumerate(groups):
            stride = held[g].shape[0] // devices
            for tile in range(group.start, group.stop):
                start = (tile - group.start) * own * block
                near = [
                    held[g][pl.ds(start + e * block + i, devices, stride=stride), :]
                    for e in range(own)
                ]
                near = jnp.concatenate(near, axis=0)
                far = pl.multiple_of(source[1] * stride + start + source[0] * block, 8)
                far = held[g][pl.ds(far, block), :]
                kind = jnp.zeros((block, 128), jnp.int32)
                for b in range(1, blocks):
                    kind += (lane + tile * 128 >= offsets[b]).astype(jnp.int32)
                line = jnp.where(kind >= slab, near, far)
                line = jnp.where(inside, line, next_plane[:, pl.ds(tile * 128, 128)])
                parts.append(line)
        line = jnp.concatenate(parts, axis=1)
        plane = square([line[:, offsets[b] : offsets[b + 1]] for b in range(blocks)], block)
        high, low = split(plane)
        left = jnp.dot(pick[...], high, preferred_element_type=jnp.float32)
        left += jnp.dot(pick[...], low, preferred_element_type=jnp.float32)
        left = jnp.where(at_rim, across[pl.ds(t, 1), :], left)
        out[r, :, pl.ds(0, half)] = left
        return left

    together = 4

    @pl.loop(0, step_rows // together)
    def _(c):
        left = [left_half(c * together + n) for n in range(together)]
        high, low = split(jnp.concatenate(left, axis=0))
        right = jnp.dot(high, flip[...], preferred_element_type=jnp.float32)
        right += jnp.dot(low, flip[...], preferred_element_type=jnp.float32)
        for n in range(together):
            r = c * together + n
            t = pl.program_id(0) * step_rows + r
            edge = jnp.sum(jnp.where(rim_lane == t, rim[...], 0.0), axis=1, keepdims=True)
            part = right[n * cols : (n + 1) * cols]
            out[r, :, pl.ds(half, half)] = jnp.where(first_lane, edge, part)


def result_block(got, next_plane, across, rim, pick_cols, slab, far_row, rim_col, col, offsets):
    block = offsets[1]
    gx = got[0][0].shape[0]
    groups = tile_groups(offsets[-1] // 128)
    devices = gx * len(got[0])
    own = block // devices
    rows, half = across.shape[0], across.shape[1] - 1
    cols = pick_cols.shape[0]
    step_rows = 8
    places = jnp.stack([slab, far_row.astype(jnp.int32), rim_col.astype(jnp.int32), col])
    cell = jnp.arange(half)
    pick = (pick_cols[:, None] == cell[None, :]).astype(jnp.bfloat16)
    flip = (cell[:, None] + cell[None, :] == half).astype(jnp.bfloat16)
    rim = jnp.pad(rim.T, ((0, 0), (0, 128 - rows)))
    whole = lambda array: pl.BlockSpec(array.shape, lambda i: (0,) * array.ndim)
    arrays = (next_plane, across[:, :half], rim, pick, flip)
    pieces = [piece.reshape(-1, 128) for group in got for piece in group]
    return pl.pallas_call(
        lambda *refs: result_kernel(offsets, own, devices, groups, *refs),
        grid=(rows // step_rows,),
        in_specs=[pl.BlockSpec(memory_space=pltpu.SMEM)] + [whole(array) for array in arrays]
        + [pl.BlockSpec(memory_space=pl.ANY)] * len(pieces),
        out_specs=pl.BlockSpec((step_rows, cols, 2 * half), lambda i: (i, 0, 0)),
        out_shape=jax.ShapeDtypeStruct((rows, cols, 2 * half), jnp.float32),
        scratch_shapes=[
            pltpu.VMEM((devices * group[0].shape[1], 128), jnp.float32) for group in got
        ] + [pltpu.SemaphoreType.DMA((len(groups), len(got[0])))],
        compiler_params=pltpu.CompilerParams(vmem_limit_bytes=VMEM_BYTES),
    )(places, *arrays, *pieces)


def tile_groups(tiles):
    return [slice(tile, min(tile + 2, tiles)) for tile in range(0, tiles, 2)]


def swap(peers, bit):
    return [(q, q ^ bit) for q in range(peers)]


def gathered(piece, peers, after):
    if after is not None:
        piece, first_hops = lax.optimization_barrier((piece, after[1:3]))
        after[1:3] = first_hops
    pieces, bit = {0: piece}, peers // 2
    while bit:
        for place in list(pieces):
            pieces[place ^ bit] = lax.ppermute(pieces[place], "gy", swap(peers, bit))
        bit //= 2
    return [pieces[place] for place in range(peers)]


def exchanged(packed):
    gy = len(packed)
    return [packed[0]] + [lax.ppermute(packed[p], "gy", swap(gy, p)) for p in range(1, gy)]


def sent_lines(got, count, after):
    gy = len(got)
    lines = [sum(got[p][:count] for p in range(first, gy, 2)) for first in range(2)]
    lines = jnp.concatenate(lines + [sum(piece[count:] for piece in got)], axis=0)
    lines = jnp.transpose(lines, (2, 1, 0, 3))
    if after is not None:
        lines, _ = lax.optimization_barrier((lines, after))
    return lax.all_to_all(lines, "gx", 0, 0, tiled=True)


def first_axis(lines, table):
    gx, _, count, half = table.shape
    table = table.reshape(gx, 2 * count, half)
    return jnp.einsum("geaw,gai->eiw", lines[:, :, : 2 * count], table, precision=HIGH)


def row_parts(rows):
    if rows < 4 * PART_STEP:
        return [slice(0, rows)]
    return [slice(PART_STEP, rows - PART_STEP), slice(0, PART_STEP), slice(rows - PART_STEP, rows)]


def square(lower, block):
    if len(lower) == 1:
        return lower[0]
    split_at = len(lower) // 2
    size = split_at * block
    first = square(lower[:split_at], block)
    corner = jnp.concatenate([line[..., :size] for line in lower[split_at:]], axis=-2)
    last = square([line[..., size:] for line in lower[split_at:]], block)
    top = jnp.concatenate([first, jnp.swapaxes(corner, -1, -2)], axis=-1)
    return jnp.concatenate([top, jnp.concatenate([corner, last], axis=-1)], axis=-2)


def solution(mesh):
    placed = (P("gx", "gy", None), P())
    return jax.shard_map(
        on_device, mesh=mesh, in_specs=placed, out_specs=P("gx", "gy", None), check_vma=False
    )
```

```python
import math

import jax
import jax.numpy as jnp
import numpy as np
from jax import lax
from jax.experimental import pallas as pl
from jax.experimental.pallas import tpu as pltpu
from jax.sharding import PartitionSpec as P

SWEEPS = 2

AXIS_ORDERS = ((0, 1, 2), (0, 2, 1), (1, 0, 2), (1, 2, 0), (2, 0, 1), (2, 1, 0))

HIGH = lax.Precision.HIGH


def ring(axis):
    peers = lax.axis_size(axis)
    up = [(i, (i + 1) % peers) for i in range(peers)]
    return up, [(j, i) for i, j in up]


FREE = ((8 - SWEEPS, 8 - SWEEPS), (0, 0))


def side_faces(block):
    cols = block.shape[1]
    right, left = ring("gy")
    before = lax.ppermute(block[:, cols - SWEEPS :], "gy", right)
    after = lax.ppermute(block[:, :SWEEPS], "gy", left)
    return jnp.concatenate([before, after], axis=1)


def end_faces(block, sides):
    rows = block.shape[0]
    up, down = ring("gx")
    last = jnp.concatenate([block[rows - SWEEPS :], sides[rows - SWEEPS :]], axis=1)
    first = jnp.concatenate([block[:SWEEPS], sides[:SWEEPS]], axis=1)
    return lax.ppermute(last, "gx", up), lax.ppermute(first, "gx", down)


def mirror(values, axis):
    return jnp.roll(jnp.flip(values, axis), 1, axis)


def symmetric_marks(marks):
    for flip_axis in range(3):
        marks = jnp.maximum(marks, mirror(marks, flip_axis))
    united = marks
    for axis_order in AXIS_ORDERS[1:]:
        united = jnp.maximum(united, jnp.transpose(marks, axis_order))
    return united


def cosine_table(length):
    position = np.arange(length)
    phases = np.mod(position[:, None] * position[None, : length // 2 + 1], length)
    return (np.cos(phases * (2.0 * math.pi / length)) / math.sqrt(length)).astype(np.float32)


MARGIN = 16
CHUNK = 16
STEP_ROWS = 16
PART_STEP = 8
VMEM_BYTES = 56 * 1024 * 1024


def split(values):
    high = values.astype(jnp.bfloat16)
    low = (values - high.astype(jnp.float32)).astype(jnp.bfloat16)
    return high, low


def fill_kernel(
    base, here, above, below, top, bottom, sides, marks, table_high, table_low,
    spectrum, alternate, edge, punched, once, high, low, folded,
):
    step_rows, cols, length = here.shape
    step = base[pl.program_id(0)]
    first_row = step * step_rows
    local_row = pl.program_id(0) * step_rows
    period = marks.shape[0]
    lane = lax.broadcasted_iota(jnp.int32, (128, 128), 1)
    signs = jnp.where(lax.broadcasted_iota(jnp.int32, (128, 128), 0) % 2 == 0, 1.0, -1.0)

    @pl.when(pl.program_id(0) == 0)
    def _():
        edge[...] = jnp.zeros_like(edge)

    def holes(row, start, size):
        row = lax.rem(first_row + row, period)
        start = start % period
        if start + size <= period:
            part = marks[row, pl.ds(start, size), :]
        else:
            part = jnp.concatenate(
                [marks[row, pl.ds(start, period - start), :], marks[row, pl.ds(0, start + size - period), :]],
                axis=0,
            )
        return jnp.concatenate([part] * (length // 128), axis=1)

    def punch(row, start, values):
        kept = jnp.where(holes(row, start, values.shape[0]) > 0.0, 0.0, values)
        punched[row, pl.ds(start, values.shape[0]), :] = kept

    def punch_row(row, source, index):
        for c in range(0, cols, CHUNK):
            punch(row, MARGIN + c, source[index, pl.ds(c, CHUNK), :])

    def punch_sides(row):
        full = first_row + row - SWEEPS
        punch(row, MARGIN - 8, sides[full, pl.ds(0, 8), :])
        punch(row, MARGIN + cols, sides[full, pl.ds(8, 8), :])

    def neighbours(ref, row, start):
        middle = ref[row, pl.ds(start, CHUNK), :]
        total = ref[row - 1, pl.ds(start, CHUNK), :] + ref[row + 1, pl.ds(start, CHUNK), :]
        total += ref[row, pl.ds(start - 1, CHUNK), :] + ref[row, pl.ds(start + 1, CHUNK), :]
        return total + pltpu.roll(middle, 1, 1) + pltpu.roll(middle, length - 1, 1)

    last = sides.shape[0] // step_rows - 1
    for edge_rows, inside, offset, outer in (
        (above, step > 0, 0, top),
        (below, step < last, step_rows + SWEEPS, bottom),
    ):
        @pl.when(inside)
        def _():
            for r in range(SWEEPS):
                punch_row(offset + r, edge_rows, r)
                punch_sides(offset + r)

        @pl.when(jnp.logical_not(inside))
        def _():
            for r in range(SWEEPS):
                punch_row(offset + r, outer, r)
                punch(offset + r, MARGIN - SWEEPS, outer[r, pl.ds(cols, SWEEPS), :])
                punch(offset + r, MARGIN + cols, outer[r, pl.ds(cols + SWEEPS, SWEEPS), :])

    @pl.loop(0, step_rows)
    def _(r):
        punch_row(r + SWEEPS, here, r)
        punch_sides(r + SWEEPS)

    @pl.loop(1, step_rows + 2 * SWEEPS - 1, unroll=2)
    def _(r):
        for start in range(MARGIN - 8, MARGIN + cols + 8, CHUNK):
            total = neighbours(punched, r, start) * holes(r, start, CHUNK)
            once[r, pl.ds(start, CHUNK), :] = punched[r, pl.ds(start, CHUNK), :] + total

    @pl.loop(0, step_rows)
    def _(r):
        for c in range(0, cols, CHUNK):
            start = MARGIN + c
            total = neighbours(once, r + SWEEPS, start) * holes(r + SWEEPS, start, CHUNK)
            filled = punched[r + SWEEPS, pl.ds(start, CHUNK), :] + total
            first, second = split(filled)
            spot = pl.ds(pl.multiple_of(r * cols + c, CHUNK), CHUNK)
            high[spot, :] = first
            low[spot, :] = second
            wrapped = filled[:, :128]
            for tile in range(1, length // 128):
                wrapped += filled[:, tile * 128 : (tile + 1) * 128]
            folded[pl.ds(c, CHUNK), :] = wrapped
        column = jnp.where(lane == local_row + r, signs, 0.0).astype(jnp.bfloat16)
        first, second = split(folded[...])
        total = jnp.dot(first, column, preferred_element_type=jnp.float32)
        total += jnp.dot(second, column, preferred_element_type=jnp.float32)
        edge[...] += total

    rows_each = 8
    half = spectrum.shape[2]
    order = lax.broadcasted_iota(jnp.int32, (rows_each, cols, half), 1)

    @pl.loop(0, step_rows // rows_each)
    def _(r):
        spot = pl.ds(pl.multiple_of(r * rows_each * cols, CHUNK), rows_each * cols)
        first, second = high[spot, :], low[spot, :]
        total = jnp.dot(first, table_low[...], preferred_element_type=jnp.float32)
        total += jnp.dot(second, table_high[...], preferred_element_type=jnp.float32)
        total += jnp.dot(first, table_high[...], preferred_element_type=jnp.float32)
        total = total.reshape(rows_each, cols, half)
        spectrum[pl.ds(r * rows_each, rows_each)] = total
        signed = jnp.sum(jnp.where(order % 2 == 0, total, -total), axis=1)
        alternate[pl.ds(pl.multiple_of(r * rows_each, rows_each), rows_each), :] = signed


def rounded_parts(table):
    rounded = lax.reduce_precision(table, 8, 7)
    return rounded.astype(jnp.bfloat16), (table - rounded).astype(jnp.bfloat16)


def marks_kernel(shifts, template, out, held):
    period = template.shape[0]
    repeats = held.shape[1] // period
    line = lax.broadcasted_iota(jnp.int32, (period, period), 0)
    across = lax.broadcasted_iota(jnp.int32, (period, period), 1)
    flip = jnp.where((line + across) % period == 0, 1.0, 0.0)
    for i in range(period):
        plane = jnp.maximum(template[i], template[-i % period]).astype(jnp.float32)
        plane = jnp.maximum(plane, jnp.dot(flip, plane, preferred_element_type=jnp.float32))
        plane = jnp.maximum(plane, jnp.dot(plane, flip, preferred_element_type=jnp.float32))
        plane = jnp.maximum(plane, plane.T)
        held[i * period : (i + 1) * period, :] = jnp.concatenate([plane] * repeats, axis=1)
    for i in range(period):
        plane = held[i * period : (i + 1) * period, :]
        turned = held[pl.ds(i, period, stride=period), :]
        back = turned[:, :period].T
        plane = jnp.maximum(jnp.maximum(plane, turned), jnp.concatenate([back] * repeats, axis=1))
        plane = jnp.where(plane == 1.0, 1.0 / 6.0, 0.0)
        shift = shifts[1]
        out[(i - shifts[0]) % period] = jnp.concatenate([plane[shift:], plane[:shift]], axis=0)


def hole_marks(template, row, col, rows, cols):
    period = template.shape[0]
    shape = (period, period, 128)
    if rows % period == 0 and cols % period == 0:
        shifts = (-SWEEPS % period, -MARGIN % period)
        return pl.pallas_call(
            lambda *refs: marks_kernel(shifts, *refs),
            in_specs=[pl.BlockSpec(memory_space=pltpu.VMEM)],
            out_specs=pl.BlockSpec(memory_space=pltpu.VMEM),
            out_shape=jax.ShapeDtypeStruct(shape, jnp.float32),
            scratch_shapes=[pltpu.VMEM((period * period, 128), jnp.float32)],
        )(template)
    shifts = (jnp.mod(row * rows - SWEEPS, period), jnp.mod(col * cols - MARGIN, period))
    marks = jnp.roll(symmetric_marks(template), (-shifts[0], -shifts[1]), (0, 1))
    return jnp.tile(marks.astype(jnp.float32) / 6.0, (1, 1, 128 // period))


def fill_constants(intensity, template, row, col, main):
    rows, cols, _ = intensity.shape
    high = main.astype(jnp.bfloat16)
    low = (main - high.astype(np.float32)).astype(jnp.bfloat16)
    return hole_marks(template, row, col, rows, cols), jnp.asarray(high), jnp.asarray(low)


def filled_spectrum(intensity, arrays, first, parts):
    rows, cols, length = intensity.shape
    half = length // 2
    aligned = all(edge % STEP_ROWS == 0 for part in parts for edge in (part.start, part.stop))
    step_rows = STEP_ROWS if aligned else PART_STEP
    starts = [start for part in parts for start in range(part.start, part.stop, step_rows)]
    count = step_rows * len(starts)
    steps = jnp.stack([(first + start) // step_rows for start in starts])
    pairs = step_rows // SWEEPS
    last = rows // SWEEPS - 1
    whole = lambda array: pl.BlockSpec(array.shape, lambda i, b: (0,) * array.ndim)
    before = lambda i, b: (jnp.maximum(b[i] * pairs - 1, 0), 0, 0)
    after = lambda i, b: (jnp.minimum((b[i] + 1) * pairs, last), 0, 0)
    padded = (step_rows + 2 * SWEEPS, cols + 2 * MARGIN, length)
    return pl.pallas_call(
        fill_kernel,
        grid_spec=pltpu.PrefetchScalarGridSpec(
            num_scalar_prefetch=1,
            grid=(len(starts),),
            in_specs=[
                pl.BlockSpec((step_rows, cols, length), lambda i, b: (b[i], 0, 0)),
                pl.BlockSpec((SWEEPS, cols, length), before),
                pl.BlockSpec((SWEEPS, cols, length), after),
            ] + [whole(array) for array in arrays],
            out_specs=[
                pl.BlockSpec((step_rows, cols, half), lambda i, b: (i, 0, 0)),
                pl.BlockSpec((step_rows, half), lambda i, b: (i, 0)),
                pl.BlockSpec((cols, 128), lambda i, b: (0, 0)),
            ],
            scratch_shapes=[
                pltpu.VMEM(padded, jnp.float32),
                pltpu.VMEM(padded, jnp.float32),
                pltpu.VMEM((step_rows * cols, length), jnp.bfloat16),
                pltpu.VMEM((step_rows * cols, length), jnp.bfloat16),
                pltpu.VMEM((cols, 128), jnp.float32),
            ],
        ),
        out_shape=[
            jax.ShapeDtypeStruct((count, cols, half), jnp.float32),
            jax.ShapeDtypeStruct((count, half), jnp.float32),
            jax.ShapeDtypeStruct((cols, 128), jnp.float32),
        ],
        compiler_params=pltpu.CompilerParams(vmem_limit_bytes=VMEM_BYTES),
        cost_estimate=pl.CostEstimate(
            flops=count * cols * length * half * 6,
            bytes_accessed=count * cols * (length + half) * 4,
            transcendentals=0,
        ),
    )(steps, intensity, intensity, intensity, *arrays)


def pack(section, offsets):
    block = offsets[1]
    units = [section[b * block : (b + 1) * block, : (b + 1) * block] for b in range(len(offsets) - 1)]
    return jnp.concatenate(units, axis=1)


def three_dots(left, right):
    total = jnp.dot(left[1], right[0], preferred_element_type=jnp.float32)
    total += jnp.dot(left[0], right[1], preferred_element_type=jnp.float32)
    return total + jnp.dot(left[0], right[0], preferred_element_type=jnp.float32)


def section_kernel(
    offsets, planes, opening, closing, me, weights, kept, got, cols_high, cols_low, rows_high,
    rows_low, *refs
):
    step, steps = pl.program_id(0), pl.num_programs(0)
    step_rows = kept.shape[0]
    half, count = rows_high.shape
    before = None if opening else refs[0]
    refs = refs if opening else refs[1:]
    rim, corner = refs[:2] if closing else (None, None)
    *outs, total, lines, packed = refs[2:] if closing else refs
    block, width = total.shape[1:]
    gy, (_, own, gx, _) = len(outs), outs[0].shape

    def place(layer, values, slot=0):
        packed[slot] = values
        for e in range(own):
            for p in range(gy):
                start = pl.multiple_of((e * gy + (p ^ me[0])) * gx, gx)
                outs[p][layer, e] = packed[slot, pl.ds(start, gx), :]

    @pl.when(step == 0)
    def _():
        total[...] = jnp.zeros_like(total) if opening else before[...]

    for r in range(step_rows):
        layer = step * step_rows + r
        values = jnp.concatenate([kept[r], got[r]], axis=0)
        section = three_dots((cols_high[...], cols_low[...]), split(values))
        section = section + section.T
        line = pack(section, offsets)
        place(layer, line, r)
        for m in range(planes):
            total[m] += weights[m, layer] * line
        for m in range(planes - 1):
            row = (m + 1) * (half // planes)
            lines[m, pl.ds(layer, 1), :] = section[row : row + 1]

    @pl.when(step == steps - 1)
    def _():
        for m in range(planes - 1):
            plane = three_dots((rows_high[...], rows_low[...]), split(lines[m]))
            total[m] += pack(plane + plane.T, offsets)
        if closing:
            total[planes - 1] += pack(rim[...] + rim[...].T, offsets)
            for m in range(planes):
                place(count + m, total[m])
            place(count + planes, jnp.zeros((block, width), jnp.float32) + corner[...])


def packed_section(col, kept, got, first, table_pair, table_rows, marks, rim, corner, before, offsets, shape, closing):
    _, cols, half = kept.shape
    count = table_rows.shape[0]
    planes, block, width = len(marks), offsets[1], offsets[-1]
    gx, gy = shape
    opening = before is None
    step_rows = 4
    layers = count + (planes + 1 if closing else 0)
    whole = lambda array: pl.BlockSpec(array.shape, lambda i: (0,) * array.ndim)
    weights = jnp.stack([table_rows[:, m] for m in marks])
    arrays = rounded_parts(table_pair.T) + rounded_parts(table_rows[:, :half].T)
    arrays += (() if opening else (before,)) + ((rim, corner[None]) if closing else ())
    out = jax.ShapeDtypeStruct((layers, block // (gx * gy), gx, width), jnp.float32)
    outs = [out] * gy + [jax.ShapeDtypeStruct((planes, block, width), jnp.float32)]
    rows_spec = pl.BlockSpec((step_rows, cols, half), lambda i: (i + first // step_rows, 0, 0))
    return pl.pallas_call(
        lambda *refs: section_kernel(offsets, planes, opening, closing, *refs),
        grid=(count // step_rows,),
        in_specs=[pl.BlockSpec(memory_space=pltpu.SMEM)] * 2 + [rows_spec, rows_spec]
        + [whole(array) for array in arrays],
        out_specs=[whole(out) for out in outs],
        out_shape=outs,
        scratch_shapes=[
            pltpu.VMEM((planes, count, half), jnp.float32),
            pltpu.VMEM((step_rows, block, width), jnp.float32),
        ],
        compiler_params=pltpu.CompilerParams(vmem_limit_bytes=VMEM_BYTES),
        cost_estimate=pl.CostEstimate(
            flops=count * 12 * cols * half * half,
            bytes_accessed=count * cols * half * 16,
            transcendentals=0,
        ),
    )(col.reshape(1), weights, kept, got, *arrays)


def on_device(intensity, template):
    rows, cols, length = intensity.shape
    gx, gy = lax.axis_size("gx"), lax.axis_size("gy")
    row, col = lax.axis_index("gx"), lax.axis_index("gy")
    devices, half = gx * gy, length // 2
    block = max(devices, rows)
    blocks, own, slabs = half // block, block // devices, gx // 2
    offsets = [block * b * (b + 1) // 2 for b in range(blocks + 1)]
    width = offsets[blocks]
    table = jnp.asarray(cosine_table(length))
    main = table[:, :half]

    pair_rows = rows // 2
    parts = row_parts(pair_rows)
    counts = [part.stop - part.start for part in parts]
    core = lax.rem(col, 2)
    constants = fill_constants(intensity, template, row, col, cosine_table(length)[:, :half])
    sides = side_faces(intensity)
    given_first, kept_first = (1 - core) * pair_rows, core * pair_rows
    inner = parts[0].start >= SWEEPS and parts[0].stop <= pair_rows - SWEEPS
    side_columns = jnp.pad(sides, ((0, 0),) + FREE)
    blank = jnp.zeros((SWEEPS, cols + 2 * SWEEPS, length), jnp.float32)
    ends = (blank, blank) if inner else end_faces(intensity, sides)

    def fill(some, start):
        arrays = tuple(ends) + (side_columns,) + constants
        return list(filled_spectrum(intensity, arrays, start, some))

    given, kept = [fill(parts[:1], given_first)], []
    outer = ends
    if inner:
        given[0], late_sides = lax.optimization_barrier((given[0], sides))
        outer = end_faces(intensity, late_sides)
    kept.append(fill(parts[:1], kept_first))
    ends = outer

    table_cols = lax.dynamic_slice_in_dim(table, col * cols, cols, 0)
    kept_rows = lax.dynamic_slice_in_dim(table, row * rows + kept_first, pair_rows, 0)
    marks = [rows * (m + 1) for m in range(slabs)]
    mates = lax.dynamic_slice_in_dim(main, (col + 1 - 2 * core) * cols, cols, 0)
    table_pair = jnp.concatenate([table_cols[:, :half], mates], axis=0)
    table_parts = main.reshape(gx, 2, pair_rows, half) / 6.0
    table_parts = jnp.where(core == 0, table_parts, table_parts[:, ::-1])
    table_parts = [table_parts[:, :, part] for part in parts]
    side = rim = corner = None
    values, packed, lines = 0.0, None, None
    for c, count in enumerate(counts):
        closing = c == len(counts) - 1
        if c == 1:
            behind = (given_first, kept_first), packed
            starts, packed = lax.optimization_barrier(behind)
            given.append(fill(parts[1:], starts[0]))
            kept.append(fill(parts[1:], starts[1]))
        flanks = [piece[1:] for piece in given + kept]
        if c > 1:
            flanks, packed = lax.optimization_barrier((flanks, packed))
        if c > 0:
            got_lines = exchanged(packed)
        if c == 1:
            behind = given[1][0], kept[1][0], got_lines
            given[1][0], kept[1][0], got_lines = lax.optimization_barrier(behind)
        if c < 2:
            got = lax.ppermute(given[c][0], "gy", swap(gy, 1))
            held = kept[c][0]
        if c > 0:
            lines = sent_lines(got_lines, counts[c - 1], lines)
            values = values + first_axis(lines, table_parts[c - 1])
        if closing:
            given_rows = lax.dynamic_slice_in_dim(table, row * rows + given_first, pair_rows, 0)
            ordered_rows = [held_rows[part] for held_rows in (given_rows, kept_rows) for part in parts]
            ordered_rows = jnp.concatenate(ordered_rows, axis=0)
            alternate = jnp.concatenate([piece[0] for piece in flanks], axis=0) / math.sqrt(length)
            edge = [piece[1][:, : piece[0].shape[0]] for piece in flanks]
            edge = jnp.concatenate(edge, axis=1)
            edge = jnp.einsum("ba,bk->ak", edge / math.sqrt(length), table_cols, precision=HIGH)
            edge = edge + jnp.concatenate([alternate, edge[:, half:]], axis=1)
            rim = jnp.einsum("aj,ak->jk", ordered_rows[:, :half], edge[:, :half], precision=HIGH)
            corner = 2.0 * jnp.einsum("a,ak->k", ordered_rows[:, half], edge, precision=HIGH)
            corner = corner + jnp.einsum("aj,a->j", ordered_rows, edge[:, half], precision=HIGH)
            corner = jnp.pad(corner, (0, width - half - 1))

        *packed, side = packed_section(
            col, held, got, sum(counts[1:c]), table_pair, kept_rows[parts[c]], marks,
            rim, corner, side, offsets, (gx, gy), closing,
        )
    lines = sent_lines(exchanged(packed), counts[-1], lines)
    values = values + first_axis(lines, table_parts[-1])
    side = jnp.sum(lines[:, :, 2 * counts[-1] :], axis=0) / 6.0
    turned = values.reshape(own, blocks, own, devices, width)
    turned = jnp.transpose(turned, (3, 1, 2, 0, 4))
    turned = [turned[:, b, :, :, : offsets[b + 1]] for b in range(blocks)]
    turned = lax.all_to_all(jnp.concatenate(turned, axis=3), ("gy", "gx"), 0, 0, tiled=True)
    turned = jnp.transpose(turned, (1, 2, 0, 3)).reshape(own, block, -1)

    slab = jnp.minimum(row, gx - 1 - row)
    far_row, far_col = row >= slabs, col >= gy // 2
    pick_rows = jnp.arange(rows)
    pick_rows = slab * rows + jnp.where(far_row, rows - pick_rows, pick_rows)
    pick_cols = jnp.arange(cols)
    pick_cols = jnp.where(far_col, (gy - col) * cols - pick_cols, col * cols + pick_cols)

    if rows == block:
        got, piece = [], None
        for messages in slab_messages(values, turned, side, offsets, slabs):
            if piece is not None:
                messages, piece = lax.optimization_barrier((messages, piece))
                got.append(gathered(piece, gy, got[-1] if got else None))
            piece = lax.all_to_all(messages, "gx", 0, 0, tiled=True)
        got.append(gathered(piece, gy, got[-1] if got else None))
        tiles = width // 128
        start = tile_groups(tiles)[0].stop * own * block
        side = jnp.stack([piece[:, start : start + 3 * own * tiles] for piece in got[0]])
        bit = gy // 2
        while bit:
            paired = side.reshape((-1, 2, bit) + side.shape[1:])
            side = jnp.where((col & bit) == 0, paired, paired[:, ::-1]).reshape(side.shape)
            bit //= 2
        side = side.reshape(devices, own, 3, width)
        side = jnp.transpose(side, (2, 1, 0, 3)).reshape(3, block, width)
        next_plane, across = side[0], rim_rows(side[1:], offsets, pick_rows)
        rim_col = col == gy // 2
        rim = across[:, pick_cols]
        return result_block(
            got, next_plane, across, rim, pick_cols, slab, far_row, rim_col, col, offsets
        )

    side = lax.all_gather(side, ("gy", "gx"), axis=0)
    side = jnp.transpose(side, (2, 1, 0, 3)).reshape(slabs + 1, block, width)
    across = rim_rows(side[slabs - 1 :], offsets, pick_rows)
    next_plane = lax.dynamic_index_in_dim(side, slab, 0, keepdims=False)
    sums = axis_order_sums(values, turned, offsets, block)
    messages = []
    for s in range(slabs):
        base, first = s * rows // block, s * rows
        units = []
        for b in range(blocks):
            size = (b + 1) * block
            near = jnp.zeros((own, rows, size))
            far = jnp.zeros((own, block, size))
            if b >= base:
                near = jnp.stack([sums[b][e][first : first + rows, :size] for e in range(own)])
            else:
                far = jnp.stack([sums[base][e][b * block : size, :size] for e in range(own)])
            units.append(jnp.concatenate([near, far], axis=1))
        messages.append(jnp.concatenate(units, axis=2))
    messages = jnp.stack(messages + messages[::-1])
    got = lax.all_to_all(messages, "gx", 0, 0, tiled=True)
    got = lax.all_gather(got, "gy", axis=0, tiled=True)
    got = jnp.swapaxes(got, 0, 1).reshape(block, rows + block, width)
    base = slab * rows // block
    lower = []
    for b in range(blocks):
        lanes = slice(offsets[b], offsets[b + 1])
        near = jnp.swapaxes(got[:, :rows, lanes], 0, 1)
        far = lax.dynamic_slice_in_dim(got[:, rows:, lanes], lax.rem(slab * rows, block), rows, 0)
        lower.append(jnp.where(b >= base, near, far))
    lower = jnp.concatenate(lower, axis=2)
    lower = jnp.concatenate([lower, next_plane[None]], axis=0)
    body = square([lower[:, :, offsets[b] : offsets[b + 1]] for b in range(blocks)], block)
    body = body[pick_rows - slab * rows]
    body = jnp.concatenate([body, across[:, None, :half]], axis=1)[:, pick_cols]
    body = jnp.concatenate([body, across[:, pick_cols][:, :, None]], axis=2)
    return jnp.concatenate([body, jnp.flip(body[:, :, 1:half], 2)], axis=2)


def rim_rows(side, offsets, pick_rows):
    blocks, block = len(offsets) - 1, offsets[1]
    half = blocks * block
    last = square([side[0][:, offsets[b] : offsets[b + 1]] for b in range(blocks)], block)
    rim = side[1, 0, : half + 1]
    last = jnp.concatenate([last, rim[None, :half]], axis=0)
    return jnp.concatenate([last, rim[:, None]], axis=1)[pick_rows]


def axis_order_sums(values, turned, offsets, block):
    start = 0
    sums = []
    for top in range(len(offsets) - 1):
        size = (top + 1) * block
        parts = []
        for e in range(values.shape[0]):
            part = values[e, :size, offsets[top] : offsets[top] + size]
            lower = [turned[e, :, start + offsets[b] : start + offsets[b + 1]] for b in range(top + 1)]
            parts.append(part + part.T + square(lower, block))
        sums.append(parts)
        start += offsets[top + 1]
    return sums


def message_kernel(offsets, slabs, values, turned, side, *messages):
    blocks, block = len(offsets) - 1, offsets[1]
    values, turned = values[...], turned[...]
    own = values.shape[0]
    sums = axis_order_sums(values, turned, offsets, block)
    groups = tile_groups(offsets[-1] // 128)
    side_start = groups[0].stop * own * block
    messages[0][:, side_start:] = jnp.zeros_like(messages[0][:, side_start:])
    for s in range(slabs):
        places = s, 2 * slabs - 1 - s
        for e in range(own):
            units = []
            for b in range(blocks):
                size = (b + 1) * block
                if b >= s:
                    units.append(sums[b][e][s * block : (s + 1) * block, :size])
                else:
                    units.append(sums[s][e][b * block : size, :size])
            line = jnp.concatenate(units, axis=1)
            for group, out in zip(groups, messages):
                for tile in range(group.start, group.stop):
                    start = ((tile - group.start) * own + e) * block
                    for place in places:
                        out[place, start : start + block] = line[:, tile * 128 : (tile + 1) * 128]
            row = side_start + 3 * e * groups[-1].stop
            for plane in (s, slabs - 1, slabs):
                for tile in range(groups[-1].stop):
                    part = side[e, plane : plane + 1, tile * 128 : (tile + 1) * 128]
                    for place in places:
                        messages[0][place, row : row + 1] = part
                    row += 1


def slab_messages(values, turned, side, offsets, slabs):
    own, block, tiles = values.shape[0], offsets[1], offsets[-1] // 128
    sizes = [(group.stop - group.start) * own * block for group in tile_groups(tiles)]
    sizes[0] += -(-3 * own * tiles // 8) * 8
    return pl.pallas_call(
        lambda *refs: message_kernel(offsets, slabs, *refs),
        in_specs=[pl.BlockSpec(memory_space=pltpu.VMEM)] * 3,
        out_specs=[pl.BlockSpec(memory_space=pltpu.VMEM)] * len(sizes),
        out_shape=[jax.ShapeDtypeStruct((2 * slabs, size, 128), jnp.float32) for size in sizes],
        compiler_params=pltpu.CompilerParams(vmem_limit_bytes=VMEM_BYTES),
    )(values, turned, side)


def result_kernel(
    offsets, own, devices, groups, places, next_plane, across, rim, pick, flip, *refs
):
    blocks, block = len(offsets) - 1, offsets[1]
    tiles = offsets[-1] // 128
    peers = (len(refs) - 2) // len(groups) - 1
    pieces, out = refs[: peers * len(groups)], refs[peers * len(groups)]
    held, sems = refs[peers * len(groups) + 1 : -1], refs[-1]
    step_rows, cols, length = out.shape
    half = length // 2
    slab, far_row, rim_col, me = places[0], places[1], places[2], places[3]
    lane = lax.broadcasted_iota(jnp.int32, (block, 128), 1)
    at_rim = lax.broadcasted_iota(jnp.int32, (cols, half), 0) + (1 - rim_col) == 0
    first_lane = lax.broadcasted_iota(jnp.int32, (cols, 128), 1) == 0

    @pl.when(pl.program_id(0) == 0)
    def _():
        copies = []
        for g in range(len(groups)):
            for peer in range(peers):
                piece = pieces[g * peers + peer]
                size = piece.shape[0]
                spot = pl.ds(pl.multiple_of((me ^ peer) * size, size), size)
                copies.append(pltpu.make_async_copy(piece, held[g].at[spot], sems.at[g, peer]))
        for copy in copies:
            copy.start()
        for copy in copies:
            copy.wait()

    def left_half(r, may_pass):
        t = pl.program_id(0) * step_rows + r
        i = jnp.where(far_row == 1, block - t, t)
        inside = (jnp.zeros((block, 128), jnp.int32) + i) < block
        i = jnp.minimum(i, block - 1)
        source = lax.div(i, devices), lax.rem(i, devices)
        parts = []
        for g, group in enumerate(groups):
            stride = held[g].shape[0] // devices
            for tile in range(group.start, group.stop):
                start = (tile - group.start) * own * block
                near = [
                    held[g][pl.ds(start + e * block + i, devices, stride=stride), :]
                    for e in range(own)
                ]
                near = jnp.concatenate(near, axis=0)
                line = near
                if tile * 128 < offsets[blocks - 1]:
                    far = pl.multiple_of(source[1] * stride + start + source[0] * block, 8)
                    far = held[g][pl.ds(far, block), :]
                    kind = jnp.zeros((block, 128), jnp.int32)
                    for b in range(1, blocks):
                        kind += (lane + tile * 128 >= offsets[b]).astype(jnp.int32)
                    line = jnp.where(kind >= slab, near, far)
                if may_pass:
                    line = jnp.where(inside, line, next_plane[:, pl.ds(tile * 128, 128)])
                parts.append(line)
        line = jnp.concatenate(parts, axis=1)
        plane = square([line[:, offsets[b] : offsets[b + 1]] for b in range(blocks)], block)
        high, low = split(plane)
        left = jnp.dot(pick[...], high, preferred_element_type=jnp.float32)
        left += jnp.dot(pick[...], low, preferred_element_type=jnp.float32)
        left = jnp.where(at_rim, across[pl.ds(t, 1), :], left)
        out[r, :, pl.ds(0, half)] = left
        return left

    together = 4

    @pl.loop(0, step_rows // together)
    def _(c):
        left = [left_half(c * together + n, n == 0) for n in range(together)]
        high, low = split(jnp.concatenate(left, axis=0))
        right = jnp.dot(high, flip[...], preferred_element_type=jnp.float32)
        right += jnp.dot(low, flip[...], preferred_element_type=jnp.float32)
        for n in range(together):
            r = c * together + n
            t = pl.program_id(0) * step_rows + r
            edge = pltpu.roll(rim[...], lax.rem(128 - t, 128), 1)
            part = right[n * cols : (n + 1) * cols]
            out[r, :, pl.ds(half, 128)] = jnp.where(first_lane, edge, part[:, :128])
            out[r, :, pl.ds(half + 128, half - 128)] = part[:, 128:]


def result_block(got, next_plane, across, rim, pick_cols, slab, far_row, rim_col, col, offsets):
    block = offsets[1]
    gx = got[0][0].shape[0]
    groups = tile_groups(offsets[-1] // 128)
    devices = gx * len(got[0])
    own = block // devices
    rows, half = across.shape[0], across.shape[1] - 1
    cols = pick_cols.shape[0]
    step_rows = 8
    places = jnp.stack([slab, far_row.astype(jnp.int32), rim_col.astype(jnp.int32), col])
    cell = jnp.arange(half)
    pick = (pick_cols[:, None] == cell[None, :]).astype(jnp.bfloat16)
    flip = (cell[:, None] + cell[None, :] == half).astype(jnp.bfloat16)
    rim = jnp.pad(rim.T, ((0, 0), (0, 128 - rows)))
    whole = lambda array: pl.BlockSpec(array.shape, lambda i: (0,) * array.ndim)
    arrays = (next_plane, across[:, :half], rim, pick, flip)
    pieces = [piece.reshape(-1, 128) for group in got for piece in group]
    return pl.pallas_call(
        lambda *refs: result_kernel(offsets, own, devices, groups, *refs),
        grid=(rows // step_rows,),
        in_specs=[pl.BlockSpec(memory_space=pltpu.SMEM)] + [whole(array) for array in arrays]
        + [pl.BlockSpec(memory_space=pl.ANY)] * len(pieces),
        out_specs=pl.BlockSpec((step_rows, cols, 2 * half), lambda i: (i, 0, 0)),
        out_shape=jax.ShapeDtypeStruct((rows, cols, 2 * half), jnp.float32),
        scratch_shapes=[
            pltpu.VMEM((devices * group[0].shape[1], 128), jnp.float32) for group in got
        ] + [pltpu.SemaphoreType.DMA((len(groups), len(got[0])))],
        compiler_params=pltpu.CompilerParams(vmem_limit_bytes=VMEM_BYTES),
    )(places, *arrays, *pieces)


def tile_groups(tiles):
    return [slice(tile, min(tile + 2, tiles)) for tile in range(0, tiles, 2)]


def swap(peers, bit):
    return [(q, q ^ bit) for q in range(peers)]


def gathered(piece, peers, after):
    if after is not None:
        piece, first_hops = lax.optimization_barrier((piece, after[1:3]))
        after[1:3] = first_hops
    pieces, bit = {0: piece}, peers // 2
    while bit:
        for place in list(pieces):
            pieces[place ^ bit] = lax.ppermute(pieces[place], "gy", swap(peers, bit))
        bit //= 2
    return [pieces[place] for place in range(peers)]


def exchanged(packed):
    gy = len(packed)
    return [packed[0]] + [lax.ppermute(packed[p], "gy", swap(gy, p)) for p in range(1, gy)]


def sent_lines(got, count, after):
    gy = len(got)
    lines = [sum(got[p][:count] for p in range(first, gy, 2)) for first in range(2)]
    lines = jnp.concatenate(lines + [sum(piece[count:] for piece in got)], axis=0)
    lines = jnp.transpose(lines, (2, 1, 0, 3))
    if after is not None:
        lines, _ = lax.optimization_barrier((lines, after))
    return lax.all_to_all(lines, "gx", 0, 0, tiled=True)


def first_axis(lines, table):
    gx, _, count, half = table.shape
    table = table.reshape(gx, 2 * count, half)
    return jnp.einsum("geaw,gai->eiw", lines[:, :, : 2 * count], table, precision=HIGH)


def row_parts(rows):
    if rows < 4 * PART_STEP:
        return [slice(0, rows)]
    return [slice(PART_STEP, rows - PART_STEP), slice(0, PART_STEP), slice(rows - PART_STEP, rows)]


def square(lower, block):
    if len(lower) == 1:
        return lower[0]
    split_at = len(lower) // 2
    size = split_at * block
    first = square(lower[:split_at], block)
    corner = jnp.concatenate([line[..., :size] for line in lower[split_at:]], axis=-2)
    last = square([line[..., size:] for line in lower[split_at:]], block)
    top = jnp.concatenate([first, jnp.swapaxes(corner, -1, -2)], axis=-1)
    return jnp.concatenate([top, jnp.concatenate([corner, last], axis=-1)], axis=-2)


def solution(mesh):
    placed = (P("gx", "gy", None), P())
    return jax.shard_map(
        on_device, mesh=mesh, in_specs=placed, out_specs=P("gx", "gy", None), check_vma=False
    )
```

```python
import math

import jax
import jax.numpy as jnp
import numpy as np
from jax import lax
from jax.experimental import pallas as pl
from jax.experimental.pallas import tpu as pltpu
from jax.sharding import PartitionSpec as P

SWEEPS = 2

AXIS_ORDERS = ((0, 1, 2), (0, 2, 1), (1, 0, 2), (1, 2, 0), (2, 0, 1), (2, 1, 0))

HIGH = lax.Precision.HIGH


def ring(axis):
    peers = lax.axis_size(axis)
    up = [(i, (i + 1) % peers) for i in range(peers)]
    return up, [(j, i) for i, j in up]


FREE = ((8 - SWEEPS, 8 - SWEEPS), (0, 0))


def side_faces(block):
    cols = block.shape[1]
    right, left = ring("gy")
    before = lax.ppermute(block[:, cols - SWEEPS :], "gy", right)
    after = lax.ppermute(block[:, :SWEEPS], "gy", left)
    return jnp.concatenate([before, after], axis=1)


def end_faces(block, sides):
    rows = block.shape[0]
    up, down = ring("gx")
    last = jnp.concatenate([block[rows - SWEEPS :], sides[rows - SWEEPS :]], axis=1)
    first = jnp.concatenate([block[:SWEEPS], sides[:SWEEPS]], axis=1)
    return lax.ppermute(last, "gx", up), lax.ppermute(first, "gx", down)


def mirror(values, axis):
    return jnp.roll(jnp.flip(values, axis), 1, axis)


def symmetric_marks(marks):
    for flip_axis in range(3):
        marks = jnp.maximum(marks, mirror(marks, flip_axis))
    united = marks
    for axis_order in AXIS_ORDERS[1:]:
        united = jnp.maximum(united, jnp.transpose(marks, axis_order))
    return united


def cosine_table(length):
    position = np.arange(length)
    phases = np.mod(position[:, None] * position[None, : length // 2 + 1], length)
    return (np.cos(phases * (2.0 * math.pi / length)) / math.sqrt(length)).astype(np.float32)


MARGIN = 16
CHUNK = 16
STEP_ROWS = 16
PART_STEP = 8
VMEM_BYTES = 56 * 1024 * 1024


def split(values):
    high = values.astype(jnp.bfloat16)
    low = (values - high.astype(jnp.float32)).astype(jnp.bfloat16)
    return high, low


def fill_kernel(
    base, here, above, below, sides, marks, table_high, table_low, top, bottom,
    spectrum, alternate, edge, punched, once, high, low, folded,
):
    step_rows, cols, length = here.shape
    step = base[pl.program_id(0)]
    first_row = step * step_rows
    local_row = pl.program_id(0) * step_rows
    period = marks.shape[0]
    lane = lax.broadcasted_iota(jnp.int32, (128, 128), 1)
    signs = jnp.where(lax.broadcasted_iota(jnp.int32, (128, 128), 0) % 2 == 0, 1.0, -1.0)

    @pl.when(pl.program_id(0) == 0)
    def _():
        edge[...] = jnp.zeros_like(edge)

    def holes(row, start, size):
        row = lax.rem(first_row + row, period)
        start = start % period
        if start + size <= period:
            part = marks[row, pl.ds(start, size), :]
        else:
            part = jnp.concatenate(
                [marks[row, pl.ds(start, period - start), :], marks[row, pl.ds(0, start + size - period), :]],
                axis=0,
            )
        return jnp.concatenate([part] * (length // 128), axis=1)

    def punch(row, start, values):
        kept = jnp.where(holes(row, start, values.shape[0]) > 0.0, 0.0, values)
        punched[row, pl.ds(start, values.shape[0]), :] = kept

    def punch_row(row, source, index):
        for c in range(0, cols, CHUNK):
            punch(row, MARGIN + c, source[index, pl.ds(c, CHUNK), :])

    def punch_sides(row):
        full = first_row + row - SWEEPS
        punch(row, MARGIN - 8, sides[full, pl.ds(0, 8), :])
        punch(row, MARGIN + cols, sides[full, pl.ds(8, 8), :])

    def neighbours(ref, row, start):
        middle = ref[row, pl.ds(start, CHUNK), :]
        total = ref[row - 1, pl.ds(start, CHUNK), :] + ref[row + 1, pl.ds(start, CHUNK), :]
        total += ref[row, pl.ds(start - 1, CHUNK), :] + ref[row, pl.ds(start + 1, CHUNK), :]
        return total + pltpu.roll(middle, 1, 1) + pltpu.roll(middle, length - 1, 1)

    last = sides.shape[0] // step_rows - 1
    for edge_rows, inside, offset, outer in (
        (above, step > 0, 0, top),
        (below, step < last, step_rows + SWEEPS, bottom),
    ):
        if outer is None:
            for r in range(SWEEPS):
                punch_row(offset + r, edge_rows, r)
                punch_sides(offset + r)
            continue

        @pl.when(inside)
        def _():
            for r in range(SWEEPS):
                punch_row(offset + r, edge_rows, r)
                punch_sides(offset + r)

        @pl.when(jnp.logical_not(inside))
        def _():
            for r in range(SWEEPS):
                punch_row(offset + r, outer, r)
                punch(offset + r, MARGIN - SWEEPS, outer[r, pl.ds(cols, SWEEPS), :])
                punch(offset + r, MARGIN + cols, outer[r, pl.ds(cols + SWEEPS, SWEEPS), :])

    @pl.loop(0, step_rows)
    def _(r):
        punch_row(r + SWEEPS, here, r)
        punch_sides(r + SWEEPS)

    @pl.loop(1, step_rows + 2 * SWEEPS - 1, unroll=2)
    def _(r):
        for start in range(MARGIN - 8, MARGIN + cols + 8, CHUNK):
            total = neighbours(punched, r, start) * holes(r, start, CHUNK)
            once[r, pl.ds(start, CHUNK), :] = punched[r, pl.ds(start, CHUNK), :] + total

    @pl.loop(0, step_rows)
    def _(r):
        for c in range(0, cols, CHUNK):
            start = MARGIN + c
            total = neighbours(once, r + SWEEPS, start) * holes(r + SWEEPS, start, CHUNK)
            filled = punched[r + SWEEPS, pl.ds(start, CHUNK), :] + total
            first, second = split(filled)
            spot = pl.ds(pl.multiple_of(r * cols + c, CHUNK), CHUNK)
            high[spot, :] = first
            low[spot, :] = second
            wrapped = filled[:, :128]
            for tile in range(1, length // 128):
                wrapped += filled[:, tile * 128 : (tile + 1) * 128]
            folded[pl.ds(c, CHUNK), :] = wrapped
        column = jnp.where(lane == local_row + r, signs, 0.0).astype(jnp.bfloat16)
        first, second = split(folded[...])
        total = jnp.dot(first, column, preferred_element_type=jnp.float32)
        total += jnp.dot(second, column, preferred_element_type=jnp.float32)
        edge[...] += total

    rows_each = 8
    half = spectrum.shape[2]
    order = lax.broadcasted_iota(jnp.int32, (rows_each, cols, half), 1)

    @pl.loop(0, step_rows // rows_each)
    def _(r):
        spot = pl.ds(pl.multiple_of(r * rows_each * cols, CHUNK), rows_each * cols)
        first, second = high[spot, :], low[spot, :]
        total = jnp.dot(first, table_low[...], preferred_element_type=jnp.float32)
        total += jnp.dot(second, table_high[...], preferred_element_type=jnp.float32)
        total += jnp.dot(first, table_high[...], preferred_element_type=jnp.float32)
        total = total.reshape(rows_each, cols, half)
        spectrum[pl.ds(r * rows_each, rows_each)] = total
        signed = jnp.sum(jnp.where(order % 2 == 0, total, -total), axis=1)
        alternate[pl.ds(pl.multiple_of(r * rows_each, rows_each), rows_each), :] = signed


def rounded_parts(table):
    rounded = lax.reduce_precision(table, 8, 7)
    return rounded.astype(jnp.bfloat16), (table - rounded).astype(jnp.bfloat16)


def marks_kernel(shifts, template, out, held):
    period = template.shape[0]
    repeats = held.shape[1] // period
    line = lax.broadcasted_iota(jnp.int32, (period, period), 0)
    across = lax.broadcasted_iota(jnp.int32, (period, period), 1)
    flip = jnp.where((line + across) % period == 0, 1.0, 0.0)
    for i in range(period):
        plane = jnp.maximum(template[i], template[-i % period]).astype(jnp.float32)
        plane = jnp.maximum(plane, jnp.dot(flip, plane, preferred_element_type=jnp.float32))
        plane = jnp.maximum(plane, jnp.dot(plane, flip, preferred_element_type=jnp.float32))
        plane = jnp.maximum(plane, plane.T)
        held[i * period : (i + 1) * period, :] = jnp.concatenate([plane] * repeats, axis=1)
    for i in range(period):
        plane = held[i * period : (i + 1) * period, :]
        turned = held[pl.ds(i, period, stride=period), :]
        back = turned[:, :period].T
        plane = jnp.maximum(jnp.maximum(plane, turned), jnp.concatenate([back] * repeats, axis=1))
        plane = jnp.where(plane == 1.0, 1.0 / 6.0, 0.0)
        shift = shifts[1]
        out[(i - shifts[0]) % period] = jnp.concatenate([plane[shift:], plane[:shift]], axis=0)


def hole_marks(template, row, col, rows, cols):
    period = template.shape[0]
    shape = (period, period, 128)
    if rows % period == 0 and cols % period == 0:
        shifts = (-SWEEPS % period, -MARGIN % period)
        return pl.pallas_call(
            lambda *refs: marks_kernel(shifts, *refs),
            in_specs=[pl.BlockSpec(memory_space=pltpu.VMEM)],
            out_specs=pl.BlockSpec(memory_space=pltpu.VMEM),
            out_shape=jax.ShapeDtypeStruct(shape, jnp.float32),
            scratch_shapes=[pltpu.VMEM((period * period, 128), jnp.float32)],
        )(template)
    shifts = (jnp.mod(row * rows - SWEEPS, period), jnp.mod(col * cols - MARGIN, period))
    marks = jnp.roll(symmetric_marks(template), (-shifts[0], -shifts[1]), (0, 1))
    return jnp.tile(marks.astype(jnp.float32) / 6.0, (1, 1, 128 // period))


def fill_constants(intensity, template, row, col, main):
    rows, cols, _ = intensity.shape
    high = main.astype(jnp.bfloat16)
    low = (main - high.astype(np.float32)).astype(jnp.bfloat16)
    return hole_marks(template, row, col, rows, cols), jnp.asarray(high), jnp.asarray(low)


def filled_spectrum(intensity, arrays, first, parts):
    rows, cols, length = intensity.shape
    half = length // 2
    aligned = all(edge % STEP_ROWS == 0 for part in parts for edge in (part.start, part.stop))
    step_rows = STEP_ROWS if aligned else PART_STEP
    starts = [start for part in parts for start in range(part.start, part.stop, step_rows)]
    count = step_rows * len(starts)
    steps = jnp.stack([(first + start) // step_rows for start in starts])
    pairs = step_rows // SWEEPS
    last = rows // SWEEPS - 1
    whole = lambda array: pl.BlockSpec(array.shape, lambda i, b: (0,) * array.ndim)
    before = lambda i, b: (jnp.maximum(b[i] * pairs - 1, 0), 0, 0)
    after = lambda i, b: (jnp.minimum((b[i] + 1) * pairs, last), 0, 0)
    padded = (step_rows + 2 * SWEEPS, cols + 2 * MARGIN, length)
    ends = 4 + len(arrays)

    def kernel(*refs):
        if len(arrays) == 4:
            refs = refs[:ends] + (None, None) + refs[ends:]
        fill_kernel(*refs)

    return pl.pallas_call(
        kernel,
        grid_spec=pltpu.PrefetchScalarGridSpec(
            num_scalar_prefetch=1,
            grid=(len(starts),),
            in_specs=[
                pl.BlockSpec((step_rows, cols, length), lambda i, b: (b[i], 0, 0)),
                pl.BlockSpec((SWEEPS, cols, length), before),
                pl.BlockSpec((SWEEPS, cols, length), after),
            ] + [whole(array) for array in arrays],
            out_specs=[
                pl.BlockSpec((step_rows, cols, half), lambda i, b: (i, 0, 0)),
                pl.BlockSpec((step_rows, half), lambda i, b: (i, 0)),
                pl.BlockSpec((cols, 128), lambda i, b: (0, 0)),
            ],
            scratch_shapes=[
                pltpu.VMEM(padded, jnp.float32),
                pltpu.VMEM(padded, jnp.float32),
                pltpu.VMEM((step_rows * cols, length), jnp.bfloat16),
                pltpu.VMEM((step_rows * cols, length), jnp.bfloat16),
                pltpu.VMEM((cols, 128), jnp.float32),
            ],
        ),
        out_shape=[
            jax.ShapeDtypeStruct((count, cols, half), jnp.float32),
            jax.ShapeDtypeStruct((count, half), jnp.float32),
            jax.ShapeDtypeStruct((cols, 128), jnp.float32),
        ],
        compiler_params=pltpu.CompilerParams(vmem_limit_bytes=VMEM_BYTES),
        cost_estimate=pl.CostEstimate(
            flops=count * cols * length * half * 6,
            bytes_accessed=count * cols * (length + half) * 4,
            transcendentals=0,
        ),
    )(steps, intensity, intensity, intensity, *arrays)


def pack(section, offsets):
    block = offsets[1]
    units = [section[b * block : (b + 1) * block, : (b + 1) * block] for b in range(len(offsets) - 1)]
    return jnp.concatenate(units, axis=1)


def three_dots(left, right):
    total = jnp.dot(left[1], right[0], preferred_element_type=jnp.float32)
    total += jnp.dot(left[0], right[1], preferred_element_type=jnp.float32)
    return total + jnp.dot(left[0], right[0], preferred_element_type=jnp.float32)


def section_kernel(
    offsets, planes, opening, closing, me, weights, kept, got, cols_high, cols_low, rows_high,
    rows_low, *refs
):
    step, steps = pl.program_id(0), pl.num_programs(0)
    step_rows = kept.shape[0]
    half, count = rows_high.shape
    before = None if opening else refs[0]
    refs = refs if opening else refs[1:]
    rim, corner = refs[:2] if closing else (None, None)
    *outs, total, lines, packed = refs[2:] if closing else refs
    block, width = total.shape[1:]
    gy, (_, own, gx, _) = len(outs), outs[0].shape

    def place(layer, values, slot=0):
        packed[slot] = values
        for e in range(own):
            for p in range(gy):
                start = pl.multiple_of((e * gy + (p ^ me[0])) * gx, gx)
                outs[p][layer, e] = packed[slot, pl.ds(start, gx), :]

    @pl.when(step == 0)
    def _():
        total[...] = jnp.zeros_like(total) if opening else before[...]

    for r in range(step_rows):
        layer = step * step_rows + r
        values = jnp.concatenate([kept[r], got[r]], axis=0)
        section = three_dots((cols_high[...], cols_low[...]), split(values))
        section = section + section.T
        line = pack(section, offsets)
        place(layer, line, r)
        for m in range(planes):
            total[m] += weights[m, layer] * line
        for m in range(planes - 1):
            row = (m + 1) * (half // planes)
            lines[m, pl.ds(layer, 1), :] = section[row : row + 1]

    @pl.when(step == steps - 1)
    def _():
        for m in range(planes - 1):
            plane = three_dots((rows_high[...], rows_low[...]), split(lines[m]))
            total[m] += pack(plane + plane.T, offsets)
        if closing:
            total[planes - 1] += pack(rim[...] + rim[...].T, offsets)
            for m in range(planes):
                place(count + m, total[m])
            place(count + planes, jnp.zeros((block, width), jnp.float32) + corner[...])


def packed_section(col, kept, got, first, table_pair, table_rows, weights, rim, corner, before, offsets, shape, closing):
    _, cols, half = kept.shape
    count = table_rows.shape[0]
    planes, block, width = weights.shape[0], offsets[1], offsets[-1]
    gx, gy = shape
    opening = before is None
    step_rows = 4
    layers = count + (planes + 1 if closing else 0)
    whole = lambda array: pl.BlockSpec(array.shape, lambda i: (0,) * array.ndim)
    arrays = rounded_parts(table_pair.T) + rounded_parts(table_rows[:, :half].T)
    arrays += (() if opening else (before,)) + ((rim, corner[None]) if closing else ())
    out = jax.ShapeDtypeStruct((layers, block // (gx * gy), gx, width), jnp.float32)
    outs = [out] * gy + [jax.ShapeDtypeStruct((planes, block, width), jnp.float32)]
    rows_spec = pl.BlockSpec((step_rows, cols, half), lambda i: (i + first // step_rows, 0, 0))
    return pl.pallas_call(
        lambda *refs: section_kernel(offsets, planes, opening, closing, *refs),
        grid=(count // step_rows,),
        in_specs=[pl.BlockSpec(memory_space=pltpu.SMEM)] * 2 + [rows_spec, rows_spec]
        + [whole(array) for array in arrays],
        out_specs=[whole(out) for out in outs],
        out_shape=outs,
        scratch_shapes=[
            pltpu.VMEM((planes, count, half), jnp.float32),
            pltpu.VMEM((step_rows, block, width), jnp.float32),
        ],
        compiler_params=pltpu.CompilerParams(vmem_limit_bytes=VMEM_BYTES),
        cost_estimate=pl.CostEstimate(
            flops=count * 12 * cols * half * half,
            bytes_accessed=count * cols * half * 16,
            transcendentals=0,
        ),
    )(col.reshape(1), weights, kept, got, *arrays)


def on_device(intensity, template):
    rows, cols, length = intensity.shape
    gx, gy = lax.axis_size("gx"), lax.axis_size("gy")
    row, col = lax.axis_index("gx"), lax.axis_index("gy")
    devices, half = gx * gy, length // 2
    block = max(devices, rows)
    blocks, own, slabs = half // block, block // devices, gx // 2
    offsets = [block * b * (b + 1) // 2 for b in range(blocks + 1)]
    width = offsets[blocks]
    table = jnp.asarray(cosine_table(length))
    main = table[:, :half]

    pair_rows = rows // 2
    parts = row_parts(pair_rows)
    counts = [part.stop - part.start for part in parts]
    core = lax.rem(col, 2)
    constants = fill_constants(intensity, template, row, col, cosine_table(length)[:, :half])
    sides = side_faces(intensity)
    given_first, kept_first = (1 - core) * pair_rows, core * pair_rows
    inner = parts[0].start >= SWEEPS and parts[0].stop <= pair_rows - SWEEPS
    side_columns = jnp.pad(sides, ((0, 0),) + FREE)
    ends = () if inner else end_faces(intensity, sides)

    def fill(some, start):
        arrays = (side_columns,) + constants + tuple(ends)
        return list(filled_spectrum(intensity, arrays, start, some))

    given, kept = [fill(parts[:1], given_first)], []
    outer = ends
    if inner:
        given[0], late_sides = lax.optimization_barrier((given[0], sides))
        outer = end_faces(intensity, late_sides)
    kept.append(fill(parts[:1], kept_first))
    ends = outer

    table_cols = lax.dynamic_slice_in_dim(table, col * cols, cols, 0)
    kept_rows = lax.dynamic_slice_in_dim(table, row * rows + kept_first, pair_rows, 0)
    marks = [rows * (m + 1) for m in range(slabs)]
    if all(start % gx == 0 for start in [pair_rows] + [part.start for part in parts]):
        weights = [jnp.asarray(cosine_table(length)[:count, marks].T) for count in counts]
    else:
        weights = [jnp.stack([kept_rows[part, m] for m in marks]) for part in parts]
    mates = lax.dynamic_slice_in_dim(main, (col + 1 - 2 * core) * cols, cols, 0)
    table_pair = jnp.concatenate([table_cols[:, :half], mates], axis=0)
    table_parts = main.reshape(gx, 2, pair_rows, half) / 6.0
    table_parts = jnp.where(core == 0, table_parts, table_parts[:, ::-1])
    table_parts = [table_parts[:, :, part] for part in parts]
    side = rim = corner = None
    values, packed, lines = 0.0, None, None
    for c, count in enumerate(counts):
        closing = c == len(counts) - 1
        if c == 1:
            behind = (given_first, kept_first), packed
            starts, packed = lax.optimization_barrier(behind)
            given.append(fill(parts[1:], starts[0]))
            kept.append(fill(parts[1:], starts[1]))
        flanks = [piece[1:] for piece in given + kept]
        if c > 1:
            flanks, packed = lax.optimization_barrier((flanks, packed))
        if c > 0:
            got_lines = exchanged(packed)
        if c == 1:
            behind = given[1][0], kept[1][0], got_lines
            given[1][0], kept[1][0], got_lines = lax.optimization_barrier(behind)
        if c < 2:
            got = lax.ppermute(given[c][0], "gy", swap(gy, 1))
            held = kept[c][0]
        if c > 0:
            lines = sent_lines(got_lines, counts[c - 1], lines)
            values = values + first_axis(lines, table_parts[c - 1])
        if closing:
            given_rows = lax.dynamic_slice_in_dim(table, row * rows + given_first, pair_rows, 0)
            ordered_rows = [held_rows[part] for held_rows in (given_rows, kept_rows) for part in parts]
            ordered_rows = jnp.concatenate(ordered_rows, axis=0)
            alternate = jnp.concatenate([piece[0] for piece in flanks], axis=0) / math.sqrt(length)
            edge = [piece[1][:, : piece[0].shape[0]] for piece in flanks]
            edge = jnp.concatenate(edge, axis=1)
            edge = jnp.einsum("ba,bk->ak", edge / math.sqrt(length), table_cols, precision=HIGH)
            edge = edge + jnp.concatenate([alternate, edge[:, half:]], axis=1)
            rim = jnp.einsum("aj,ak->jk", ordered_rows[:, :half], edge[:, :half], precision=HIGH)
            corner = 2.0 * jnp.einsum("a,ak->k", ordered_rows[:, half], edge, precision=HIGH)
            corner = corner + jnp.einsum("aj,a->j", ordered_rows, edge[:, half], precision=HIGH)
            corner = jnp.pad(corner, (0, width - half - 1))

        *packed, side = packed_section(
            col, held, got, sum(counts[1:c]), table_pair, kept_rows[parts[c]], weights[c],
            rim, corner, side, offsets, (gx, gy), closing,
        )
    lines = sent_lines(exchanged(packed), counts[-1], lines)
    values = values + first_axis(lines, table_parts[-1])
    side = jnp.sum(lines[:, :, 2 * counts[-1] :], axis=0) / 6.0
    turned = values.reshape(own, blocks, own, devices, width)
    turned = jnp.transpose(turned, (3, 1, 2, 0, 4))
    turned = [turned[:, b, :, :, : offsets[b + 1]] for b in range(blocks)]
    turned = lax.all_to_all(jnp.concatenate(turned, axis=3), ("gy", "gx"), 0, 0, tiled=True)
    turned = jnp.transpose(turned, (1, 2, 0, 3)).reshape(own, block, -1)

    slab = jnp.minimum(row, gx - 1 - row)
    far_row, far_col = row >= slabs, col >= gy // 2
    pick_rows = jnp.arange(rows)
    pick_rows = slab * rows + jnp.where(far_row, rows - pick_rows, pick_rows)
    pick_cols = jnp.arange(cols)
    pick_cols = jnp.where(far_col, (gy - col) * cols - pick_cols, col * cols + pick_cols)

    if rows == block:
        got, piece = [], None
        for messages in slab_messages(values, turned, side, offsets, slabs):
            if piece is not None:
                messages, piece = lax.optimization_barrier((messages, piece))
                got.append(gathered(piece, gy, got[-1] if got else None))
            piece = lax.all_to_all(messages, "gx", 0, 0, tiled=True)
        got.append(gathered(piece, gy, got[-1] if got else None))
        tiles = width // 128
        start = tile_groups(tiles)[0].stop * own * block
        side = jnp.stack([piece[:, start : start + 3 * own * tiles] for piece in got[0]])
        bit = gy // 2
        while bit:
            paired = side.reshape((-1, 2, bit) + side.shape[1:])
            side = jnp.where((col & bit) == 0, paired, paired[:, ::-1]).reshape(side.shape)
            bit //= 2
        side = side.reshape(devices, own, 3, width)
        side = jnp.transpose(side, (2, 1, 0, 3)).reshape(3, block, width)
        next_plane, across = side[0], rim_rows(side[1:], offsets, pick_rows)
        rim_col = col == gy // 2
        rim = across[:, pick_cols]
        return result_block(
            got, next_plane, across, rim, pick_cols, slab, far_row, rim_col, col, offsets
        )

    side = lax.all_gather(side, ("gy", "gx"), axis=0)
    side = jnp.transpose(side, (2, 1, 0, 3)).reshape(slabs + 1, block, width)
    across = rim_rows(side[slabs - 1 :], offsets, pick_rows)
    next_plane = lax.dynamic_index_in_dim(side, slab, 0, keepdims=False)
    sums = axis_order_sums(values, turned, offsets, block)
    messages = []
    for s in range(slabs):
        base, first = s * rows // block, s * rows
        units = []
        for b in range(blocks):
            size = (b + 1) * block
            near = jnp.zeros((own, rows, size))
            far = jnp.zeros((own, block, size))
            if b >= base:
                near = jnp.stack([sums[b][e][first : first + rows, :size] for e in range(own)])
            else:
                far = jnp.stack([sums[base][e][b * block : size, :size] for e in range(own)])
            units.append(jnp.concatenate([near, far], axis=1))
        messages.append(jnp.concatenate(units, axis=2))
    messages = jnp.stack(messages + messages[::-1])
    got = lax.all_to_all(messages, "gx", 0, 0, tiled=True)
    got = lax.all_gather(got, "gy", axis=0, tiled=True)
    got = jnp.swapaxes(got, 0, 1).reshape(block, rows + block, width)
    base = slab * rows // block
    lower = []
    for b in range(blocks):
        lanes = slice(offsets[b], offsets[b + 1])
        near = jnp.swapaxes(got[:, :rows, lanes], 0, 1)
        far = lax.dynamic_slice_in_dim(got[:, rows:, lanes], lax.rem(slab * rows, block), rows, 0)
        lower.append(jnp.where(b >= base, near, far))
    lower = jnp.concatenate(lower, axis=2)
    lower = jnp.concatenate([lower, next_plane[None]], axis=0)
    body = square([lower[:, :, offsets[b] : offsets[b + 1]] for b in range(blocks)], block)
    body = body[pick_rows - slab * rows]
    body = jnp.concatenate([body, across[:, None, :half]], axis=1)[:, pick_cols]
    body = jnp.concatenate([body, across[:, pick_cols][:, :, None]], axis=2)
    return jnp.concatenate([body, jnp.flip(body[:, :, 1:half], 2)], axis=2)


def rim_rows(side, offsets, pick_rows):
    blocks, block = len(offsets) - 1, offsets[1]
    half = blocks * block
    last = square([side[0][:, offsets[b] : offsets[b + 1]] for b in range(blocks)], block)
    rim = side[1, 0, : half + 1]
    last = jnp.concatenate([last, rim[None, :half]], axis=0)
    return jnp.concatenate([last, rim[:, None]], axis=1)[pick_rows]


def axis_order_sums(values, turned, offsets, block):
    start = 0
    sums = []
    for top in range(len(offsets) - 1):
        size = (top + 1) * block
        parts = []
        for e in range(values.shape[0]):
            part = values[e, :size, offsets[top] : offsets[top] + size]
            lower = [turned[e, :, start + offsets[b] : start + offsets[b + 1]] for b in range(top + 1)]
            parts.append(part + part.T + square(lower, block))
        sums.append(parts)
        start += offsets[top + 1]
    return sums


def message_kernel(offsets, slabs, values, turned, side, *messages):
    blocks, block = len(offsets) - 1, offsets[1]
    values, turned = values[...], turned[...]
    own = values.shape[0]
    sums = axis_order_sums(values, turned, offsets, block)
    groups = tile_groups(offsets[-1] // 128)
    side_start = groups[0].stop * own * block
    messages[0][:, side_start:] = jnp.zeros_like(messages[0][:, side_start:])
    for s in range(slabs):
        places = s, 2 * slabs - 1 - s
        for e in range(own):
            units = []
            for b in range(blocks):
                size = (b + 1) * block
                if b >= s:
                    units.append(sums[b][e][s * block : (s + 1) * block, :size])
                else:
                    units.append(sums[s][e][b * block : size, :size])
            line = jnp.concatenate(units, axis=1)
            for group, out in zip(groups, messages):
                for tile in range(group.start, group.stop):
                    start = ((tile - group.start) * own + e) * block
                    for place in places:
                        out[place, start : start + block] = line[:, tile * 128 : (tile + 1) * 128]
            row = side_start + 3 * e * groups[-1].stop
            for plane in (s, slabs - 1, slabs):
                for tile in range(groups[-1].stop):
                    part = side[e, plane : plane + 1, tile * 128 : (tile + 1) * 128]
                    for place in places:
                        messages[0][place, row : row + 1] = part
                    row += 1


def slab_messages(values, turned, side, offsets, slabs):
    own, block, tiles = values.shape[0], offsets[1], offsets[-1] // 128
    sizes = [(group.stop - group.start) * own * block for group in tile_groups(tiles)]
    sizes[0] += -(-3 * own * tiles // 8) * 8
    return pl.pallas_call(
        lambda *refs: message_kernel(offsets, slabs, *refs),
        in_specs=[pl.BlockSpec(memory_space=pltpu.VMEM)] * 3,
        out_specs=[pl.BlockSpec(memory_space=pltpu.VMEM)] * len(sizes),
        out_shape=[jax.ShapeDtypeStruct((2 * slabs, size, 128), jnp.float32) for size in sizes],
        compiler_params=pltpu.CompilerParams(vmem_limit_bytes=VMEM_BYTES),
    )(values, turned, side)


def result_kernel(
    offsets, own, devices, groups, places, next_plane, across, rim, pick, flip, *refs
):
    blocks, block = len(offsets) - 1, offsets[1]
    tiles = offsets[-1] // 128
    peers = (len(refs) - 2) // len(groups) - 1
    pieces, out = refs[: peers * len(groups)], refs[peers * len(groups)]
    held, sems = refs[peers * len(groups) + 1 : -1], refs[-1]
    step_rows, cols, length = out.shape
    half = length // 2
    slab, far_row, rim_col, me = places[0], places[1], places[2], places[3]
    lane = lax.broadcasted_iota(jnp.int32, (block, 128), 1)
    at_rim = lax.broadcasted_iota(jnp.int32, (cols, half), 0) + (1 - rim_col) == 0
    first_lane = lax.broadcasted_iota(jnp.int32, (cols, 128), 1) == 0

    @pl.when(pl.program_id(0) == 0)
    def _():
        copies = []
        for g in range(len(groups)):
            for peer in range(peers):
                piece = pieces[g * peers + peer]
                size = piece.shape[0]
                spot = pl.ds(pl.multiple_of((me ^ peer) * size, size), size)
                copies.append(pltpu.make_async_copy(piece, held[g].at[spot], sems.at[g, peer]))
        for copy in copies:
            copy.start()
        for copy in copies:
            copy.wait()

    def left_half(r, may_pass):
        t = pl.program_id(0) * step_rows + r
        i = jnp.where(far_row == 1, block - t, t)
        inside = (jnp.zeros((block, 128), jnp.int32) + i) < block
        i = jnp.minimum(i, block - 1)
        source = lax.div(i, devices), lax.rem(i, devices)
        parts = []
        for g, group in enumerate(groups):
            stride = held[g].shape[0] // devices
            for tile in range(group.start, group.stop):
                start = (tile - group.start) * own * block
                near = [
                    held[g][pl.ds(start + e * block + i, devices, stride=stride), :]
                    for e in range(own)
                ]
                near = jnp.concatenate(near, axis=0)
                line = near
                if tile * 128 < offsets[blocks - 1]:
                    far = pl.multiple_of(source[1] * stride + start + source[0] * block, 8)
                    far = held[g][pl.ds(far, block), :]
                    kind = jnp.zeros((block, 128), jnp.int32)
                    for b in range(1, blocks):
                        kind += (lane + tile * 128 >= offsets[b]).astype(jnp.int32)
                    line = jnp.where(kind >= slab, near, far)
                if may_pass:
                    line = jnp.where(inside, line, next_plane[:, pl.ds(tile * 128, 128)])
                parts.append(line)
        line = jnp.concatenate(parts, axis=1)
        plane = square([line[:, offsets[b] : offsets[b + 1]] for b in range(blocks)], block)
        high, low = split(plane)
        left = jnp.dot(pick[...], high, preferred_element_type=jnp.float32)
        left += jnp.dot(pick[...], low, preferred_element_type=jnp.float32)
        left = jnp.where(at_rim, across[pl.ds(t, 1), :], left)
        out[r, :, pl.ds(0, half)] = left
        return left

    together = 4

    @pl.loop(0, step_rows // together)
    def _(c):
        left = [left_half(c * together + n, n == 0) for n in range(together)]
        high, low = split(jnp.concatenate(left, axis=0))
        right = jnp.dot(high, flip[...], preferred_element_type=jnp.float32)
        right += jnp.dot(low, flip[...], preferred_element_type=jnp.float32)
        for n in range(together):
            r = c * together + n
            t = pl.program_id(0) * step_rows + r
            edge = pltpu.roll(rim[...], lax.rem(128 - t, 128), 1)
            part = right[n * cols : (n + 1) * cols]
            out[r, :, pl.ds(half, 128)] = jnp.where(first_lane, edge, part[:, :128])
            out[r, :, pl.ds(half + 128, half - 128)] = part[:, 128:]


def result_block(got, next_plane, across, rim, pick_cols, slab, far_row, rim_col, col, offsets):
    block = offsets[1]
    gx = got[0][0].shape[0]
    groups = tile_groups(offsets[-1] // 128)
    devices = gx * len(got[0])
    own = block // devices
    rows, half = across.shape[0], across.shape[1] - 1
    cols = pick_cols.shape[0]
    step_rows = 8
    places = jnp.stack([slab, far_row.astype(jnp.int32), rim_col.astype(jnp.int32), col])
    cell = jnp.arange(half)
    pick = (pick_cols[:, None] == cell[None, :]).astype(jnp.bfloat16)
    flip = (cell[:, None] + cell[None, :] == half).astype(jnp.bfloat16)
    rim = jnp.pad(rim.T, ((0, 0), (0, 128 - rows)))
    whole = lambda array: pl.BlockSpec(array.shape, lambda i: (0,) * array.ndim)
    arrays = (next_plane, across[:, :half], rim, pick, flip)
    pieces = [piece.reshape(-1, 128) for group in got for piece in group]
    return pl.pallas_call(
        lambda *refs: result_kernel(offsets, own, devices, groups, *refs),
        grid=(rows // step_rows,),
        in_specs=[pl.BlockSpec(memory_space=pltpu.SMEM)] + [whole(array) for array in arrays]
        + [pl.BlockSpec(memory_space=pl.ANY)] * len(pieces),
        out_specs=pl.BlockSpec((step_rows, cols, 2 * half), lambda i: (i, 0, 0)),
        out_shape=jax.ShapeDtypeStruct((rows, cols, 2 * half), jnp.float32),
        scratch_shapes=[
            pltpu.VMEM((devices * group[0].shape[1], 128), jnp.float32) for group in got
        ] + [pltpu.SemaphoreType.DMA((len(groups), len(got[0])))],
        compiler_params=pltpu.CompilerParams(vmem_limit_bytes=VMEM_BYTES),
    )(places, *arrays, *pieces)


def tile_groups(tiles):
    return [slice(tile, min(tile + 2, tiles)) for tile in range(0, tiles, 2)]


def swap(peers, bit):
    return [(q, q ^ bit) for q in range(peers)]


def gathered(piece, peers, after):
    if after is not None:
        piece, first_hops = lax.optimization_barrier((piece, after[1:3]))
        after[1:3] = first_hops
    pieces, bit = {0: piece}, peers // 2
    while bit:
        for place in list(pieces):
            pieces[place ^ bit] = lax.ppermute(pieces[place], "gy", swap(peers, bit))
        bit //= 2
    return [pieces[place] for place in range(peers)]


def exchanged(packed):
    gy = len(packed)
    return [packed[0]] + [lax.ppermute(packed[p], "gy", swap(gy, p)) for p in range(1, gy)]


def sent_lines(got, count, after):
    gy = len(got)
    lines = [sum(got[p][:count] for p in range(first, gy, 2)) for first in range(2)]
    lines = jnp.concatenate(lines + [sum(piece[count:] for piece in got)], axis=0)
    lines = jnp.transpose(lines, (2, 1, 0, 3))
    if after is not None:
        lines, _ = lax.optimization_barrier((lines, after))
    return lax.all_to_all(lines, "gx", 0, 0, tiled=True)


def first_axis(lines, table):
    gx, _, count, half = table.shape
    table = table.reshape(gx, 2 * count, half)
    return jnp.einsum("geaw,gai->eiw", lines[:, :, : 2 * count], table, precision=HIGH)


def row_parts(rows):
    if rows < 4 * PART_STEP:
        return [slice(0, rows)]
    return [slice(PART_STEP, rows - PART_STEP), slice(0, PART_STEP), slice(rows - PART_STEP, rows)]


def square(lower, block):
    if len(lower) == 1:
        return lower[0]
    split_at = len(lower) // 2
    size = split_at * block
    first = square(lower[:split_at], block)
    corner = jnp.concatenate([line[..., :size] for line in lower[split_at:]], axis=-2)
    last = square([line[..., size:] for line in lower[split_at:]], block)
    top = jnp.concatenate([first, jnp.swapaxes(corner, -1, -2)], axis=-1)
    return jnp.concatenate([top, jnp.concatenate([corner, last], axis=-1)], axis=-2)


def solution(mesh):
    placed = (P("gx", "gy", None), P())
    return jax.shard_map(
        on_device, mesh=mesh, in_specs=placed, out_specs=P("gx", "gy", None), check_vma=False
    )
```

```python
import math

import jax
import jax.numpy as jnp
import numpy as np
from jax import lax
from jax.experimental import pallas as pl
from jax.experimental.pallas import tpu as pltpu
from jax.sharding import PartitionSpec as P

SWEEPS = 2

AXIS_ORDERS = ((0, 1, 2), (0, 2, 1), (1, 0, 2), (1, 2, 0), (2, 0, 1), (2, 1, 0))

HIGH = lax.Precision.HIGH


def ring(axis):
    peers = lax.axis_size(axis)
    up = [(i, (i + 1) % peers) for i in range(peers)]
    return up, [(j, i) for i, j in up]


def side_faces(block):
    cols = block.shape[1]
    right, left = ring("gy")
    before = lax.ppermute(block[:, cols - SWEEPS :], "gy", right)
    after = lax.ppermute(block[:, :SWEEPS], "gy", left)
    return before, after


def end_faces(block, sides):
    rows = block.shape[0]
    up, down = ring("gx")
    last = jnp.concatenate([block[rows - SWEEPS :], sides[rows - SWEEPS :]], axis=1)
    first = jnp.concatenate([block[:SWEEPS], sides[:SWEEPS]], axis=1)
    return lax.ppermute(last, "gx", up), lax.ppermute(first, "gx", down)


def mirror(values, axis):
    return jnp.roll(jnp.flip(values, axis), 1, axis)


def symmetric_marks(marks):
    for flip_axis in range(3):
        marks = jnp.maximum(marks, mirror(marks, flip_axis))
    united = marks
    for axis_order in AXIS_ORDERS[1:]:
        united = jnp.maximum(united, jnp.transpose(marks, axis_order))
    return united


def cosine_table(length):
    position = np.arange(length)
    phases = np.mod(position[:, None] * position[None, : length // 2 + 1], length)
    return (np.cos(phases * (2.0 * math.pi / length)) / math.sqrt(length)).astype(np.float32)


MARGIN = 16
CHUNK = 16
STEP_ROWS = 16
PART_STEP = 8
VMEM_BYTES = 56 * 1024 * 1024


def split(values):
    high = values.astype(jnp.bfloat16)
    low = (values - high.astype(jnp.float32)).astype(jnp.bfloat16)
    return high, low


def fill_kernel(
    base, here, above, below, sides, marks, table_high, table_low, top, bottom,
    spectrum, alternate, edge, punched, once, high, low, folded,
):
    step_rows, cols, length = here.shape
    step = base[pl.program_id(0)]
    first_row = step * step_rows
    local_row = pl.program_id(0) * step_rows
    period = marks.shape[0]
    lane = lax.broadcasted_iota(jnp.int32, (128, 128), 1)
    signs = jnp.where(lax.broadcasted_iota(jnp.int32, (128, 128), 0) % 2 == 0, 1.0, -1.0)

    @pl.when(pl.program_id(0) == 0)
    def _():
        edge[...] = jnp.zeros_like(edge)

    def holes(row, start, size):
        row = lax.rem(first_row + row, period)
        start = start % period
        if start + size <= period:
            part = marks[row, pl.ds(start, size), :]
        else:
            part = jnp.concatenate(
                [marks[row, pl.ds(start, period - start), :], marks[row, pl.ds(0, start + size - period), :]],
                axis=0,
            )
        return jnp.concatenate([part] * (length // 128), axis=1)

    def punch(row, start, values):
        kept = jnp.where(holes(row, start, values.shape[0]) > 0.0, 0.0, values)
        punched[row, pl.ds(start, values.shape[0]), :] = kept

    def punch_row(row, source, index):
        for c in range(0, cols, CHUNK):
            punch(row, MARGIN + c, source[index, pl.ds(c, CHUNK), :])

    def punch_sides(row):
        full = first_row + row - SWEEPS
        punch(row, MARGIN - 8, sides[full, pl.ds(0, 8), :])
        punch(row, MARGIN + cols, sides[full, pl.ds(8, 8), :])

    def neighbours(ref, row, start):
        middle = ref[row, pl.ds(start, CHUNK), :]
        total = ref[row - 1, pl.ds(start, CHUNK), :] + ref[row + 1, pl.ds(start, CHUNK), :]
        total += ref[row, pl.ds(start - 1, CHUNK), :] + ref[row, pl.ds(start + 1, CHUNK), :]
        return total + pltpu.roll(middle, 1, 1) + pltpu.roll(middle, length - 1, 1)

    last = sides.shape[0] // step_rows - 1
    for edge_rows, inside, offset, outer in (
        (above, step > 0, 0, top),
        (below, step < last, step_rows + SWEEPS, bottom),
    ):
        if outer is None:
            for r in range(SWEEPS):
                punch_row(offset + r, edge_rows, r)
                punch_sides(offset + r)
            continue

        @pl.when(inside)
        def _():
            for r in range(SWEEPS):
                punch_row(offset + r, edge_rows, r)
                punch_sides(offset + r)

        @pl.when(jnp.logical_not(inside))
        def _():
            for r in range(SWEEPS):
                punch_row(offset + r, outer, r)
                punch(offset + r, MARGIN - SWEEPS, outer[r, pl.ds(cols, SWEEPS), :])
                punch(offset + r, MARGIN + cols, outer[r, pl.ds(cols + SWEEPS, SWEEPS), :])

    @pl.loop(0, step_rows)
    def _(r):
        punch_row(r + SWEEPS, here, r)
        punch_sides(r + SWEEPS)

    @pl.loop(1, step_rows + 2 * SWEEPS - 1, unroll=2)
    def _(r):
        for start in range(MARGIN - 8, MARGIN + cols + 8, CHUNK):
            total = neighbours(punched, r, start) * holes(r, start, CHUNK)
            once[r, pl.ds(start, CHUNK), :] = punched[r, pl.ds(start, CHUNK), :] + total

    @pl.loop(0, step_rows)
    def _(r):
        for c in range(0, cols, CHUNK):
            start = MARGIN + c
            total = neighbours(once, r + SWEEPS, start) * holes(r + SWEEPS, start, CHUNK)
            filled = punched[r + SWEEPS, pl.ds(start, CHUNK), :] + total
            first, second = split(filled)
            spot = pl.ds(pl.multiple_of(r * cols + c, CHUNK), CHUNK)
            high[spot, :] = first
            low[spot, :] = second
            wrapped = filled[:, :128]
            for tile in range(1, length // 128):
                wrapped += filled[:, tile * 128 : (tile + 1) * 128]
            folded[pl.ds(c, CHUNK), :] = wrapped
        column = jnp.where(lane == local_row + r, signs, 0.0).astype(jnp.bfloat16)
        first, second = split(folded[...])
        total = jnp.dot(first, column, preferred_element_type=jnp.float32)
        total += jnp.dot(second, column, preferred_element_type=jnp.float32)
        edge[...] += total

    rows_each = 8
    half = spectrum.shape[2]
    order = lax.broadcasted_iota(jnp.int32, (rows_each, cols, half), 1)

    @pl.loop(0, step_rows // rows_each)
    def _(r):
        spot = pl.ds(pl.multiple_of(r * rows_each * cols, CHUNK), rows_each * cols)
        first, second = high[spot, :], low[spot, :]
        total = jnp.dot(first, table_low[...], preferred_element_type=jnp.float32)
        total += jnp.dot(second, table_high[...], preferred_element_type=jnp.float32)
        total += jnp.dot(first, table_high[...], preferred_element_type=jnp.float32)
        total = total.reshape(rows_each, cols, half)
        spectrum[pl.ds(r * rows_each, rows_each)] = total
        signed = jnp.sum(jnp.where(order % 2 == 0, total, -total), axis=1)
        alternate[pl.ds(pl.multiple_of(r * rows_each, rows_each), rows_each), :] = signed


def rounded_parts(table):
    rounded = lax.reduce_precision(table, 8, 7)
    return rounded.astype(jnp.bfloat16), (table - rounded).astype(jnp.bfloat16)


def marks_kernel(shifts, template, out, held):
    period = template.shape[0]
    repeats = held.shape[1] // period
    line = lax.broadcasted_iota(jnp.int32, (period, period), 0)
    across = lax.broadcasted_iota(jnp.int32, (period, period), 1)
    flip = jnp.where((line + across) % period == 0, 1.0, 0.0)
    for i in range(period):
        plane = jnp.maximum(template[i], template[-i % period]).astype(jnp.float32)
        plane = jnp.maximum(plane, jnp.dot(flip, plane, preferred_element_type=jnp.float32))
        plane = jnp.maximum(plane, jnp.dot(plane, flip, preferred_element_type=jnp.float32))
        plane = jnp.maximum(plane, plane.T)
        held[i * period : (i + 1) * period, :] = jnp.concatenate([plane] * repeats, axis=1)
    for i in range(period):
        plane = held[i * period : (i + 1) * period, :]
        turned = held[pl.ds(i, period, stride=period), :]
        back = turned[:, :period].T
        plane = jnp.maximum(jnp.maximum(plane, turned), jnp.concatenate([back] * repeats, axis=1))
        plane = jnp.where(plane == 1.0, 1.0 / 6.0, 0.0)
        shift = shifts[1]
        out[(i - shifts[0]) % period] = jnp.concatenate([plane[shift:], plane[:shift]], axis=0)


def hole_marks(template, row, col, rows, cols):
    period = template.shape[0]
    shape = (period, period, 128)
    if rows % period == 0 and cols % period == 0:
        shifts = (-SWEEPS % period, -MARGIN % period)
        return pl.pallas_call(
            lambda *refs: marks_kernel(shifts, *refs),
            in_specs=[pl.BlockSpec(memory_space=pltpu.VMEM)],
            out_specs=pl.BlockSpec(memory_space=pltpu.VMEM),
            out_shape=jax.ShapeDtypeStruct(shape, jnp.float32),
            scratch_shapes=[pltpu.VMEM((period * period, 128), jnp.float32)],
        )(template)
    shifts = (jnp.mod(row * rows - SWEEPS, period), jnp.mod(col * cols - MARGIN, period))
    marks = jnp.roll(symmetric_marks(template), (-shifts[0], -shifts[1]), (0, 1))
    return jnp.tile(marks.astype(jnp.float32) / 6.0, (1, 1, 128 // period))


def fill_constants(intensity, template, row, col, main):
    rows, cols, _ = intensity.shape
    high = main.astype(jnp.bfloat16)
    low = (main - high.astype(np.float32)).astype(jnp.bfloat16)
    return hole_marks(template, row, col, rows, cols), jnp.asarray(high), jnp.asarray(low)


def filled_spectrum(intensity, arrays, first, parts):
    rows, cols, length = intensity.shape
    half = length // 2
    aligned = all(edge % STEP_ROWS == 0 for part in parts for edge in (part.start, part.stop))
    step_rows = STEP_ROWS if aligned else PART_STEP
    starts = [start for part in parts for start in range(part.start, part.stop, step_rows)]
    count = step_rows * len(starts)
    steps = jnp.stack([(first + start) // step_rows for start in starts])
    pairs = step_rows // SWEEPS
    last = rows // SWEEPS - 1
    whole = lambda array: pl.BlockSpec(array.shape, lambda i, b: (0,) * array.ndim)
    before = lambda i, b: (jnp.maximum(b[i] * pairs - 1, 0), 0, 0)
    after = lambda i, b: (jnp.minimum((b[i] + 1) * pairs, last), 0, 0)
    padded = (step_rows + 2 * SWEEPS, cols + 2 * MARGIN, length)
    ends = 4 + len(arrays)

    def kernel(*refs):
        if len(arrays) == 4:
            refs = refs[:ends] + (None, None) + refs[ends:]
        fill_kernel(*refs)

    return pl.pallas_call(
        kernel,
        grid_spec=pltpu.PrefetchScalarGridSpec(
            num_scalar_prefetch=1,
            grid=(len(starts),),
            in_specs=[
                pl.BlockSpec((step_rows, cols, length), lambda i, b: (b[i], 0, 0)),
                pl.BlockSpec((SWEEPS, cols, length), before),
                pl.BlockSpec((SWEEPS, cols, length), after),
            ] + [whole(array) for array in arrays],
            out_specs=[
                pl.BlockSpec((step_rows, cols, half), lambda i, b: (i, 0, 0)),
                pl.BlockSpec((step_rows, half), lambda i, b: (i, 0)),
                pl.BlockSpec((cols, 128), lambda i, b: (0, 0)),
            ],
            scratch_shapes=[
                pltpu.VMEM(padded, jnp.float32),
                pltpu.VMEM(padded, jnp.float32),
                pltpu.VMEM((step_rows * cols, length), jnp.bfloat16),
                pltpu.VMEM((step_rows * cols, length), jnp.bfloat16),
                pltpu.VMEM((cols, 128), jnp.float32),
            ],
        ),
        out_shape=[
            jax.ShapeDtypeStruct((count, cols, half), jnp.float32),
            jax.ShapeDtypeStruct((count, half), jnp.float32),
            jax.ShapeDtypeStruct((cols, 128), jnp.float32),
        ],
        compiler_params=pltpu.CompilerParams(vmem_limit_bytes=VMEM_BYTES),
        cost_estimate=pl.CostEstimate(
            flops=count * cols * length * half * 6,
            bytes_accessed=count * cols * (length + half) * 4,
            transcendentals=0,
        ),
    )(steps, intensity, intensity, intensity, *arrays)


def pack(section, offsets):
    block = offsets[1]
    units = [section[b * block : (b + 1) * block, : (b + 1) * block] for b in range(len(offsets) - 1)]
    return jnp.concatenate(units, axis=1)


def three_dots(left, right):
    total = jnp.dot(left[1], right[0], preferred_element_type=jnp.float32)
    total += jnp.dot(left[0], right[1], preferred_element_type=jnp.float32)
    return total + jnp.dot(left[0], right[0], preferred_element_type=jnp.float32)


def section_kernel(
    offsets, planes, opening, closing, me, weights, kept, got, cols_high, cols_low, rows_high,
    rows_low, *refs
):
    step, steps = pl.program_id(0), pl.num_programs(0)
    step_rows = kept.shape[0]
    half, count = rows_high.shape
    before = None if opening else refs[0]
    refs = refs if opening else refs[1:]
    rim, corner = refs[:2] if closing else (None, None)
    *outs, total, lines, packed = refs[2:] if closing else refs
    block, width = total.shape[1:]
    gy, (_, own, gx, _) = len(outs), outs[0].shape

    def place(layer, values, slot=0):
        packed[slot] = values
        for e in range(own):
            for p in range(gy):
                start = pl.multiple_of((e * gy + (p ^ me[0])) * gx, gx)
                outs[p][layer, e] = packed[slot, pl.ds(start, gx), :]

    @pl.when(step == 0)
    def _():
        total[...] = jnp.zeros_like(total) if opening else before[...]

    for r in range(step_rows):
        layer = step * step_rows + r
        values = jnp.concatenate([kept[r], got[r]], axis=0)
        section = three_dots((cols_high[...], cols_low[...]), split(values))
        section = section + section.T
        line = pack(section, offsets)
        place(layer, line, r)
        for m in range(planes):
            total[m] += weights[m, layer] * line
        for m in range(planes - 1):
            row = (m + 1) * (half // planes)
            lines[m, pl.ds(layer, 1), :] = section[row : row + 1]

    @pl.when(step == steps - 1)
    def _():
        for m in range(planes - 1):
            plane = three_dots((rows_high[...], rows_low[...]), split(lines[m]))
            total[m] += pack(plane + plane.T, offsets)
        if closing:
            total[planes - 1] += pack(rim[...] + rim[...].T, offsets)
            for m in range(planes):
                place(count + m, total[m])
            place(count + planes, jnp.zeros((block, width), jnp.float32) + corner[...])


def packed_section(col, kept, got, first, pair_table, row_table, weights, rim, corner, before, offsets, shape, closing):
    _, cols, half = kept.shape
    count = row_table[0].shape[1]
    planes, block, width = weights.shape[0], offsets[1], offsets[-1]
    gx, gy = shape
    opening = before is None
    step_rows = 4
    layers = count + (planes + 1 if closing else 0)
    whole = lambda array: pl.BlockSpec(array.shape, lambda i: (0,) * array.ndim)
    arrays = pair_table + row_table
    arrays += (() if opening else (before,)) + ((rim, corner[None]) if closing else ())
    out = jax.ShapeDtypeStruct((layers, block // (gx * gy), gx, width), jnp.float32)
    outs = [out] * gy + [jax.ShapeDtypeStruct((planes, block, width), jnp.float32)]
    rows_spec = pl.BlockSpec((step_rows, cols, half), lambda i: (i + first // step_rows, 0, 0))
    return pl.pallas_call(
        lambda *refs: section_kernel(offsets, planes, opening, closing, *refs),
        grid=(count // step_rows,),
        in_specs=[pl.BlockSpec(memory_space=pltpu.SMEM)] * 2 + [rows_spec, rows_spec]
        + [whole(array) for array in arrays],
        out_specs=[whole(out) for out in outs],
        out_shape=outs,
        scratch_shapes=[
            pltpu.VMEM((planes, count, half), jnp.float32),
            pltpu.VMEM((step_rows, block, width), jnp.float32),
        ],
        compiler_params=pltpu.CompilerParams(vmem_limit_bytes=VMEM_BYTES),
        cost_estimate=pl.CostEstimate(
            flops=count * 12 * cols * half * half,
            bytes_accessed=count * cols * half * 16,
            transcendentals=0,
        ),
    )(col.reshape(1), weights, kept, got, *arrays)


def on_device(intensity, template):
    rows, cols, length = intensity.shape
    gx, gy = lax.axis_size("gx"), lax.axis_size("gy")
    row, col = lax.axis_index("gx"), lax.axis_index("gy")
    devices, half = gx * gy, length // 2
    block = max(devices, rows)
    blocks, own, slabs = half // block, block // devices, gx // 2
    offsets = [block * b * (b + 1) // 2 for b in range(blocks + 1)]
    width = offsets[blocks]
    table = jnp.asarray(cosine_table(length))
    main = table[:, :half]

    pair_rows = rows // 2
    parts = row_parts(pair_rows)
    counts = [part.stop - part.start for part in parts]
    core = lax.rem(col, 2)
    given_first, kept_first = (1 - core) * pair_rows, core * pair_rows
    constants = fill_constants(intensity, template, row, col, cosine_table(length)[:, :half])
    table_cols = lax.dynamic_slice_in_dim(table, col * cols, cols, 0)
    kept_rows = lax.dynamic_slice_in_dim(table, row * rows + kept_first, pair_rows, 0)
    mates = lax.dynamic_slice_in_dim(main, (col + 1 - 2 * core) * cols, cols, 0)
    table_pair = jnp.concatenate([table_cols[:, :half], mates], axis=0)
    pair_tables = rounded_parts(table_pair.T), rounded_parts(kept_rows[parts[0], :half].T)
    before, after = side_faces(intensity)
    before, after, pair_tables = lax.optimization_barrier((before, after, pair_tables))
    sides = jnp.concatenate([before, after], axis=1)
    inner = parts[0].start >= SWEEPS and parts[0].stop <= pair_rows - SWEEPS
    room = 8 - SWEEPS
    side_columns = jnp.pad(before, ((0, 0), (room, 8), (0, 0)))
    side_columns = side_columns + jnp.pad(after, ((0, 0), (8, room), (0, 0)))
    ends = () if inner else end_faces(intensity, sides)

    def fill(some, start):
        arrays = (side_columns,) + constants + tuple(ends)
        return list(filled_spectrum(intensity, arrays, start, some))

    given, kept = [fill(parts[:1], given_first)], []
    outer = ends
    if inner:
        given[0], late_sides = lax.optimization_barrier((given[0], sides))
        outer = end_faces(intensity, late_sides)
    kept.append(fill(parts[:1], kept_first))
    ends = outer

    marks = [rows * (m + 1) for m in range(slabs)]
    if all(start % gx == 0 for start in [pair_rows] + [part.start for part in parts]):
        weights = [jnp.asarray(cosine_table(length)[:count, marks].T) for count in counts]
    else:
        weights = [jnp.stack([kept_rows[part, m] for m in marks]) for part in parts]
    table_parts = main.reshape(gx, 2, pair_rows, half) / 6.0
    table_parts = jnp.where(core == 0, table_parts, table_parts[:, ::-1])
    table_parts = [table_parts[:, :, part] for part in parts]
    side = rim = corner = None
    values, packed, lines = 0.0, None, None
    for c, count in enumerate(counts):
        closing = c == len(counts) - 1
        if c == 1:
            behind = (given_first, kept_first), packed
            starts, packed = lax.optimization_barrier(behind)
            given.append(fill(parts[1:], starts[0]))
            kept.append(fill(parts[1:], starts[1]))
        flanks = [piece[1:] for piece in given + kept]
        if c > 1:
            flanks, packed = lax.optimization_barrier((flanks, packed))
        if c > 0:
            got_lines = exchanged(packed)
        if c == 1:
            behind = given[1][0], kept[1][0], got_lines
            given[1][0], kept[1][0], got_lines = lax.optimization_barrier(behind)
        if c < 2:
            got = lax.ppermute(given[c][0], "gy", swap(gy, 1))
            held = kept[c][0]
        if c > 0:
            lines = sent_lines(got_lines, counts[c - 1], lines)
            values = values + first_axis(lines, table_parts[c - 1])
        if closing:
            given_rows = lax.dynamic_slice_in_dim(table, row * rows + given_first, pair_rows, 0)
            ordered_rows = [held_rows[part] for held_rows in (given_rows, kept_rows) for part in parts]
            ordered_rows = jnp.concatenate(ordered_rows, axis=0)
            alternate = jnp.concatenate([piece[0] for piece in flanks], axis=0) / math.sqrt(length)
            edge = [piece[1][:, : piece[0].shape[0]] for piece in flanks]
            edge = jnp.concatenate(edge, axis=1)
            edge = jnp.einsum("ba,bk->ak", edge / math.sqrt(length), table_cols, precision=HIGH)
            edge = edge + jnp.concatenate([alternate, edge[:, half:]], axis=1)
            rim = jnp.einsum("aj,ak->jk", ordered_rows[:, :half], edge[:, :half], precision=HIGH)
            corner = 2.0 * jnp.einsum("a,ak->k", ordered_rows[:, half], edge, precision=HIGH)
            corner = corner + jnp.einsum("aj,a->j", ordered_rows, edge[:, half], precision=HIGH)
            corner = jnp.pad(corner, (0, width - half - 1))

        row_table = pair_tables[1]
        if c > 0:
            row_table = rounded_parts(kept_rows[parts[c], :half].T)
        *packed, side = packed_section(
            col, held, got, sum(counts[1:c]), pair_tables[0], row_table, weights[c],
            rim, corner, side, offsets, (gx, gy), closing,
        )
    lines = sent_lines(exchanged(packed), counts[-1], lines)
    values = values + first_axis(lines, table_parts[-1])
    side = jnp.sum(lines[:, :, 2 * counts[-1] :], axis=0) / 6.0
    turned = values.reshape(own, blocks, own, devices, width)
    turned = jnp.transpose(turned, (3, 1, 2, 0, 4))
    turned = [turned[:, b, :, :, : offsets[b + 1]] for b in range(blocks)]
    turned = lax.all_to_all(jnp.concatenate(turned, axis=3), ("gy", "gx"), 0, 0, tiled=True)
    turned = jnp.transpose(turned, (1, 2, 0, 3)).reshape(own, block, -1)

    slab = jnp.minimum(row, gx - 1 - row)
    far_row, far_col = row >= slabs, col >= gy // 2
    pick_rows = jnp.arange(rows)
    pick_rows = slab * rows + jnp.where(far_row, rows - pick_rows, pick_rows)
    pick_cols = jnp.arange(cols)
    pick_cols = jnp.where(far_col, (gy - col) * cols - pick_cols, col * cols + pick_cols)

    if rows == block:
        got, piece = [], None
        for messages in slab_messages(values, turned, side, offsets, slabs):
            if piece is not None:
                messages, piece = lax.optimization_barrier((messages, piece))
                got.append(gathered(piece, gy, got[-1] if got else None))
            piece = lax.all_to_all(messages, "gx", 0, 0, tiled=True)
        got.append(gathered(piece, gy, got[-1] if got else None))
        tiles = width // 128
        start = tile_groups(tiles)[0].stop * own * block
        side = jnp.stack([piece[:, start : start + 3 * own * tiles] for piece in got[0]])
        bit = gy // 2
        while bit:
            paired = side.reshape((-1, 2, bit) + side.shape[1:])
            side = jnp.where((col & bit) == 0, paired, paired[:, ::-1]).reshape(side.shape)
            bit //= 2
        side = side.reshape(devices, own, 3, width)
        side = jnp.transpose(side, (2, 1, 0, 3)).reshape(3, block, width)
        next_plane, across = side[0], rim_rows(side[1:], offsets, pick_rows)
        rim_col = col == gy // 2
        rim = across[:, pick_cols]
        return result_block(
            got, next_plane, across, rim, pick_cols, slab, far_row, rim_col, col, offsets
        )

    side = lax.all_gather(side, ("gy", "gx"), axis=0)
    side = jnp.transpose(side, (2, 1, 0, 3)).reshape(slabs + 1, block, width)
    across = rim_rows(side[slabs - 1 :], offsets, pick_rows)
    next_plane = lax.dynamic_index_in_dim(side, slab, 0, keepdims=False)
    sums = axis_order_sums(values, turned, offsets, block)
    messages = []
    for s in range(slabs):
        base, first = s * rows // block, s * rows
        units = []
        for b in range(blocks):
            size = (b + 1) * block
            near = jnp.zeros((own, rows, size))
            far = jnp.zeros((own, block, size))
            if b >= base:
                near = jnp.stack([sums[b][e][first : first + rows, :size] for e in range(own)])
            else:
                far = jnp.stack([sums[base][e][b * block : size, :size] for e in range(own)])
            units.append(jnp.concatenate([near, far], axis=1))
        messages.append(jnp.concatenate(units, axis=2))
    messages = jnp.stack(messages + messages[::-1])
    got = lax.all_to_all(messages, "gx", 0, 0, tiled=True)
    got = lax.all_gather(got, "gy", axis=0, tiled=True)
    got = jnp.swapaxes(got, 0, 1).reshape(block, rows + block, width)
    base = slab * rows // block
    lower = []
    for b in range(blocks):
        lanes = slice(offsets[b], offsets[b + 1])
        near = jnp.swapaxes(got[:, :rows, lanes], 0, 1)
        far = lax.dynamic_slice_in_dim(got[:, rows:, lanes], lax.rem(slab * rows, block), rows, 0)
        lower.append(jnp.where(b >= base, near, far))
    lower = jnp.concatenate(lower, axis=2)
    lower = jnp.concatenate([lower, next_plane[None]], axis=0)
    body = square([lower[:, :, offsets[b] : offsets[b + 1]] for b in range(blocks)], block)
    body = body[pick_rows - slab * rows]
    body = jnp.concatenate([body, across[:, None, :half]], axis=1)[:, pick_cols]
    body = jnp.concatenate([body, across[:, pick_cols][:, :, None]], axis=2)
    return jnp.concatenate([body, jnp.flip(body[:, :, 1:half], 2)], axis=2)


def rim_rows(side, offsets, pick_rows):
    blocks, block = len(offsets) - 1, offsets[1]
    half = blocks * block
    last = square([side[0][:, offsets[b] : offsets[b + 1]] for b in range(blocks)], block)
    rim = side[1, 0, : half + 1]
    last = jnp.concatenate([last, rim[None, :half]], axis=0)
    return jnp.concatenate([last, rim[:, None]], axis=1)[pick_rows]


def axis_order_sums(values, turned, offsets, block):
    start = 0
    sums = []
    for top in range(len(offsets) - 1):
        size = (top + 1) * block
        parts = []
        for e in range(values.shape[0]):
            part = values[e, :size, offsets[top] : offsets[top] + size]
            lower = [turned[e, :, start + offsets[b] : start + offsets[b + 1]] for b in range(top + 1)]
            parts.append(part + part.T + square(lower, block))
        sums.append(parts)
        start += offsets[top + 1]
    return sums


def message_kernel(offsets, slabs, values, turned, side, *messages):
    blocks, block = len(offsets) - 1, offsets[1]
    values, turned = values[...], turned[...]
    own = values.shape[0]
    sums = axis_order_sums(values, turned, offsets, block)
    groups = tile_groups(offsets[-1] // 128)
    side_start = groups[0].stop * own * block
    messages[0][:, side_start:] = jnp.zeros_like(messages[0][:, side_start:])
    for s in range(slabs):
        places = s, 2 * slabs - 1 - s
        for e in range(own):
            units = []
            for b in range(blocks):
                size = (b + 1) * block
                if b >= s:
                    units.append(sums[b][e][s * block : (s + 1) * block, :size])
                else:
                    units.append(sums[s][e][b * block : size, :size])
            line = jnp.concatenate(units, axis=1)
            for group, out in zip(groups, messages):
                for tile in range(group.start, group.stop):
                    start = ((tile - group.start) * own + e) * block
                    for place in places:
                        out[place, start : start + block] = line[:, tile * 128 : (tile + 1) * 128]
            row = side_start + 3 * e * groups[-1].stop
            for plane in (s, slabs - 1, slabs):
                for tile in range(groups[-1].stop):
                    part = side[e, plane : plane + 1, tile * 128 : (tile + 1) * 128]
                    for place in places:
                        messages[0][place, row : row + 1] = part
                    row += 1


def slab_messages(values, turned, side, offsets, slabs):
    own, block, tiles = values.shape[0], offsets[1], offsets[-1] // 128
    sizes = [(group.stop - group.start) * own * block for group in tile_groups(tiles)]
    sizes[0] += -(-3 * own * tiles // 8) * 8
    return pl.pallas_call(
        lambda *refs: message_kernel(offsets, slabs, *refs),
        in_specs=[pl.BlockSpec(memory_space=pltpu.VMEM)] * 3,
        out_specs=[pl.BlockSpec(memory_space=pltpu.VMEM)] * len(sizes),
        out_shape=[jax.ShapeDtypeStruct((2 * slabs, size, 128), jnp.float32) for size in sizes],
        compiler_params=pltpu.CompilerParams(vmem_limit_bytes=VMEM_BYTES),
    )(values, turned, side)


def result_kernel(
    offsets, own, devices, groups, places, next_plane, across, rim, pick, flip, *refs
):
    blocks, block = len(offsets) - 1, offsets[1]
    tiles = offsets[-1] // 128
    peers = (len(refs) - 2) // len(groups) - 1
    pieces, out = refs[: peers * len(groups)], refs[peers * len(groups)]
    held, sems = refs[peers * len(groups) + 1 : -1], refs[-1]
    step_rows, cols, length = out.shape
    half = length // 2
    slab, far_row, rim_col, me = places[0], places[1], places[2], places[3]
    lane = lax.broadcasted_iota(jnp.int32, (block, 128), 1)
    at_rim = lax.broadcasted_iota(jnp.int32, (cols, half), 0) + (1 - rim_col) == 0
    first_lane = lax.broadcasted_iota(jnp.int32, (cols, 128), 1) == 0

    @pl.when(pl.program_id(0) == 0)
    def _():
        copies = []
        for g in range(len(groups)):
            for peer in range(peers):
                piece = pieces[g * peers + peer]
                size = piece.shape[0]
                spot = pl.ds(pl.multiple_of((me ^ peer) * size, size), size)
                copies.append(pltpu.make_async_copy(piece, held[g].at[spot], sems.at[g, peer]))
        for copy in copies:
            copy.start()
        for copy in copies:
            copy.wait()

    def left_half(r, may_pass):
        t = pl.program_id(0) * step_rows + r
        i = jnp.where(far_row == 1, block - t, t)
        inside = (jnp.zeros((block, 128), jnp.int32) + i) < block
        i = jnp.minimum(i, block - 1)
        source = lax.div(i, devices), lax.rem(i, devices)
        parts = []
        for g, group in enumerate(groups):
            stride = held[g].shape[0] // devices
            for tile in range(group.start, group.stop):
                start = (tile - group.start) * own * block
                near = [
                    held[g][pl.ds(start + e * block + i, devices, stride=stride), :]
                    for e in range(own)
                ]
                near = jnp.concatenate(near, axis=0)
                line = near
                if tile * 128 < offsets[blocks - 1]:
                    far = pl.multiple_of(source[1] * stride + start + source[0] * block, 8)
                    far = held[g][pl.ds(far, block), :]
                    kind = jnp.zeros((block, 128), jnp.int32)
                    for b in range(1, blocks):
                        kind += (lane + tile * 128 >= offsets[b]).astype(jnp.int32)
                    line = jnp.where(kind >= slab, near, far)
                if may_pass:
                    line = jnp.where(inside, line, next_plane[:, pl.ds(tile * 128, 128)])
                parts.append(line)
        line = jnp.concatenate(parts, axis=1)
        plane = square([line[:, offsets[b] : offsets[b + 1]] for b in range(blocks)], block)
        high, low = split(plane)
        left = jnp.dot(pick[...], high, preferred_element_type=jnp.float32)
        left += jnp.dot(pick[...], low, preferred_element_type=jnp.float32)
        left = jnp.where(at_rim, across[pl.ds(t, 1), :], left)
        out[r, :, pl.ds(0, half)] = left
        return left

    together = 4

    @pl.loop(0, step_rows // together)
    def _(c):
        left = [left_half(c * together + n, n == 0) for n in range(together)]
        high, low = split(jnp.concatenate(left, axis=0))
        right = jnp.dot(high, flip[...], preferred_element_type=jnp.float32)
        right += jnp.dot(low, flip[...], preferred_element_type=jnp.float32)
        for n in range(together):
            r = c * together + n
            t = pl.program_id(0) * step_rows + r
            edge = pltpu.roll(rim[...], lax.rem(128 - t, 128), 1)
            part = right[n * cols : (n + 1) * cols]
            out[r, :, pl.ds(half, 128)] = jnp.where(first_lane, edge, part[:, :128])
            out[r, :, pl.ds(half + 128, half - 128)] = part[:, 128:]


def result_block(got, next_plane, across, rim, pick_cols, slab, far_row, rim_col, col, offsets):
    block = offsets[1]
    gx = got[0][0].shape[0]
    groups = tile_groups(offsets[-1] // 128)
    devices = gx * len(got[0])
    own = block // devices
    rows, half = across.shape[0], across.shape[1] - 1
    cols = pick_cols.shape[0]
    step_rows = 8
    places = jnp.stack([slab, far_row.astype(jnp.int32), rim_col.astype(jnp.int32), col])
    cell = jnp.arange(half)
    pick = (pick_cols[:, None] == cell[None, :]).astype(jnp.bfloat16)
    flip = (cell[:, None] + cell[None, :] == half).astype(jnp.bfloat16)
    rim = jnp.pad(rim.T, ((0, 0), (0, 128 - rows)))
    whole = lambda array: pl.BlockSpec(array.shape, lambda i: (0,) * array.ndim)
    arrays = (next_plane, across[:, :half], rim, pick, flip)
    pieces = [piece.reshape(-1, 128) for group in got for piece in group]
    return pl.pallas_call(
        lambda *refs: result_kernel(offsets, own, devices, groups, *refs),
        grid=(rows // step_rows,),
        in_specs=[pl.BlockSpec(memory_space=pltpu.SMEM)] + [whole(array) for array in arrays]
        + [pl.BlockSpec(memory_space=pl.ANY)] * len(pieces),
        out_specs=pl.BlockSpec((step_rows, cols, 2 * half), lambda i: (i, 0, 0)),
        out_shape=jax.ShapeDtypeStruct((rows, cols, 2 * half), jnp.float32),
        scratch_shapes=[
            pltpu.VMEM((devices * group[0].shape[1], 128), jnp.float32) for group in got
        ] + [pltpu.SemaphoreType.DMA((len(groups), len(got[0])))],
        compiler_params=pltpu.CompilerParams(vmem_limit_bytes=VMEM_BYTES),
    )(places, *arrays, *pieces)


def tile_groups(tiles):
    return [slice(tile, min(tile + 2, tiles)) for tile in range(0, tiles, 2)]


def swap(peers, bit):
    return [(q, q ^ bit) for q in range(peers)]


def gathered(piece, peers, after):
    if after is not None:
        piece, first_hops = lax.optimization_barrier((piece, after[1:3]))
        after[1:3] = first_hops
    pieces, bit = {0: piece}, peers // 2
    while bit:
        for place in list(pieces):
            pieces[place ^ bit] = lax.ppermute(pieces[place], "gy", swap(peers, bit))
        bit //= 2
    return [pieces[place] for place in range(peers)]


def exchanged(packed):
    gy = len(packed)
    return [packed[0]] + [lax.ppermute(packed[p], "gy", swap(gy, p)) for p in range(1, gy)]


def sent_lines(got, count, after):
    gy = len(got)
    lines = [sum(got[p][:count] for p in range(first, gy, 2)) for first in range(2)]
    lines = jnp.concatenate(lines + [sum(piece[count:] for piece in got)], axis=0)
    lines = jnp.transpose(lines, (2, 1, 0, 3))
    if after is not None:
        lines, _ = lax.optimization_barrier((lines, after))
    return lax.all_to_all(lines, "gx", 0, 0, tiled=True)


def first_axis(lines, table):
    gx, _, count, half = table.shape
    table = table.reshape(gx, 2 * count, half)
    return jnp.einsum("geaw,gai->eiw", lines[:, :, : 2 * count], table, precision=HIGH)


def row_parts(rows):
    if rows < 4 * PART_STEP:
        return [slice(0, rows)]
    return [slice(PART_STEP, rows - PART_STEP), slice(0, PART_STEP), slice(rows - PART_STEP, rows)]


def square(lower, block):
    if len(lower) == 1:
        return lower[0]
    split_at = len(lower) // 2
    size = split_at * block
    first = square(lower[:split_at], block)
    corner = jnp.concatenate([line[..., :size] for line in lower[split_at:]], axis=-2)
    last = square([line[..., size:] for line in lower[split_at:]], block)
    top = jnp.concatenate([first, jnp.swapaxes(corner, -1, -2)], axis=-1)
    return jnp.concatenate([top, jnp.concatenate([corner, last], axis=-1)], axis=-2)


def solution(mesh):
    placed = (P("gx", "gy", None), P())
    return jax.shard_map(
        on_device, mesh=mesh, in_specs=placed, out_specs=P("gx", "gy", None), check_vma=False
    )
```

```python
import math

import jax
import jax.numpy as jnp
import numpy as np
from jax import lax
from jax.experimental import pallas as pl
from jax.experimental.pallas import tpu as pltpu
from jax.sharding import PartitionSpec as P

SWEEPS = 2

AXIS_ORDERS = ((0, 1, 2), (0, 2, 1), (1, 0, 2), (1, 2, 0), (2, 0, 1), (2, 1, 0))

HIGH = lax.Precision.HIGH


def ring(axis):
    peers = lax.axis_size(axis)
    up = [(i, (i + 1) % peers) for i in range(peers)]
    return up, [(j, i) for i, j in up]


def side_faces(block):
    cols = block.shape[1]
    right, left = ring("gy")
    before = lax.ppermute(block[:, cols - SWEEPS :], "gy", right)
    after = lax.ppermute(block[:, :SWEEPS], "gy", left)
    return before, after


def end_faces(block, sides):
    rows = block.shape[0]
    up, down = ring("gx")
    last = jnp.concatenate([block[rows - SWEEPS :], sides[rows - SWEEPS :]], axis=1)
    first = jnp.concatenate([block[:SWEEPS], sides[:SWEEPS]], axis=1)
    return lax.ppermute(last, "gx", up), lax.ppermute(first, "gx", down)


def mirror(values, axis):
    return jnp.roll(jnp.flip(values, axis), 1, axis)


def symmetric_marks(marks):
    for flip_axis in range(3):
        marks = jnp.maximum(marks, mirror(marks, flip_axis))
    united = marks
    for axis_order in AXIS_ORDERS[1:]:
        united = jnp.maximum(united, jnp.transpose(marks, axis_order))
    return united


def cosine_table(length):
    position = np.arange(length)
    phases = np.mod(position[:, None] * position[None, : length // 2 + 1], length)
    return (np.cos(phases * (2.0 * math.pi / length)) / math.sqrt(length)).astype(np.float32)


MARGIN = 16
CHUNK = 16
STEP_ROWS = 16
PART_STEP = 8
VMEM_BYTES = 56 * 1024 * 1024


def split(values):
    high = values.astype(jnp.bfloat16)
    low = (values - high.astype(jnp.float32)).astype(jnp.bfloat16)
    return high, low


def fill_kernel(
    base, here, above, below, sides, marks, table_high, table_low, top, bottom,
    spectrum, alternate, edge, punched, once, high, low, folded,
):
    step_rows, cols, length = here.shape
    step = base[pl.program_id(0)]
    first_row = step * step_rows
    local_row = pl.program_id(0) * step_rows
    period = marks.shape[0]
    lane = lax.broadcasted_iota(jnp.int32, (128, 128), 1)
    signs = jnp.where(lax.broadcasted_iota(jnp.int32, (128, 128), 0) % 2 == 0, 1.0, -1.0)

    @pl.when(pl.program_id(0) == 0)
    def _():
        edge[...] = jnp.zeros_like(edge)

    def holes(row, start, size):
        row = lax.rem(first_row + row, period)
        start = start % period
        if start + size <= period:
            part = marks[row, pl.ds(start, size), :]
        else:
            part = jnp.concatenate(
                [marks[row, pl.ds(start, period - start), :], marks[row, pl.ds(0, start + size - period), :]],
                axis=0,
            )
        return jnp.concatenate([part] * (length // 128), axis=1)

    def punch(row, start, values):
        kept = jnp.where(holes(row, start, values.shape[0]) > 0.0, 0.0, values)
        punched[row, pl.ds(start, values.shape[0]), :] = kept

    def punch_row(row, source, index):
        for c in range(0, cols, CHUNK):
            punch(row, MARGIN + c, source[index, pl.ds(c, CHUNK), :])

    def punch_sides(row):
        full = first_row + row - SWEEPS
        punch(row, MARGIN - 8, sides[full, pl.ds(0, 8), :])
        punch(row, MARGIN + cols, sides[full, pl.ds(8, 8), :])

    def neighbours(ref, row, start):
        middle = ref[row, pl.ds(start, CHUNK), :]
        total = ref[row - 1, pl.ds(start, CHUNK), :] + ref[row + 1, pl.ds(start, CHUNK), :]
        total += ref[row, pl.ds(start - 1, CHUNK), :] + ref[row, pl.ds(start + 1, CHUNK), :]
        return total + pltpu.roll(middle, 1, 1) + pltpu.roll(middle, length - 1, 1)

    last = sides.shape[0] // step_rows - 1
    for edge_rows, inside, offset, outer in (
        (above, step > 0, 0, top),
        (below, step < last, step_rows + SWEEPS, bottom),
    ):
        if outer is None:
            for r in range(SWEEPS):
                punch_row(offset + r, edge_rows, r)
                punch_sides(offset + r)
            continue

        @pl.when(inside)
        def _():
            for r in range(SWEEPS):
                punch_row(offset + r, edge_rows, r)
                punch_sides(offset + r)

        @pl.when(jnp.logical_not(inside))
        def _():
            for r in range(SWEEPS):
                punch_row(offset + r, outer, r)
                punch(offset + r, MARGIN - SWEEPS, outer[r, pl.ds(cols, SWEEPS), :])
                punch(offset + r, MARGIN + cols, outer[r, pl.ds(cols + SWEEPS, SWEEPS), :])

    @pl.loop(0, step_rows)
    def _(r):
        punch_row(r + SWEEPS, here, r)
        punch_sides(r + SWEEPS)

    @pl.loop(1, step_rows + 2 * SWEEPS - 1, unroll=2)
    def _(r):
        for start in range(MARGIN - 8, MARGIN + cols + 8, CHUNK):
            total = neighbours(punched, r, start) * holes(r, start, CHUNK)
            once[r, pl.ds(start, CHUNK), :] = punched[r, pl.ds(start, CHUNK), :] + total

    @pl.loop(0, step_rows)
    def _(r):
        for c in range(0, cols, CHUNK):
            start = MARGIN + c
            total = neighbours(once, r + SWEEPS, start) * holes(r + SWEEPS, start, CHUNK)
            filled = punched[r + SWEEPS, pl.ds(start, CHUNK), :] + total
            first, second = split(filled)
            spot = pl.ds(pl.multiple_of(r * cols + c, CHUNK), CHUNK)
            high[spot, :] = first
            low[spot, :] = second
            wrapped = filled[:, :128]
            for tile in range(1, length // 128):
                wrapped += filled[:, tile * 128 : (tile + 1) * 128]
            folded[pl.ds(c, CHUNK), :] = wrapped
        column = jnp.where(lane == local_row + r, signs, 0.0).astype(jnp.bfloat16)
        first, second = split(folded[...])
        total = jnp.dot(first, column, preferred_element_type=jnp.float32)
        total += jnp.dot(second, column, preferred_element_type=jnp.float32)
        edge[...] += total

    rows_each = 8
    half = spectrum.shape[2]
    order = lax.broadcasted_iota(jnp.int32, (rows_each, cols, half), 1)

    @pl.loop(0, step_rows // rows_each)
    def _(r):
        spot = pl.ds(pl.multiple_of(r * rows_each * cols, CHUNK), rows_each * cols)
        first, second = high[spot, :], low[spot, :]
        total = jnp.dot(first, table_low[...], preferred_element_type=jnp.float32)
        total += jnp.dot(second, table_high[...], preferred_element_type=jnp.float32)
        total += jnp.dot(first, table_high[...], preferred_element_type=jnp.float32)
        total = total.reshape(rows_each, cols, half)
        spectrum[pl.ds(r * rows_each, rows_each)] = total
        signed = jnp.sum(jnp.where(order % 2 == 0, total, -total), axis=1)
        alternate[pl.ds(pl.multiple_of(r * rows_each, rows_each), rows_each), :] = signed


def rounded_parts(table):
    rounded = lax.reduce_precision(table, 8, 7)
    return rounded.astype(jnp.bfloat16), (table - rounded).astype(jnp.bfloat16)


def marks_kernel(shifts, template, out, held):
    period = template.shape[0]
    repeats = held.shape[1] // period
    line = lax.broadcasted_iota(jnp.int32, (period, period), 0)
    across = lax.broadcasted_iota(jnp.int32, (period, period), 1)
    flip = jnp.where((line + across) % period == 0, 1.0, 0.0)
    for i in range(period):
        plane = jnp.maximum(template[i], template[-i % period]).astype(jnp.float32)
        plane = jnp.maximum(plane, jnp.dot(flip, plane, preferred_element_type=jnp.float32))
        plane = jnp.maximum(plane, jnp.dot(plane, flip, preferred_element_type=jnp.float32))
        plane = jnp.maximum(plane, plane.T)
        held[i * period : (i + 1) * period, :] = jnp.concatenate([plane] * repeats, axis=1)
    for i in range(period):
        plane = held[i * period : (i + 1) * period, :]
        turned = held[pl.ds(i, period, stride=period), :]
        back = turned[:, :period].T
        plane = jnp.maximum(jnp.maximum(plane, turned), jnp.concatenate([back] * repeats, axis=1))
        plane = jnp.where(plane == 1.0, 1.0 / 6.0, 0.0)
        shift = shifts[1]
        out[(i - shifts[0]) % period] = jnp.concatenate([plane[shift:], plane[:shift]], axis=0)


def hole_marks(template, row, col, rows, cols):
    period = template.shape[0]
    shape = (period, period, 128)
    if rows % period == 0 and cols % period == 0:
        shifts = (-SWEEPS % period, -MARGIN % period)
        return pl.pallas_call(
            lambda *refs: marks_kernel(shifts, *refs),
            in_specs=[pl.BlockSpec(memory_space=pltpu.VMEM)],
            out_specs=pl.BlockSpec(memory_space=pltpu.VMEM),
            out_shape=jax.ShapeDtypeStruct(shape, jnp.float32),
            scratch_shapes=[pltpu.VMEM((period * period, 128), jnp.float32)],
        )(template)
    shifts = (jnp.mod(row * rows - SWEEPS, period), jnp.mod(col * cols - MARGIN, period))
    marks = jnp.roll(symmetric_marks(template), (-shifts[0], -shifts[1]), (0, 1))
    return jnp.tile(marks.astype(jnp.float32) / 6.0, (1, 1, 128 // period))


def fill_constants(intensity, template, row, col, main):
    rows, cols, _ = intensity.shape
    high = main.astype(jnp.bfloat16)
    low = (main - high.astype(np.float32)).astype(jnp.bfloat16)
    return hole_marks(template, row, col, rows, cols), jnp.asarray(high), jnp.asarray(low)


def filled_spectrum(intensity, arrays, first, parts):
    rows, cols, length = intensity.shape
    half = length // 2
    aligned = all(edge % STEP_ROWS == 0 for part in parts for edge in (part.start, part.stop))
    step_rows = STEP_ROWS if aligned else PART_STEP
    starts = [start for part in parts for start in range(part.start, part.stop, step_rows)]
    count = step_rows * len(starts)
    steps = jnp.stack([(first + start) // step_rows for start in starts])
    pairs = step_rows // SWEEPS
    last = rows // SWEEPS - 1
    whole = lambda array: pl.BlockSpec(array.shape, lambda i, b: (0,) * array.ndim)
    before = lambda i, b: (jnp.maximum(b[i] * pairs - 1, 0), 0, 0)
    after = lambda i, b: (jnp.minimum((b[i] + 1) * pairs, last), 0, 0)
    padded = (step_rows + 2 * SWEEPS, cols + 2 * MARGIN, length)
    ends = 4 + len(arrays)

    def kernel(*refs):
        if len(arrays) == 4:
            refs = refs[:ends] + (None, None) + refs[ends:]
        fill_kernel(*refs)

    return pl.pallas_call(
        kernel,
        grid_spec=pltpu.PrefetchScalarGridSpec(
            num_scalar_prefetch=1,
            grid=(len(starts),),
            in_specs=[
                pl.BlockSpec((step_rows, cols, length), lambda i, b: (b[i], 0, 0)),
                pl.BlockSpec((SWEEPS, cols, length), before),
                pl.BlockSpec((SWEEPS, cols, length), after),
            ] + [whole(array) for array in arrays],
            out_specs=[
                pl.BlockSpec((step_rows, cols, half), lambda i, b: (i, 0, 0)),
                pl.BlockSpec((step_rows, half), lambda i, b: (i, 0)),
                pl.BlockSpec((cols, 128), lambda i, b: (0, 0)),
            ],
            scratch_shapes=[
                pltpu.VMEM(padded, jnp.float32),
                pltpu.VMEM(padded, jnp.float32),
                pltpu.VMEM((step_rows * cols, length), jnp.bfloat16),
                pltpu.VMEM((step_rows * cols, length), jnp.bfloat16),
                pltpu.VMEM((cols, 128), jnp.float32),
            ],
        ),
        out_shape=[
            jax.ShapeDtypeStruct((count, cols, half), jnp.float32),
            jax.ShapeDtypeStruct((count, half), jnp.float32),
            jax.ShapeDtypeStruct((cols, 128), jnp.float32),
        ],
        compiler_params=pltpu.CompilerParams(vmem_limit_bytes=VMEM_BYTES),
        cost_estimate=pl.CostEstimate(
            flops=count * cols * length * half * 6,
            bytes_accessed=count * cols * (length + half) * 4,
            transcendentals=0,
        ),
    )(steps, intensity, intensity, intensity, *arrays)


def pack(section, offsets):
    block = offsets[1]
    units = [section[b * block : (b + 1) * block, : (b + 1) * block] for b in range(len(offsets) - 1)]
    return jnp.concatenate(units, axis=1)


def three_dots(left, right):
    total = jnp.dot(left[1], right[0], preferred_element_type=jnp.float32)
    total += jnp.dot(left[0], right[1], preferred_element_type=jnp.float32)
    return total + jnp.dot(left[0], right[0], preferred_element_type=jnp.float32)


def section_kernel(
    offsets, planes, opening, closing, me, weights, kept, got, cols_high, cols_low, rows_high,
    rows_low, *refs
):
    step, steps = pl.program_id(0), pl.num_programs(0)
    step_rows = kept.shape[0]
    half, count = rows_high.shape
    before = None if opening else refs[0]
    refs = refs if opening else refs[1:]
    rim, corner = refs[:2] if closing else (None, None)
    *outs, total, lines, packed = refs[2:] if closing else refs
    block, width = total.shape[1:]
    gy, (_, own, gx, _) = len(outs), outs[0].shape

    def place(layer, values, slot=0):
        packed[slot] = values
        for e in range(own):
            for p in range(gy):
                start = pl.multiple_of((e * gy + (p ^ me[0])) * gx, gx)
                outs[p][layer, e] = packed[slot, pl.ds(start, gx), :]

    @pl.when(step == 0)
    def _():
        total[...] = jnp.zeros_like(total) if opening else before[...]

    for r in range(step_rows):
        layer = step * step_rows + r
        values = jnp.concatenate([kept[r], got[r]], axis=0)
        section = three_dots((cols_high[...], cols_low[...]), split(values))
        section = section + section.T
        line = pack(section, offsets)
        place(layer, line, r)
        for m in range(planes):
            total[m] += weights[m, layer] * line
        for m in range(planes - 1):
            row = (m + 1) * (half // planes)
            lines[m, pl.ds(layer, 1), :] = section[row : row + 1]

    @pl.when(step == steps - 1)
    def _():
        for m in range(planes - 1):
            plane = three_dots((rows_high[...], rows_low[...]), split(lines[m]))
            total[m] += pack(plane + plane.T, offsets)
        if closing:
            total[planes - 1] += pack(rim[...] + rim[...].T, offsets)
            for m in range(planes):
                place(count + m, total[m])
            place(count + planes, jnp.zeros((block, width), jnp.float32) + corner[...])


def packed_section(col, kept, got, first, pair_table, row_table, weights, rim, corner, before, offsets, shape, closing):
    _, cols, half = kept.shape
    count = row_table[0].shape[1]
    planes, block, width = weights.shape[0], offsets[1], offsets[-1]
    gx, gy = shape
    opening = before is None
    step_rows = 4
    layers = count + (planes + 1 if closing else 0)
    whole = lambda array: pl.BlockSpec(array.shape, lambda i: (0,) * array.ndim)
    arrays = pair_table + row_table
    arrays += (() if opening else (before,)) + ((rim, corner[None]) if closing else ())
    out = jax.ShapeDtypeStruct((layers, block // (gx * gy), gx, width), jnp.float32)
    outs = [out] * gy + [jax.ShapeDtypeStruct((planes, block, width), jnp.float32)]
    kept_spec = pl.BlockSpec((step_rows, cols, half), lambda i: (i, 0, 0))
    rows_spec = pl.BlockSpec((step_rows, cols, half), lambda i: (i + first // step_rows, 0, 0))
    return pl.pallas_call(
        lambda *refs: section_kernel(offsets, planes, opening, closing, *refs),
        grid=(count // step_rows,),
        in_specs=[pl.BlockSpec(memory_space=pltpu.SMEM)] * 2 + [kept_spec, rows_spec]
        + [whole(array) for array in arrays],
        out_specs=[whole(out) for out in outs],
        out_shape=outs,
        scratch_shapes=[
            pltpu.VMEM((planes, count, half), jnp.float32),
            pltpu.VMEM((step_rows, block, width), jnp.float32),
        ],
        compiler_params=pltpu.CompilerParams(vmem_limit_bytes=VMEM_BYTES),
        cost_estimate=pl.CostEstimate(
            flops=count * 12 * cols * half * half,
            bytes_accessed=count * cols * half * 16,
            transcendentals=0,
        ),
    )(col.reshape(1), weights, kept, got, *arrays)


def on_device(intensity, template):
    rows, cols, length = intensity.shape
    gx, gy = lax.axis_size("gx"), lax.axis_size("gy")
    row, col = lax.axis_index("gx"), lax.axis_index("gy")
    devices, half = gx * gy, length // 2
    block = max(devices, rows)
    blocks, own, slabs = half // block, block // devices, gx // 2
    offsets = [block * b * (b + 1) // 2 for b in range(blocks + 1)]
    width = offsets[blocks]
    table = jnp.asarray(cosine_table(length))
    main = table[:, :half]

    pair_rows = rows // 2
    parts = row_parts(pair_rows)
    counts = [part.stop - part.start for part in parts]
    core = lax.rem(col, 2)
    given_first, kept_first = (1 - core) * pair_rows, core * pair_rows
    constants = fill_constants(intensity, template, row, col, cosine_table(length)[:, :half])
    table_cols = lax.dynamic_slice_in_dim(table, col * cols, cols, 0)
    kept_rows = lax.dynamic_slice_in_dim(table, row * rows + kept_first, pair_rows, 0)
    mates = lax.dynamic_slice_in_dim(main, (col + 1 - 2 * core) * cols, cols, 0)
    table_pair = jnp.concatenate([table_cols[:, :half], mates], axis=0)
    pair_tables = rounded_parts(table_pair.T), rounded_parts(kept_rows[parts[0], :half].T)
    before, after = side_faces(intensity)
    before, after, pair_tables = lax.optimization_barrier((before, after, pair_tables))
    sides = jnp.concatenate([before, after], axis=1)
    inner = parts[0].start >= SWEEPS and parts[0].stop <= pair_rows - SWEEPS
    room = 8 - SWEEPS
    side_columns = jnp.pad(before, ((0, 0), (room, 8), (0, 0)))
    side_columns = side_columns + jnp.pad(after, ((0, 0), (8, room), (0, 0)))
    ends = () if inner else end_faces(intensity, sides)

    def fill(some, start):
        arrays = (side_columns,) + constants + tuple(ends)
        return list(filled_spectrum(intensity, arrays, start, some))

    given, kept = [fill(parts[:1], given_first)], []
    outer = ends
    if inner:
        given[0], late_sides = lax.optimization_barrier((given[0], sides))
        outer = end_faces(intensity, late_sides)
    kept.append(fill(parts[:1], kept_first))
    ends = outer

    marks = [rows * (m + 1) for m in range(slabs)]
    if all(start % gx == 0 for start in [pair_rows] + [part.start for part in parts]):
        weights = [jnp.asarray(cosine_table(length)[:count, marks].T) for count in counts]
    else:
        weights = [jnp.stack([kept_rows[part, m] for m in marks]) for part in parts]
    table_parts = main.reshape(gx, 2, pair_rows, half) / 6.0
    table_parts = jnp.where(core == 0, table_parts, table_parts[:, ::-1])
    table_parts = [table_parts[:, :, part] for part in parts]
    side = rim = corner = None
    values, packed, lines = 0.0, None, None
    for c, count in enumerate(counts):
        closing = c == len(counts) - 1
        if c == 1:
            behind = (given_first, kept_first), packed
            starts, packed = lax.optimization_barrier(behind)
            given.append(fill(parts[1:], starts[0]))
            kept.extend(fill([part], starts[1]) for part in parts[1:])
        flanks = [piece[1:] for piece in given + kept]
        if c > 1:
            flanks, packed = lax.optimization_barrier((flanks, packed))
        if c > 0:
            got_lines = exchanged(packed)
        if c == 1:
            behind = given[1][0], kept[1][0], got_lines
            given[1][0], kept[1][0], got_lines = lax.optimization_barrier(behind)
        if c < 2:
            got = lax.ppermute(given[c][0], "gy", swap(gy, 1))
        if c > 0:
            lines = sent_lines(got_lines, counts[c - 1], lines)
            values = values + first_axis(lines, table_parts[c - 1])
        if closing:
            given_rows = lax.dynamic_slice_in_dim(table, row * rows + given_first, pair_rows, 0)
            ordered_rows = [held_rows[part] for held_rows in (given_rows, kept_rows) for part in parts]
            ordered_rows = jnp.concatenate(ordered_rows, axis=0)
            alternate = jnp.concatenate([piece[0] for piece in flanks], axis=0) / math.sqrt(length)
            edge = [piece[1][:, : piece[0].shape[0]] for piece in flanks]
            edge = jnp.concatenate(edge, axis=1)
            edge = jnp.einsum("ba,bk->ak", edge / math.sqrt(length), table_cols, precision=HIGH)
            edge = edge + jnp.concatenate([alternate, edge[:, half:]], axis=1)
            rim = jnp.einsum("aj,ak->jk", ordered_rows[:, :half], edge[:, :half], precision=HIGH)
            corner = 2.0 * jnp.einsum("a,ak->k", ordered_rows[:, half], edge, precision=HIGH)
            corner = corner + jnp.einsum("aj,a->j", ordered_rows, edge[:, half], precision=HIGH)
            corner = jnp.pad(corner, (0, width - half - 1))

        row_table = pair_tables[1]
        if c > 0:
            row_table = rounded_parts(kept_rows[parts[c], :half].T)
        *packed, side = packed_section(
            col, kept[c][0], got, sum(counts[1:c]), pair_tables[0], row_table, weights[c],
            rim, corner, side, offsets, (gx, gy), closing,
        )
    lines = sent_lines(exchanged(packed), counts[-1], lines)
    values = values + first_axis(lines, table_parts[-1])
    side = jnp.sum(lines[:, :, 2 * counts[-1] :], axis=0) / 6.0
    turned = values.reshape(own, blocks, own, devices, width)
    turned = jnp.transpose(turned, (3, 1, 2, 0, 4))
    turned = [turned[:, b, :, :, : offsets[b + 1]] for b in range(blocks)]
    turned = lax.all_to_all(jnp.concatenate(turned, axis=3), ("gy", "gx"), 0, 0, tiled=True)
    turned = jnp.transpose(turned, (1, 2, 0, 3)).reshape(own, block, -1)

    slab = jnp.minimum(row, gx - 1 - row)
    far_row, far_col = row >= slabs, col >= gy // 2
    pick_rows = jnp.arange(rows)
    pick_rows = slab * rows + jnp.where(far_row, rows - pick_rows, pick_rows)
    pick_cols = jnp.arange(cols)
    pick_cols = jnp.where(far_col, (gy - col) * cols - pick_cols, col * cols + pick_cols)

    if rows == block:
        got, piece = [], None
        for messages in slab_messages(values, turned, side, offsets, slabs):
            if piece is not None:
                messages, piece = lax.optimization_barrier((messages, piece))
                got.append(gathered(piece, gy, got[-1] if got else None))
            piece = lax.all_to_all(messages, "gx", 0, 0, tiled=True)
        got.append(gathered(piece, gy, got[-1] if got else None))
        tiles = width // 128
        start = tile_groups(tiles)[0].stop * own * block
        side = jnp.stack([piece[:, start : start + 3 * own * tiles] for piece in got[0]])
        bit = gy // 2
        while bit:
            paired = side.reshape((-1, 2, bit) + side.shape[1:])
            side = jnp.where((col & bit) == 0, paired, paired[:, ::-1]).reshape(side.shape)
            bit //= 2
        side = side.reshape(devices, own, 3, width)
        side = jnp.transpose(side, (2, 1, 0, 3)).reshape(3, block, width)
        next_plane, across = side[0], rim_rows(side[1:], offsets, pick_rows)
        rim_col = col == gy // 2
        rim = across[:, pick_cols]
        return result_block(
            got, next_plane, across, rim, pick_cols, slab, far_row, rim_col, col, offsets
        )

    side = lax.all_gather(side, ("gy", "gx"), axis=0)
    side = jnp.transpose(side, (2, 1, 0, 3)).reshape(slabs + 1, block, width)
    across = rim_rows(side[slabs - 1 :], offsets, pick_rows)
    next_plane = lax.dynamic_index_in_dim(side, slab, 0, keepdims=False)
    sums = axis_order_sums(values, turned, offsets, block)
    messages = []
    for s in range(slabs):
        base, first = s * rows // block, s * rows
        units = []
        for b in range(blocks):
            size = (b + 1) * block
            near = jnp.zeros((own, rows, size))
            far = jnp.zeros((own, block, size))
            if b >= base:
                near = jnp.stack([sums[b][e][first : first + rows, :size] for e in range(own)])
            else:
                far = jnp.stack([sums[base][e][b * block : size, :size] for e in range(own)])
            units.append(jnp.concatenate([near, far], axis=1))
        messages.append(jnp.concatenate(units, axis=2))
    messages = jnp.stack(messages + messages[::-1])
    got = lax.all_to_all(messages, "gx", 0, 0, tiled=True)
    got = lax.all_gather(got, "gy", axis=0, tiled=True)
    got = jnp.swapaxes(got, 0, 1).reshape(block, rows + block, width)
    base = slab * rows // block
    lower = []
    for b in range(blocks):
        lanes = slice(offsets[b], offsets[b + 1])
        near = jnp.swapaxes(got[:, :rows, lanes], 0, 1)
        far = lax.dynamic_slice_in_dim(got[:, rows:, lanes], lax.rem(slab * rows, block), rows, 0)
        lower.append(jnp.where(b >= base, near, far))
    lower = jnp.concatenate(lower, axis=2)
    lower = jnp.concatenate([lower, next_plane[None]], axis=0)
    body = square([lower[:, :, offsets[b] : offsets[b + 1]] for b in range(blocks)], block)
    body = body[pick_rows - slab * rows]
    body = jnp.concatenate([body, across[:, None, :half]], axis=1)[:, pick_cols]
    body = jnp.concatenate([body, across[:, pick_cols][:, :, None]], axis=2)
    return jnp.concatenate([body, jnp.flip(body[:, :, 1:half], 2)], axis=2)


def rim_rows(side, offsets, pick_rows):
    blocks, block = len(offsets) - 1, offsets[1]
    half = blocks * block
    last = square([side[0][:, offsets[b] : offsets[b + 1]] for b in range(blocks)], block)
    rim = side[1, 0, : half + 1]
    last = jnp.concatenate([last, rim[None, :half]], axis=0)
    return jnp.concatenate([last, rim[:, None]], axis=1)[pick_rows]


def axis_order_sums(values, turned, offsets, block):
    start = 0
    sums = []
    for top in range(len(offsets) - 1):
        size = (top + 1) * block
        parts = []
        for e in range(values.shape[0]):
            part = values[e, :size, offsets[top] : offsets[top] + size]
            lower = [turned[e, :, start + offsets[b] : start + offsets[b + 1]] for b in range(top + 1)]
            parts.append(part + part.T + square(lower, block))
        sums.append(parts)
        start += offsets[top + 1]
    return sums


def message_kernel(offsets, slabs, values, turned, side, *messages):
    blocks, block = len(offsets) - 1, offsets[1]
    values, turned = values[...], turned[...]
    own = values.shape[0]
    sums = axis_order_sums(values, turned, offsets, block)
    groups = tile_groups(offsets[-1] // 128)
    side_start = groups[0].stop * own * block
    messages[0][:, side_start:] = jnp.zeros_like(messages[0][:, side_start:])
    for s in range(slabs):
        places = s, 2 * slabs - 1 - s
        for e in range(own):
            units = []
            for b in range(blocks):
                size = (b + 1) * block
                if b >= s:
                    units.append(sums[b][e][s * block : (s + 1) * block, :size])
                else:
                    units.append(sums[s][e][b * block : size, :size])
            line = jnp.concatenate(units, axis=1)
            for group, out in zip(groups, messages):
                for tile in range(group.start, group.stop):
                    start = ((tile - group.start) * own + e) * block
                    for place in places:
                        out[place, start : start + block] = line[:, tile * 128 : (tile + 1) * 128]
            row = side_start + 3 * e * groups[-1].stop
            for plane in (s, slabs - 1, slabs):
                for tile in range(groups[-1].stop):
                    part = side[e, plane : plane + 1, tile * 128 : (tile + 1) * 128]
                    for place in places:
                        messages[0][place, row : row + 1] = part
                    row += 1


def slab_messages(values, turned, side, offsets, slabs):
    own, block, tiles = values.shape[0], offsets[1], offsets[-1] // 128
    sizes = [(group.stop - group.start) * own * block for group in tile_groups(tiles)]
    sizes[0] += -(-3 * own * tiles // 8) * 8
    return pl.pallas_call(
        lambda *refs: message_kernel(offsets, slabs, *refs),
        in_specs=[pl.BlockSpec(memory_space=pltpu.VMEM)] * 3,
        out_specs=[pl.BlockSpec(memory_space=pltpu.VMEM)] * len(sizes),
        out_shape=[jax.ShapeDtypeStruct((2 * slabs, size, 128), jnp.float32) for size in sizes],
        compiler_params=pltpu.CompilerParams(vmem_limit_bytes=VMEM_BYTES),
    )(values, turned, side)


def result_kernel(
    offsets, own, devices, groups, places, next_plane, across, rim, pick, flip, *refs
):
    blocks, block = len(offsets) - 1, offsets[1]
    tiles = offsets[-1] // 128
    peers = (len(refs) - 2) // len(groups) - 1
    pieces, out = refs[: peers * len(groups)], refs[peers * len(groups)]
    held, sems = refs[peers * len(groups) + 1 : -1], refs[-1]
    step_rows, cols, length = out.shape
    half = length // 2
    slab, far_row, rim_col, me = places[0], places[1], places[2], places[3]
    lane = lax.broadcasted_iota(jnp.int32, (block, 128), 1)
    at_rim = lax.broadcasted_iota(jnp.int32, (cols, half), 0) + (1 - rim_col) == 0
    first_lane = lax.broadcasted_iota(jnp.int32, (cols, 128), 1) == 0

    @pl.when(pl.program_id(0) == 0)
    def _():
        copies = []
        for g in range(len(groups)):
            for peer in range(peers):
                piece = pieces[g * peers + peer]
                size = piece.shape[0]
                spot = pl.ds(pl.multiple_of((me ^ peer) * size, size), size)
                copies.append(pltpu.make_async_copy(piece, held[g].at[spot], sems.at[g, peer]))
        for copy in copies:
            copy.start()
        for copy in copies:
            copy.wait()

    def left_half(r, may_pass):
        t = pl.program_id(0) * step_rows + r
        i = jnp.where(far_row == 1, block - t, t)
        inside = (jnp.zeros((block, 128), jnp.int32) + i) < block
        i = jnp.minimum(i, block - 1)
        source = lax.div(i, devices), lax.rem(i, devices)
        parts = []
        for g, group in enumerate(groups):
            stride = held[g].shape[0] // devices
            for tile in range(group.start, group.stop):
                start = (tile - group.start) * own * block
                near = [
                    held[g][pl.ds(start + e * block + i, devices, stride=stride), :]
                    for e in range(own)
                ]
                near = jnp.concatenate(near, axis=0)
                line = near
                if tile * 128 < offsets[blocks - 1]:
                    far = pl.multiple_of(source[1] * stride + start + source[0] * block, 8)
                    far = held[g][pl.ds(far, block), :]
                    kind = jnp.zeros((block, 128), jnp.int32)
                    for b in range(1, blocks):
                        kind += (lane + tile * 128 >= offsets[b]).astype(jnp.int32)
                    line = jnp.where(kind >= slab, near, far)
                if may_pass:
                    line = jnp.where(inside, line, next_plane[:, pl.ds(tile * 128, 128)])
                parts.append(line)
        line = jnp.concatenate(parts, axis=1)
        plane = square([line[:, offsets[b] : offsets[b + 1]] for b in range(blocks)], block)
        high, low = split(plane)
        left = jnp.dot(pick[...], high, preferred_element_type=jnp.float32)
        left += jnp.dot(pick[...], low, preferred_element_type=jnp.float32)
        left = jnp.where(at_rim, across[pl.ds(t, 1), :], left)
        out[r, :, pl.ds(0, half)] = left
        return left

    together = 4

    @pl.loop(0, step_rows // together)
    def _(c):
        left = [left_half(c * together + n, n == 0) for n in range(together)]
        high, low = split(jnp.concatenate(left, axis=0))
        right = jnp.dot(high, flip[...], preferred_element_type=jnp.float32)
        right += jnp.dot(low, flip[...], preferred_element_type=jnp.float32)
        for n in range(together):
            r = c * together + n
            t = pl.program_id(0) * step_rows + r
            edge = pltpu.roll(rim[...], lax.rem(128 - t, 128), 1)
            part = right[n * cols : (n + 1) * cols]
            out[r, :, pl.ds(half, 128)] = jnp.where(first_lane, edge, part[:, :128])
            out[r, :, pl.ds(half + 128, half - 128)] = part[:, 128:]


def result_block(got, next_plane, across, rim, pick_cols, slab, far_row, rim_col, col, offsets):
    block = offsets[1]
    gx = got[0][0].shape[0]
    groups = tile_groups(offsets[-1] // 128)
    devices = gx * len(got[0])
    own = block // devices
    rows, half = across.shape[0], across.shape[1] - 1
    cols = pick_cols.shape[0]
    step_rows = 8
    places = jnp.stack([slab, far_row.astype(jnp.int32), rim_col.astype(jnp.int32), col])
    cell = jnp.arange(half)
    pick = (pick_cols[:, None] == cell[None, :]).astype(jnp.bfloat16)
    flip = (cell[:, None] + cell[None, :] == half).astype(jnp.bfloat16)
    rim = jnp.pad(rim.T, ((0, 0), (0, 128 - rows)))
    whole = lambda array: pl.BlockSpec(array.shape, lambda i: (0,) * array.ndim)
    arrays = (next_plane, across[:, :half], rim, pick, flip)
    pieces = [piece.reshape(-1, 128) for group in got for piece in group]
    return pl.pallas_call(
        lambda *refs: result_kernel(offsets, own, devices, groups, *refs),
        grid=(rows // step_rows,),
        in_specs=[pl.BlockSpec(memory_space=pltpu.SMEM)] + [whole(array) for array in arrays]
        + [pl.BlockSpec(memory_space=pl.ANY)] * len(pieces),
        out_specs=pl.BlockSpec((step_rows, cols, 2 * half), lambda i: (i, 0, 0)),
        out_shape=jax.ShapeDtypeStruct((rows, cols, 2 * half), jnp.float32),
        scratch_shapes=[
            pltpu.VMEM((devices * group[0].shape[1], 128), jnp.float32) for group in got
        ] + [pltpu.SemaphoreType.DMA((len(groups), len(got[0])))],
        compiler_params=pltpu.CompilerParams(vmem_limit_bytes=VMEM_BYTES),
    )(places, *arrays, *pieces)


def tile_groups(tiles):
    return [slice(tile, min(tile + 2, tiles)) for tile in range(0, tiles, 2)]


def swap(peers, bit):
    return [(q, q ^ bit) for q in range(peers)]


def gathered(piece, peers, after):
    if after is not None:
        piece, first_hops = lax.optimization_barrier((piece, after[1:3]))
        after[1:3] = first_hops
    pieces, bit = {0: piece}, peers // 2
    while bit:
        for place in list(pieces):
            pieces[place ^ bit] = lax.ppermute(pieces[place], "gy", swap(peers, bit))
        bit //= 2
    return [pieces[place] for place in range(peers)]


def exchanged(packed):
    gy = len(packed)
    return [packed[0]] + [lax.ppermute(packed[p], "gy", swap(gy, p)) for p in range(1, gy)]


def sent_lines(got, count, after):
    gy = len(got)
    lines = [sum(got[p][:count] for p in range(first, gy, 2)) for first in range(2)]
    lines = jnp.concatenate(lines + [sum(piece[count:] for piece in got)], axis=0)
    lines = jnp.transpose(lines, (2, 1, 0, 3))
    if after is not None:
        lines, _ = lax.optimization_barrier((lines, after))
    return lax.all_to_all(lines, "gx", 0, 0, tiled=True)


def first_axis(lines, table):
    gx, _, count, half = table.shape
    table = table.reshape(gx, 2 * count, half)
    return jnp.einsum("geaw,gai->eiw", lines[:, :, : 2 * count], table, precision=HIGH)


def row_parts(rows):
    if rows < 4 * PART_STEP:
        return [slice(0, rows)]
    return [slice(PART_STEP, rows - PART_STEP), slice(0, PART_STEP), slice(rows - PART_STEP, rows)]


def square(lower, block):
    if len(lower) == 1:
        return lower[0]
    split_at = len(lower) // 2
    size = split_at * block
    first = square(lower[:split_at], block)
    corner = jnp.concatenate([line[..., :size] for line in lower[split_at:]], axis=-2)
    last = square([line[..., size:] for line in lower[split_at:]], block)
    top = jnp.concatenate([first, jnp.swapaxes(corner, -1, -2)], axis=-1)
    return jnp.concatenate([top, jnp.concatenate([corner, last], axis=-1)], axis=-2)


def solution(mesh):
    placed = (P("gx", "gy", None), P())
    return jax.shard_map(
        on_device, mesh=mesh, in_specs=placed, out_specs=P("gx", "gy", None), check_vma=False
    )
```
